32 devices in a mesh: section: 4 (over y, x), dp: 8 (over z, core).
Axes of the slice: x: 2, y: 2, z: 4, core: 2. Of those that a mesh axis runs over, the one named last changes fastest.
Arguments:
- codes: int32 [16, 264], P('dp'), may hold values from 0 to 16383
- labels: int32 [16, 264], P('dp'), may hold values from 0 to 16383
- picks: int32 [16, 32], P('dp'), may hold values from 0 to 263
- classes: int32 [16, 3], P('dp'), may hold values from 0 to 999
- null_mask: int32 [16, 3], P('dp'), may hold values 0 or 1
- starts: int32 [16, 4], P('dp'), may hold values from 0 to 264, as said below
- master: float32 [69632, 768], P(('section', 'dp'))
- momentum: float32 [69632, 768], P(('section', 'dp'))
- average: float32 [69632, 768], P(('section', 'dp'))
Outputs:
- loss_sum: float32 [], replicated
- token_count: float32 [], replicated
- grad_norm: float32 [], replicated
- new_master: float32 [69632, 768], P(('section', 'dp'))
- new_momentum: float32 [69632, 768], P(('section', 'dp'))
- new_average: float32 [69632, 768], P(('section', 'dp'))
The draws below stay inside these ranges and needn't reach their ends.
Inputs may be any that keep to these rules, and one draw needn't show every extreme that they name: In each row starts[r,0] = 0, the columns do not fall, and the last column is the row's live length; every segment but the first and last of a row holds 257 slots; the last row's live length is 264.
All inputs are finite; a program needn't handle non-finite values. No bound on the sum of `null_mask` on one device may be relied on, other than what follows from the above.
Results may differ from the reference program's by a relative error of at most 0.024.
The reference program's roundings to bfloat16 on the way count: a program that leaves them out, or rounds other values in their place, can miss the bound.
Values may be sent and summed in bfloat16 or wider, within the bound.
A program may use at most 768 MiB of HBM per device.

```python
import math
import jax
import jax.numpy as jnp
from jax import lax

D = 768
HEADS = 12
HD = 64
FF = 2048
VOCAB = 16384
CLASSES = 1001
SLOTS = 264
PICKS = 32
IMG = 257
SEGS = 3
ROWS = 16
P_ROWS = 17408
N_SECTION = 4


def layered_values(key):
    total_rows = 4 * P_ROWS
    normal_part = jax.random.normal(jax.random.fold_in(key, 11), (total_rows, D), jnp.float32)
    noise_all = normal_part
    row_ids = jnp.arange(total_rows)[:, None]
    section_ids = row_ids // P_ROWS
    local_row = row_ids % P_ROWS
    column = jnp.arange(D, dtype=jnp.float32)[None, :]
    rising = (0.6 + 1.2 * column / (D - 1)) * (1.0 + 0.1 * noise_all)
    offset_rows = 4 * D
    layer_scale = jnp.where(local_row < 3 * D, D ** (-0.5), jnp.where(local_row < offset_rows, math.sqrt(max(IMG // 4, 1) / D), jnp.where(local_row < offset_rows + 2 * FF, D ** (-0.5), jnp.where(local_row < offset_rows + 3 * FF, FF ** (-0.5), D ** (-0.5)))))
    is_gain = (local_row >= offset_rows + 3 * FF) & (local_row < offset_rows + 3 * FF + 2)
    layer_part = jnp.where(is_gain, rising, layer_scale * noise_all)
    embed_part = D ** (-0.5) * noise_all
    head_part = jnp.where(local_row == VOCAB, rising, jnp.where(local_row < VOCAB, 1.5 * D ** (-0.5), D ** (-0.5)) * noise_all)
    return jnp.where(section_ids == 0, embed_part, jnp.where(section_ids == 3, head_part, layer_part))


def draw_master(key, part):
    return layered_values(key)


def draw_average(key, part):
    shared = layered_values(key)
    key = jax.random.fold_in(key, 7)
    own_part = layered_values(key)
    return 0.5 * shared + 0.85 * own_part


def draw_momentum(key, part):
    key = jax.random.fold_in(key, 5)
    shape_all = (4 * P_ROWS, D)
    step_size = 0.15 / math.sqrt(4 * P_ROWS * D)
    sign_pick = jnp.where(jax.random.bernoulli(key, 0.5, shape_all), 1.0, -1.0)
    factor = jnp.exp(jax.random.uniform(jax.random.fold_in(key, 1), shape_all, jnp.float32, math.log(0.5), math.log(2.0)))
    return sign_pick * step_size * factor


def draw_starts(key, part):
    key = jax.random.fold_in(key, 3)
    row_ids = jnp.arange(ROWS, dtype=jnp.int32)
    span_rows = SLOTS - SLOTS // 3
    jitter = jax.random.randint(key, (ROWS,), 0, SLOTS // 12 + 1)
    live_end = SLOTS // 3 + span_rows * row_ids // max(ROWS - 1, 1) - jnp.where(row_ids < ROWS - 1, jitter, 0)
    shift_in = jax.random.randint(jax.random.fold_in(key, 1), (ROWS, 1), 0, IMG)
    middle = jnp.minimum(jnp.arange(1, SEGS, dtype=jnp.int32)[None, :] * IMG - shift_in, live_end[:, None])
    return jnp.concatenate([jnp.zeros((ROWS, 1), jnp.int32), middle.astype(jnp.int32), live_end[:, None].astype(jnp.int32)], axis=1)


def touch_ends(entries, stream_key, least, largest):
    longest = entries.shape.index(max(entries.shape))
    spots = []
    for shift in (0, 1):
        where = [jax.random.randint(jax.random.fold_in(stream_key, axis), (), 0, length) for axis, length in enumerate(entries.shape)]
        where[longest] = (where[longest] + shift) % entries.shape[longest]
        spots.append(tuple(where))
    return entries.at[spots[0]].set(least).at[spots[1]].set(largest)


def setup_inputs(seed: int = 0) -> dict:
    key_list = jax.random.split(jax.random.key(seed), 10)
    return {
        "codes": touch_ends(jax.random.randint(key_list[0], (ROWS, SLOTS), 0, VOCAB), jax.random.fold_in(key_list[0], 1), 0, VOCAB - 1).astype(jnp.int32),
        "labels": touch_ends(jax.random.randint(key_list[1], (ROWS, SLOTS), 0, VOCAB), jax.random.fold_in(key_list[1], 1), 0, VOCAB - 1).astype(jnp.int32),
        "picks": touch_ends(jax.random.randint(key_list[2], (ROWS, PICKS), 0, SLOTS), jax.random.fold_in(key_list[2], 1), 0, SLOTS - 1).astype(jnp.int32),
        "classes": touch_ends(jax.random.randint(key_list[3], (ROWS, SEGS), 0, CLASSES - 1), jax.random.fold_in(key_list[3], 1), 0, (CLASSES - 1) - 1).astype(jnp.int32),
        "null_mask": touch_ends((jax.random.randint(key_list[4], (ROWS, SEGS), 0, 10) < 1).astype(jnp.int32), jax.random.fold_in(key_list[4], 1), 0, 1),
        "starts": draw_starts(jax.random.fold_in(key_list[9], 71), 0),
        "master": draw_master(jax.random.fold_in(key_list[9], 71), 0),
        "momentum": draw_momentum(jax.random.fold_in(key_list[9], 71), 0),
        "average": draw_average(jax.random.fold_in(key_list[9], 71), 0),
    }


highest = lax.Precision.HIGHEST
rope_base = 10000.0
clip_limit = 1.0
rate_factor = 0.25
momentum_decay = 0.9
average_decay = 0.8
norm_eps = 1e-06

@jax.custom_vjp
def low(v):
    return lax.optimization_barrier(v.astype(jnp.bfloat16)).astype(jnp.float32)

@jax.custom_vjp
def low_back(v):
    return v

def low_keep(v):
    return (low(v), None)

def low_pass(kept, grad):
    return (grad,)

def back_keep(v):
    return (v, None)

def back_low(kept, grad):
    return (low(grad),)
low.defvjp(low_keep, low_pass)
low_back.defvjp(back_keep, back_low)

def boundary(value_in):
    return low_back(low(value_in))

def matmul_hi(left, right):
    return jnp.dot(left, right, precision=highest, preferred_element_type=jnp.float32)

def matmul_cols(left, right):
    return lax.dot_general(left, right, (((1,), (1,)), ((), ())), precision=highest, preferred_element_type=jnp.float32)

def rms_scale(value_in, gain):
    return value_in * lax.rsqrt(lax.optimization_barrier(jnp.mean(value_in * value_in, axis=-1, keepdims=True)) + 1e-06) * gain

def rotate(value_in, cosine, sine_part):
    half_size = value_in.shape[-1] // 2
    first_half = value_in[..., :half_size]
    second_half = value_in[..., half_size:]
    return jnp.concatenate([first_half * cosine - second_half * sine_part, second_half * cosine + first_half * sine_part], axis=-1)

def row_layout(starts_row, classes_row, null_row, codes_row):
    slot_ids = jnp.arange(SLOTS, dtype=jnp.int32)
    segment = lax.optimization_barrier(jnp.sum((starts_row[None, 1:] <= slot_ids[:, None]).astype(jnp.int32), axis=1)).astype(jnp.int32)
    seg_start = jnp.take(starts_row, segment)
    position = slot_ids - seg_start
    live_end = starts_row[SEGS]
    is_first = (position == 0) & (slot_ids < live_end)
    clamped = jnp.minimum(segment, SEGS - 1)
    class_row = jnp.where(jnp.take(null_row, clamped) > 0, CLASSES - 1, jnp.take(classes_row, clamped))
    row_index = jnp.where(is_first, VOCAB + class_row, codes_row).astype(jnp.int32)
    following = jnp.concatenate([segment[1:], jnp.full((1,), SEGS + 1, jnp.int32)])
    counted = (following == segment) & (slot_ids + 1 < live_end)
    allowed = (segment[:, None] == segment[None, :]) & (slot_ids[None, :] <= slot_ids[:, None])
    frequency = rope_base ** (-jnp.arange(HD // 2, dtype=jnp.float32) * 2.0 / HD)
    angles = position.astype(jnp.float32)[:, None] * frequency[None, :]
    return (row_index, counted, allowed, jnp.cos(angles)[:, None, :], jnp.sin(angles)[:, None, :])

def layer_forward(stream, weights, cosine, sine_part, allowed):
    offset_rows = 4 * D
    w_query = weights[:D]
    w_key = weights[D:2 * D]
    w_value = weights[2 * D:3 * D]
    w_out = weights[3 * D:4 * D]
    w_gate = weights[offset_rows:offset_rows + FF]
    w_up = weights[offset_rows + FF:offset_rows + 2 * FF]
    w_down = weights[offset_rows + 2 * FF:offset_rows + 3 * FF]
    gain_attn = weights[offset_rows + 3 * FF]
    gain_mlp = weights[offset_rows + 3 * FF + 1]
    normed_a = low(rms_scale(stream, gain_attn))
    query_raw = low_back(matmul_hi(normed_a, w_query)).reshape(SLOTS, HEADS, HD)
    key_raw = low_back(matmul_hi(normed_a, w_key)).reshape(SLOTS, HEADS, HD)
    query_rows = low(rotate(query_raw, cosine, sine_part) * HD ** (-0.5))
    key_rows = low(rotate(key_raw, cosine, sine_part))
    value_rows = low(low_back(matmul_hi(normed_a, w_value))).reshape(SLOTS, HEADS, HD)
    scores = low_back(jnp.einsum('qhd,khd->hqk', query_rows, key_rows, precision=highest))
    attn_probs = low(jax.nn.softmax(jnp.where(allowed[None], scores, -1e+30), axis=-1))
    attn_mixed = low(low_back(jnp.einsum('hqk,khd->qhd', attn_probs, value_rows, precision=highest))).reshape(SLOTS, D)
    hidden = stream + low_back(matmul_hi(attn_mixed, w_out))
    normed_b = low(rms_scale(hidden, gain_mlp))
    gate_proj = low_back(matmul_cols(normed_b, w_gate))
    up_proj = low_back(matmul_cols(normed_b, w_up))
    inner_act = low(jax.nn.silu(gate_proj) * up_proj)
    return hidden + matmul_hi(inner_act, w_down)

def head_loss(stream, weights, labels_row, counted, picks_row):
    picked = jnp.take(stream, picks_row, axis=0)
    normed = low(rms_scale(picked, weights[VOCAB]))
    logits = low_back(matmul_cols(normed, weights[:VOCAB]))
    log_total = jax.nn.logsumexp(logits, axis=-1)
    picked_labels = jnp.take(labels_row, picks_row)
    target = jnp.take_along_axis(logits, picked_labels[:, None], axis=1)[:, 0]
    picked_counted = jnp.take(counted, picks_row)
    loss_row = jnp.sum(jnp.where(picked_counted, log_total - target, 0.0))
    return (loss_row, jnp.sum(picked_counted.astype(jnp.float32)))

def row_objective(lowered, codes_row, labels_row, picks_row, classes_row, null_row, starts_row):
    row_index, counted, allowed, cosine, sine_part = row_layout(starts_row, classes_row, null_row, codes_row)
    stream = boundary(jnp.take(lowered[0], row_index, axis=0) * math.sqrt(D))
    for layer_num in range(N_SECTION - 2):
        stream = boundary(layer_forward(stream, lowered[layer_num + 1], cosine, sine_part, allowed))
    return head_loss(stream, lowered[N_SECTION - 1], labels_row, counted, picks_row)

def reference(codes, labels, picks, classes, null_mask, starts, master, momentum, average):
    lowered = low(master).reshape(N_SECTION, P_ROWS, D)
    learn_rate = rate_factor * math.sqrt(N_SECTION * P_ROWS)

    def one_row(carry, row_data):
        grad_acc, loss_acc, count_acc = carry
        loss_row, pull_back, count_row = jax.vjp(lambda weights: row_objective(weights, *row_data), lowered, has_aux=True)
        grad_row, = pull_back(jnp.ones((), jnp.float32))
        return ((grad_acc + grad_row, loss_acc + loss_row, count_acc + count_row), None)
    start_carry = (jnp.zeros_like(lowered), jnp.zeros((), jnp.float32), jnp.zeros((), jnp.float32))
    (grad_acc, loss_sum, token_count), _ = lax.scan(one_row, start_carry, (codes, labels, picks, classes, null_mask, starts))
    grad_all = grad_acc.reshape(N_SECTION * P_ROWS, D)
    grad_norm = jnp.sqrt(jnp.sum(grad_all * grad_all))
    clipped = grad_all * jnp.minimum(1.0, clip_limit / (grad_norm + norm_eps))
    new_momentum = momentum_decay * momentum + clipped
    new_master = master - learn_rate * (clipped + momentum_decay * new_momentum)
    new_average = average_decay * average + (1.0 - average_decay) * new_master
    return (loss_sum, token_count, grad_norm, new_master, new_momentum, new_average)
```

```python
import functools
import math

import jax
import jax.numpy as jnp
from jax import lax
from jax.experimental import pallas as pl
from jax.experimental.pallas import tpu as pltpu
from jax.sharding import PartitionSpec as P

D = 768
HEADS = 12
HD = 64
FF = 2048
VOCAB = 16384
CLASSES = 1001
SLOTS = 264
SP = 272
PICKS = 32
SEGS = 3
MATS = 4 * D + 3 * FF
WROWS = 9232

F32 = jnp.float32
BF16 = jnp.bfloat16

rope_base = 10000.0
clip_limit = 1.0
rate_factor = 0.25
momentum_decay = 0.9
average_decay = 0.8
norm_eps = 1e-06


def nn(left, right):
    return jnp.dot(left, right, preferred_element_type=F32)


def tn(left, right):
    return lax.dot_general(left, right, (((0,), (0,)), ((), ())), preferred_element_type=F32)


def nt(left, right):
    return lax.dot_general(left, right, (((1,), (1,)), ((), ())), preferred_element_type=F32)


def rms_scale(value_in, gain):
    return (
        value_in * lax.rsqrt(jnp.mean(value_in * value_in, axis=-1, keepdims=True) + norm_eps) * gain
    )


def rms_pull(value_in, gain, grad):
    inv = lax.rsqrt(jnp.mean(value_in * value_in, axis=-1, keepdims=True) + norm_eps)
    unit = value_in * inv
    scaled = grad * gain
    grad_in = inv * (scaled - unit * jnp.mean(scaled * unit, axis=-1, keepdims=True))
    return grad_in, jnp.sum(grad * unit, axis=0)


def row_layout(starts_row, classes_row, null_row, codes_row):
    slot_ids = jnp.arange(SLOTS, dtype=jnp.int32)
    segment = jnp.sum((starts_row[None, 1:] <= slot_ids[:, None]).astype(jnp.int32), axis=1)
    seg_start = jnp.sum(
        jnp.where(segment[:, None] == jnp.arange(SEGS + 1)[None, :], starts_row[None, :], 0), axis=1
    )
    position = slot_ids - seg_start
    live_end = starts_row[SEGS]
    is_first = (position == 0) & (slot_ids < live_end)
    clamped = jnp.minimum(segment, SEGS - 1)
    hit = clamped[:, None] == jnp.arange(SEGS)[None, :]
    class_row = jnp.sum(
        jnp.where(hit, jnp.where(null_row > 0, CLASSES - 1, classes_row)[None, :], 0), axis=1
    )
    row_index = jnp.where(is_first, VOCAB + class_row, codes_row)
    following = jnp.concatenate([segment[1:], jnp.full((1,), SEGS + 1, jnp.int32)])
    counted = (following == segment) & (slot_ids + 1 < live_end)
    return row_index, counted, segment, position


MESH = pl.DeviceIdType.MESH
ANY = pl.BlockSpec(memory_space=pl.ANY)
VMEM = pl.BlockSpec(memory_space=pltpu.VMEM)

HALF = 1088
CH = 64
NCH = HALF // CH
CC = 48
NCC = 11
LANE = 4 * HALF
LAG = 2
WINDOW = 2
HOP = 3


def place():
    sec = lax.axis_index("section")
    dp = lax.axis_index("dp")
    z = dp // 2
    c = lax.rem(dp, 2)
    par = lax.rem(sec, 2)
    home = jnp.logical_or(sec == 1, sec == 2)
    return sec, dp, z, c, par, home


def greet_neighbours(sec, dp, z, c, par):
    barrier = pltpu.get_barrier_semaphore()

    def greet(s, e):
        pl.semaphore_signal(barrier, 1, device_id=(s, e), device_id_type=MESH)

    greet(sec, dp + 1 - 2 * c)
    greet(sec + 1 - 2 * par, dp)
    pl.when(z > 0)(lambda: greet(sec, dp - 2))
    pl.when(z < 3)(lambda: greet(sec, dp + 2))
    pl.semaphore_wait(barrier, 2 + (z > 0).astype(jnp.int32) + (z < 3).astype(jnp.int32))


def hop_targets(sec, dp, c, par):
    return {
        "up": (sec, dp + 2),
        "down": (sec, dp - 2),
        "x": (sec + 1 - 2 * par, dp),
        "core": (sec, dp + 1 - 2 * c),
    }


HOPS = ("up", "down", "x", "core")


def tree(z, c, home):
    both = jnp.logical_and
    either = jnp.logical_or
    far = z >= 2
    mid = both(z >= 1, z <= 2)
    never = z < 0
    out = []
    for block in (0, 1):
        for half in (0, 1):
            mine = home if half == 0 else jnp.logical_not(home)
            other = jnp.logical_not(mine)
            source = both(z == block, home)
            at_owner_col = both(z == block, jnp.logical_not(home))
            if block == 0:
                sends = dict(up=either(z == 0, both(mid, mine)), down=never)
                from_up = never
            else:
                sends = dict(up=both(mid, mine), down=z == 1)
                from_up = z == 0
            sends["x"] = either(source, both(far, mine))
            from_x = either(at_owner_col, both(far, other))
            from_down = jnp.logical_not(either(source, either(from_x, from_up)))
            aside = 1 - home.astype(jnp.int32)
            turn = jnp.logical_and(far, other).astype(jnp.int32) + far.astype(jnp.int32) * half
            near = 1 - far.astype(jnp.int32)
            depth = jnp.abs(z - block) + near * aside + turn
            out.append((source, sends, dict(up=from_up, down=from_down, x=from_x), depth))
    lane0 = c == 0
    source = both(both(z == 2, home), lane0)
    sends = dict(
        up=both(z == 2, lane0),
        down=both(mid, lane0),
        x=source,
        core=lane0,
    )
    parents = dict(
        up=both(z <= 1, lane0),
        down=both(z == 3, lane0),
        x=both(both(z == 2, jnp.logical_not(home)), lane0),
    )
    depth = jnp.abs(z - 2) + 1 - home.astype(jnp.int32)
    out.append((source, sends, parents, depth))
    return out


def open_kernel(
    table, index, out, x0, own_sem, recv_sem, recv_c, core_sem, send_sem,
    sent, mine, rx_core, rx_up, rx_down, swap_send, swap_recv, x_send, x_recv, line_send,
    up_recv, down_recv,
):
    sec, dp, z, c, par, home = place()
    targets = hop_targets(sec, dp, c, par)
    classes = tree(z, c, home)
    greet_neighbours(sec, dp, z, c, par)

    def keep(rows):
        return pltpu.make_async_copy(
            table.at[pl.ds(0, rows)],
            out.at[pl.ds(pl.multiple_of(dp * 2 * HALF, 16), rows)],
            own_sem,
        )

    def keep_all():
        keep(2 * HALF).start()
        keep(2 * HALF).wait()

    def keep_few():
        keep(NCC * CC).start()
        keep(NCC * CC).wait()

    pl.when(jnp.logical_and(home, z < 2))(keep_all)
    pl.when(classes[4][0])(keep_few)

    def base(k, lane):
        if k == 4:
            return 4 * 2 * HALF
        return 2 * HALF * (2 * (k // 2) + lane) + HALF * (k % 2)

    def copy(k, hop, j, rows, recv, slot):
        part = out.at[pl.ds(pl.multiple_of(base(k, c) + j * rows, 16), rows)]
        return pltpu.make_async_remote_copy(
            src_ref=part,
            dst_ref=part,
            send_sem=send_sem.at[k, HOPS.index(hop), slot],
            recv_sem=recv,
            device_id=targets[hop],
            device_id_type=MESH,
        )

    def piece(k, j, rows):
        source, sends, _, _ = classes[k]
        recv = recv_c.at[j] if k == 4 else recv_sem.at[k, j]
        slot = lax.rem(j, WINDOW)

        def send(hop):
            to = core_sem.at[k] if hop == "core" else recv
            one = copy(k, hop, j, rows, to, slot)
            pl.when(j >= WINDOW)(one.wait_send)
            one.start()

        pl.when(jnp.logical_not(source))(copy(k, "x", j, rows, recv, slot).wait_recv)
        for hop in HOPS[:3]:
            pl.when(sends[hop])(lambda hop=hop: send(hop))
        send("core")

    def counts(k):
        return (NCC, CC) if k == 4 else (NCH, CH)

    first = sec == 0
    second = sec == 1

    def slot(k):
        return pl.ds(pl.multiple_of(k * SP, 16), SP)

    def order(i):
        low = (z <= 1).astype(jnp.int32)
        return low * (3 - i) + (1 - low) * i

    def swap(k):
        return pltpu.make_async_remote_copy(
            src_ref=sent.at[slot(k)],
            dst_ref=rx_core.at[slot(k)],
            send_sem=swap_send,
            recv_sem=swap_recv.at[k],
            device_id=targets["core"],
            device_id_type=MESH,
        )

    def cross(zz):
        return pltpu.make_async_remote_copy(
            src_ref=mine.at[slot(4 + zz)],
            dst_ref=mine.at[slot(zz)],
            send_sem=x_send,
            recv_sem=x_recv.at[zz],
            device_id=targets["x"],
            device_id_type=MESH,
        )

    def go_up(zz):
        return pltpu.make_async_remote_copy(
            src_ref=mine.at[slot(zz)],
            dst_ref=rx_down.at[slot(zz)],
            send_sem=line_send,
            recv_sem=down_recv.at[zz],
            device_id=targets["up"],
            device_id_type=MESH,
        )

    def go_down(zz):
        return pltpu.make_async_remote_copy(
            src_ref=mine.at[slot(zz)],
            dst_ref=rx_up.at[slot(zz)],
            send_sem=line_send,
            recv_sem=up_recv.at[zz],
            device_id=targets["down"],
            device_id_type=MESH,
        )

    def add(k, ref):
        there = slot(k)
        mine[there, :] = (mine[there, :].astype(F32) + ref[there, :].astype(F32)).astype(BF16)

    def look(row):
        local = index[pl.ds(pl.multiple_of(row * SP, 16), SP), :]
        ids = lax.broadcasted_iota(jnp.int32, (SP, 2 * HALF), 1)
        onehot = jnp.where(ids == local, 1.0, 0.0).astype(BF16)
        return (nn(onehot, table[...]) * math.sqrt(D)).astype(BF16)

    def lookup(i):
        b = i // 2
        zz = order(b // 2)
        p = 1 - lax.rem(b, 2)
        k = 4 * p + zz

        def for_other():
            sent[slot(k), :] = look(2 * (2 * zz + 1 - c) + p)
            swap(k).start()

        def for_self():
            mine[slot(k), :] = look(2 * (2 * zz + c) + p)
            swap(k).wait_recv()
            add(k, rx_core)
            pl.when(p == 1)(lambda: cross(zz).start())

        pl.when(lax.rem(i, 2) == 0)(for_other)
        pl.when(lax.rem(i, 2) == 1)(for_self)

    def chain(zz):
        def from_below():
            go_up(zz).wait_recv()
            add(zz, rx_down)

        def from_above():
            go_down(zz).wait_recv()
            add(zz, rx_up)

        pl.when(second)(cross(zz).wait_recv)
        pl.when(jnp.logical_and(zz >= z, z > 0))(from_below)
        pl.when(jnp.logical_and(zz <= z, z < 3))(from_above)
        pl.when(zz > z)(lambda: go_up(zz).start())
        pl.when(zz < z)(lambda: go_down(zz).start())

    def chains(i):
        for o in range(4):
            zz = order(o)
            hops = jnp.maximum(
                z * (zz >= z).astype(jnp.int32), (3 - z) * (zz <= z).astype(jnp.int32)
            )
            pl.when(i == 4 * o + 3 + 2 * sec + HOP * hops)(lambda zz=zz: chain(zz))

    def step(i, carry):
        for k in range(5):
            count, rows = counts(k)
            j = i - LAG * classes[k][3]
            now = jnp.logical_and(j >= 0, j < count)
            if k == 4:
                now = jnp.logical_and(now, c == 0)
            pl.when(now)(lambda k=k, j=j, rows=rows: piece(k, j, rows))
        pl.when(jnp.logical_and(first, i < 16))(lambda: lookup(i))
        pl.when(sec < 2)(lambda: chains(i))
        return carry

    lax.fori_loop(0, max(NCH + 5 * LAG, 12 + 3 + 2 + 3 * HOP + 1), step, 0)

    def blocks(count, sem):
        return pltpu.make_async_remote_copy(
            src_ref=mine.at[pl.ds(0, count * SP)],
            dst_ref=mine.at[pl.ds(0, count * SP)],
            send_sem=sem,
            recv_sem=sem,
            device_id=targets["core"],
            device_id_type=MESH,
        )

    def finish():
        x0[...] = mine[slot(z), :]
        blocks(3, line_send).wait_send()

    def none():
        x0[...] = jnp.zeros_like(x0)

    def sent_first():
        blocks(8, swap_send).wait_send()
        blocks(4, x_send).wait_send()

    pl.when(first)(sent_first)
    pl.when(sec < 2)(finish)
    pl.when(sec >= 2)(none)

    def drain(k):
        count, rows = counts(k)
        _, sends, _, _ = classes[k]
        for j in range(count - WINDOW, count):
            for hop in HOPS[:3]:
                one = copy(k, hop, j, rows, core_sem.at[k], j % WINDOW)
                pl.when(sends[hop])(one.wait_send)
            copy(k, "core", j, rows, core_sem.at[k], j % WINDOW).wait_send()

    def came(k):
        count, rows = counts(k)
        part = out.at[pl.ds(pl.multiple_of(base(k, 1 - c), 16), count * rows)]
        pltpu.make_async_remote_copy(
            src_ref=part,
            dst_ref=part,
            send_sem=send_sem.at[k, 3, 0],
            recv_sem=core_sem.at[k],
            device_id=targets["core"],
            device_id_type=MESH,
        ).wait_recv()

    for k in range(4):
        drain(k)
        came(k)
    pl.when(c == 0)(lambda: drain(4))
    pl.when(c == 1)(lambda: came(4))


def gather_and_embed(table, index):
    rows = lambda n: pltpu.VMEM((n * SP, D), BF16)
    return pl.pallas_call(
        open_kernel,
        out_shape=(
            jax.ShapeDtypeStruct((WROWS, D), BF16),
            jax.ShapeDtypeStruct((SP, D), BF16),
        ),
        in_specs=[VMEM, VMEM],
        out_specs=(VMEM, VMEM),
        scratch_shapes=[
            pltpu.SemaphoreType.DMA,
            pltpu.SemaphoreType.DMA((4, NCH)),
            pltpu.SemaphoreType.DMA((NCC,)),
            pltpu.SemaphoreType.DMA((5,)),
            pltpu.SemaphoreType.DMA((5, 4, WINDOW)),
            rows(8),
            rows(8),
            rows(8),
            rows(4),
            rows(4),
            pltpu.SemaphoreType.DMA,
            pltpu.SemaphoreType.DMA((8,)),
            pltpu.SemaphoreType.DMA,
            pltpu.SemaphoreType.DMA((4,)),
            pltpu.SemaphoreType.DMA,
            pltpu.SemaphoreType.DMA((4,)),
            pltpu.SemaphoreType.DMA((4,)),
        ],
        compiler_params=pltpu.CompilerParams(
            collective_id=0, has_side_effects=True, vmem_limit_bytes=56 * 2**20
        ),
        name="gather_and_embed",
    )(table, index)


def close_kernel(
    grads, start, block, index, out, squares, loc, rx_core, rx_up, rx_down, rx_x, total, summed,
    all_dx, load_sem, core_sem, core_c, recv_sem, recv_c, core_send, send_sem, out_sem,
    dx_own, dx_send, line_recv, cross_recv, dx_core_send, dx_core_recv,
):
    sec, dp, z, c, par, home = place()
    targets = hop_targets(sec, dp, c, par)
    classes = tree(z, c, home)
    rx = dict(up=rx_up, down=rx_down, x=rx_x)
    del start

    def base(k, lane):
        if k == 4:
            return 4 * 2 * HALF
        return 2 * HALF * (2 * (k // 2) + lane) + HALF * (k % 2)

    def held(k):
        return k * HALF

    def load(k):
        rows = NCC * CC if k == 4 else HALF
        return pltpu.make_async_copy(
            grads.at[pl.ds(pl.multiple_of(base(k, c), 16), rows)],
            loc.at[pl.ds(held(k), rows)],
            load_sem.at[k],
        )

    for k in range(5):
        load(k).start()
    greet_neighbours(sec, dp, z, c, par)

    def to_core(k, j, rows):
        sem = core_c.at[j] if k == 4 else core_sem.at[k, j]
        return pltpu.make_async_remote_copy(
            src_ref=grads.at[pl.ds(pl.multiple_of(base(k, 1 - c) + j * rows, 16), rows)],
            dst_ref=rx_core.at[pl.ds(pl.multiple_of(held(k) + j * rows, 16), rows)],
            send_sem=core_send.at[k],
            recv_sem=sem,
            device_id=targets["core"],
            device_id_type=MESH,
        )

    def start_core(j, carry):
        for k in range(4):
            to_core(k, j, CH).start()
        pl.when(jnp.logical_and(j < NCC, c == 1))(lambda: to_core(4, j, CC).start())
        return carry

    lax.fori_loop(0, NCH, start_core, 0)
    for k in range(5):
        load(k).wait()

    def onward(k, hop, j, rows):
        back = dict(up="down", down="up", x="x")[hop]
        index = ("up", "down", "x").index(back)
        part = pl.ds(pl.multiple_of(held(k) + j * rows, 16), rows)
        return pltpu.make_async_remote_copy(
            src_ref=loc.at[part],
            dst_ref=rx[back].at[part],
            send_sem=send_sem.at[k],
            recv_sem=recv_c.at[index, j] if k == 4 else recv_sem.at[index, k, j],
            device_id=targets[hop],
            device_id_type=MESH,
        )

    def landed(k, hop, j, rows):
        index = ("up", "down", "x").index(hop)
        part = pl.ds(pl.multiple_of(held(k) + j * rows, 16), rows)
        return pltpu.make_async_remote_copy(
            src_ref=loc.at[part],
            dst_ref=rx[hop].at[part],
            send_sem=send_sem.at[k],
            recv_sem=recv_c.at[index, j] if k == 4 else recv_sem.at[index, k, j],
            device_id=targets[hop],
            device_id_type=MESH,
        )

    def write_out(k, j, rows):
        offset = j * rows if k == 4 else HALF * (k % 2) + j * rows
        part = pl.ds(pl.multiple_of(offset, 16), rows)
        return pltpu.make_async_copy(total.at[part], out.at[part], out_sem)

    def start_of(k, j, rows):
        part = pl.ds(pl.multiple_of(held(k) + j * rows, 16), rows)
        to_core(k, j, rows).wait_recv()
        acc = summed.at[pl.ds(0, rows)]
        acc[...] = loc[part, :].astype(F32) + rx_core[part, :].astype(F32)
        return part, acc

    def gathered(k, j, rows):
        part, acc = start_of(k, j, rows)
        for hop in HOPS[:3]:

            def add(hop=hop):
                landed(k, hop, j, rows).wait_recv()
                acc[...] += rx[hop][part, :].astype(F32)

            pl.when(classes[k][1][hop])(add)
        return part, acc

    def pass_on(k, j, rows, part, acc):
        loc[part, :] = acc[...].astype(BF16)
        for hop in HOPS[:3]:
            pl.when(classes[k][2][hop])(lambda hop=hop: onward(k, hop, j, rows).start())

    def relay(k, j, rows):
        part, acc = gathered(k, j, rows)
        pass_on(k, j, rows, part, acc)

    def finish(k, j, rows):
        _, acc = gathered(k, j, rows)
        offset = j * rows if k == 4 else HALF * (k % 2) + j * rows
        value = acc[...]
        total[pl.ds(pl.multiple_of(offset, 16), rows), :] = value
        write_out(k, j, rows).start()
        count_squares(value)

    first = sec == 0
    second = sec == 1
    in_line = sec < 2
    both = jnp.logical_and

    def dx_part(p, zz):
        return all_dx.at[pl.ds(pl.multiple_of((2 * (2 * zz + c) + p) * SP, 16), SP)]

    def move(p, zz, send, recv, target):
        return pltpu.make_async_remote_copy(
            src_ref=dx_part(p, zz),
            dst_ref=dx_part(p, zz),
            send_sem=send,
            recv_sem=recv,
            device_id=target,
            device_id_type=MESH,
        )

    def line(zz, hop):
        return move(par, zz, dx_send, line_recv.at[zz], targets[hop])

    def cross(zz):
        return move(1, zz, dx_send, cross_recv.at[zz], targets["x"])

    def dx_to_core(p, zz):
        return move(p, zz, dx_core_send, dx_core_recv, targets["core"])

    def aside(zz):
        pl.when(first)(lambda: dx_to_core(0, zz).start())
        pl.when(second)(lambda: cross(zz).start())

    def crossed(zz):
        cross(zz).wait_recv()
        dx_to_core(1, zz).start()

    def blocks(count, send, recv):
        return pltpu.make_async_remote_copy(
            src_ref=all_dx.at[pl.ds(0, count * SP)],
            dst_ref=all_dx.at[pl.ds(0, count * SP)],
            send_sem=send,
            recv_sem=recv,
            device_id=targets["core"],
            device_id_type=MESH,
        )

    def own_block():
        own = pltpu.make_async_copy(block, dx_part(par, z), dx_own)
        own.start()
        own.wait()
        pl.when(z < 3)(lambda: line(z, "up").start())
        pl.when(z > 0)(lambda: line(z, "down").start())
        aside(z)

    pl.when(in_line)(own_block)

    def from_below(k):
        line(z - k, "up").wait_recv()
        pl.when(z < 3)(lambda: line(z - k, "up").start())
        aside(z - k)

    def from_above(k):
        line(z + k, "down").wait_recv()
        pl.when(z > 0)(lambda: line(z + k, "down").start())
        aside(z + k)

    def tile(t):
        there = pl.ds(pl.multiple_of(t * 128, 128), 128)
        ids = lax.broadcasted_iota(jnp.int32, (128, 16 * SP), 0) + t * 128
        onehot = jnp.where(ids == index[...], 1.0, 0.0).astype(BF16)
        value = nn(onehot, all_dx[...]) * math.sqrt(D)
        total[there, :] = value
        pltpu.make_async_copy(total.at[there], out.at[there], out_sem).start()
        count_squares(value)

    def collect(i):
        for k in range(1, 4):
            pl.when(both(i == HOP * k, z >= k))(lambda k=k: from_below(k))
            pl.when(both(i == HOP * k, z + k <= 3))(lambda k=k: from_above(k))

    def embed(i):
        pl.when(i == HOP)(lambda: crossed(z))
        for k in range(1, 4):
            pl.when(both(i == HOP * (k + 1), z >= k))(lambda k=k: crossed(z - k))
            pl.when(both(i == HOP * (k + 1), z + k <= 3))(lambda k=k: crossed(z + k))
        begin = 4 * HOP + 2
        pl.when(i == begin)(lambda: blocks(8, dx_core_send, dx_core_recv).wait_recv())
        for half in range(2):
            t = 2 * (i - begin) + half
            pl.when(both(t >= 0, t < 17))(lambda t=t: tile(t))

    squares[...] = jnp.zeros_like(squares)

    def count_squares(value):
        folded = value * value
        size = folded.shape[0]
        while size > 8 and size % 16 == 0:
            size //= 2
            folded = folded[:size] + folded[size:]
        for part in range(size // 8):
            squares[...] += folded[part * 8 : (part + 1) * 8]

    def step(i, carry):
        for k in range(5):
            count, rows = (NCC, CC) if k == 4 else (NCH, CH)
            source, _, _, depth = classes[k]
            j = i - LAG * ((5, 5, 4, 4, 3)[k] - depth)
            now = jnp.logical_and(j >= 0, j < count)
            if k == 4:
                now = jnp.logical_and(now, c == 0)
            pl.when(jnp.logical_and(now, jnp.logical_not(source)))(
                lambda k=k, j=j, rows=rows: relay(k, j, rows)
            )
            pl.when(jnp.logical_and(now, source))(lambda k=k, j=j, rows=rows: finish(k, j, rows))
        pl.when(in_line)(lambda: collect(i))
        pl.when(first)(lambda: embed(i))
        return carry

    lax.fori_loop(0, max(NCH + 5 * LAG, 4 * HOP + 2 + 9), step, 0)
    pl.when(first)(lambda: blocks(8, dx_core_send, dx_core_recv).wait_send())

    def dx_sent(count):
        blocks(count, dx_send, dx_core_recv).wait_send()

    middle = both(z >= 1, z <= 2)
    ends = jnp.logical_not(middle)
    pl.when(both(first, ends))(lambda: dx_sent(1))
    pl.when(both(first, middle))(lambda: dx_sent(5))
    pl.when(both(second, ends))(lambda: dx_sent(5))
    pl.when(both(second, middle))(lambda: dx_sent(9))
    for k in range(5):
        rows = NCC * CC if k == 4 else HALF
        source, _, parents, _ = classes[k]
        whole = pl.ds(held(k), rows)
        sent_core = pltpu.make_async_remote_copy(
            src_ref=grads.at[pl.ds(0, rows)],
            dst_ref=rx_core.at[whole],
            send_sem=core_send.at[k],
            recv_sem=core_c.at[0],
            device_id=targets["core"],
            device_id_type=MESH,
        )
        sent = pltpu.make_async_remote_copy(
            src_ref=loc.at[whole],
            dst_ref=rx_x.at[whole],
            send_sem=send_sem.at[k],
            recv_sem=core_c.at[0],
            device_id=targets["x"],
            device_id_type=MESH,
        )
        if k == 4:
            pl.when(c == 1)(sent_core.wait_send)
            pl.when(jnp.logical_and(jnp.logical_not(source), c == 0))(sent.wait_send)
        else:
            sent_core.wait_send()
            pl.when(jnp.logical_not(source))(sent.wait_send)
    done_all = pltpu.make_async_copy(total, out, out_sem)
    part = pl.ds(0, NCC * CC)
    done_few = pltpu.make_async_copy(total.at[part], out.at[part], out_sem)
    pl.when(jnp.logical_or(jnp.logical_and(home, z < 2), sec == 0))(done_all.wait)
    pl.when(classes[4][0])(done_few.wait)


def reduce_and_scatter(grads, start, block, index):
    rows = LANE + NCC * CC
    return pl.pallas_call(
        close_kernel,
        out_shape=(
            jax.ShapeDtypeStruct((2 * HALF, D), F32),
            jax.ShapeDtypeStruct((8, D), F32),
        ),
        in_specs=[ANY, ANY, VMEM, VMEM],
        out_specs=(ANY, VMEM),
        input_output_aliases={1: 0},
        scratch_shapes=[pltpu.VMEM((rows, D), BF16)] * 5
        + [
            pltpu.VMEM((2 * HALF, D), F32),
            pltpu.VMEM((CH, D), F32),
            pltpu.VMEM((16 * SP, D), BF16),
            pltpu.SemaphoreType.DMA((5,)),
            pltpu.SemaphoreType.DMA((4, NCH)),
            pltpu.SemaphoreType.DMA((NCC,)),
            pltpu.SemaphoreType.DMA((3, 4, NCH)),
            pltpu.SemaphoreType.DMA((3, NCC)),
            pltpu.SemaphoreType.DMA((5,)),
            pltpu.SemaphoreType.DMA((5,)),
            pltpu.SemaphoreType.DMA,
            pltpu.SemaphoreType.DMA,
            pltpu.SemaphoreType.DMA,
            pltpu.SemaphoreType.DMA((4,)),
            pltpu.SemaphoreType.DMA((4,)),
            pltpu.SemaphoreType.DMA,
            pltpu.SemaphoreType.DMA,
        ],
        compiler_params=pltpu.CompilerParams(
            collective_id=1, has_side_effects=True, vmem_limit_bytes=60 * 2**20
        ),
        name="reduce_and_scatter",
    )(grads, start, block, index)


def share_kernel(n_sec, n_dp, block, out, send_sem, recv_sem, own_sem):
    sec = lax.axis_index("section")
    dp = lax.axis_index("dp")
    n = n_sec * n_dp
    me = sec * n_dp + dp
    barrier = pltpu.get_barrier_semaphore()
    own = pltpu.make_async_copy(block, out.at[me], own_sem)
    own.start()

    def peer(k):
        other = lax.rem(me + k, n)
        return (other // n_dp, lax.rem(other, n_dp))

    def greet(k, carry):
        pl.semaphore_signal(barrier, 1, device_id=peer(k), device_id_type=MESH)
        return carry

    lax.fori_loop(1, n, greet, 0)
    pl.semaphore_wait(barrier, n - 1)

    def send(k, carry):
        pltpu.make_async_remote_copy(
            src_ref=block,
            dst_ref=out.at[me],
            send_sem=send_sem,
            recv_sem=recv_sem,
            device_id=peer(k),
            device_id_type=MESH,
        ).start()
        return carry

    lax.fori_loop(1, n, send, 0)
    every = pltpu.make_async_remote_copy(
        src_ref=out.at[pl.ds(0, n - 1)],
        dst_ref=out.at[pl.ds(0, n - 1)],
        send_sem=send_sem,
        recv_sem=recv_sem,
        device_id=peer(1),
        device_id_type=MESH,
    )
    own.wait()
    every.wait_send()
    every.wait_recv()


def share(block, n_sec, n_dp, cid, name):
    return pl.pallas_call(
        functools.partial(share_kernel, n_sec, n_dp),
        out_shape=jax.ShapeDtypeStruct((n_sec * n_dp,) + block.shape, block.dtype),
        in_specs=[VMEM],
        out_specs=VMEM,
        scratch_shapes=[
            pltpu.SemaphoreType.DMA,
            pltpu.SemaphoreType.DMA,
            pltpu.SemaphoreType.DMA,
        ],
        compiler_params=pltpu.CompilerParams(collective_id=cid, has_side_effects=True),
        name=name,
    )(block)


def share_row_kernel(n_dp, block, out, send_sem, recv_sem, own_sem):
    sec = lax.axis_index("section")
    me = lax.axis_index("dp")
    barrier = pltpu.get_barrier_semaphore()
    own = pltpu.make_async_copy(block, out.at[me], own_sem)
    own.start()
    for k in range(1, n_dp):
        pl.semaphore_signal(
            barrier, 1, device_id=(sec, lax.rem(me + k, n_dp)), device_id_type=MESH
        )
    pl.semaphore_wait(barrier, n_dp - 1)
    for k in range(1, n_dp):
        pltpu.make_async_remote_copy(
            src_ref=block,
            dst_ref=out.at[me],
            send_sem=send_sem,
            recv_sem=recv_sem,
            device_id=(sec, lax.rem(me + k, n_dp)),
            device_id_type=MESH,
        ).start()
    every = pltpu.make_async_remote_copy(
        src_ref=out.at[pl.ds(0, n_dp - 1)],
        dst_ref=out.at[pl.ds(0, n_dp - 1)],
        send_sem=send_sem,
        recv_sem=recv_sem,
        device_id=(sec, lax.rem(me + 1, n_dp)),
        device_id_type=MESH,
    )
    own.wait()
    every.wait_send()
    every.wait_recv()


def share_row(block, n_dp, cid, name):
    return pl.pallas_call(
        functools.partial(share_row_kernel, n_dp),
        out_shape=jax.ShapeDtypeStruct((n_dp,) + block.shape, block.dtype),
        in_specs=[VMEM],
        out_specs=VMEM,
        scratch_shapes=[
            pltpu.SemaphoreType.DMA,
            pltpu.SemaphoreType.DMA,
            pltpu.SemaphoreType.DMA,
        ],
        compiler_params=pltpu.CompilerParams(collective_id=cid, has_side_effects=True),
        name=name,
    )(block)


def picked_kernel(block, out, own_sem, send_sem, recv_sem, core_send, core_recv):
    sec, dp, z, c, par, home = place()
    last = sec == 3
    upper = sec >= 2
    barrier = pltpu.get_barrier_semaphore()

    def greet(s, e):
        pl.semaphore_signal(barrier, 1, device_id=(s, e), device_id_type=MESH)

    def rows(p, zz, lane):
        return pl.ds(pl.multiple_of((2 * (2 * zz + lane) + p) * PICKS, PICKS), PICKS)

    def greet_senders():
        for k in range(4):
            greet(2, 2 * k + c)
        for k in range(1, 4):
            greet(3, 2 * lax.rem(z + k, 4) + c)
        greet(3, dp + 1 - 2 * c)

    pl.when(last)(greet_senders)

    def to(k):
        zz = lax.rem(z + k, 4)
        return pltpu.make_async_remote_copy(
            src_ref=block,
            dst_ref=out.at[rows(par, z, c)],
            send_sem=send_sem,
            recv_sem=recv_sem.at[par, z],
            device_id=(3, 2 * zz + c),
            device_id_type=MESH,
        )

    def forward(p, k):
        zz = lax.rem(z + k, 4)
        return pltpu.make_async_remote_copy(
            src_ref=out.at[rows(p, zz, c)],
            dst_ref=out.at[rows(p, zz, c)],
            send_sem=core_send,
            recv_sem=core_recv,
            device_id=(3, dp + 1 - 2 * c),
            device_id_type=MESH,
        )

    def came(p, k):
        zz = lax.rem(z + k, 4)
        return pltpu.make_async_remote_copy(
            src_ref=block,
            dst_ref=out.at[rows(p, zz, c)],
            send_sem=send_sem,
            recv_sem=recv_sem.at[p, zz],
            device_id=(3, dp),
            device_id_type=MESH,
        )

    def every(count):
        return pltpu.make_async_remote_copy(
            src_ref=out.at[pl.ds(0, count * PICKS)],
            dst_ref=out.at[pl.ds(0, count * PICKS)],
            send_sem=core_send,
            recv_sem=core_recv,
            device_id=(3, dp),
            device_id_type=MESH,
        )

    def all_sent(count):
        return pltpu.make_async_remote_copy(
            src_ref=out.at[pl.ds(0, count * PICKS)],
            dst_ref=out.at[pl.ds(0, count * PICKS)],
            send_sem=send_sem,
            recv_sem=core_recv,
            device_id=(3, dp),
            device_id_type=MESH,
        )

    def second():
        pl.semaphore_wait(barrier, 4)
        for k in range(4):
            to(k).start()
        all_sent(4).wait_send()

    def third():
        own = pltpu.make_async_copy(block, out.at[rows(1, z, c)], own_sem)
        own.start()
        pl.semaphore_wait(barrier, 4)
        for k in range(1, 4):
            to(k).start()
        own.wait()
        forward(1, 0).start()
        for k in range(4):
            came(0, k).wait_recv()
            forward(0, k).start()
            if k:
                came(1, k).wait_recv()
                forward(1, k).start()
        all_sent(3).wait_send()
        every(8).wait_send()
        every(8).wait_recv()

    def none():
        out[...] = jnp.zeros_like(out)

    pl.when(sec == 2)(second)
    pl.when(last)(third)
    pl.when(jnp.logical_not(last))(none)


def share_picked(block):
    return pl.pallas_call(
        picked_kernel,
        out_shape=jax.ShapeDtypeStruct((16 * PICKS, D), BF16),
        in_specs=[VMEM],
        out_specs=VMEM,
        scratch_shapes=[
            pltpu.SemaphoreType.DMA,
            pltpu.SemaphoreType.DMA,
            pltpu.SemaphoreType.DMA((2, 4)),
            pltpu.SemaphoreType.DMA,
            pltpu.SemaphoreType.DMA,
        ],
        compiler_params=pltpu.CompilerParams(collective_id=4, has_side_effects=True),
        name="share_picked",
    )(block)


def unpick_kernel(part, out, rx_core, low, rx, core_send, core_recv, send_sem, recv_sem):
    sec, dp, z, c, par, home = place()
    barrier = pltpu.get_barrier_semaphore()

    def greet(s, e):
        pl.semaphore_signal(barrier, 1, device_id=(s, e), device_id_type=MESH)

    def greet_senders():
        for k in range(4):
            pl.when(jnp.logical_or(sec == 2, 2 * k + c != dp))(lambda k=k: greet(3, 2 * k + c))

    pl.when(sec >= 2)(greet_senders)
    pl.when(sec == 3)(lambda: greet(3, dp + 1 - 2 * c))

    def row(p, zz, lane):
        return (2 * (2 * zz + lane) + p) * PICKS

    def swap(p, zz):
        place_there = (2 * zz + p) * PICKS
        return pltpu.make_async_remote_copy(
            src_ref=part.at[pl.ds(pl.multiple_of(row(p, zz, 1 - c), PICKS), PICKS)],
            dst_ref=rx_core.at[pl.ds(place_there, PICKS)],
            send_sem=core_send,
            recv_sem=core_recv,
            device_id=(3, dp + 1 - 2 * c),
            device_id_type=MESH,
        )

    def to(p, k):
        zz = lax.rem(z + k, 4)
        return pltpu.make_async_remote_copy(
            src_ref=low.at[pl.ds(pl.multiple_of((2 * zz + p) * PICKS, PICKS), PICKS)],
            dst_ref=rx.at[z],
            send_sem=send_sem,
            recv_sem=recv_sem,
            device_id=(2 + p, 2 * zz + c),
            device_id_type=MESH,
        )

    def third():
        pl.semaphore_wait(barrier, 8)
        for zz in range(4):
            for p in range(2):
                swap(p, zz).start()
        whole = pltpu.make_async_remote_copy(
            src_ref=rx_core,
            dst_ref=rx_core,
            send_sem=core_send,
            recv_sem=core_recv,
            device_id=(3, dp),
            device_id_type=MESH,
        )
        whole.wait_recv()
        for zz in range(4):
            for p in range(2):
                there = pl.ds((2 * zz + p) * PICKS, PICKS)
                mine = part[pl.ds(pl.multiple_of(row(p, zz, c), PICKS), PICKS), :]
                low[there, :] = (mine + rx_core[there, :]).astype(BF16)
        for k in range(4):
            to(0, k).start()
            if k:
                to(1, k).start()
        whole.wait_send()
        pltpu.make_async_remote_copy(
            src_ref=low.at[pl.ds(0, 7 * PICKS)],
            dst_ref=low.at[pl.ds(0, 7 * PICKS)],
            send_sem=send_sem,
            recv_sem=recv_sem,
            device_id=(3, dp),
            device_id_type=MESH,
        ).wait_send()
        pltpu.make_async_remote_copy(
            src_ref=rx.at[pl.ds(0, 3)],
            dst_ref=rx.at[pl.ds(0, 3)],
            send_sem=send_sem,
            recv_sem=recv_sem,
            device_id=(3, dp),
            device_id_type=MESH,
        ).wait_recv()
        rx[z] = low[pl.ds(pl.multiple_of((2 * z + 1) * PICKS, PICKS), PICKS), :]

    def second():
        pltpu.make_async_remote_copy(
            src_ref=rx,
            dst_ref=rx,
            send_sem=send_sem,
            recv_sem=recv_sem,
            device_id=(3, dp),
            device_id_type=MESH,
        ).wait_recv()

    def none():
        rx[...] = jnp.zeros_like(rx)

    pl.when(sec == 3)(third)
    pl.when(sec == 2)(second)
    pl.when(sec < 2)(none)
    summed = rx[0].astype(F32)
    for k in range(1, 4):
        summed = summed + rx[k].astype(F32)
    out[...] = summed


def unpick(part):
    return pl.pallas_call(
        unpick_kernel,
        out_shape=jax.ShapeDtypeStruct((PICKS, D), F32),
        in_specs=[VMEM],
        out_specs=VMEM,
        scratch_shapes=[
            pltpu.VMEM((8 * PICKS, D), F32),
            pltpu.VMEM((8 * PICKS, D), BF16),
            pltpu.VMEM((4, PICKS, D), BF16),
            pltpu.SemaphoreType.DMA,
            pltpu.SemaphoreType.DMA,
            pltpu.SemaphoreType.DMA,
            pltpu.SemaphoreType.DMA,
        ],
        compiler_params=pltpu.CompilerParams(collective_id=5, has_side_effects=True),
        name="unpick",
    )(part)


NEG = -1e30
FT = 256


def turn(block, cosine, sine, lanes):
    ahead = pltpu.roll(block, 96, 1)
    behind = pltpu.roll(block, 32, 1)
    return block * cosine + jnp.where(lax.rem(lanes, 64) < 32, ahead, behind) * sine


def see(seg_rows, seg_cols):
    rows = lax.broadcasted_iota(jnp.int32, (SP, SP), 0)
    cols = lax.broadcasted_iota(jnp.int32, (SP, SP), 1)
    allowed = jnp.logical_and(seg_rows[...] == seg_cols[...], cols <= rows)
    return jnp.where(allowed, 0.0, NEG)


def softmax_of(scores, unseen):
    masked = scores + unseen
    grown = jnp.exp(masked - jnp.max(masked, axis=-1, keepdims=True))
    return grown / jnp.sum(grown, axis=-1, keepdims=True)


def weight_copies(w_any, w, sems):
    bounds = (0, 3 * D, 4 * D, 4 * D + FF, 4 * D + 2 * FF, MATS, WROWS)
    return [
        pltpu.make_async_copy(
            w_any.at[pl.ds(lo, hi - lo)], w.at[pl.ds(lo, hi - lo)], sems.at[i]
        )
        for i, (lo, hi) in enumerate(zip(bounds[:-1], bounds[1:]))
    ]


def forward_kernel(
    x, w_any, cosine, sine, seg_rows, seg_cols, y, q, k, v, o, h, gate, up, w, m, unseen, sems
):
    copies = weight_copies(w_any, w, sems)
    for i in (5, 0, 1, 2, 3, 4):
        copies[i].start()
    unseen[...] = see(seg_rows, seg_cols)
    lanes = lax.broadcasted_iota(jnp.int32, (SP, 128), 1)
    first = lanes < 64
    copies[5].wait()
    gains = w[pl.ds(MATS, 16), :].astype(F32)
    stream = x[...].astype(F32)
    a1 = rms_scale(stream, gains[0:1]).astype(BF16)
    copies[0].wait()

    def project(b, carry):
        cols = pl.ds(pl.multiple_of(b * 256, 256), 256)
        raw_q = nn(a1, w[pl.ds(0, D), cols])
        raw_k = nn(a1, w[pl.ds(D, D), cols])
        raw_v = nn(a1, w[pl.ds(2 * D, D), cols])
        v[:, cols] = raw_v.astype(BF16)
        for part in range(2):
            there = pl.ds(pl.multiple_of(b * 256 + part * 128, 128), 128)
            here = slice(part * 128, (part + 1) * 128)
            turned_q = turn(raw_q[:, here], cosine[...], sine[...], lanes)
            q[:, there] = (turned_q * HD ** (-0.5)).astype(BF16)
            k[:, there] = turn(raw_k[:, here], cosine[...], sine[...], lanes).astype(BF16)
        return carry

    lax.fori_loop(0, D // 256, project, 0)

    def attend(b, carry):
        cols = pl.ds(pl.multiple_of(b * 128, 128), 128)
        qb, kb, vb = q[:, cols], k[:, cols], v[:, cols]
        zero = jnp.zeros_like(qb)
        p0 = softmax_of(nt(jnp.where(first, qb, zero), kb), unseen[...]).astype(BF16)
        p1 = softmax_of(nt(jnp.where(first, zero, qb), kb), unseen[...]).astype(BF16)
        o[:, cols] = jnp.where(first, nn(p0, vb), nn(p1, vb)).astype(BF16)
        return carry

    lax.fori_loop(0, HEADS // 2, attend, 0)
    copies[1].wait()
    for b in range(3):
        cols = pl.ds(b * 256, 256)
        h[:, cols] = x[:, cols].astype(F32) + nn(o[...], w[pl.ds(3 * D, D), cols])
    a2 = rms_scale(h[...], gains[1:2]).astype(BF16)
    copies[2].wait()
    copies[3].wait()

    def widen(b, carry):
        cols = pl.ds(pl.multiple_of(b * FT, FT), FT)
        g = nt(a2, w[pl.ds(pl.multiple_of(4 * D + b * FT, FT), FT), :])
        u = nt(a2, w[pl.ds(pl.multiple_of(4 * D + FF + b * FT, FT), FT), :])
        gate[:, cols] = g
        up[:, cols] = u
        m[:, cols] = (g / (1.0 + jnp.exp(-g)) * u).astype(BF16)
        return carry

    lax.fori_loop(0, FF // FT, widen, 0)
    copies[4].wait()

    def narrow(b, carry):
        cols = pl.ds(pl.multiple_of(b * 256, 256), 256)
        y[:, cols] = (h[:, cols] + nn(m[...], w[pl.ds(4 * D + 2 * FF, FF), cols])).astype(BF16)
        return carry

    lax.fori_loop(0, 3, narrow, 0)


def forward_call(x, weights, cosine, sine, seg_rows, seg_cols):
    low = jax.ShapeDtypeStruct((SP, D), BF16)
    wide = jax.ShapeDtypeStruct((SP, FF), F32)
    return pl.pallas_call(
        forward_kernel,
        out_shape=(low, low, low, low, low, jax.ShapeDtypeStruct((SP, D), F32), wide, wide),
        in_specs=[VMEM, ANY, VMEM, VMEM, VMEM, VMEM],
        out_specs=(VMEM,) * 8,
        scratch_shapes=[
            pltpu.VMEM((WROWS, D), BF16),
            pltpu.VMEM((SP, FF), BF16),
            pltpu.VMEM((SP, SP), F32),
            pltpu.SemaphoreType.DMA((6,)),
        ],
        compiler_params=pltpu.CompilerParams(vmem_limit_bytes=48 * 2**20),
        name="layer_forward",
    )(x, weights, cosine, sine, seg_rows, seg_cols)


def rms_back(value_in, gain, grad):
    inv = lax.rsqrt(jnp.mean(value_in * value_in, axis=-1, keepdims=True) + norm_eps)
    unit = value_in * inv
    scaled = grad * gain
    grad_in = inv * (scaled - unit * jnp.mean(scaled * unit, axis=-1, keepdims=True))
    return grad_in, jnp.sum(grad * unit, axis=0, keepdims=True)


def backward_kernel(
    with_weights, dy, x, w_any, cosine, sine, seg_rows, seg_cols, q, k, v, o, h, gate, up, *refs
):
    if with_weights:
        dx, grads, w, dgate, dup, m, da, do, dq, dk, dv, unseen, sems = refs
    else:
        dx, w, dgate, dup, m, da, do, dq, dk, dv, unseen, sems = refs
    copies = weight_copies(w_any, w, sems)
    for i in (4, 5, 2, 3, 1, 0):
        copies[i].start()
    unseen[...] = see(seg_rows, seg_cols)
    lanes = lax.broadcasted_iota(jnp.int32, (SP, 128), 1)
    first = lanes < 64
    copies[4].wait()

    def open_mlp(b, carry):
        cols = pl.ds(pl.multiple_of(b * FT, FT), FT)
        dm = nt(dy[...], w[pl.ds(pl.multiple_of(4 * D + 2 * FF + b * FT, FT), FT), :])
        g = gate[:, cols]
        u = up[:, cols]
        sig = 1.0 / (1.0 + jnp.exp(-g))
        dgate[:, cols] = (dm * u * sig * (1.0 + g * (1.0 - sig))).astype(BF16)
        dup[:, cols] = (dm * g * sig).astype(BF16)
        if with_weights:
            m[:, cols] = (g * sig * u).astype(BF16)
        return carry

    lax.fori_loop(0, FF // FT, open_mlp, 0)
    copies[5].wait()
    gains = w[pl.ds(MATS, 16), :].astype(F32)
    copies[2].wait()
    copies[3].wait()

    def close_mlp(b, carry):
        cols = pl.ds(pl.multiple_of(b * 256, 256), 256)
        da[:, cols] = nn(dgate[...], w[pl.ds(4 * D, FF), cols]) + nn(
            dup[...], w[pl.ds(4 * D + FF, FF), cols]
        )
        return carry

    lax.fori_loop(0, 3, close_mlp, 0)
    dh, dg_mlp = rms_back(h[...], gains[1:2], da[...])
    dh = dh + dy[...].astype(F32)
    db = dh.astype(BF16)
    copies[1].wait()
    for b in range(3):
        do[:, pl.ds(b * 256, 256)] = nt(db, w[pl.ds(3 * D + b * 256, 256), :]).astype(BF16)

    def attend(b, carry):
        cols = pl.ds(pl.multiple_of(b * 128, 128), 128)
        qb, kb, vb, dob = q[:, cols], k[:, cols], v[:, cols], do[:, cols]
        zero = jnp.zeros_like(qb)
        parts = []
        for head in range(2):
            keep = first if head == 0 else jnp.logical_not(first)
            probs = softmax_of(nt(jnp.where(keep, qb, zero), kb), unseen[...])
            dprobs = nt(jnp.where(keep, dob, zero), vb)
            along = jnp.sum(probs * dprobs, axis=-1, keepdims=True)
            dscores = (probs * (dprobs - along)).astype(BF16)
            parts.append((nn(dscores, kb), tn(dscores, qb), tn(probs.astype(BF16), dob)))
        dqb = jnp.where(first, parts[0][0], parts[1][0]) * HD ** (-0.5)
        dkb = jnp.where(first, parts[0][1], parts[1][1])
        dq[:, cols] = turn(dqb, cosine[...], -sine[...], lanes).astype(BF16)
        dk[:, cols] = turn(dkb, cosine[...], -sine[...], lanes).astype(BF16)
        dv[:, cols] = jnp.where(first, parts[0][2], parts[1][2]).astype(BF16)
        return carry

    lax.fori_loop(0, HEADS // 2, attend, 0)
    copies[0].wait()
    for b in range(3):
        rows = lambda i, b=b: w[pl.ds(i * D + b * 256, 256), :]
        da[:, pl.ds(b * 256, 256)] = (
            nt(dq[...], rows(0)) + nt(dk[...], rows(1)) + nt(dv[...], rows(2))
        )
    stream = x[...].astype(F32)
    dstream, dg_attn = rms_back(stream, gains[0:1], da[...])
    dx[...] = (dstream + dh).astype(BF16)
    if not with_weights:
        return
    a1 = rms_scale(stream, gains[0:1]).astype(BF16)
    a2 = rms_scale(h[...], gains[1:2]).astype(BF16)
    for b in range(3):
        cols = slice(b * 256, (b + 1) * 256)
        piece = a1[:, cols]
        for i, right in enumerate((dq, dk, dv)):
            grads[pl.ds(i * D + b * 256, 256), :] = tn(piece, right[...]).astype(BF16)
        grads[pl.ds(3 * D + b * 256, 256), :] = tn(o[:, cols], db).astype(BF16)

    def outer(b, carry):
        cols = pl.ds(pl.multiple_of(b * FT, FT), FT)
        base = 4 * D + b * FT
        for i, (left, right) in enumerate(((dgate, a2), (dup, a2), (m, dy))):
            there = pl.ds(pl.multiple_of(base + i * FF, FT), FT)
            grads[there, :] = tn(left[:, cols], right[...]).astype(BF16)
        return carry

    lax.fori_loop(0, FF // FT, outer, 0)
    tail = lax.broadcasted_iota(jnp.int32, (16, D), 0)
    grads[pl.ds(MATS, 16), :] = jnp.where(
        tail == 0, dg_attn, jnp.where(tail == 1, dg_mlp, 0.0)
    ).astype(BF16)


def backward_call(with_weights, dy, x, weights, cosine, sine, seg_rows, seg_cols, kept):
    low = jax.ShapeDtypeStruct((SP, D), BF16)
    out_shape = (low, jax.ShapeDtypeStruct((WROWS, D), BF16)) if with_weights else low
    wide = pltpu.VMEM((SP, FF), BF16)
    narrow = pltpu.VMEM((SP, D), BF16)
    return pl.pallas_call(
        functools.partial(backward_kernel, with_weights),
        out_shape=out_shape,
        in_specs=[VMEM, VMEM, ANY] + [VMEM] * 11,
        out_specs=(VMEM, VMEM) if with_weights else VMEM,
        scratch_shapes=[
            pltpu.VMEM((WROWS, D), BF16),
            wide,
            wide,
            wide,
            pltpu.VMEM((SP, D), F32),
            narrow,
            narrow,
            narrow,
            narrow,
            pltpu.VMEM((SP, SP), F32),
            pltpu.SemaphoreType.DMA((6,)),
        ],
        compiler_params=pltpu.CompilerParams(vmem_limit_bytes=60 * 2**20),
        name="layer_backward_weights" if with_weights else "layer_backward",
    )(dy, x, weights, cosine, sine, seg_rows, seg_cols, *kept)


def shards(codes, labels, picks, classes, null_mask, starts, master, momentum, average):
    sec = lax.axis_index("section")
    d = lax.axis_index("dp")
    n_dp = lax.axis_size("dp")
    n_sec = lax.axis_size("section")
    par = lax.rem(sec, 2)
    own = master.shape[0]
    learn_rate = rate_factor * math.sqrt(own * n_sec * n_dp)
    embed_factor = math.sqrt(D)
    beside = [(0, 1), (1, 0), (2, 3), (3, 2)]
    fast = n_sec == 4 and n_dp == 8 and own == 2 * HALF
    table = master.astype(BF16)
    gain_row = lax.slice_in_dim(table, VOCAB % own, VOCAB % own + 1)[0].astype(F32)
    gain_at = VOCAB // own

    row_index, counted, segment, position = jax.vmap(row_layout)(starts, classes, null_mask, codes)
    picked_labels = jnp.take_along_axis(labels, picks, axis=1)
    picked_counts = jnp.take_along_axis(counted, picks, axis=1).astype(jnp.int32)
    row_index = jnp.pad(row_index, ((0, 0), (0, SP - SLOTS)), constant_values=-1)
    info = jnp.concatenate([row_index, picked_labels, picked_counts], axis=1)
    if fast:
        block = jnp.concatenate([info.reshape(-1).astype(F32), gain_row])
        block = jnp.pad(block, (0, 2048 - block.shape[0])).reshape(16, 128)
        info = share(block, n_sec, n_dp, 2, "share_info").reshape(n_sec, n_dp, 2048)
        g_f = info[3, gain_at, 2 * (SP + 2 * PICKS) :][:D]
        info = info[0, :, : 2 * (SP + 2 * PICKS)].reshape(2 * n_dp, -1).astype(jnp.int32)
    else:
        info = lax.all_gather(info, "dp", axis=0, tiled=True)
        holds = (sec == 3) & (d == gain_at)
        g_f = lax.psum(jnp.where(holds, gain_row, 0.0), ("section", "dp"))
    all_index = info[:, :SP].reshape(-1)
    all_labels = info[:, SP : SP + PICKS].reshape(-1)
    all_counts = info[:, SP + PICKS :].reshape(-1).astype(F32)
    segment = jnp.pad(segment[par], (0, SP - SLOTS), constant_values=SEGS + 2)
    position = jnp.pad(position[par], (0, SP - SLOTS))
    frequency = rope_base ** (-jnp.arange(HD // 2, dtype=F32) * 2.0 / HD)
    angles = position.astype(F32)[:, None] * frequency[None, :]
    cosine = jnp.tile(jnp.cos(angles), (1, 4))
    sine = jnp.tile(jnp.concatenate([-jnp.sin(angles), jnp.sin(angles)], axis=1), (1, 2))
    around = (cosine, sine, segment[:, None], segment[None, :])

    local = jnp.where(sec == 0, all_index, -1) - d * own
    if fast:
        weights, x0 = gather_and_embed(table, local[:, None])
    else:
        gathered = lax.all_gather(table, "dp", axis=0, tiled=True)[:WROWS]
        other = lax.ppermute(gathered, "section", beside)
        weights = jnp.where((sec == 1) | (sec == 2), gathered, other)
        onehot = (local[:, None] == jnp.arange(own)[None, :]).astype(BF16)
        looked = (nn(onehot, table) * embed_factor).astype(BF16)
        looked = lax.psum_scatter(looked, "dp", scatter_dimension=0, tiled=True).reshape(2, SP, D)
        from_first = lax.ppermute(looked[1], "section", [(0, 1)])
        x0 = jnp.where(sec == 0, looked[0], from_first)

    y0 = forward_call(x0, weights, *around)[0]
    x = jnp.where(sec < 2, x0, lax.ppermute(y0, "section", [(0, 2), (1, 3)]))
    y, *kept = forward_call(x, weights, *around)

    my_picks = picks[par]
    picked = jnp.take(y, my_picks, axis=0)
    if fast:
        all_picked = share_picked(picked)
    else:
        all_picked = lax.all_gather(picked, ("section", "dp"), axis=0, tiled=False)
        all_picked = all_picked.reshape(n_sec, n_dp, PICKS, D)[2:].transpose(1, 0, 2, 3)
    all_picked = all_picked.reshape(-1, D).astype(F32)
    af = jnp.where(sec == 3, rms_scale(all_picked, g_f), 0.0).astype(BF16)
    vocab_ids = d * own + jnp.arange(own)
    logits = jnp.where(vocab_ids[None, :] < VOCAB, nt(af, table), -1e30)
    local_max = jnp.max(logits, axis=1)
    hit = vocab_ids[None, :] == all_labels[:, None]
    sums = jnp.stack(
        [
            local_max,
            jnp.sum(jnp.exp(logits - local_max[:, None]), axis=1),
            jnp.sum(jnp.where(hit, logits, 0.0), axis=1),
        ]
    )
    if fast:
        block = jnp.pad(sums.reshape(-1, 128), ((0, 4), (0, 0)))
        every = share_row(block, n_dp, 3, "share_sums")[:, :12].reshape(n_dp, 3, -1)
    else:
        every = lax.all_gather(sums, "dp", axis=0, tiled=False)
    top = jnp.max(every[:, 0], axis=0)
    total = jnp.sum(every[:, 1] * jnp.exp(every[:, 0] - top), axis=0)
    target = jnp.sum(every[:, 2], axis=0)
    log_total = top + jnp.log(total)
    loss_part = jnp.where(
        (sec == 3) & (d == 0), jnp.sum(jnp.where(all_counts > 0, log_total - target, 0.0)), 0.0
    )
    count_sum = jnp.sum(all_counts)
    dlogits = (jnp.exp(logits - log_total[:, None]) - hit.astype(F32)) * all_counts[:, None]
    dlogits = jnp.where(sec == 3, dlogits, 0.0).astype(BF16)
    d_table = tn(dlogits, af)
    if fast:
        daf = unpick(nn(dlogits, table))
    else:
        daf = lax.psum(nn(dlogits, table), "dp")
        daf = lax.dynamic_slice_in_dim(daf, d * 2 * PICKS, 2 * PICKS).reshape(2, PICKS, D)
        daf = jnp.where(sec == 3, daf[1], lax.ppermute(daf[0], "section", [(3, 2)]))
    d_own, dg_f = rms_pull(picked.astype(F32), g_f, daf)
    dg_f = jnp.where(sec >= 2, dg_f, 0.0)
    spread = (jnp.arange(SP)[:, None] == my_picks[None, :]).astype(F32)
    d_top = jnp.dot(spread, d_own, precision=lax.Precision.HIGHEST).astype(BF16)
    dx1 = backward_call(False, d_top, x, weights, *around, kept)
    dy = jnp.where(sec < 2, lax.ppermute(dx1, "section", [(2, 0), (3, 1)]), d_top)
    dx0, grads = backward_call(True, dy, x, weights, *around, kept)

    if fast:
        grad, squares = reduce_and_scatter(grads, d_table, dx0, local[None, :])
        squares = jnp.sum(squares) + jnp.sum(d_table * d_table)
    else:
        grads = grads.astype(F32) + lax.ppermute(grads, "section", beside).astype(F32)
        grads = jnp.pad(grads.astype(BF16), ((0, own * n_dp - WROWS), (0, 0)))
        grad = lax.psum_scatter(grads, "dp", scatter_dimension=0, tiled=True).astype(F32)
        grad = jnp.where(sec == 3, d_table, grad)
        pair = jnp.stack([dx0, lax.ppermute(dx0, "section", [(1, 0)])])
        all_dx = lax.all_gather(pair, "dp", axis=0, tiled=True).reshape(-1, D)
        grad = jnp.where(sec == 0, tn(onehot, all_dx) * embed_factor, grad)
        squares = jnp.sum(grad * grad)

    if fast:
        block = jnp.concatenate([dg_f, jnp.stack([squares, loss_part]), jnp.zeros((254,), F32)])
        totals = jnp.sum(share(block.reshape(8, 128), n_sec, n_dp, 8, "share_norm"), axis=0)
        totals = totals.reshape(-1)
        dg_f, squares, loss_sum = totals[:D], totals[D], totals[D + 1]
    else:
        dg_f, squares, loss_sum = lax.psum((dg_f, squares, loss_part), ("section", "dp"))
    grad_norm = jnp.sqrt(squares + jnp.sum(dg_f * dg_f))
    gain_here = (jnp.arange(own) == VOCAB % own)[:, None] & (sec == 3) & (d == gain_at)
    grad = grad + jnp.where(gain_here, dg_f[None, :], 0.0)
    clipped = grad * jnp.minimum(1.0, clip_limit / (grad_norm + norm_eps))
    new_momentum = momentum_decay * momentum + clipped
    new_master = master - learn_rate * (clipped + momentum_decay * new_momentum)
    new_average = average_decay * average + (1.0 - average_decay) * new_master
    return loss_sum, count_sum, grad_norm, new_master, new_momentum, new_average


def solution(mesh):
    split = P("dp", None)
    whole = P(("section", "dp"), None)
    return jax.shard_map(
        shards,
        mesh=mesh,
        in_specs=(split,) * 6 + (whole,) * 3,
        out_specs=(P(), P(), P(), whole, whole, whole),
        check_vma=False,
    )
```

```python
import functools
import math

import jax
import jax.numpy as jnp
from jax import lax
from jax.experimental import pallas as pl
from jax.experimental.pallas import tpu as pltpu
from jax.sharding import PartitionSpec as P

D = 768
HEADS = 12
HD = 64
FF = 2048
VOCAB = 16384
CLASSES = 1001
SLOTS = 264
SP = 272
PICKS = 32
SEGS = 3
MATS = 4 * D + 3 * FF
WROWS = 9232

F32 = jnp.float32
BF16 = jnp.bfloat16

rope_base = 10000.0
clip_limit = 1.0
rate_factor = 0.25
momentum_decay = 0.9
average_decay = 0.8
norm_eps = 1e-06


def nn(left, right):
    return jnp.dot(left, right, preferred_element_type=F32)


def tn(left, right):
    return lax.dot_general(left, right, (((0,), (0,)), ((), ())), preferred_element_type=F32)


def nt(left, right):
    return lax.dot_general(left, right, (((1,), (1,)), ((), ())), preferred_element_type=F32)


def rms_scale(value_in, gain):
    return (
        value_in * lax.rsqrt(jnp.mean(value_in * value_in, axis=-1, keepdims=True) + norm_eps) * gain
    )


def rms_pull(value_in, gain, grad):
    inv = lax.rsqrt(jnp.mean(value_in * value_in, axis=-1, keepdims=True) + norm_eps)
    unit = value_in * inv
    scaled = grad * gain
    grad_in = inv * (scaled - unit * jnp.mean(scaled * unit, axis=-1, keepdims=True))
    return grad_in, jnp.sum(grad * unit, axis=0)


def row_layout(starts_row, classes_row, null_row, codes_row):
    slot_ids = jnp.arange(SLOTS, dtype=jnp.int32)
    segment = jnp.sum((starts_row[None, 1:] <= slot_ids[:, None]).astype(jnp.int32), axis=1)
    seg_start = jnp.sum(
        jnp.where(segment[:, None] == jnp.arange(SEGS + 1)[None, :], starts_row[None, :], 0), axis=1
    )
    position = slot_ids - seg_start
    live_end = starts_row[SEGS]
    is_first = (position == 0) & (slot_ids < live_end)
    clamped = jnp.minimum(segment, SEGS - 1)
    hit = clamped[:, None] == jnp.arange(SEGS)[None, :]
    class_row = jnp.sum(
        jnp.where(hit, jnp.where(null_row > 0, CLASSES - 1, classes_row)[None, :], 0), axis=1
    )
    row_index = jnp.where(is_first, VOCAB + class_row, codes_row)
    following = jnp.concatenate([segment[1:], jnp.full((1,), SEGS + 1, jnp.int32)])
    counted = (following == segment) & (slot_ids + 1 < live_end)
    return row_index, counted, segment, position


MESH = pl.DeviceIdType.MESH
ANY = pl.BlockSpec(memory_space=pl.ANY)
VMEM = pl.BlockSpec(memory_space=pltpu.VMEM)
SMEM = pl.BlockSpec(memory_space=pltpu.SMEM)

HALF = 1088
CH = 64
NCH = HALF // CH
CC = 48
NCC = 11
LANE = 4 * HALF
LAG = 3
WINDOW = 2
HOP = 3
TURN = 6


def place():
    sec = lax.axis_index("section")
    dp = lax.axis_index("dp")
    z = dp // 2
    c = lax.rem(dp, 2)
    par = lax.rem(sec, 2)
    home = jnp.logical_or(sec == 1, sec == 2)
    return sec, dp, z, c, par, home


def greet_neighbours(sec, dp, z, c, par, turns):
    barrier = pltpu.get_barrier_semaphore()

    def greet(s, e):
        pl.semaphore_signal(barrier, 1, device_id=(s, e), device_id_type=MESH)

    greet(sec, dp + 1 - 2 * c)
    greet(sec + 1 - 2 * par, dp)
    pl.when(z > 0)(lambda: greet(sec, dp - 2))
    pl.when(z < 3)(lambda: greet(sec, dp + 2))
    count = 2 + (z > 0).astype(jnp.int32) + (z < 3).astype(jnp.int32)
    for sender, receiver in turns:
        pl.when(sec == receiver)(lambda sender=sender: greet(sender, dp))
        count = count + (sec == sender).astype(jnp.int32)
    pl.semaphore_wait(barrier, count)


def hop_targets(sec, dp, c, par):
    return {
        "up": (sec, dp + 2),
        "down": (sec, dp - 2),
        "x": (sec + 1 - 2 * par, dp),
        "core": (sec, dp + 1 - 2 * c),
    }


HOPS = ("up", "down", "x", "core")


def tree(z, c, home):
    both = jnp.logical_and
    either = jnp.logical_or
    no = jnp.logical_not
    far = z >= 2
    mid = both(z >= 1, z <= 2)
    never = z < 0
    away = no(home)
    as_int = lambda flag: flag.astype(jnp.int32)
    out = []
    for block in (0, 1):
        for half in (0, 1):
            mine = home if half == 0 else away
            other = no(mine)
            source = both(z == block, home)
            if half == 0:
                early = (lambda j: j < TURN) if block == 0 else (lambda j: j < 0)
                near_x = lambda j, block=block, early=early: both(z == 1 - block, early(j))
                hop_x = lambda j, near_x=near_x: both(home, near_x(j))
                got_x = lambda j, near_x=near_x: both(away, near_x(j))
                along = lambda j, early=early: either(home, no(early(j)))
            else:
                hop_x = lambda j, block=block: both(away, z == 1 - block)
                got_x = lambda j, block=block: both(home, z == 1 - block)
                along = lambda j: away
            at_owner = both(z == block, away)
            if block == 0:
                up = lambda j, along=along, mine=mine: either(both(z == 0, along(j)), both(mid, mine))
                down = lambda j: never
                from_up = lambda j: never
            else:
                up = lambda j, mine=mine: both(mid, mine)
                down = lambda j, along=along: both(z == 1, along(j))
                from_up = lambda j, got_x=got_x: both(z == 0, no(got_x(j)))
            send_x = lambda j, source=source, mine=mine, hop_x=hop_x: either(
                either(source, both(far, mine)), hop_x(j)
            )
            from_x = lambda j, at_owner=at_owner, other=other, got_x=got_x: either(
                either(at_owner, both(far, other)), got_x(j)
            )
            from_down = lambda j, source=source, from_x=from_x, from_up=from_up: no(
                either(source, either(from_x(j), from_up(j)))
            )
            depth = jnp.abs(z - block) + as_int(far) * (half + as_int(other))
            if half == 0:
                depth = depth + (1 - as_int(far)) * as_int(away)
            else:
                depth = depth + (1 - as_int(far)) * jnp.where(
                    away, 1, 2 * as_int(z == 1 - block)
                )
            out.append(
                (source, dict(up=up, down=down, x=send_x), dict(up=from_up, down=from_down, x=from_x), depth)
            )
    lane0 = c == 0
    source = both(both(z == 2, home), lane0)
    sends = dict(
        up=lambda j: both(z == 2, lane0),
        down=lambda j: both(mid, lane0),
        x=lambda j: source,
    )
    parents = dict(
        up=lambda j: both(z <= 1, lane0),
        down=lambda j: both(z == 3, lane0),
        x=lambda j: both(both(z == 2, away), lane0),
    )
    out.append((source, sends, parents, jnp.abs(z - 2) + as_int(away)))
    return out


def segment_of(starts, r, slot):
    bounds = [starts[r, j] for j in range(SEGS + 1)]
    count = lambda at: functools.reduce(
        jnp.add, [(at >= bounds[j]).astype(jnp.int32) for j in range(1, SEGS + 1)]
    )
    segment = count(slot)
    begin = jnp.where(
        segment == 0, bounds[0], jnp.where(segment == 1, bounds[1], jnp.where(segment == 2, bounds[2], bounds[3]))
    )
    counted = jnp.logical_and(count(slot + 1) == segment, slot + 1 < bounds[SEGS])
    return segment, slot - begin, counted, slot < bounds[SEGS]


def open_kernel(
    table, codes, labels, picks, starts, classes, nulls, frequency, out, x0, info, gain, cosine,
    sine, own_sem, recv_sem, recv_c, core_sem, send_sem, sent, mine, rx_core, rx_up, rx_down,
    swap_send, swap_recv, x_send, x_recv, line_send, up_recv, down_recv, last_send, last_recv,
    note, note_send, note_recv, gain_send, gain_recv,
):
    sec, dp, z, c, par, home = place()
    targets = hop_targets(sec, dp, c, par)
    classes_of = tree(z, c, home)
    gain_dp = VOCAB // (2 * HALF)
    holds_gain = jnp.logical_and(sec == 3, dp == gain_dp)

    barrier = pltpu.get_barrier_semaphore()

    def greet(s, e):
        pl.semaphore_signal(barrier, 1, device_id=(s, e), device_id_type=MESH)

    for k in range(1, 8):
        greet(sec, lax.rem(dp + k, 8))
    greet(sec + 1 - 2 * par, dp)
    pl.when(sec == 2)(lambda: greet(0, dp))
    pl.when(sec == 1)(lambda: greet(2, dp))
    pl.when(jnp.logical_and(sec == 2, dp != gain_dp))(lambda: greet(3, gain_dp))

    slot_row = lax.broadcasted_iota(jnp.int32, (1, SLOTS), 1)
    note[...] = jnp.full(note.shape, -1, jnp.int32)
    for r in range(2):
        segment, position, _, live = segment_of(starts, r, slot_row)
        names = [classes[r, j] + (CLASSES - 1 - classes[r, j]) * nulls[r, j] for j in range(SEGS)]
        name = jnp.where(segment == 0, names[0], jnp.where(segment == 1, names[1], names[2]))
        opens = jnp.logical_and(position == 0, live)
        note[r : r + 1, :SLOTS] = jnp.where(opens, VOCAB + name, codes[r : r + 1, :])
        chosen = picks[r : r + 1, :]
        ids = lax.broadcasted_iota(jnp.int32, (SLOTS, PICKS), 0)
        label_col = column(labels[r : r + 1, :], SLOTS)
        note[2 + r : 3 + r, :PICKS] = jnp.sum(
            jnp.where(ids == chosen, label_col, 0), axis=0, keepdims=True
        )
        note[4 + r : 5 + r, :PICKS] = segment_of(starts, r, chosen)[2].astype(jnp.int32)
    info[dp] = note[...]
    count = 8 + jnp.logical_or(sec == 0, sec == 2).astype(jnp.int32)
    pl.semaphore_wait(barrier, count + 7 * holds_gain.astype(jnp.int32))
    for k in range(1, 8):
        pltpu.make_async_remote_copy(
            src_ref=note,
            dst_ref=info.at[dp],
            send_sem=note_send,
            recv_sem=note_recv,
            device_id=(sec, lax.rem(dp + k, 8)),
            device_id_type=MESH,
        ).start()
    noted = pltpu.make_async_remote_copy(
        src_ref=info.at[pl.ds(0, 7)],
        dst_ref=info.at[pl.ds(0, 7)],
        send_sem=note_send,
        recv_sem=note_recv,
        device_id=targets["core"],
        device_id_type=MESH,
    )

    gain_rows = table.at[pl.ds(VOCAB % (2 * HALF), 16)]

    def gain_to(s, e):
        return pltpu.make_async_remote_copy(
            src_ref=gain_rows,
            dst_ref=gain,
            send_sem=gain_send,
            recv_sem=gain_recv,
            device_id=(s, e),
            device_id_type=MESH,
        )

    def send_gain():
        for e in range(8):
            gain_to(2, e).start()
            if e != gain_dp:
                gain_to(3, e).start()
        gain[...] = gain_rows[...]

    pl.when(holds_gain)(send_gain)

    def keep(rows):
        return pltpu.make_async_copy(
            table.at[pl.ds(0, rows)],
            out.at[pl.ds(pl.multiple_of(dp * 2 * HALF, 16), rows)],
            own_sem,
        )

    def keep_all():
        keep(2 * HALF).start()
        keep(2 * HALF).wait()

    def keep_few():
        keep(NCC * CC).start()
        keep(NCC * CC).wait()

    pl.when(jnp.logical_and(home, z < 2))(keep_all)
    pl.when(classes_of[4][0])(keep_few)

    def base(k, lane):
        if k == 4:
            return 4 * 2 * HALF
        return 2 * HALF * (2 * (k // 2) + lane) + HALF * (k % 2)

    def copy(k, hop, j, rows, recv, slot):
        part = out.at[pl.ds(pl.multiple_of(base(k, c) + j * rows, 16), rows)]
        return pltpu.make_async_remote_copy(
            src_ref=part,
            dst_ref=part,
            send_sem=send_sem.at[k, HOPS.index(hop), slot],
            recv_sem=recv,
            device_id=targets[hop],
            device_id_type=MESH,
        )

    def piece(k, j, rows):
        source, sends, _, _ = classes_of[k]
        recv = recv_c.at[j] if k == 4 else recv_sem.at[k, j]
        slot = lax.rem(j, WINDOW)

        def send(hop):
            to = core_sem.at[k] if hop == "core" else recv
            one = copy(k, hop, j, rows, to, slot)
            before = True if hop == "core" else sends[hop](j - WINDOW)
            pl.when(jnp.logical_and(j >= WINDOW, before))(one.wait_send)
            one.start()

        pl.when(jnp.logical_not(source))(copy(k, "x", j, rows, recv, slot).wait_recv)
        for hop in HOPS[:3]:
            pl.when(sends[hop](j))(lambda hop=hop: send(hop))
        send("core")

    def counts(k):
        return (NCC, CC) if k == 4 else (NCH, CH)

    first = sec == 0
    second = sec == 2

    def slot(k):
        return pl.ds(pl.multiple_of(k * SP, 16), SP)

    def order(i):
        low = (z <= 1).astype(jnp.int32)
        return low * (3 - i) + (1 - low) * i

    def swap(k):
        return pltpu.make_async_remote_copy(
            src_ref=sent.at[slot(k)],
            dst_ref=rx_core.at[slot(k)],
            send_sem=swap_send,
            recv_sem=swap_recv.at[k],
            device_id=targets["core"],
            device_id_type=MESH,
        )

    def cross(zz):
        return pltpu.make_async_remote_copy(
            src_ref=mine.at[slot(4 + zz)],
            dst_ref=mine.at[slot(zz)],
            send_sem=x_send,
            recv_sem=x_recv.at[zz],
            device_id=(2, dp),
            device_id_type=MESH,
        )

    def go_up(zz):
        return pltpu.make_async_remote_copy(
            src_ref=mine.at[slot(zz)],
            dst_ref=rx_down.at[slot(zz)],
            send_sem=line_send,
            recv_sem=down_recv.at[zz],
            device_id=targets["up"],
            device_id_type=MESH,
        )

    def go_down(zz):
        return pltpu.make_async_remote_copy(
            src_ref=mine.at[slot(zz)],
            dst_ref=rx_up.at[slot(zz)],
            send_sem=line_send,
            recv_sem=up_recv.at[zz],
            device_id=targets["down"],
            device_id_type=MESH,
        )

    def add(k, ref):
        there = slot(k)
        mine[there, :] = (mine[there, :].astype(F32) + ref[there, :].astype(F32)).astype(BF16)

    def look(row):
        local = column(info[row // 2, pl.ds(lax.rem(row, 2), 1), :][:, :SP], SP) - dp * 2 * HALF
        ids = lax.broadcasted_iota(jnp.int32, (SP, 2 * HALF), 1)
        onehot = jnp.where(ids == local, 1.0, 0.0).astype(BF16)
        return (nn(onehot, table[...]) * math.sqrt(D)).astype(BF16)

    def lookup(b):
        zz = order(b // 2)
        p = 1 - lax.rem(b, 2)
        k = 4 * p + zz
        sent[slot(k), :] = look(2 * (2 * zz + 1 - c) + p)
        swap(k).start()
        mine[slot(k), :] = look(2 * (2 * zz + c) + p)
        swap(k).wait_recv()
        add(k, rx_core)
        pl.when(p == 1)(lambda: cross(zz).start())

    def chain(zz):
        def from_below():
            go_up(zz).wait_recv()
            add(zz, rx_down)

        def from_above():
            go_down(zz).wait_recv()
            add(zz, rx_up)

        pl.when(second)(cross(zz).wait_recv)
        pl.when(jnp.logical_and(zz >= z, z > 0))(from_below)
        pl.when(jnp.logical_and(zz <= z, z < 3))(from_above)
        pl.when(zz > z)(lambda: go_up(zz).start())
        pl.when(zz < z)(lambda: go_down(zz).start())

    def chains(i):
        for o in range(4):
            zz = order(o)
            hops = jnp.maximum(
                z * (zz >= z).astype(jnp.int32), (3 - z) * (zz <= z).astype(jnp.int32)
            )
            pl.when(i == 2 * o + 2 + sec + HOP * hops)(lambda zz=zz: chain(zz))

    segment, position, _, _ = segment_of(starts, par, lax.broadcasted_iota(jnp.int32, (SP, 128), 0))
    angles = position.astype(F32) * frequency[...]
    lanes = lax.broadcasted_iota(jnp.int32, (SP, 128), 1)
    cosine[...] = jnp.cos(angles)
    sine[...] = jnp.where(lax.rem(lanes, 64) < 32, -1.0, 1.0) * jnp.sin(angles)
    noted.wait_recv()

    def step(i, carry):
        for k in range(5):
            count, rows = counts(k)
            j = i - LAG * classes_of[k][3]
            now = jnp.logical_and(j >= 0, j < count)
            if k == 4:
                now = jnp.logical_and(now, c == 0)
            pl.when(now)(lambda k=k, j=j, rows=rows: piece(k, j, rows))
        pl.when(jnp.logical_and(first, i < 8))(lambda: lookup(i))
        pl.when(jnp.logical_or(first, second))(lambda: chains(i))
        pl.when(jnp.logical_and(second, i == last_step))(lambda: last().start())
        return carry

    last_step = 6 + 2 + 2 + 3 * HOP + 1

    def last():
        return pltpu.make_async_remote_copy(
            src_ref=mine.at[slot(z)],
            dst_ref=x0,
            send_sem=last_send,
            recv_sem=last_recv,
            device_id=(1, dp),
            device_id_type=MESH,
        )

    lax.fori_loop(0, max(NCH + 5 * LAG, last_step + 1), step, 0)

    def blocks(count, sem):
        return pltpu.make_async_remote_copy(
            src_ref=mine.at[pl.ds(0, count * SP)],
            dst_ref=mine.at[pl.ds(0, count * SP)],
            send_sem=sem,
            recv_sem=sem,
            device_id=targets["core"],
            device_id_type=MESH,
        )

    def end_first():
        blocks(8, swap_send).wait_send()
        blocks(4, x_send).wait_send()
        blocks(3, line_send).wait_send()
        x0[...] = mine[slot(z), :]

    def end_second():
        blocks(3, line_send).wait_send()
        last().wait_send()

    def none():
        x0[...] = jnp.zeros_like(x0)

    pl.when(first)(end_first)
    pl.when(second)(end_second)
    pl.when(sec == 1)(last().wait_recv)
    pl.when(sec >= 2)(none)

    noted.wait_send()

    def gain_sent():
        for e in range(15):
            gain_to(2, 0).wait_send()

    pl.when(holds_gain)(gain_sent)
    pl.when(jnp.logical_and(sec >= 2, jnp.logical_not(holds_gain)))(gain_to(2, dp).wait_recv)

    def drain(k):
        count, rows = counts(k)
        _, sends, _, _ = classes_of[k]
        for j in range(count - WINDOW, count):
            for hop in HOPS[:3]:
                one = copy(k, hop, j, rows, core_sem.at[k], j % WINDOW)
                pl.when(sends[hop](j))(one.wait_send)
            copy(k, "core", j, rows, core_sem.at[k], j % WINDOW).wait_send()
        if k == 0:
            for j in range(TURN - WINDOW, TURN):
                one = copy(k, "x", j, rows, core_sem.at[k], j % WINDOW)
                last_one = jnp.logical_not(sends["x"](j + WINDOW))
                pl.when(jnp.logical_and(sends["x"](j), last_one))(one.wait_send)

    def came(k):
        count, rows = counts(k)
        part = out.at[pl.ds(pl.multiple_of(base(k, 1 - c), 16), count * rows)]
        pltpu.make_async_remote_copy(
            src_ref=part,
            dst_ref=part,
            send_sem=send_sem.at[k, 3, 0],
            recv_sem=core_sem.at[k],
            device_id=targets["core"],
            device_id_type=MESH,
        ).wait_recv()

    for k in range(4):
        drain(k)
        came(k)
    pl.when(c == 0)(lambda: drain(4))
    pl.when(c == 1)(lambda: came(4))


def gather_and_embed(table, codes, labels, picks, starts, classes, nulls, frequency):
    rows = lambda n: pltpu.VMEM((n * SP, D), BF16)
    return pl.pallas_call(
        open_kernel,
        out_shape=(
            jax.ShapeDtypeStruct((WROWS, D), BF16),
            jax.ShapeDtypeStruct((SP, D), BF16),
            jax.ShapeDtypeStruct((8, 8, 384), jnp.int32),
            jax.ShapeDtypeStruct((16, D), BF16),
            jax.ShapeDtypeStruct((SP, 128), F32),
            jax.ShapeDtypeStruct((SP, 128), F32),
        ),
        in_specs=[VMEM] * 4 + [SMEM] * 3 + [VMEM],
        out_specs=(VMEM,) * 6,
        scratch_shapes=[
            pltpu.SemaphoreType.DMA,
            pltpu.SemaphoreType.DMA((4, NCH)),
            pltpu.SemaphoreType.DMA((NCC,)),
            pltpu.SemaphoreType.DMA((5,)),
            pltpu.SemaphoreType.DMA((5, 4, WINDOW)),
            rows(8),
            rows(8),
            rows(8),
            rows(4),
            rows(4),
            pltpu.SemaphoreType.DMA,
            pltpu.SemaphoreType.DMA((8,)),
            pltpu.SemaphoreType.DMA,
            pltpu.SemaphoreType.DMA((4,)),
            pltpu.SemaphoreType.DMA,
            pltpu.SemaphoreType.DMA((4,)),
            pltpu.SemaphoreType.DMA((4,)),
            pltpu.SemaphoreType.DMA,
            pltpu.SemaphoreType.DMA,
            pltpu.VMEM((8, 384), jnp.int32),
        ]
        + [pltpu.SemaphoreType.DMA] * 4,
        compiler_params=pltpu.CompilerParams(
            collective_id=0, has_side_effects=True, vmem_limit_bytes=56 * 2**20
        ),
        name="gather_and_embed",
    )(table, codes, labels, picks, starts, classes, nulls, frequency)


def close_kernel(
    grads, start, block, index, out, squares, loc, rx_core, rx_up, rx_down, rx_x, total, summed,
    all_dx, load_sem, core_sem, core_c, recv_sem, recv_c, core_send, send_sem, out_sem,
    dx_own, dx_send, line_recv, cross_recv, turn_recv, dx_core_send, dx_core_recv,
):
    sec, dp, z, c, par, home = place()
    targets = hop_targets(sec, dp, c, par)
    classes = tree(z, c, home)
    rx = dict(up=rx_up, down=rx_down, x=rx_x)
    del start

    def base(k, lane):
        if k == 4:
            return 4 * 2 * HALF
        return 2 * HALF * (2 * (k // 2) + lane) + HALF * (k % 2)

    def held(k):
        return k * HALF

    def load(k):
        rows = NCC * CC if k == 4 else HALF
        return pltpu.make_async_copy(
            grads.at[pl.ds(pl.multiple_of(base(k, c), 16), rows)],
            loc.at[pl.ds(held(k), rows)],
            load_sem.at[k],
        )

    for k in range(5):
        load(k).start()
    greet_neighbours(sec, dp, z, c, par, ((1, 2), (2, 0)))

    def to_core(k, j, rows):
        sem = core_c.at[j] if k == 4 else core_sem.at[k, j]
        return pltpu.make_async_remote_copy(
            src_ref=grads.at[pl.ds(pl.multiple_of(base(k, 1 - c) + j * rows, 16), rows)],
            dst_ref=rx_core.at[pl.ds(pl.multiple_of(held(k) + j * rows, 16), rows)],
            send_sem=core_send.at[k],
            recv_sem=sem,
            device_id=targets["core"],
            device_id_type=MESH,
        )

    def start_core(j, carry):
        for k in range(4):
            to_core(k, j, CH).start()
        pl.when(jnp.logical_and(j < NCC, c == 1))(lambda: to_core(4, j, CC).start())
        return carry

    lax.fori_loop(0, NCH, start_core, 0)
    for k in range(5):
        load(k).wait()

    def onward(k, hop, j, rows):
        back = dict(up="down", down="up", x="x")[hop]
        index = ("up", "down", "x").index(back)
        part = pl.ds(pl.multiple_of(held(k) + j * rows, 16), rows)
        return pltpu.make_async_remote_copy(
            src_ref=loc.at[part],
            dst_ref=rx[back].at[part],
            send_sem=send_sem.at[k],
            recv_sem=recv_c.at[index, j] if k == 4 else recv_sem.at[index, k, j],
            device_id=targets[hop],
            device_id_type=MESH,
        )

    def landed(k, hop, j, rows):
        index = ("up", "down", "x").index(hop)
        part = pl.ds(pl.multiple_of(held(k) + j * rows, 16), rows)
        return pltpu.make_async_remote_copy(
            src_ref=loc.at[part],
            dst_ref=rx[hop].at[part],
            send_sem=send_sem.at[k],
            recv_sem=recv_c.at[index, j] if k == 4 else recv_sem.at[index, k, j],
            device_id=targets[hop],
            device_id_type=MESH,
        )

    def write_out(k, j, rows):
        offset = j * rows if k == 4 else HALF * (k % 2) + j * rows
        part = pl.ds(pl.multiple_of(offset, 16), rows)
        return pltpu.make_async_copy(total.at[part], out.at[part], out_sem)

    def start_of(k, j, rows):
        part = pl.ds(pl.multiple_of(held(k) + j * rows, 16), rows)
        to_core(k, j, rows).wait_recv()
        acc = summed.at[pl.ds(0, rows)]
        acc[...] = loc[part, :].astype(F32) + rx_core[part, :].astype(F32)
        return part, acc

    def gathered(k, j, rows):
        part, acc = start_of(k, j, rows)
        for hop in HOPS[:3]:

            def add(hop=hop):
                landed(k, hop, j, rows).wait_recv()
                acc[...] += rx[hop][part, :].astype(F32)

            pl.when(classes[k][1][hop](j))(add)
        return part, acc

    def pass_on(k, j, rows, part, acc):
        loc[part, :] = acc[...].astype(BF16)
        for hop in HOPS[:3]:
            pl.when(classes[k][2][hop](j))(lambda hop=hop: onward(k, hop, j, rows).start())

    def relay(k, j, rows):
        part, acc = gathered(k, j, rows)
        pass_on(k, j, rows, part, acc)

    def finish(k, j, rows):
        _, acc = gathered(k, j, rows)
        offset = j * rows if k == 4 else HALF * (k % 2) + j * rows
        value = acc[...]
        total[pl.ds(pl.multiple_of(offset, 16), rows), :] = value
        write_out(k, j, rows).start()
        count_squares(value)

    first = sec == 0
    second = sec == 2
    in_line = jnp.logical_or(first, second)
    p_line = second.astype(jnp.int32)
    both = jnp.logical_and

    def dx_part(p, zz):
        return all_dx.at[pl.ds(pl.multiple_of((2 * (2 * zz + c) + p) * SP, 16), SP)]

    def move(p, zz, send, recv, target):
        return pltpu.make_async_remote_copy(
            src_ref=dx_part(p, zz),
            dst_ref=dx_part(p, zz),
            send_sem=send,
            recv_sem=recv,
            device_id=target,
            device_id_type=MESH,
        )

    def line(zz, hop):
        return move(p_line, zz, dx_send, line_recv.at[zz], targets[hop])

    def cross(zz):
        return move(1, zz, dx_send, cross_recv.at[zz], (0, dp))

    def dx_to_core(p, zz):
        return move(p, zz, dx_core_send, dx_core_recv, targets["core"])

    def aside(zz):
        pl.when(first)(lambda: dx_to_core(0, zz).start())
        pl.when(second)(lambda: cross(zz).start())

    def crossed(zz):
        cross(zz).wait_recv()
        dx_to_core(1, zz).start()

    def blocks(count, send, recv):
        return pltpu.make_async_remote_copy(
            src_ref=all_dx.at[pl.ds(0, count * SP)],
            dst_ref=all_dx.at[pl.ds(0, count * SP)],
            send_sem=send,
            recv_sem=recv,
            device_id=targets["core"],
            device_id_type=MESH,
        )

    turned = pltpu.make_async_remote_copy(
        src_ref=block,
        dst_ref=dx_part(1, z),
        send_sem=dx_send,
        recv_sem=turn_recv,
        device_id=(2, dp),
        device_id_type=MESH,
    )
    pl.when(sec == 1)(turned.start)

    def pass_own():
        pl.when(z < 3)(lambda: line(z, "up").start())
        pl.when(z > 0)(lambda: line(z, "down").start())
        aside(z)

    def own_first():
        own = pltpu.make_async_copy(block, dx_part(0, z), dx_own)
        own.start()
        own.wait()
        pass_own()

    def own_second():
        turned.wait_recv()
        pass_own()

    pl.when(first)(own_first)

    def from_below(k):
        line(z - k, "up").wait_recv()
        pl.when(z < 3)(lambda: line(z - k, "up").start())
        aside(z - k)

    def from_above(k):
        line(z + k, "down").wait_recv()
        pl.when(z > 0)(lambda: line(z + k, "down").start())
        aside(z + k)

    def tile(t):
        there = pl.ds(pl.multiple_of(t * 128, 128), 128)
        ids = lax.broadcasted_iota(jnp.int32, (128, 16 * SP), 0) + t * 128
        onehot = jnp.where(ids == index[...], 1.0, 0.0).astype(BF16)
        value = nn(onehot, all_dx[...]) * math.sqrt(D)
        total[there, :] = value
        pltpu.make_async_copy(total.at[there], out.at[there], out_sem).start()
        count_squares(value)

    def collect(i):
        pl.when(both(second, i == HOP))(own_second)
        for k in range(1, 4):
            now = i == HOP * (k + p_line)
            pl.when(both(now, z >= k))(lambda k=k: from_below(k))
            pl.when(both(now, z + k <= 3))(lambda k=k: from_above(k))

    def embed(i):
        pl.when(i == 2 * HOP)(lambda: crossed(z))
        for k in range(1, 4):
            pl.when(both(i == HOP * (k + 2), z >= k))(lambda k=k: crossed(z - k))
            pl.when(both(i == HOP * (k + 2), z + k <= 3))(lambda k=k: crossed(z + k))
        begin = 5 * HOP + 1
        pl.when(i == begin)(lambda: blocks(8, dx_core_send, dx_core_recv).wait_recv())
        for half in range(2):
            t = 2 * (i - begin) + half
            pl.when(both(t >= 0, t < 17))(lambda t=t: tile(t))

    squares[...] = jnp.zeros_like(squares)

    def count_squares(value):
        folded = value * value
        size = folded.shape[0]
        while size > 8 and size % 16 == 0:
            size //= 2
            folded = folded[:size] + folded[size:]
        for part in range(size // 8):
            squares[...] += folded[part * 8 : (part + 1) * 8]

    def step(i, carry):
        for k in range(5):
            count, rows = (NCC, CC) if k == 4 else (NCH, CH)
            source, _, _, depth = classes[k]
            j = i - LAG * ((5, 5, 4, 4, 3)[k] - depth)
            now = jnp.logical_and(j >= 0, j < count)
            if k == 4:
                now = jnp.logical_and(now, c == 0)
            pl.when(jnp.logical_and(now, jnp.logical_not(source)))(
                lambda k=k, j=j, rows=rows: relay(k, j, rows)
            )
            pl.when(jnp.logical_and(now, source))(lambda k=k, j=j, rows=rows: finish(k, j, rows))
        pl.when(in_line)(lambda: collect(i))
        pl.when(first)(lambda: embed(i))
        return carry

    lax.fori_loop(0, max(NCH + 5 * LAG, 5 * HOP + 1 + 9), step, 0)
    pl.when(first)(lambda: blocks(8, dx_core_send, dx_core_recv).wait_send())

    def dx_sent(count):
        blocks(count, dx_send, dx_core_recv).wait_send()

    middle = both(z >= 1, z <= 2)
    ends = jnp.logical_not(middle)
    pl.when(jnp.logical_or(sec == 1, both(first, ends)))(lambda: dx_sent(1))
    pl.when(both(first, middle))(lambda: dx_sent(5))
    pl.when(both(second, ends))(lambda: dx_sent(5))
    pl.when(both(second, middle))(lambda: dx_sent(9))
    for k in range(5):
        rows = NCC * CC if k == 4 else HALF
        source, _, parents, _ = classes[k]
        whole = pl.ds(held(k), rows)
        sent_core = pltpu.make_async_remote_copy(
            src_ref=grads.at[pl.ds(0, rows)],
            dst_ref=rx_core.at[whole],
            send_sem=core_send.at[k],
            recv_sem=core_c.at[0],
            device_id=targets["core"],
            device_id_type=MESH,
        )
        sent = pltpu.make_async_remote_copy(
            src_ref=loc.at[whole],
            dst_ref=rx_x.at[whole],
            send_sem=send_sem.at[k],
            recv_sem=core_c.at[0],
            device_id=targets["x"],
            device_id_type=MESH,
        )
        if k == 4:
            pl.when(c == 1)(sent_core.wait_send)
            pl.when(jnp.logical_and(jnp.logical_not(source), c == 0))(sent.wait_send)
        else:
            sent_core.wait_send()
            pl.when(jnp.logical_not(source))(sent.wait_send)
    done_all = pltpu.make_async_copy(total, out, out_sem)
    part = pl.ds(0, NCC * CC)
    done_few = pltpu.make_async_copy(total.at[part], out.at[part], out_sem)
    pl.when(jnp.logical_or(jnp.logical_and(home, z < 2), sec == 0))(done_all.wait)
    pl.when(classes[4][0])(done_few.wait)


def reduce_and_scatter(grads, start, block, index):
    rows = LANE + NCC * CC
    return pl.pallas_call(
        close_kernel,
        out_shape=(
            jax.ShapeDtypeStruct((2 * HALF, D), F32),
            jax.ShapeDtypeStruct((8, D), F32),
        ),
        in_specs=[ANY, ANY, VMEM, VMEM],
        out_specs=(ANY, VMEM),
        input_output_aliases={1: 0},
        scratch_shapes=[pltpu.VMEM((rows, D), BF16)] * 5
        + [
            pltpu.VMEM((2 * HALF, D), F32),
            pltpu.VMEM((CH, D), F32),
            pltpu.VMEM((16 * SP, D), BF16),
            pltpu.SemaphoreType.DMA((5,)),
            pltpu.SemaphoreType.DMA((4, NCH)),
            pltpu.SemaphoreType.DMA((NCC,)),
            pltpu.SemaphoreType.DMA((3, 4, NCH)),
            pltpu.SemaphoreType.DMA((3, NCC)),
            pltpu.SemaphoreType.DMA((5,)),
            pltpu.SemaphoreType.DMA((5,)),
            pltpu.SemaphoreType.DMA,
            pltpu.SemaphoreType.DMA,
            pltpu.SemaphoreType.DMA,
            pltpu.SemaphoreType.DMA((4,)),
            pltpu.SemaphoreType.DMA((4,)),
            pltpu.SemaphoreType.DMA,
            pltpu.SemaphoreType.DMA,
            pltpu.SemaphoreType.DMA,
        ],
        compiler_params=pltpu.CompilerParams(
            collective_id=1, has_side_effects=True, vmem_limit_bytes=60 * 2**20
        ),
        name="reduce_and_scatter",
    )(grads, start, block, index)


def share_kernel(n_sec, n_dp, block, out, send_sem, recv_sem, own_sem):
    sec = lax.axis_index("section")
    dp = lax.axis_index("dp")
    n = n_sec * n_dp
    me = sec * n_dp + dp
    barrier = pltpu.get_barrier_semaphore()
    own = pltpu.make_async_copy(block, out.at[me], own_sem)
    own.start()

    def peer(k):
        other = lax.rem(me + k, n)
        return (other // n_dp, lax.rem(other, n_dp))

    def greet(k, carry):
        pl.semaphore_signal(barrier, 1, device_id=peer(k), device_id_type=MESH)
        return carry

    lax.fori_loop(1, n, greet, 0)
    pl.semaphore_wait(barrier, n - 1)

    def send(k, carry):
        pltpu.make_async_remote_copy(
            src_ref=block,
            dst_ref=out.at[me],
            send_sem=send_sem,
            recv_sem=recv_sem,
            device_id=peer(k),
            device_id_type=MESH,
        ).start()
        return carry

    lax.fori_loop(1, n, send, 0)
    every = pltpu.make_async_remote_copy(
        src_ref=out.at[pl.ds(0, n - 1)],
        dst_ref=out.at[pl.ds(0, n - 1)],
        send_sem=send_sem,
        recv_sem=recv_sem,
        device_id=peer(1),
        device_id_type=MESH,
    )
    own.wait()
    every.wait_send()
    every.wait_recv()


def share(block, n_sec, n_dp, cid, name):
    return pl.pallas_call(
        functools.partial(share_kernel, n_sec, n_dp),
        out_shape=jax.ShapeDtypeStruct((n_sec * n_dp,) + block.shape, block.dtype),
        in_specs=[VMEM],
        out_specs=VMEM,
        scratch_shapes=[
            pltpu.SemaphoreType.DMA,
            pltpu.SemaphoreType.DMA,
            pltpu.SemaphoreType.DMA,
        ],
        compiler_params=pltpu.CompilerParams(collective_id=cid, has_side_effects=True),
        name=name,
    )(block)


NEG = -1e30
FT = 256


def turn(block, cosine, sine, lanes):
    ahead = pltpu.roll(block, 96, 1)
    behind = pltpu.roll(block, 32, 1)
    return block * cosine + jnp.where(lax.rem(lanes, 64) < 32, ahead, behind) * sine


def see(starts):
    par = lax.rem(lax.axis_index("section"), 2)
    rows = lax.broadcasted_iota(jnp.int32, (SP, SP), 0)
    cols = lax.broadcasted_iota(jnp.int32, (SP, SP), 1)
    same = segment_of(starts, par, rows)[0] == segment_of(starts, par, cols)[0]
    allowed = jnp.logical_and(same, cols <= rows)
    return jnp.where(allowed, 0.0, NEG)


def softmax_of(scores, unseen):
    masked = scores + unseen
    grown = jnp.exp(masked - jnp.max(masked, axis=-1, keepdims=True))
    return grown / jnp.sum(grown, axis=-1, keepdims=True)


def weight_copies(w_any, w, sems):
    bounds = (0, 3 * D, 4 * D, 4 * D + FF, 4 * D + 2 * FF, MATS, WROWS)
    return [
        pltpu.make_async_copy(
            w_any.at[pl.ds(lo, hi - lo)], w.at[pl.ds(lo, hi - lo)], sems.at[i]
        )
        for i, (lo, hi) in enumerate(zip(bounds[:-1], bounds[1:]))
    ]


def forward_kernel(
    x, w_any, cosine, sine, starts, y, q, k, v, o, h, gate, up, w, m, unseen, sems
):
    copies = weight_copies(w_any, w, sems)
    for i in (5, 0, 1, 2, 3, 4):
        copies[i].start()
    unseen[...] = see(starts)
    lanes = lax.broadcasted_iota(jnp.int32, (SP, 128), 1)
    first = lanes < 64
    copies[5].wait()
    gains = w[pl.ds(MATS, 16), :].astype(F32)
    stream = x[...].astype(F32)
    a1 = rms_scale(stream, gains[0:1]).astype(BF16)
    copies[0].wait()

    def project(b, carry):
        cols = pl.ds(pl.multiple_of(b * 256, 256), 256)
        raw_q = nn(a1, w[pl.ds(0, D), cols])
        raw_k = nn(a1, w[pl.ds(D, D), cols])
        raw_v = nn(a1, w[pl.ds(2 * D, D), cols])
        v[:, cols] = raw_v.astype(BF16)
        for part in range(2):
            there = pl.ds(pl.multiple_of(b * 256 + part * 128, 128), 128)
            here = slice(part * 128, (part + 1) * 128)
            turned_q = turn(raw_q[:, here], cosine[...], sine[...], lanes)
            q[:, there] = (turned_q * HD ** (-0.5)).astype(BF16)
            k[:, there] = turn(raw_k[:, here], cosine[...], sine[...], lanes).astype(BF16)
        return carry

    lax.fori_loop(0, D // 256, project, 0)

    def attend(b, carry):
        cols = pl.ds(pl.multiple_of(b * 128, 128), 128)
        qb, kb, vb = q[:, cols], k[:, cols], v[:, cols]
        zero = jnp.zeros_like(qb)
        p0 = softmax_of(nt(jnp.where(first, qb, zero), kb), unseen[...]).astype(BF16)
        p1 = softmax_of(nt(jnp.where(first, zero, qb), kb), unseen[...]).astype(BF16)
        o[:, cols] = jnp.where(first, nn(p0, vb), nn(p1, vb)).astype(BF16)
        return carry

    lax.fori_loop(0, HEADS // 2, attend, 0)
    copies[1].wait()
    for b in range(3):
        cols = pl.ds(b * 256, 256)
        h[:, cols] = x[:, cols].astype(F32) + nn(o[...], w[pl.ds(3 * D, D), cols])
    a2 = rms_scale(h[...], gains[1:2]).astype(BF16)
    copies[2].wait()
    copies[3].wait()

    def widen(b, carry):
        cols = pl.ds(pl.multiple_of(b * FT, FT), FT)
        g = nt(a2, w[pl.ds(pl.multiple_of(4 * D + b * FT, FT), FT), :])
        u = nt(a2, w[pl.ds(pl.multiple_of(4 * D + FF + b * FT, FT), FT), :])
        gate[:, cols] = g
        up[:, cols] = u
        m[:, cols] = (g / (1.0 + jnp.exp(-g)) * u).astype(BF16)
        return carry

    lax.fori_loop(0, FF // FT, widen, 0)
    copies[4].wait()

    def narrow(b, carry):
        cols = pl.ds(pl.multiple_of(b * 256, 256), 256)
        y[:, cols] = (h[:, cols] + nn(m[...], w[pl.ds(4 * D + 2 * FF, FF), cols])).astype(BF16)
        return carry

    lax.fori_loop(0, 3, narrow, 0)


def forward_call(x, weights, cosine, sine, starts):
    low = jax.ShapeDtypeStruct((SP, D), BF16)
    wide = jax.ShapeDtypeStruct((SP, FF), F32)
    return pl.pallas_call(
        forward_kernel,
        out_shape=(low, low, low, low, low, jax.ShapeDtypeStruct((SP, D), F32), wide, wide),
        in_specs=[VMEM, ANY, VMEM, VMEM, SMEM],
        out_specs=(VMEM,) * 8,
        scratch_shapes=[
            pltpu.VMEM((WROWS, D), BF16),
            pltpu.VMEM((SP, FF), BF16),
            pltpu.VMEM((SP, SP), F32),
            pltpu.SemaphoreType.DMA((6,)),
        ],
        compiler_params=pltpu.CompilerParams(vmem_limit_bytes=48 * 2**20),
        name="layer_forward",
    )(x, weights, cosine, sine, starts)


def rms_back(value_in, gain, grad):
    inv = lax.rsqrt(jnp.mean(value_in * value_in, axis=-1, keepdims=True) + norm_eps)
    unit = value_in * inv
    scaled = grad * gain
    grad_in = inv * (scaled - unit * jnp.mean(scaled * unit, axis=-1, keepdims=True))
    return grad_in, jnp.sum(grad * unit, axis=0, keepdims=True)


def backward_kernel(
    with_weights, dy, x, w_any, cosine, sine, starts, q, k, v, o, h, gate, up, *refs
):
    if with_weights:
        dx, grads, w, dgate, dup, m, da, do, dq, dk, dv, unseen, sems = refs
    else:
        dx, w, dgate, dup, m, da, do, dq, dk, dv, unseen, sems = refs
    copies = weight_copies(w_any, w, sems)
    for i in (4, 5, 2, 3, 1, 0):
        copies[i].start()
    unseen[...] = see(starts)
    lanes = lax.broadcasted_iota(jnp.int32, (SP, 128), 1)
    first = lanes < 64
    copies[4].wait()

    def open_mlp(b, carry):
        cols = pl.ds(pl.multiple_of(b * FT, FT), FT)
        dm = nt(dy[...], w[pl.ds(pl.multiple_of(4 * D + 2 * FF + b * FT, FT), FT), :])
        g = gate[:, cols]
        u = up[:, cols]
        sig = 1.0 / (1.0 + jnp.exp(-g))
        dgate[:, cols] = (dm * u * sig * (1.0 + g * (1.0 - sig))).astype(BF16)
        dup[:, cols] = (dm * g * sig).astype(BF16)
        if with_weights:
            m[:, cols] = (g * sig * u).astype(BF16)
        return carry

    lax.fori_loop(0, FF // FT, open_mlp, 0)
    copies[5].wait()
    gains = w[pl.ds(MATS, 16), :].astype(F32)
    copies[2].wait()
    copies[3].wait()

    def close_mlp(b, carry):
        cols = pl.ds(pl.multiple_of(b * 256, 256), 256)
        da[:, cols] = nn(dgate[...], w[pl.ds(4 * D, FF), cols]) + nn(
            dup[...], w[pl.ds(4 * D + FF, FF), cols]
        )
        return carry

    lax.fori_loop(0, 3, close_mlp, 0)
    dh, dg_mlp = rms_back(h[...], gains[1:2], da[...])
    dh = dh + dy[...].astype(F32)
    db = dh.astype(BF16)
    copies[1].wait()
    for b in range(3):
        do[:, pl.ds(b * 256, 256)] = nt(db, w[pl.ds(3 * D + b * 256, 256), :]).astype(BF16)

    def attend(b, carry):
        cols = pl.ds(pl.multiple_of(b * 128, 128), 128)
        qb, kb, vb, dob = q[:, cols], k[:, cols], v[:, cols], do[:, cols]
        zero = jnp.zeros_like(qb)
        parts = []
        for head in range(2):
            keep = first if head == 0 else jnp.logical_not(first)
            probs = softmax_of(nt(jnp.where(keep, qb, zero), kb), unseen[...])
            dprobs = nt(jnp.where(keep, dob, zero), vb)
            along = jnp.sum(probs * dprobs, axis=-1, keepdims=True)
            dscores = (probs * (dprobs - along)).astype(BF16)
            parts.append((nn(dscores, kb), tn(dscores, qb), tn(probs.astype(BF16), dob)))
        dqb = jnp.where(first, parts[0][0], parts[1][0]) * HD ** (-0.5)
        dkb = jnp.where(first, parts[0][1], parts[1][1])
        dq[:, cols] = turn(dqb, cosine[...], -sine[...], lanes).astype(BF16)
        dk[:, cols] = turn(dkb, cosine[...], -sine[...], lanes).astype(BF16)
        dv[:, cols] = jnp.where(first, parts[0][2], parts[1][2]).astype(BF16)
        return carry

    lax.fori_loop(0, HEADS // 2, attend, 0)
    copies[0].wait()
    for b in range(3):
        rows = lambda i, b=b: w[pl.ds(i * D + b * 256, 256), :]
        da[:, pl.ds(b * 256, 256)] = (
            nt(dq[...], rows(0)) + nt(dk[...], rows(1)) + nt(dv[...], rows(2))
        )
    stream = x[...].astype(F32)
    dstream, dg_attn = rms_back(stream, gains[0:1], da[...])
    dx[...] = (dstream + dh).astype(BF16)
    if not with_weights:
        return
    a1 = rms_scale(stream, gains[0:1]).astype(BF16)
    a2 = rms_scale(h[...], gains[1:2]).astype(BF16)
    for b in range(3):
        cols = slice(b * 256, (b + 1) * 256)
        piece = a1[:, cols]
        for i, right in enumerate((dq, dk, dv)):
            grads[pl.ds(i * D + b * 256, 256), :] = tn(piece, right[...]).astype(BF16)
        grads[pl.ds(3 * D + b * 256, 256), :] = tn(o[:, cols], db).astype(BF16)

    def outer(b, carry):
        cols = pl.ds(pl.multiple_of(b * FT, FT), FT)
        base = 4 * D + b * FT
        for i, (left, right) in enumerate(((dgate, a2), (dup, a2), (m, dy))):
            there = pl.ds(pl.multiple_of(base + i * FF, FT), FT)
            grads[there, :] = tn(left[:, cols], right[...]).astype(BF16)
        return carry

    lax.fori_loop(0, FF // FT, outer, 0)
    tail = lax.broadcasted_iota(jnp.int32, (16, D), 0)
    grads[pl.ds(MATS, 16), :] = jnp.where(
        tail == 0, dg_attn, jnp.where(tail == 1, dg_mlp, 0.0)
    ).astype(BF16)


def backward_call(with_weights, dy, x, weights, cosine, sine, starts, kept):
    low = jax.ShapeDtypeStruct((SP, D), BF16)
    out_shape = (low, jax.ShapeDtypeStruct((WROWS, D), BF16)) if with_weights else low
    wide = pltpu.VMEM((SP, FF), BF16)
    narrow = pltpu.VMEM((SP, D), BF16)
    return pl.pallas_call(
        functools.partial(backward_kernel, with_weights),
        out_shape=out_shape,
        in_specs=[VMEM, VMEM, ANY, VMEM, VMEM, SMEM] + [VMEM] * 7,
        out_specs=(VMEM, VMEM) if with_weights else VMEM,
        scratch_shapes=[
            pltpu.VMEM((WROWS, D), BF16),
            wide,
            wide,
            wide,
            pltpu.VMEM((SP, D), F32),
            narrow,
            narrow,
            narrow,
            narrow,
            pltpu.VMEM((SP, SP), F32),
            pltpu.SemaphoreType.DMA((6,)),
        ],
        compiler_params=pltpu.CompilerParams(vmem_limit_bytes=60 * 2**20),
        name="layer_backward_weights" if with_weights else "layer_backward",
    )(dy, x, weights, cosine, sine, starts, *kept)


HEAD_T = 256


def column(row, size):
    there = lax.broadcasted_iota(jnp.int32, (size, size), 0)
    here = lax.broadcasted_iota(jnp.int32, (size, size), 1)
    zero = jnp.zeros((), row.dtype)
    return jnp.sum(jnp.where(there == here, row, zero), axis=1, keepdims=True)


def as_rows(values):
    there = lax.broadcasted_iota(jnp.int32, (128, 128), 0)
    here = lax.broadcasted_iota(jnp.int32, (128, 128), 1)
    return [
        jnp.sum(
            jnp.where(there == here, values[k * 128 : (k + 1) * 128], 0.0), axis=0, keepdims=True
        )
        for k in range(4)
    ]


def head_kernel(
    y, picks, info, gain, table, d_top, d_table, small, mine, picked, af, scores, dlow, labels,
    counts, stat, stats, daf, rx_core, low, rx, fresh, zero_sem, own_sem, pick_send, pick_recv,
    core_send, core_recv, stat_send, stat_recv, swap_send, swap_recv, daf_send, daf_recv,
):
    sec, dp, z, c, par, home = place()
    last = sec == 3
    upper = sec >= 2
    barrier = pltpu.get_barrier_semaphore()
    other_core = (3, dp + 1 - 2 * c)

    def greet(s, e):
        pl.semaphore_signal(barrier, 1, device_id=(s, e), device_id_type=MESH)

    def greet_second():
        for k in range(4):
            greet(3, 2 * k + c)
        pl.semaphore_wait(barrier, 4)

    def greet_third():
        for k in range(4):
            greet(2, 2 * k + c)
        for k in range(1, 8):
            greet(3, lax.rem(dp + k, 8))
        pl.semaphore_wait(barrier, 11)

    all_zero = pltpu.make_async_copy(fresh, d_table, zero_sem)

    def zeros():
        fresh[...] = jnp.zeros_like(fresh)
        all_zero.start()

    pl.when(jnp.logical_not(last))(zeros)
    small[...] = jnp.zeros_like(small)
    pick_row = picks[pl.ds(par, 1), :]
    pick_col = column(pick_row, PICKS)

    def choose():
        ids = lax.broadcasted_iota(jnp.int32, (PICKS, SP), 1)
        mine[...] = nn(jnp.where(ids == pick_col, 1.0, 0.0).astype(BF16), y[...]).astype(BF16)

    pl.when(upper)(choose)
    pl.when(sec == 2)(greet_second)
    pl.when(last)(greet_third)

    def rows(p, zz, lane):
        return pl.ds(pl.multiple_of((2 * (2 * zz + lane) + p) * PICKS, PICKS), PICKS)

    def pick_to(k):
        zz = lax.rem(z + k, 4)
        return pltpu.make_async_remote_copy(
            src_ref=mine,
            dst_ref=picked.at[rows(par, z, c)],
            send_sem=pick_send,
            recv_sem=pick_recv.at[par, z],
            device_id=(3, 2 * zz + c),
            device_id_type=MESH,
        )

    def came(p, k):
        zz = lax.rem(z + k, 4)
        return pltpu.make_async_remote_copy(
            src_ref=mine,
            dst_ref=picked.at[rows(p, zz, c)],
            send_sem=pick_send,
            recv_sem=pick_recv.at[p, zz],
            device_id=other_core,
            device_id_type=MESH,
        )

    def forward(p, k):
        part = picked.at[rows(p, lax.rem(z + k, 4), c)]
        return pltpu.make_async_remote_copy(
            src_ref=part,
            dst_ref=part,
            send_sem=core_send,
            recv_sem=core_recv,
            device_id=other_core,
            device_id_type=MESH,
        )

    def span(ref, count, send, recv):
        part = ref.at[pl.ds(0, count)]
        return pltpu.make_async_remote_copy(
            src_ref=part,
            dst_ref=part,
            send_sem=send,
            recv_sem=recv,
            device_id=other_core,
            device_id_type=MESH,
        )

    def pick_second():
        for k in (1, 2, 3, 0):
            pick_to(k).start()

    def pick_third():
        own = pltpu.make_async_copy(mine, picked.at[rows(1, z, c)], own_sem)
        own.start()
        for k in range(1, 4):
            pick_to(k).start()
        for e in range(8):
            for p in range(2):
                at = pl.ds((2 * e + p) * PICKS, PICKS)
                labels[at, :] = column(info[e, 2 + p : 3 + p, :][:, :PICKS], PICKS)
                counts[at, :] = column(info[e, 4 + p : 5 + p, :][:, :PICKS].astype(F32), PICKS)
        own.wait()
        forward(1, 0).start()
        for k in range(4):
            came(0, k).wait_recv()
            forward(0, k).start()
            if k:
                came(1, k).wait_recv()
                forward(1, k).start()
        span(picked, 8 * PICKS, core_send, core_recv).wait_recv()

    pl.when(sec == 2)(pick_second)
    pl.when(last)(pick_third)
    g_f = gain[...].astype(F32)[0:1]
    own = 2 * HALF
    tiles = [(t * HEAD_T, HEAD_T) for t in range(own // HEAD_T)] + [
        (own - own % HEAD_T, own % HEAD_T)
    ]

    def over_tiles(body):
        def step(t, carry):
            body(pl.multiple_of(t * HEAD_T, HEAD_T), HEAD_T)
            return carry

        lax.fori_loop(0, own // HEAD_T, step, 0)
        body(own - own % HEAD_T, own % HEAD_T)

    def forward_part():
        af[...] = rms_scale(picked[...].astype(F32), g_f).astype(BF16)
        fold = lambda op, block: functools.reduce(
            op, [block[:, k * 128 : (k + 1) * 128] for k in range(block.shape[1] // 128)]
        )
        top = daf.at[:, pl.ds(0, 128)]
        top[...] = jnp.full((16 * PICKS, 128), NEG, F32)

        def product(start, size):
            ids = lax.broadcasted_iota(jnp.int32, (16 * PICKS, size), 1) + (dp * own + start)
            block = nt(af[...], table[pl.ds(start, size), :])
            block = jnp.where(ids < VOCAB, block, NEG)
            scores[:, pl.ds(start, size)] = block
            top[...] = jnp.maximum(top[...], fold(jnp.maximum, block))

        over_tiles(product)
        top_col = jnp.max(top[...], axis=1, keepdims=True)
        total = daf.at[:, pl.ds(128, 128)]
        target = daf.at[:, pl.ds(256, 128)]
        total[...] = jnp.zeros((16 * PICKS, 128), F32)
        target[...] = jnp.zeros((16 * PICKS, 128), F32)

        def exponents(start, size):
            ids = lax.broadcasted_iota(jnp.int32, (16 * PICKS, size), 1) + (dp * own + start)
            block = scores[:, pl.ds(start, size)]
            grown = jnp.exp(block - top_col)
            scores[:, pl.ds(start, size)] = grown
            total[...] += fold(jnp.add, grown)
            target[...] += fold(jnp.add, jnp.where(ids == labels[...], block, 0.0))

        over_tiles(exponents)
        stat[...] = jnp.zeros_like(stat)
        columns = (
            top_col,
            jnp.sum(total[...], axis=1, keepdims=True),
            jnp.sum(target[...], axis=1, keepdims=True),
        )
        for k, values in enumerate(columns):
            for i, row in enumerate(as_rows(values)):
                stat[4 * k + i : 4 * k + i + 1, :] = row
        stats[dp] = stat[...]
        for k in range(1, 8):
            pltpu.make_async_remote_copy(
                src_ref=stat,
                dst_ref=stats.at[dp],
                send_sem=stat_send,
                recv_sem=stat_recv,
                device_id=(3, lax.rem(dp + k, 8)),
                device_id_type=MESH,
            ).start()
        every = span(stats, 7, stat_send, stat_recv)
        every.wait_recv()
        tops = [stats[e, 0:4, :] for e in range(8)]
        best = functools.reduce(jnp.maximum, tops)
        sums = sum(stats[e, 4:8, :] * jnp.exp(tops[e] - best) for e in range(8))
        hits = sum(stats[e, 8:12, :] for e in range(8))
        log_total = best + jnp.log(sums)
        log_col = jnp.concatenate([column(log_total[k : k + 1], 128) for k in range(4)], axis=0)
        hit_col = jnp.concatenate([column(hits[k : k + 1], 128) for k in range(4)], axis=0)
        loss = jnp.sum(
            jnp.where(counts[...] > 0, log_col - hit_col, 0.0), axis=0, keepdims=True
        )
        lane = lax.broadcasted_iota(jnp.int32, (1, 128), 1)
        small[6:7, :] = jnp.where(jnp.logical_and(lane == 0, dp == 0), loss, 0.0)
        shrink = jnp.exp(top_col - log_col)

        def slopes(start, size):
            ids = lax.broadcasted_iota(jnp.int32, (16 * PICKS, size), 1) + (dp * own + start)
            hit = jnp.where(ids == labels[...], 1.0, 0.0)
            block = (scores[:, pl.ds(start, size)] * shrink - hit) * counts[...]
            dlow[:, pl.ds(start, size)] = block.astype(BF16)

        over_tiles(slopes)
        for b in range(3):
            cols = pl.ds(b * 256, 256)
            daf[:, cols] = nn(dlow[...], table[:, cols])
        every.wait_send()
        span(picked, 3 * PICKS, pick_send, core_recv).wait_send()
        span(picked, 8 * PICKS, core_send, core_recv).wait_send()

    def swap(p, zz):
        return pltpu.make_async_remote_copy(
            src_ref=daf.at[rows(p, zz, 1 - c)],
            dst_ref=rx_core.at[pl.ds((2 * zz + p) * PICKS, PICKS)],
            send_sem=swap_send,
            recv_sem=swap_recv,
            device_id=other_core,
            device_id_type=MESH,
        )

    def back_to(p, k):
        zz = lax.rem(z + k, 4)
        return pltpu.make_async_remote_copy(
            src_ref=low.at[pl.ds(pl.multiple_of((2 * zz + p) * PICKS, PICKS), PICKS)],
            dst_ref=rx.at[z],
            send_sem=daf_send,
            recv_sem=daf_recv,
            device_id=(2 + p, 2 * zz + c),
            device_id_type=MESH,
        )

    def table_part(start, size):
        there = pl.ds(start, size)
        value = tn(dlow[:, there], af[...])
        fresh[there, :] = value
        pltpu.make_async_copy(fresh.at[there], d_table.at[there], zero_sem).start()
        folded = jnp.sum(value * value, axis=0, keepdims=True)
        small[7:8, :] += functools.reduce(
            jnp.add, [folded[:, k * 128 : (k + 1) * 128] for k in range(6)]
        )

    def third():
        forward_part()
        for zz in range(4):
            for p in range(2):
                swap(p, zz).start()
        table_part(own - own % HEAD_T, own % HEAD_T)
        span(rx_core, 8 * PICKS, swap_send, swap_recv).wait_recv()
        for zz in range(4):
            for p in range(2):
                there = pl.ds((2 * zz + p) * PICKS, PICKS)
                low[there, :] = (daf[rows(p, zz, c), :] + rx_core[there, :]).astype(BF16)
        for k in (1, 2, 3, 0):
            back_to(0, k).start()
            if k:
                back_to(1, k).start()

        def step(t, carry):
            table_part(pl.multiple_of(t * HEAD_T, HEAD_T), HEAD_T)
            return carry

        lax.fori_loop(0, own // HEAD_T, step, 0)
        rx[z] = low[pl.ds(pl.multiple_of((2 * z + 1) * PICKS, PICKS), PICKS), :]
        span(rx_core, 8 * PICKS, swap_send, swap_recv).wait_send()
        span(low, 7 * PICKS, daf_send, daf_recv).wait_send()
        span(rx, 3, daf_send, daf_recv).wait_recv()

    def second():
        span(picked, 4 * PICKS, pick_send, core_recv).wait_send()
        span(rx, 4, daf_send, daf_recv).wait_recv()

    pl.when(last)(third)
    pl.when(sec == 2)(second)

    def finish():
        summed = rx[0].astype(F32)
        for k in range(1, 4):
            summed = summed + rx[k].astype(F32)
        grad, dg_f = rms_back(mine[...].astype(F32), g_f, summed)
        for k in range(6):
            small[k : k + 1, :] = dg_f[:, k * 128 : (k + 1) * 128]
        ids = lax.broadcasted_iota(jnp.int32, (SP, PICKS), 0)
        spread = jnp.where(ids == pick_row, 1.0, 0.0).astype(BF16)
        rest = grad
        out = jnp.zeros((SP, D), F32)
        for _ in range(3):
            part = rest.astype(BF16)
            out = out + nn(spread, part)
            rest = rest - part.astype(F32)
        d_top[...] = out.astype(BF16)

    def none():
        d_top[...] = jnp.zeros_like(d_top)

    pl.when(upper)(finish)
    pl.when(jnp.logical_not(upper))(none)
    all_zero.wait()


def head_call(y, picks, info, gain, table):
    low = lambda *shape: pltpu.VMEM(shape, BF16)
    wide = lambda *shape: pltpu.VMEM(shape, F32)
    n = 16 * PICKS
    return pl.pallas_call(
        head_kernel,
        out_shape=(
            jax.ShapeDtypeStruct((SP, D), BF16),
            jax.ShapeDtypeStruct((2 * HALF, D), F32),
            jax.ShapeDtypeStruct((8, 128), F32),
        ),
        in_specs=[VMEM] * 5,
        out_specs=(VMEM, ANY, VMEM),
        scratch_shapes=[
            low(PICKS, D),
            low(n, D),
            low(n, D),
            wide(n, 2 * HALF),
            low(n, 2 * HALF),
            pltpu.VMEM((n, 1), jnp.int32),
            wide(n, 1),
            wide(16, 128),
            wide(8, 16, 128),
            wide(n, D),
            wide(8 * PICKS, D),
            low(8 * PICKS, D),
            low(4, PICKS, D),
            wide(2 * HALF, D),
            pltpu.SemaphoreType.DMA,
            pltpu.SemaphoreType.DMA,
            pltpu.SemaphoreType.DMA,
            pltpu.SemaphoreType.DMA((2, 4)),
        ]
        + [pltpu.SemaphoreType.DMA] * 8,
        compiler_params=pltpu.CompilerParams(
            collective_id=3, has_side_effects=True, vmem_limit_bytes=56 * 2**20
        ),
        name="head",
    )(y, picks, info, gain, table)


def open_anywhere(codes, labels, picks, classes, null_mask, starts, table, frequency):
    sec = lax.axis_index("section")
    d = lax.axis_index("dp")
    par = lax.rem(sec, 2)
    own = table.shape[0]
    row_index, counted, _, position = jax.vmap(row_layout)(starts, classes, null_mask, codes)
    picked_labels = jnp.take_along_axis(labels, picks, axis=1)
    picked_counts = jnp.take_along_axis(counted, picks, axis=1).astype(jnp.int32)
    row_index = jnp.pad(row_index, ((0, 0), (0, SP - SLOTS)), constant_values=-1)
    info = jnp.concatenate([row_index, picked_labels, picked_counts], axis=1)
    info = lax.all_gather(info, "dp", axis=0, tiled=True)
    all_labels = info[:, SP : SP + PICKS].reshape(-1)
    all_counts = info[:, SP + PICKS :].reshape(-1).astype(F32)
    gain_row = lax.slice_in_dim(table, VOCAB % own, VOCAB % own + 1)[0].astype(F32)
    holds = (sec == 3) & (d == VOCAB // own)
    g_f = lax.psum(jnp.where(holds, gain_row, 0.0), ("section", "dp"))
    position = jnp.pad(position[par], (0, SP - SLOTS))
    angles = position.astype(F32)[:, None] * frequency[None, :]
    cosine = jnp.tile(jnp.cos(angles), (1, 4))
    sine = jnp.tile(jnp.concatenate([-jnp.sin(angles), jnp.sin(angles)], axis=1), (1, 2))
    gathered = lax.all_gather(table, "dp", axis=0, tiled=True)[:WROWS]
    other = lax.ppermute(gathered, "section", [(0, 1), (1, 0), (2, 3), (3, 2)])
    weights = jnp.where((sec == 1) | (sec == 2), gathered, other)
    local = jnp.where(sec == 0, info[:, :SP].reshape(-1), -1) - d * own
    onehot = (local[:, None] == jnp.arange(own)[None, :]).astype(BF16)
    looked = (nn(onehot, table) * math.sqrt(D)).astype(BF16)
    looked = lax.psum_scatter(looked, "dp", scatter_dimension=0, tiled=True).reshape(2, SP, D)
    from_first = lax.ppermute(looked[1], "section", [(0, 1)])
    x0 = jnp.where(sec == 0, looked[0], from_first)
    return weights, x0, local, all_labels, all_counts, g_f, cosine, sine


def head_anywhere(y, my_picks, all_labels, all_counts, g_f, table):
    sec = lax.axis_index("section")
    d = lax.axis_index("dp")
    n_sec = lax.axis_size("section")
    n_dp = lax.axis_size("dp")
    own = table.shape[0]
    picked = jnp.take(y, my_picks, axis=0)
    all_picked = lax.all_gather(picked, ("section", "dp"), axis=0, tiled=False)
    all_picked = all_picked.reshape(n_sec, n_dp, PICKS, D)[2:].transpose(1, 0, 2, 3)
    all_picked = all_picked.reshape(-1, D).astype(F32)
    af = jnp.where(sec == 3, rms_scale(all_picked, g_f), 0.0).astype(BF16)
    vocab_ids = d * own + jnp.arange(own)
    logits = jnp.where(vocab_ids[None, :] < VOCAB, nt(af, table), NEG)
    local_max = jnp.max(logits, axis=1)
    hit = vocab_ids[None, :] == all_labels[:, None]
    sums = jnp.stack(
        [
            local_max,
            jnp.sum(jnp.exp(logits - local_max[:, None]), axis=1),
            jnp.sum(jnp.where(hit, logits, 0.0), axis=1),
        ]
    )
    every = lax.all_gather(sums, "dp", axis=0, tiled=False)
    top = jnp.max(every[:, 0], axis=0)
    total = jnp.sum(every[:, 1] * jnp.exp(every[:, 0] - top), axis=0)
    target = jnp.sum(every[:, 2], axis=0)
    log_total = top + jnp.log(total)
    loss_part = jnp.where(
        (sec == 3) & (d == 0), jnp.sum(jnp.where(all_counts > 0, log_total - target, 0.0)), 0.0
    )
    dlogits = (jnp.exp(logits - log_total[:, None]) - hit.astype(F32)) * all_counts[:, None]
    dlogits = jnp.where(sec == 3, dlogits, 0.0).astype(BF16)
    d_table = tn(dlogits, af)
    daf = lax.psum(nn(dlogits, table), "dp")
    daf = lax.dynamic_slice_in_dim(daf, d * 2 * PICKS, 2 * PICKS).reshape(2, PICKS, D)
    daf = jnp.where(sec == 3, daf[1], lax.ppermute(daf[0], "section", [(3, 2)]))
    d_own, dg_f = rms_pull(picked.astype(F32), g_f, daf)
    dg_f = jnp.where(sec >= 2, dg_f, 0.0)
    spread = (jnp.arange(SP)[:, None] == my_picks[None, :]).astype(F32)
    d_top = jnp.dot(spread, d_own, precision=lax.Precision.HIGHEST).astype(BF16)
    return d_top, d_table, dg_f, loss_part


def shards(codes, labels, picks, classes, null_mask, starts, master, momentum, average):
    sec = lax.axis_index("section")
    d = lax.axis_index("dp")
    n_dp = lax.axis_size("dp")
    n_sec = lax.axis_size("section")
    par = lax.rem(sec, 2)
    own = master.shape[0]
    learn_rate = rate_factor * math.sqrt(own * n_sec * n_dp)
    beside = [(0, 1), (1, 0), (2, 3), (3, 2)]
    fast = n_sec == 4 and n_dp == 8 and own == 2 * HALF
    table = master.astype(BF16)
    gain_at = VOCAB // own
    frequency = rope_base ** (-jnp.arange(HD // 2, dtype=F32) * 2.0 / HD)

    if fast:
        wide = jnp.tile(frequency[None, :], (1, 4))
        weights, x0, info, gain, cosine, sine = gather_and_embed(
            table, codes, labels, picks, starts, classes, null_mask, wide
        )
        all_index = info[:, :2, :SP].reshape(-1)
        local = jnp.where(sec == 0, all_index, -1) - d * own
    else:
        opened = open_anywhere(codes, labels, picks, classes, null_mask, starts, table, frequency)
        weights, x0, local, all_labels, all_counts, g_f, cosine, sine = opened
    around = (cosine, sine, starts)

    y0 = forward_call(x0, weights, *around)[0]
    x = jnp.where(sec < 2, x0, lax.ppermute(y0, "section", [(0, 2), (1, 3)]))
    y, *kept = forward_call(x, weights, *around)

    if fast:
        d_top, d_table, small = head_call(y, picks, info, gain, table)
    else:
        d_top, d_table, dg_f, loss_part = head_anywhere(
            y, picks[par], all_labels, all_counts, g_f, table
        )

    dx1 = backward_call(False, d_top, x, weights, *around, kept)
    dy = jnp.where(sec < 2, lax.ppermute(dx1, "section", [(2, 0), (3, 1)]), d_top)
    dx0, grads = backward_call(True, dy, x, weights, *around, kept)

    if fast:
        grad, squares = reduce_and_scatter(grads, d_table, dx0, local[None, :])
        squares = squares.reshape(-1, 6, 128).sum(axis=(0, 1))
        small = small + jnp.where(jnp.arange(8)[:, None] == 7, squares[None, :], 0.0)
        totals = jnp.sum(share(small, n_sec, n_dp, 8, "share_norm"), axis=0)
        dg_f, loss_sum, squares = totals[:6].reshape(-1), totals[6, 0], jnp.sum(totals[7])
        count_sum = jnp.sum(info[:, 4:6, :PICKS].astype(F32))
    else:
        grads = grads.astype(F32) + lax.ppermute(grads, "section", beside).astype(F32)
        grads = jnp.pad(grads.astype(BF16), ((0, own * n_dp - WROWS), (0, 0)))
        grad = lax.psum_scatter(grads, "dp", scatter_dimension=0, tiled=True).astype(F32)
        grad = jnp.where(sec == 3, d_table, grad)
        pair = jnp.stack([dx0, lax.ppermute(dx0, "section", [(1, 0)])])
        all_dx = lax.all_gather(pair, "dp", axis=0, tiled=True).reshape(-1, D)
        onehot = (jnp.arange(own)[:, None] == local[None, :]).astype(BF16)
        grad = jnp.where(sec == 0, nn(onehot, all_dx) * math.sqrt(D), grad)
        totals = (dg_f, jnp.sum(grad * grad), loss_part)
        dg_f, squares, loss_sum = lax.psum(totals, ("section", "dp"))
        count_sum = jnp.sum(all_counts)
    grad_norm = jnp.sqrt(squares + jnp.sum(dg_f * dg_f))
    gain_here = (jnp.arange(own) == VOCAB % own)[:, None] & (sec == 3) & (d == gain_at)
    grad = grad + jnp.where(gain_here, dg_f[None, :], 0.0)
    clipped = grad * jnp.minimum(1.0, clip_limit / (grad_norm + norm_eps))
    new_momentum = momentum_decay * momentum + clipped
    new_master = master - learn_rate * (clipped + momentum_decay * new_momentum)
    new_average = average_decay * average + (1.0 - average_decay) * new_master
    return loss_sum, count_sum, grad_norm, new_master, new_momentum, new_average


def solution(mesh):
    split = P("dp", None)
    whole = P(("section", "dp"), None)
    return jax.shard_map(
        shards,
        mesh=mesh,
        in_specs=(split,) * 6 + (whole,) * 3,
        out_specs=(P(), P(), P(), whole, whole, whole),
        check_vma=False,
    )
```

```python
import functools
import math

import jax
import jax.numpy as jnp
from jax import lax
from jax.experimental import pallas as pl
from jax.experimental.pallas import tpu as pltpu
from jax.sharding import PartitionSpec as P

D = 768
HEADS = 12
HD = 64
FF = 2048
VOCAB = 16384
CLASSES = 1001
SLOTS = 264
SP = 272
PICKS = 32
SEGS = 3
MATS = 4 * D + 3 * FF
WROWS = 9232

F32 = jnp.float32
BF16 = jnp.bfloat16

rope_base = 10000.0
clip_limit = 1.0
rate_factor = 0.25
momentum_decay = 0.9
average_decay = 0.8
norm_eps = 1e-06


def nn(left, right):
    return jnp.dot(left, right, preferred_element_type=F32)


def tn(left, right):
    return lax.dot_general(left, right, (((0,), (0,)), ((), ())), preferred_element_type=F32)


def nt(left, right):
    return lax.dot_general(left, right, (((1,), (1,)), ((), ())), preferred_element_type=F32)


def rms_scale(value_in, gain):
    return (
        value_in * lax.rsqrt(jnp.mean(value_in * value_in, axis=-1, keepdims=True) + norm_eps) * gain
    )


def rms_pull(value_in, gain, grad):
    inv = lax.rsqrt(jnp.mean(value_in * value_in, axis=-1, keepdims=True) + norm_eps)
    unit = value_in * inv
    scaled = grad * gain
    grad_in = inv * (scaled - unit * jnp.mean(scaled * unit, axis=-1, keepdims=True))
    return grad_in, jnp.sum(grad * unit, axis=0)


def row_layout(starts_row, classes_row, null_row, codes_row):
    slot_ids = jnp.arange(SLOTS, dtype=jnp.int32)
    segment = jnp.sum((starts_row[None, 1:] <= slot_ids[:, None]).astype(jnp.int32), axis=1)
    seg_start = jnp.sum(
        jnp.where(segment[:, None] == jnp.arange(SEGS + 1)[None, :], starts_row[None, :], 0), axis=1
    )
    position = slot_ids - seg_start
    live_end = starts_row[SEGS]
    is_first = (position == 0) & (slot_ids < live_end)
    clamped = jnp.minimum(segment, SEGS - 1)
    hit = clamped[:, None] == jnp.arange(SEGS)[None, :]
    class_row = jnp.sum(
        jnp.where(hit, jnp.where(null_row > 0, CLASSES - 1, classes_row)[None, :], 0), axis=1
    )
    row_index = jnp.where(is_first, VOCAB + class_row, codes_row)
    following = jnp.concatenate([segment[1:], jnp.full((1,), SEGS + 1, jnp.int32)])
    counted = (following == segment) & (slot_ids + 1 < live_end)
    return row_index, counted, segment, position


MESH = pl.DeviceIdType.MESH
ANY = pl.BlockSpec(memory_space=pl.ANY)
VMEM = pl.BlockSpec(memory_space=pltpu.VMEM)
SMEM = pl.BlockSpec(memory_space=pltpu.SMEM)

OWN = 2176
SPLIT = 1152
COUNT = (18, 16, 18, 16, 11)
ROWS = (64, 64, 64, 64, 48)
HELD = (0, SPLIT, OWN, OWN + SPLIT, 2 * OWN)
LANE = 2 * OWN + 11 * 48
LAG = 2
WINDOW = 2
HOP = 2
PIECES = ((0, 64), (64, 64), (128, 64), (192, 64), (256, 16))
TURN = 6
CHOP = 4
CLAG = 3
AHEAD = 4


def class_base(k, lane):
    if k == 4:
        return 4 * OWN
    return OWN * (2 * (k // 2) + lane) + SPLIT * (k % 2)


def place():
    sec = lax.axis_index("section")
    dp = lax.axis_index("dp")
    z = dp // 2
    c = lax.rem(dp, 2)
    par = lax.rem(sec, 2)
    home = jnp.logical_or(sec == 1, sec == 2)
    return sec, dp, z, c, par, home


def greet_neighbours(sec, dp, z, c, par, turns):
    barrier = pltpu.get_barrier_semaphore()

    def greet(s, e):
        pl.semaphore_signal(barrier, 1, device_id=(s, e), device_id_type=MESH)

    greet(sec, dp + 1 - 2 * c)
    greet(sec + 1 - 2 * par, dp)
    pl.when(z > 0)(lambda: greet(sec, dp - 2))
    pl.when(z < 3)(lambda: greet(sec, dp + 2))
    count = 2 + (z > 0).astype(jnp.int32) + (z < 3).astype(jnp.int32)
    for sender, receiver in turns:
        pl.when(sec == receiver)(lambda sender=sender: greet(sender, dp))
        count = count + (sec == sender).astype(jnp.int32)
    pl.semaphore_wait(barrier, count)


def hop_targets(sec, dp, c, par):
    return {
        "up": (sec, dp + 2),
        "down": (sec, dp - 2),
        "x": (sec + 1 - 2 * par, dp),
        "core": (sec, dp + 1 - 2 * c),
    }


HOPS = ("up", "down", "x", "core")


def tree(z, c, home):
    both = jnp.logical_and
    either = jnp.logical_or
    no = jnp.logical_not
    far = z >= 2
    mid = both(z >= 1, z <= 2)
    never = z < 0
    away = no(home)
    as_int = lambda flag: flag.astype(jnp.int32)
    out = []
    for block in (0, 1):
        for half in (0, 1):
            mine = home if half == 0 else away
            other = no(mine)
            source = both(z == block, home)
            if half == 0:
                early = (lambda j: j < TURN) if block == 0 else (lambda j: j < 0)
                near_x = lambda j, block=block, early=early: both(z == 1 - block, early(j))
                hop_x = lambda j, near_x=near_x: both(home, near_x(j))
                got_x = lambda j, near_x=near_x: both(away, near_x(j))
                along = lambda j, early=early: either(home, no(early(j)))
            else:
                hop_x = lambda j, block=block: both(away, z == 1 - block)
                got_x = lambda j, block=block: both(home, z == 1 - block)
                along = lambda j: away
            at_owner = both(z == block, away)
            if block == 0:
                up = lambda j, along=along, mine=mine: either(both(z == 0, along(j)), both(mid, mine))
                down = lambda j: never
                from_up = lambda j: never
            else:
                up = lambda j, mine=mine: both(mid, mine)
                down = lambda j, along=along: both(z == 1, along(j))
                from_up = lambda j, got_x=got_x: both(z == 0, no(got_x(j)))
            send_x = lambda j, source=source, mine=mine, hop_x=hop_x: either(
                either(source, both(far, mine)), hop_x(j)
            )
            from_x = lambda j, at_owner=at_owner, other=other, got_x=got_x: either(
                either(at_owner, both(far, other)), got_x(j)
            )
            from_down = lambda j, source=source, from_x=from_x, from_up=from_up: no(
                either(source, either(from_x(j), from_up(j)))
            )
            depth = jnp.abs(z - block) + as_int(far) * (half + as_int(other))
            if half == 0:
                depth = depth + (1 - as_int(far)) * as_int(away)
            else:
                depth = depth + (1 - as_int(far)) * jnp.where(
                    away, 1, 2 * as_int(z == 1 - block)
                )
            out.append(
                (source, dict(up=up, down=down, x=send_x), dict(up=from_up, down=from_down, x=from_x), depth)
            )
    lane0 = c == 0
    source = both(both(z == 2, home), lane0)
    sends = dict(
        up=lambda j: both(z == 2, lane0),
        down=lambda j: both(mid, lane0),
        x=lambda j: source,
    )
    parents = dict(
        up=lambda j: both(z <= 1, lane0),
        down=lambda j: both(z == 3, lane0),
        x=lambda j: both(both(z == 2, away), lane0),
    )
    out.append((source, sends, parents, jnp.abs(z - 2) + as_int(away)))
    return out


def segment_of(starts, r, slot):
    bounds = [starts[r, j] for j in range(SEGS + 1)]
    count = lambda at: functools.reduce(
        jnp.add, [(at >= bounds[j]).astype(jnp.int32) for j in range(1, SEGS + 1)]
    )
    segment = count(slot)
    begin = jnp.where(
        segment == 0, bounds[0], jnp.where(segment == 1, bounds[1], jnp.where(segment == 2, bounds[2], bounds[3]))
    )
    counted = jnp.logical_and(count(slot + 1) == segment, slot + 1 < bounds[SEGS])
    return segment, slot - begin, counted, slot < bounds[SEGS]


def open_kernel(
    master, codes, labels, picks, starts, classes, nulls, frequency, out, x0, info, gain, cosine,
    sine, table, exact, master_sem, own_sem, recv_sem, recv_c, core_sem, send_sem, sent, mine, rx_core, rx_up, rx_down,
    swap_send, swap_recv, x_send, x_recv, line_send, up_recv, down_recv, last_send, last_recv,
    note, note_send, note_recv, gain_send, gain_recv,
):
    sec, dp, z, c, par, home = place()
    targets = hop_targets(sec, dp, c, par)
    classes_of = tree(z, c, home)
    gain_dp = VOCAB // (OWN)
    holds_gain = jnp.logical_and(sec == 3, dp == gain_dp)

    parts = [pl.ds(k * (OWN // 4), OWN // 4) for k in range(4)]
    fetch = [
        pltpu.make_async_copy(master.at[part], exact.at[part], master_sem.at[k])
        for k, part in enumerate(parts)
    ]
    for one in fetch:
        one.start()

    barrier = pltpu.get_barrier_semaphore()

    def greet(s, e):
        pl.semaphore_signal(barrier, 1, device_id=(s, e), device_id_type=MESH)

    for k in range(1, 8):
        greet(sec, lax.rem(dp + k, 8))
    greet(sec + 1 - 2 * par, dp)
    pl.when(sec == 2)(lambda: greet(0, dp))
    pl.when(sec == 1)(lambda: greet(2, dp))
    pl.when(jnp.logical_and(sec == 2, dp != gain_dp))(lambda: greet(3, gain_dp))

    slot_row = lax.broadcasted_iota(jnp.int32, (1, SLOTS), 1)
    note[...] = jnp.full(note.shape, -1, jnp.int32)
    for r in range(2):
        segment, position, _, live = segment_of(starts, r, slot_row)
        names = [classes[r, j] + (CLASSES - 1 - classes[r, j]) * nulls[r, j] for j in range(SEGS)]
        name = jnp.where(segment == 0, names[0], jnp.where(segment == 1, names[1], names[2]))
        opens = jnp.logical_and(position == 0, live)
        note[r : r + 1, :SLOTS] = jnp.where(opens, VOCAB + name, codes[r : r + 1, :])
        chosen = picks[r : r + 1, :]
        ids = lax.broadcasted_iota(jnp.int32, (SLOTS, PICKS), 0)
        label_col = column(labels[r : r + 1, :], SLOTS)
        note[2 + r : 3 + r, :PICKS] = jnp.sum(
            jnp.where(ids == chosen, label_col, 0), axis=0, keepdims=True
        )
        note[4 + r : 5 + r, :PICKS] = segment_of(starts, r, chosen)[2].astype(jnp.int32)
    info[dp] = note[...]
    for one, part in zip(fetch, parts):
        one.wait()
        table[part, :] = exact[part, :].astype(BF16)
    count = 8 + jnp.logical_or(sec == 0, sec == 2).astype(jnp.int32)
    pl.semaphore_wait(barrier, count + 7 * holds_gain.astype(jnp.int32))
    for k in range(1, 8):
        pltpu.make_async_remote_copy(
            src_ref=note,
            dst_ref=info.at[dp],
            send_sem=note_send,
            recv_sem=note_recv,
            device_id=(sec, lax.rem(dp + k, 8)),
            device_id_type=MESH,
        ).start()
    noted = pltpu.make_async_remote_copy(
        src_ref=info.at[pl.ds(0, 7)],
        dst_ref=info.at[pl.ds(0, 7)],
        send_sem=note_send,
        recv_sem=note_recv,
        device_id=targets["core"],
        device_id_type=MESH,
    )

    gain_rows = table.at[pl.ds(VOCAB % (OWN), 16)]

    def gain_to(s, e):
        return pltpu.make_async_remote_copy(
            src_ref=gain_rows,
            dst_ref=gain,
            send_sem=gain_send,
            recv_sem=gain_recv,
            device_id=(s, e),
            device_id_type=MESH,
        )

    def send_gain():
        for e in range(8):
            gain_to(2, e).start()
            if e != gain_dp:
                gain_to(3, e).start()
        gain[...] = gain_rows[...]

    pl.when(holds_gain)(send_gain)

    def keep(rows):
        return pltpu.make_async_copy(
            table.at[pl.ds(0, rows)],
            out.at[pl.ds(pl.multiple_of(dp * OWN, 16), rows)],
            own_sem,
        )

    def keep_all():
        keep(OWN).start()
        keep(OWN).wait()

    def keep_few():
        keep(11 * 48).start()
        keep(11 * 48).wait()

    pl.when(jnp.logical_and(home, z < 2))(keep_all)
    pl.when(classes_of[4][0])(keep_few)

    def copy(k, hop, j, rows, recv, slot):
        part = out.at[pl.ds(pl.multiple_of(class_base(k, c) + j * rows, 16), rows)]
        return pltpu.make_async_remote_copy(
            src_ref=part,
            dst_ref=part,
            send_sem=send_sem.at[k, HOPS.index(hop), slot],
            recv_sem=recv,
            device_id=targets[hop],
            device_id_type=MESH,
        )

    def piece(k, j, rows):
        source, sends, _, _ = classes_of[k]
        recv = recv_c.at[j] if k == 4 else recv_sem.at[k, j]
        slot = lax.rem(j, WINDOW)

        def send(hop):
            to = core_sem.at[k] if hop == "core" else recv
            one = copy(k, hop, j, rows, to, slot)
            before = True if hop == "core" else sends[hop](j - WINDOW)
            pl.when(jnp.logical_and(j >= WINDOW, before))(one.wait_send)
            one.start()

        pl.when(jnp.logical_not(source))(copy(k, "x", j, rows, recv, slot).wait_recv)
        for hop in HOPS[:3]:
            pl.when(sends[hop](j))(lambda hop=hop: send(hop))
        send("core")

    def counts(k):
        return COUNT[k], ROWS[k]

    first = sec == 0
    second = sec == 2

    def slot(k):
        return pl.ds(pl.multiple_of(k * SP, 16), SP)

    def order(i):
        low = (z <= 1).astype(jnp.int32)
        return low * (3 - i) + (1 - low) * i

    def swap(k):
        return pltpu.make_async_remote_copy(
            src_ref=sent.at[slot(k)],
            dst_ref=rx_core.at[slot(k)],
            send_sem=swap_send,
            recv_sem=swap_recv.at[k],
            device_id=targets["core"],
            device_id_type=MESH,
        )

    def cross(zz):
        return pltpu.make_async_remote_copy(
            src_ref=mine.at[slot(4 + zz)],
            dst_ref=mine.at[slot(zz)],
            send_sem=x_send,
            recv_sem=x_recv.at[zz],
            device_id=(2, dp),
            device_id_type=MESH,
        )

    def piece_of(k, q):
        start, size = PIECES[q]
        return pl.ds(pl.multiple_of(k * SP + start, 16), size)

    def go(zz, q, ref, recv, hop):
        return pltpu.make_async_remote_copy(
            src_ref=mine.at[piece_of(zz, q)],
            dst_ref=ref.at[piece_of(zz, q)],
            send_sem=line_send,
            recv_sem=recv.at[zz, q],
            device_id=targets[hop],
            device_id_type=MESH,
        )

    def go_up(zz, q):
        return go(zz, q, rx_down, down_recv, "up")

    def go_down(zz, q):
        return go(zz, q, rx_up, up_recv, "down")

    def add(there, ref):
        mine[there, :] = (mine[there, :].astype(F32) + ref[there, :].astype(F32)).astype(BF16)

    def look(row):
        local = column(info[row // 2, pl.ds(lax.rem(row, 2), 1), :][:, :SP], SP) - dp * OWN
        ids = lax.broadcasted_iota(jnp.int32, (SP, OWN), 1)
        onehot = jnp.where(ids == local, 1.0, 0.0).astype(BF16)
        return (nn(onehot, table[...]) * math.sqrt(D)).astype(BF16)

    def lookup(b):
        zz = order(b // 2)
        p = 1 - lax.rem(b, 2)
        k = 4 * p + zz
        sent[slot(k), :] = look(2 * (2 * zz + 1 - c) + p)
        swap(k).start()
        mine[slot(k), :] = look(2 * (2 * zz + c) + p)
        swap(k).wait_recv()
        add(slot(k), rx_core)
        pl.when(p == 1)(lambda: cross(zz).start())

    def chain(zz, q):
        def from_below():
            go_up(zz, q).wait_recv()
            add(piece_of(zz, q), rx_down)

        def from_above():
            go_down(zz, q).wait_recv()
            add(piece_of(zz, q), rx_up)

        if q == 0:
            pl.when(second)(cross(zz).wait_recv)
        pl.when(jnp.logical_and(zz >= z, z > 0))(from_below)
        pl.when(jnp.logical_and(zz <= z, z < 3))(from_above)
        pl.when(zz > z)(lambda: go_up(zz, q).start())
        pl.when(zz < z)(lambda: go_down(zz, q).start())

    def chains(i):
        for o in range(4):
            zz = order(o)
            hops = jnp.maximum(
                z * (zz >= z).astype(jnp.int32), (3 - z) * (zz <= z).astype(jnp.int32)
            )
            for q in range(5):
                now = i == 2 * o + 2 + sec + HOP * hops + q
                pl.when(now)(lambda zz=zz, q=q: chain(zz, q))

    segment, position, _, _ = segment_of(starts, par, lax.broadcasted_iota(jnp.int32, (SP, 128), 0))
    angles = position.astype(F32) * frequency[...]
    lanes = lax.broadcasted_iota(jnp.int32, (SP, 128), 1)
    cosine[...] = jnp.cos(angles)
    sine[...] = jnp.where(lax.rem(lanes, 64) < 32, -1.0, 1.0) * jnp.sin(angles)
    noted.wait_recv()

    def step(i, carry):
        for k in range(5):
            count, rows = counts(k)
            j = i - LAG * classes_of[k][3]
            now = jnp.logical_and(j >= 0, j < count)
            if k == 4:
                now = jnp.logical_and(now, c == 0)
            pl.when(now)(lambda k=k, j=j, rows=rows: piece(k, j, rows))
        pl.when(jnp.logical_and(first, i < 8))(lambda: lookup(i))
        pl.when(jnp.logical_or(first, second))(lambda: chains(i))
        pl.when(jnp.logical_and(second, i == last_step))(lambda: last().start())
        return carry

    last_step = 6 + 2 + 2 + 3 * HOP + 4 + 1

    def last():
        return pltpu.make_async_remote_copy(
            src_ref=mine.at[slot(z)],
            dst_ref=x0,
            send_sem=last_send,
            recv_sem=last_recv,
            device_id=(1, dp),
            device_id_type=MESH,
        )

    lax.fori_loop(0, max(18 + 5 * LAG, last_step + 1), step, 0)

    def blocks(count, sem):
        return pltpu.make_async_remote_copy(
            src_ref=mine.at[pl.ds(0, count * SP)],
            dst_ref=mine.at[pl.ds(0, count * SP)],
            send_sem=sem,
            recv_sem=sem,
            device_id=targets["core"],
            device_id_type=MESH,
        )

    def end_first():
        blocks(8, swap_send).wait_send()
        blocks(4, x_send).wait_send()
        blocks(3, line_send).wait_send()
        x0[...] = mine[slot(z), :]

    def end_second():
        blocks(3, line_send).wait_send()
        last().wait_send()

    def none():
        x0[...] = jnp.zeros_like(x0)

    pl.when(first)(end_first)
    pl.when(second)(end_second)
    pl.when(sec == 1)(last().wait_recv)
    pl.when(sec >= 2)(none)

    noted.wait_send()

    def gain_sent():
        for e in range(15):
            gain_to(2, 0).wait_send()

    pl.when(holds_gain)(gain_sent)
    pl.when(jnp.logical_and(sec >= 2, jnp.logical_not(holds_gain)))(gain_to(2, dp).wait_recv)

    def drain(k):
        count, rows = counts(k)
        _, sends, _, _ = classes_of[k]
        for j in range(count - WINDOW, count):
            for hop in HOPS[:3]:
                one = copy(k, hop, j, rows, core_sem.at[k], j % WINDOW)
                pl.when(sends[hop](j))(one.wait_send)
            copy(k, "core", j, rows, core_sem.at[k], j % WINDOW).wait_send()
        if k == 0:
            for j in range(TURN - WINDOW, TURN):
                one = copy(k, "x", j, rows, core_sem.at[k], j % WINDOW)
                last_one = jnp.logical_not(sends["x"](j + WINDOW))
                pl.when(jnp.logical_and(sends["x"](j), last_one))(one.wait_send)

    def came(k):
        count, rows = counts(k)
        part = out.at[pl.ds(pl.multiple_of(class_base(k, 1 - c), 16), count * rows)]
        pltpu.make_async_remote_copy(
            src_ref=part,
            dst_ref=part,
            send_sem=send_sem.at[k, 3, 0],
            recv_sem=core_sem.at[k],
            device_id=targets["core"],
            device_id_type=MESH,
        ).wait_recv()

    for k in range(4):
        drain(k)
        came(k)
    pl.when(c == 0)(lambda: drain(4))
    pl.when(c == 1)(lambda: came(4))


def gather_and_embed(master, codes, labels, picks, starts, classes, nulls, frequency):
    rows = lambda n: pltpu.VMEM((n * SP, D), BF16)
    return pl.pallas_call(
        open_kernel,
        out_shape=(
            jax.ShapeDtypeStruct((WROWS, D), BF16),
            jax.ShapeDtypeStruct((SP, D), BF16),
            jax.ShapeDtypeStruct((8, 8, 384), jnp.int32),
            jax.ShapeDtypeStruct((16, D), BF16),
            jax.ShapeDtypeStruct((SP, 128), F32),
            jax.ShapeDtypeStruct((SP, 128), F32),
            jax.ShapeDtypeStruct((OWN, D), BF16),
        ),
        in_specs=[ANY] + [VMEM] * 3 + [SMEM] * 3 + [VMEM],
        out_specs=(VMEM,) * 7,
        scratch_shapes=[
            pltpu.VMEM((OWN, D), F32),
            pltpu.SemaphoreType.DMA((4,)),
            pltpu.SemaphoreType.DMA,
            pltpu.SemaphoreType.DMA((4, 18)),
            pltpu.SemaphoreType.DMA((11,)),
            pltpu.SemaphoreType.DMA((5,)),
            pltpu.SemaphoreType.DMA((5, 4, WINDOW)),
            rows(8),
            rows(8),
            rows(8),
            rows(4),
            rows(4),
            pltpu.SemaphoreType.DMA,
            pltpu.SemaphoreType.DMA((8,)),
            pltpu.SemaphoreType.DMA,
            pltpu.SemaphoreType.DMA((4,)),
            pltpu.SemaphoreType.DMA,
            pltpu.SemaphoreType.DMA((4, 5)),
            pltpu.SemaphoreType.DMA((4, 5)),
            pltpu.SemaphoreType.DMA,
            pltpu.SemaphoreType.DMA,
            pltpu.VMEM((8, 384), jnp.int32),
        ]
        + [pltpu.SemaphoreType.DMA] * 4,
        compiler_params=pltpu.CompilerParams(
            collective_id=0, has_side_effects=True, vmem_limit_bytes=56 * 2**20
        ),
        name="gather_and_embed",
    )(master, codes, labels, picks, starts, classes, nulls, frequency)


def close_kernel(
    left_any, right_any, tail, start, block, index, out, squares, left, right, loc, sent, rx_core,
    rx_up, rx_down, rx_x, summed, ring, all_dx, load_sem, core_sem, recv_sem, recv_c, core_send,
    send_sem, ring_sem, dx_own, dx_send, line_recv, cross_recv, turn_recv, dx_core_send,
    dx_core_recv, ready,
):
    sec, dp, z, c, par, home = place()
    targets = hop_targets(sec, dp, c, par)
    classes = tree(z, c, home)
    loads = [
        pltpu.make_async_copy(left_any, left, load_sem.at[0]),
        pltpu.make_async_copy(right_any, right, load_sem.at[1]),
    ]
    for one in loads:
        one.start()
    del start
    greet_neighbours(sec, dp, z, c, par, ((1, 2), (0, 2)))
    pl.when(sec == 0)(
        lambda: pl.semaphore_signal(ready, 1, device_id=(2, dp), device_id_type=MESH)
    )
    for one in loads:
        one.wait()

    def place_of(hop, k, j):
        offset = j * ROWS[k]
        if hop == "down":
            base = (0, 0, 0, SPLIT, OWN)[k]
        elif hop == "up":
            base = (0, SPLIT, OWN, OWN, OWN + SPLIT)[k]
        else:
            base = HELD[k]
        return pl.ds(pl.multiple_of(base + offset, 16), ROWS[k])

    def gradient(first_row, size):
        first_row = jnp.int32(first_row)
        bounds = (D, 2 * D, 3 * D, 4 * D, 4 * D + 2 * FF)
        matrix = functools.reduce(
            jnp.add, [(first_row >= bound).astype(jnp.int32) for bound in bounds]
        )
        cols = pl.ds(pl.multiple_of(first_row, 128), size)
        return tn(left[:, cols], right[matrix]).astype(BF16)

    def core_copy(k, offset, rows, sem):
        part = pl.ds(pl.multiple_of(HELD[k] + offset, 16), rows)
        return pltpu.make_async_remote_copy(
            src_ref=sent.at[part],
            dst_ref=rx_core.at[part],
            send_sem=core_send,
            recv_sem=sem,
            device_id=targets["core"],
            device_id_type=MESH,
        )

    def form(k, t):
        there = pl.ds(pl.multiple_of(HELD[k] + 128 * t, 128), 128)
        sent[there, :] = gradient(class_base(k, 1 - c) + 128 * t, 128)
        core_copy(k, 128 * t, 128, core_sem.at[k, t]).start()
        loc[there, :] = gradient(class_base(k, c) + 128 * t, 128)

    last_rows = 11 * 48

    def form_last(into):
        for t in range(4):
            into[pl.ds(HELD[4] + 128 * t, 128), :] = gradient(4 * OWN + 128 * t, 128)
        into[pl.ds(HELD[4] + 512, 16), :] = tail[...]

    def form_for_other():
        form_last(sent)
        core_copy(4, 0, last_rows, core_sem.at[4, 0]).start()

    squares[...] = jnp.zeros_like(squares)

    def count_squares(value):
        folded = value * value
        size = folded.shape[0]
        while size > 8 and size % 16 == 0:
            size //= 2
            folded = folded[:size] + folded[size:]
        for part in range(size // 8):
            for n in range(D // 128):
                squares[...] += folded[part * 8 : (part + 1) * 8, n * 128 : (n + 1) * 128]

    rx = dict(up=rx_up, down=rx_down, x=rx_x)

    def onward(k, hop, j):
        back = dict(up="down", down="up", x="x")[hop]
        return landing(k, back, hop, j)

    def landing(k, back, hop, j):
        index = ("up", "down", "x").index(back)
        part = pl.ds(pl.multiple_of(HELD[k] + j * ROWS[k], 16), ROWS[k])
        return pltpu.make_async_remote_copy(
            src_ref=loc.at[part],
            dst_ref=rx[back].at[place_of(back, k, j)],
            send_sem=send_sem.at[k],
            recv_sem=recv_c.at[index, j] if k == 4 else recv_sem.at[index, k, j],
            device_id=targets[hop],
            device_id_type=MESH,
        )

    def gathered(k, j):
        part = pl.ds(pl.multiple_of(HELD[k] + j * ROWS[k], 16), ROWS[k])
        if k == 4:
            pl.when(j == 0)(lambda: core_copy(4, 0, last_rows, core_sem.at[4, 0]).wait_recv())
        else:
            pl.when(lax.rem(j, 2) == 0)(
                lambda: core_copy(k, 64 * j, 128, core_sem.at[k, j // 2]).wait_recv()
            )
        acc = summed.at[pl.ds(0, ROWS[k])]
        acc[...] = loc[part, :].astype(F32) + rx_core[part, :].astype(F32)
        for hop in HOPS[:3]:
            if (hop, k) in (("down", 0), ("down", 1)):
                continue

            def add(hop=hop):
                landing(k, hop, hop, j).wait_recv()
                acc[...] += rx[hop][place_of(hop, k, j), :].astype(F32)

            pl.when(classes[k][1][hop](j))(add)
        return part, acc

    def relay(k, j):
        part, acc = gathered(k, j)
        loc[part, :] = acc[...].astype(BF16)
        for hop in HOPS[:3]:
            pl.when(classes[k][2][hop](j))(lambda hop=hop: onward(k, hop, j).start())

    def write(slot, rows, offset):
        return pltpu.make_async_copy(
            ring.at[pl.ds(pl.multiple_of(slot * 64, 64), rows)],
            out.at[pl.ds(pl.multiple_of(offset, 16), rows)],
            ring_sem.at[slot],
        )

    def finish(k, j):
        _, acc = gathered(k, j)
        slot = 4 * (k % 2) + lax.rem(j, 4)
        copy = write(slot, ROWS[k], SPLIT * (k % 2) + j * ROWS[k])
        pl.when(j >= 4)(copy.wait)
        value = acc[...]
        ring[pl.ds(pl.multiple_of(slot * 64, 64), ROWS[k]), :] = value
        copy.start()
        count_squares(value)

    first = sec == 0
    second = sec == 2
    in_line = jnp.logical_or(first, second)
    p_line = second.astype(jnp.int32)
    both = jnp.logical_and

    def dx_part(p, zz):
        return all_dx.at[pl.ds(pl.multiple_of((2 * (2 * zz + c) + p) * SP, 16), SP)]

    def move(p, zz, send, recv, target):
        return pltpu.make_async_remote_copy(
            src_ref=dx_part(p, zz),
            dst_ref=dx_part(p, zz),
            send_sem=send,
            recv_sem=recv,
            device_id=target,
            device_id_type=MESH,
        )

    def line(zz, hop):
        return move(p_line, zz, dx_send, line_recv.at[zz], targets[hop])

    def cross(zz):
        return move(1, zz, dx_send, cross_recv.at[zz], (0, dp))

    def dx_to_core(p, zz):
        return move(p, zz, dx_core_send, dx_core_recv, targets["core"])

    def aside(zz):
        pl.when(first)(lambda: dx_to_core(0, zz).start())
        pl.when(second)(lambda: cross(zz).start())

    def crossed(zz):
        cross(zz).wait_recv()
        dx_to_core(1, zz).start()

    def blocks(count, send, recv):
        return pltpu.make_async_remote_copy(
            src_ref=all_dx.at[pl.ds(0, count * SP)],
            dst_ref=all_dx.at[pl.ds(0, count * SP)],
            send_sem=send,
            recv_sem=recv,
            device_id=targets["core"],
            device_id_type=MESH,
        )

    turned = pltpu.make_async_remote_copy(
        src_ref=block,
        dst_ref=dx_part(1, z),
        send_sem=dx_send,
        recv_sem=turn_recv,
        device_id=(2, dp),
        device_id_type=MESH,
    )
    pl.when(sec == 1)(turned.start)

    def pass_own():
        pl.when(z < 3)(lambda: line(z, "up").start())
        pl.when(z > 0)(lambda: line(z, "down").start())
        aside(z)

    def own_first():
        own = pltpu.make_async_copy(block, dx_part(0, z), dx_own)
        own.start()
        own.wait()
        pass_own()

    def own_second():
        turned.wait_recv()
        pl.semaphore_wait(ready, 1)
        pass_own()

    pl.when(first)(own_first)

    def from_below(k):
        line(z - k, "up").wait_recv()
        pl.when(z < 3)(lambda: line(z - k, "up").start())
        aside(z - k)

    def from_above(k):
        line(z + k, "down").wait_recv()
        pl.when(z > 0)(lambda: line(z + k, "down").start())
        aside(z + k)

    def tile(t):
        ids = lax.broadcasted_iota(jnp.int32, (SP, 16 * SP), 0) + t * SP
        onehot = jnp.where(ids == index[...], 1.0, 0.0).astype(BF16)
        value = nn(onehot, all_dx[...]) * math.sqrt(D)
        slot = lax.rem(t, 2)
        copy = write_tile(slot, t)
        pl.when(t >= 2)(copy.wait)
        ring[pl.ds(pl.multiple_of(slot * SP, 16), SP), :] = value
        copy.start()
        count_squares(value)

    def write_tile(slot, t):
        return pltpu.make_async_copy(
            ring.at[pl.ds(pl.multiple_of(slot * SP, 16), SP)],
            out.at[pl.ds(pl.multiple_of(t * SP, 16), SP)],
            ring_sem.at[slot],
        )

    def collect(i):
        pl.when(both(second, i == CHOP + AHEAD))(own_second)
        for k in range(1, 4):
            now = i == CHOP * (k + p_line) + AHEAD * p_line
            pl.when(both(now, z >= k))(lambda k=k: from_below(k))
            pl.when(both(now, z + k <= 3))(lambda k=k: from_above(k))

    begin = 5 * CHOP + 1

    def embed(i):
        pl.when(i == 2 * CHOP)(lambda: crossed(z))
        for k in range(1, 4):
            pl.when(both(i == CHOP * (k + 2), z >= k))(lambda k=k: crossed(z - k))
            pl.when(both(i == CHOP * (k + 2), z + k <= 3))(lambda k=k: crossed(z + k))
        pl.when(i == begin)(lambda: blocks(8, dx_core_send, dx_core_recv).wait_recv())
        t = i - begin
        pl.when(both(t >= 0, t < OWN // SP))(lambda: tile(t))

    def step(i, carry):
        for k in range(4):
            pl.when(both(lax.rem(i, 2) == 0, i < COUNT[k]))(lambda k=k: form(k, i // 2))
        pl.when(both(i == 1, c == 0))(lambda: form_last(loc))
        pl.when(both(i == 1, c == 1))(form_for_other)
        for k in range(5):
            source, _, _, depth = classes[k]
            j = i - CLAG * ((5, 5, 4, 4, 3)[k] - depth) - (2 if k == 4 else 0)
            now = both(j >= 0, j < COUNT[k])
            if k == 4:
                now = both(now, c == 0)
            pl.when(both(now, jnp.logical_not(source)))(lambda k=k, j=j: relay(k, j))
            pl.when(both(now, source))(lambda k=k, j=j: finish(k, j))
        pl.when(in_line)(lambda: collect(i))
        pl.when(first)(lambda: embed(i))
        return carry

    lax.fori_loop(0, max(18 + 5 * CLAG, begin + OWN // SP), step, 0)
    pl.when(first)(lambda: blocks(8, dx_core_send, dx_core_recv).wait_send())

    def dx_sent(count):
        blocks(count, dx_send, dx_core_recv).wait_send()

    middle = both(z >= 1, z <= 2)
    ends = jnp.logical_not(middle)
    pl.when(jnp.logical_or(sec == 1, both(first, ends)))(lambda: dx_sent(1))
    pl.when(both(first, middle))(lambda: dx_sent(5))
    pl.when(both(second, ends))(lambda: dx_sent(5))
    pl.when(both(second, middle))(lambda: dx_sent(9))
    def sent_core(rows):
        part = pl.ds(0, rows)
        pltpu.make_async_remote_copy(
            src_ref=sent.at[part],
            dst_ref=rx_core.at[part],
            send_sem=core_send,
            recv_sem=core_sem.at[4, 0],
            device_id=targets["core"],
            device_id_type=MESH,
        ).wait_send()

    pl.when(c == 0)(lambda: sent_core(2 * OWN))
    pl.when(c == 1)(lambda: sent_core(LANE))
    for k in range(5):
        part = pl.ds(HELD[k], COUNT[k] * ROWS[k])
        gone = pltpu.make_async_remote_copy(
            src_ref=loc.at[part],
            dst_ref=rx_x.at[part],
            send_sem=send_sem.at[k],
            recv_sem=core_sem.at[4, 0],
            device_id=targets["x"],
            device_id_type=MESH,
        )
        away = jnp.logical_not(classes[k][0])
        pl.when(both(away, c == 0) if k == 4 else away)(gone.wait_send)

    def drain_half(k):
        for j in range(COUNT[k] - 4, COUNT[k]):
            write(4 * (k % 2) + j % 4, ROWS[k], 0).wait()

    def drain_tiles():
        for slot in range(2):
            write_tile(slot, 0).wait()

    for k in range(5):
        pl.when(classes[k][0])(lambda k=k: drain_half(k))
    pl.when(first)(drain_tiles)


def reduce_and_scatter(left, right, tail, start, block, index):
    low = lambda *shape: pltpu.VMEM(shape, BF16)
    dma = pltpu.SemaphoreType.DMA
    return pl.pallas_call(
        close_kernel,
        out_shape=(
            jax.ShapeDtypeStruct((OWN, D), F32),
            jax.ShapeDtypeStruct((8, 128), F32),
        ),
        in_specs=[ANY, ANY, VMEM, ANY, VMEM, VMEM],
        out_specs=(ANY, VMEM),
        input_output_aliases={3: 0},
        scratch_shapes=[
            low(SP, MATS),
            low(6, SP, D),
            low(LANE, D),
            low(LANE, D),
            low(LANE, D),
            low(OWN + SPLIT + 11 * 48, D),
            low(OWN + 11 * 48, D),
            low(LANE, D),
            pltpu.VMEM((64, D), F32),
            pltpu.VMEM((2 * SP, D), F32),
            low(16 * SP, D),
            dma((2,)),
            dma((5, 9)),
            dma((3, 4, 18)),
            dma((3, 11)),
            dma,
            dma((5,)),
            dma((8,)),
            dma,
            dma,
            dma((4,)),
            dma((4,)),
            dma,
            dma,
            dma,
            pltpu.SemaphoreType.REGULAR,
        ],
        compiler_params=pltpu.CompilerParams(
            collective_id=1, has_side_effects=True, vmem_limit_bytes=63 * 2**20
        ),
        name="reduce_and_scatter",
    )(left, right, tail, start, block, index)


def norm_kernel(n_sec, n_dp, small, squares, out, block, every, send_sem, recv_sem):
    sec = lax.axis_index("section")
    dp = lax.axis_index("dp")
    n = n_sec * n_dp
    me = sec * n_dp + dp
    barrier = pltpu.get_barrier_semaphore()

    def peer(k):
        other = lax.rem(me + k, n)
        return (other // n_dp, lax.rem(other, n_dp))

    def greet(k, carry):
        pl.semaphore_signal(barrier, 1, device_id=peer(k), device_id_type=MESH)
        return carry

    lax.fori_loop(1, n, greet, 0)
    block[...] = small[...]
    block[7:8, :] += jnp.sum(squares[...], axis=0, keepdims=True)
    every[me] = block[...]
    pl.semaphore_wait(barrier, n - 1)

    def send(k, carry):
        pltpu.make_async_remote_copy(
            src_ref=block,
            dst_ref=every.at[me],
            send_sem=send_sem,
            recv_sem=recv_sem,
            device_id=peer(k),
            device_id_type=MESH,
        ).start()
        return carry

    lax.fori_loop(1, n, send, 0)
    others = pltpu.make_async_remote_copy(
        src_ref=every.at[pl.ds(0, n - 1)],
        dst_ref=every.at[pl.ds(0, n - 1)],
        send_sem=send_sem,
        recv_sem=recv_sem,
        device_id=peer(1),
        device_id_type=MESH,
    )
    others.wait_recv()
    total = every[0]
    for k in range(1, n):
        total = total + every[k]
    gains = jnp.sum(total[0:6] * total[0:6], axis=0, keepdims=True)
    norm = jnp.sqrt(jnp.sum(gains + total[7:8], axis=1, keepdims=True))
    out[0:8, :] = total
    out[8:16, :] = jnp.broadcast_to(norm, (8, 128))
    others.wait_send()


def share_norm(small, squares, n_sec, n_dp):
    return pl.pallas_call(
        functools.partial(norm_kernel, n_sec, n_dp),
        out_shape=jax.ShapeDtypeStruct((16, 128), F32),
        in_specs=[VMEM, VMEM],
        out_specs=VMEM,
        scratch_shapes=[
            pltpu.VMEM((8, 128), F32),
            pltpu.VMEM((n_sec * n_dp, 8, 128), F32),
            pltpu.SemaphoreType.DMA,
            pltpu.SemaphoreType.DMA,
        ],
        compiler_params=pltpu.CompilerParams(collective_id=8, has_side_effects=True),
        name="share_norm",
    )(small, squares)


NEG = -1e30
FT = 256


def turn(block, cosine, sine, lanes):
    ahead = pltpu.roll(block, 96, 1)
    behind = pltpu.roll(block, 32, 1)
    return block * cosine + jnp.where(lax.rem(lanes, 64) < 32, ahead, behind) * sine


def see(starts):
    par = lax.rem(lax.axis_index("section"), 2)
    rows = lax.broadcasted_iota(jnp.int32, (SP, SP), 0)
    cols = lax.broadcasted_iota(jnp.int32, (SP, SP), 1)
    same = segment_of(starts, par, rows)[0] == segment_of(starts, par, cols)[0]
    allowed = jnp.logical_and(same, cols <= rows)
    return jnp.where(allowed, 0.0, NEG)


def hide(starts):
    par = lax.rem(lax.axis_index("section"), 2)
    rows = lax.broadcasted_iota(jnp.int32, (SP, SP), 0)
    cols = lax.broadcasted_iota(jnp.int32, (SP, SP), 1)
    same = segment_of(starts, par, rows)[0] == segment_of(starts, par, cols)[0]
    return jnp.where(jnp.logical_and(same, rows <= cols), 0.0, NEG)


def softmax_of(scores, unseen):
    masked = scores + unseen
    grown = jnp.exp(masked - jnp.max(masked, axis=-1, keepdims=True))
    return grown / jnp.sum(grown, axis=-1, keepdims=True)


def weight_copies(w_any, w, sems):
    bounds = (0, 3 * D, 4 * D, 4 * D + FF, 4 * D + 2 * FF, MATS, WROWS)
    return [
        pltpu.make_async_copy(
            w_any.at[pl.ds(lo, hi - lo)], w.at[pl.ds(lo, hi - lo)], sems.at[i]
        )
        for i, (lo, hi) in enumerate(zip(bounds[:-1], bounds[1:]))
    ]


def forward_kernel(keep, x, w_any, cosine, sine, starts, y, *refs):
    kept = refs[:7] if keep else ()
    q, k, v, o, h, gate, up, w, m, unseen, sems, keep_sems = refs[len(kept) :]

    def put(i):
        if keep:
            pltpu.make_async_copy((q, k, v, o, h, gate, up)[i], kept[i], keep_sems.at[i]).start()

    copies = weight_copies(w_any, w, sems)
    for i in (5, 0, 1, 2, 3, 4):
        copies[i].start()
    unseen[...] = see(starts)
    lanes = lax.broadcasted_iota(jnp.int32, (SP, 128), 1)
    first = lanes < 64
    copies[5].wait()
    gains = w[pl.ds(MATS, 16), :].astype(F32)
    stream = x[...].astype(F32)
    a1 = rms_scale(stream, gains[0:1]).astype(BF16)
    copies[0].wait()

    def project(b, carry):
        cols = pl.ds(pl.multiple_of(b * 256, 256), 256)
        raw_q = nn(a1, w[pl.ds(0, D), cols])
        raw_k = nn(a1, w[pl.ds(D, D), cols])
        raw_v = nn(a1, w[pl.ds(2 * D, D), cols])
        v[:, cols] = raw_v.astype(BF16)
        for part in range(2):
            there = pl.ds(pl.multiple_of(b * 256 + part * 128, 128), 128)
            here = slice(part * 128, (part + 1) * 128)
            turned_q = turn(raw_q[:, here], cosine[...], sine[...], lanes)
            q[:, there] = (turned_q * HD ** (-0.5)).astype(BF16)
            k[:, there] = turn(raw_k[:, here], cosine[...], sine[...], lanes).astype(BF16)
        return carry

    lax.fori_loop(0, D // 256, project, 0, unroll=True)
    for i in range(3):
        put(i)

    def attend(b, carry):
        cols = pl.ds(pl.multiple_of(b * 128, 128), 128)
        qb, kb, vb = q[:, cols], k[:, cols], v[:, cols]
        zero = jnp.zeros_like(qb)
        p0 = softmax_of(nt(jnp.where(first, qb, zero), kb), unseen[...]).astype(BF16)
        p1 = softmax_of(nt(jnp.where(first, zero, qb), kb), unseen[...]).astype(BF16)
        o[:, cols] = jnp.where(first, nn(p0, vb), nn(p1, vb)).astype(BF16)
        return carry

    lax.fori_loop(0, HEADS // 2, attend, 0, unroll=True)
    put(3)
    copies[1].wait()
    for b in range(3):
        cols = pl.ds(b * 256, 256)
        h[:, cols] = x[:, cols].astype(F32) + nn(o[...], w[pl.ds(3 * D, D), cols])
    put(4)
    a2 = rms_scale(h[...], gains[1:2]).astype(BF16)
    copies[2].wait()
    copies[3].wait()

    def widen(b, carry):
        cols = pl.ds(pl.multiple_of(b * FT, FT), FT)
        g = nt(a2, w[pl.ds(pl.multiple_of(4 * D + b * FT, FT), FT), :])
        u = nt(a2, w[pl.ds(pl.multiple_of(4 * D + FF + b * FT, FT), FT), :])
        gate[:, cols] = g
        up[:, cols] = u
        m[:, cols] = (g / (1.0 + jnp.exp(-g)) * u).astype(BF16)
        return carry

    lax.fori_loop(0, FF // FT, widen, 0, unroll=True)
    put(5)
    put(6)
    copies[4].wait()

    def narrow(b, carry):
        cols = pl.ds(pl.multiple_of(b * 256, 256), 256)
        y[:, cols] = (h[:, cols] + nn(m[...], w[pl.ds(4 * D + 2 * FF, FF), cols])).astype(BF16)
        return carry

    lax.fori_loop(0, 3, narrow, 0, unroll=True)
    for i, part in enumerate(kept):
        pltpu.make_async_copy((q, k, v, o, h, gate, up)[i], part, keep_sems.at[i]).wait()


KEPT = ((D, BF16), (D, BF16), (D, BF16), (D, BF16), (D, F32), (FF, F32), (FF, F32))


def forward_call(keep, x, weights, cosine, sine, starts):
    low = jax.ShapeDtypeStruct((SP, D), BF16)
    kept = tuple(jax.ShapeDtypeStruct((SP, n), t) for n, t in KEPT) if keep else ()
    return pl.pallas_call(
        functools.partial(forward_kernel, keep),
        out_shape=(low,) + kept,
        in_specs=[VMEM, ANY, VMEM, VMEM, SMEM],
        out_specs=(VMEM,) + (ANY,) * len(kept),
        scratch_shapes=[pltpu.VMEM((SP, n), t) for n, t in KEPT]
        + [
            pltpu.VMEM((WROWS, D), BF16),
            pltpu.VMEM((SP, FF), BF16),
            pltpu.VMEM((SP, SP), F32),
            pltpu.SemaphoreType.DMA((6,)),
            pltpu.SemaphoreType.DMA((7,)),
        ],
        compiler_params=pltpu.CompilerParams(vmem_limit_bytes=56 * 2**20),
        name="layer_forward_kept" if keep else "layer_forward",
    )(x, weights, cosine, sine, starts)


def rms_back(value_in, gain, grad):
    inv = lax.rsqrt(jnp.mean(value_in * value_in, axis=-1, keepdims=True) + norm_eps)
    unit = value_in * inv
    scaled = grad * gain
    grad_in = inv * (scaled - unit * jnp.mean(scaled * unit, axis=-1, keepdims=True))
    return grad_in, jnp.sum(grad * unit, axis=0, keepdims=True)


def backward_kernel(dy, x, w_any, cosine, sine, starts, *refs):
    kept, refs = refs[:7], refs[7:]
    dx, left, right, tail, refs = *refs[:4], refs[4:]
    q, k, v, o, h, gate, up, w, dgate, dup, m, da, do, dq, dk, dv, a1, a2, db, *refs = refs
    unseen, sems, keep_sems, out_sems = refs
    outs = []

    def put(source, target):
        copy = pltpu.make_async_copy(source, target, out_sems.at[len(outs)])
        copy.start()
        outs.append(copy)
    copies = weight_copies(w_any, w, sems)
    taken = [
        pltpu.make_async_copy(part, (q, k, v, o, h, gate, up)[i], keep_sems.at[i])
        for i, part in enumerate(kept)
    ]
    for one in (
        copies[4], taken[5], taken[6], copies[5], copies[2], copies[3], taken[4], copies[1],
        taken[0], taken[1], taken[2], copies[0], taken[3],
    ):
        one.start()
    unseen[...] = hide(starts)
    lanes = lax.broadcasted_iota(jnp.int32, (SP, 128), 1)
    first = lanes < 64
    copies[4].wait()
    taken[5].wait()
    taken[6].wait()

    def open_mlp(b, carry):
        cols = pl.ds(pl.multiple_of(b * FT, FT), FT)
        dm = nt(dy[...], w[pl.ds(pl.multiple_of(4 * D + 2 * FF + b * FT, FT), FT), :])
        g = gate[:, cols]
        u = up[:, cols]
        sig = 1.0 / (1.0 + jnp.exp(-g))
        dgate[:, cols] = (dm * u * sig * (1.0 + g * (1.0 - sig))).astype(BF16)
        dup[:, cols] = (dm * g * sig).astype(BF16)
        m[:, cols] = (g * sig * u).astype(BF16)
        return carry

    lax.fori_loop(0, FF // FT, open_mlp, 0, unroll=True)
    for i, part in enumerate((dgate, dup, m)):
        put(part, left.at[:, pl.ds(4 * D + i * FF, FF)])
    put(dy, right.at[5])
    copies[5].wait()
    gains = w[pl.ds(MATS, 16), :].astype(F32)
    copies[2].wait()
    copies[3].wait()

    def close_mlp(b, carry):
        cols = pl.ds(pl.multiple_of(b * 256, 256), 256)
        da[:, cols] = nn(dgate[...], w[pl.ds(4 * D, FF), cols]) + nn(
            dup[...], w[pl.ds(4 * D + FF, FF), cols]
        )
        return carry

    lax.fori_loop(0, 3, close_mlp, 0, unroll=True)
    taken[4].wait()
    dh, dg_mlp = rms_back(h[...], gains[1:2], da[...])
    dh = dh + dy[...].astype(F32)
    db[...] = dh.astype(BF16)
    a2[...] = rms_scale(h[...], gains[1:2]).astype(BF16)
    put(db, right.at[3])
    put(a2, right.at[4])
    copies[1].wait()
    for b in range(3):
        do[:, pl.ds(b * 256, 256)] = nt(db[...], w[pl.ds(3 * D + b * 256, 256), :]).astype(BF16)

    for i in range(3):
        taken[i].wait()

    def attend(b, carry):
        cols = pl.ds(pl.multiple_of(b * 128, 128), 128)
        qb, kb, vb, dob = q[:, cols], k[:, cols], v[:, cols], do[:, cols]
        zero = jnp.zeros_like(qb)
        parts = []
        for head in range(2):
            keep = first if head == 0 else jnp.logical_not(first)
            masked = nt(jnp.where(keep, kb, zero), qb) + unseen[...]
            grown = jnp.exp(masked - jnp.max(masked, axis=0, keepdims=True))
            probs = grown / jnp.sum(grown, axis=0, keepdims=True)
            dprobs = nt(jnp.where(keep, vb, zero), dob)
            along = jnp.sum(probs * dprobs, axis=0, keepdims=True)
            dscores = (probs * (dprobs - along)).astype(BF16)
            parts.append((tn(dscores, kb), nn(dscores, qb), nn(probs.astype(BF16), dob)))
        dqb = jnp.where(first, parts[0][0], parts[1][0]) * HD ** (-0.5)
        dkb = jnp.where(first, parts[0][1], parts[1][1])
        dq[:, cols] = turn(dqb, cosine[...], -sine[...], lanes).astype(BF16)
        dk[:, cols] = turn(dkb, cosine[...], -sine[...], lanes).astype(BF16)
        dv[:, cols] = jnp.where(first, parts[0][2], parts[1][2]).astype(BF16)
        return carry

    lax.fori_loop(0, HEADS // 2, attend, 0, unroll=True)
    for i, part in enumerate((dq, dk, dv)):
        put(part, right.at[i])
    copies[0].wait()
    for b in range(3):
        rows = lambda i, b=b: w[pl.ds(i * D + b * 256, 256), :]
        da[:, pl.ds(b * 256, 256)] = (
            nt(dq[...], rows(0)) + nt(dk[...], rows(1)) + nt(dv[...], rows(2))
        )
    stream = x[...].astype(F32)
    a1[...] = rms_scale(stream, gains[0:1]).astype(BF16)
    for i in range(3):
        put(a1, left.at[:, pl.ds(i * D, D)])
    taken[3].wait()
    put(o, left.at[:, pl.ds(3 * D, D)])
    dstream, dg_attn = rms_back(stream, gains[0:1], da[...])
    dx[...] = (dstream + dh).astype(BF16)
    ids = lax.broadcasted_iota(jnp.int32, (16, D), 0)
    tail[...] = jnp.where(ids == 0, dg_attn, jnp.where(ids == 1, dg_mlp, 0.0)).astype(BF16)
    for copy in outs:
        copy.wait()


def backward_call(dy, x, weights, cosine, sine, starts, kept):
    wide = pltpu.VMEM((SP, FF), BF16)
    narrow = pltpu.VMEM((SP, D), BF16)
    return pl.pallas_call(
        backward_kernel,
        out_shape=(
            jax.ShapeDtypeStruct((SP, D), BF16),
            jax.ShapeDtypeStruct((SP, MATS), BF16),
            jax.ShapeDtypeStruct((6, SP, D), BF16),
            jax.ShapeDtypeStruct((16, D), BF16),
        ),
        in_specs=[VMEM, VMEM, ANY, VMEM, VMEM, SMEM] + [ANY] * 7,
        out_specs=(VMEM, ANY, ANY, VMEM),
        scratch_shapes=[pltpu.VMEM((SP, n), t) for n, t in KEPT]
        + [
            pltpu.VMEM((WROWS, D), BF16),
            wide,
            wide,
            wide,
            pltpu.VMEM((SP, D), F32),
        ]
        + [narrow] * 7
        + [
            pltpu.VMEM((SP, SP), F32),
            pltpu.SemaphoreType.DMA((6,)),
            pltpu.SemaphoreType.DMA((7,)),
            pltpu.SemaphoreType.DMA((13,)),
        ],
        compiler_params=pltpu.CompilerParams(vmem_limit_bytes=60 * 2**20),
        name="layer_backward",
    )(dy, x, weights, cosine, sine, starts, *kept)


def matrix_gradients(left, right, tail):
    parts = [(0, 0), (D, 1), (2 * D, 2), (3 * D, 3), (4 * D, 4), (4 * D + FF, 4), (4 * D + 2 * FF, 5)]
    ends = [start for start, _ in parts[1:]] + [MATS]
    rows = [
        tn(left[:, start:end], right[i]).astype(BF16) for (start, i), end in zip(parts, ends)
    ]
    return jnp.concatenate(rows + [tail], axis=0)


HEAD_T = 256


def column(row, size):
    there = lax.broadcasted_iota(jnp.int32, (size, size), 0)
    here = lax.broadcasted_iota(jnp.int32, (size, size), 1)
    zero = jnp.zeros((), row.dtype)
    return jnp.sum(jnp.where(there == here, row, zero), axis=1, keepdims=True)


def as_rows(values):
    there = lax.broadcasted_iota(jnp.int32, (128, 128), 0)
    here = lax.broadcasted_iota(jnp.int32, (128, 128), 1)
    return [
        jnp.sum(
            jnp.where(there == here, values[k * 128 : (k + 1) * 128], 0.0), axis=0, keepdims=True
        )
        for k in range(4)
    ]


def head_kernel(
    y, picks, info, gain, table, d_top, d_table, small, mine, picked, af, scores, dlow, labels,
    counts, stat, stats, daf, rx_core, low, rx, fresh, zero_sem, own_sem, pick_send, pick_recv,
    core_send, core_recv, stat_send, stat_recv, swap_send, swap_recv, daf_send, daf_recv,
):
    sec, dp, z, c, par, home = place()
    last = sec == 3
    upper = sec >= 2
    barrier = pltpu.get_barrier_semaphore()
    other_core = (3, dp + 1 - 2 * c)

    def greet(s, e):
        pl.semaphore_signal(barrier, 1, device_id=(s, e), device_id_type=MESH)

    def greet_second():
        for k in range(4):
            greet(3, 2 * k + c)
        pl.semaphore_wait(barrier, 4)

    def greet_third():
        for k in range(4):
            greet(2, 2 * k + c)
        for k in range(1, 8):
            greet(3, lax.rem(dp + k, 8))
        pl.semaphore_wait(barrier, 11)

    all_zero = pltpu.make_async_copy(fresh, d_table, zero_sem)

    def zeros():
        fresh[...] = jnp.zeros_like(fresh)
        all_zero.start()

    pl.when(jnp.logical_not(last))(zeros)
    small[...] = jnp.zeros_like(small)
    pick_row = picks[pl.ds(par, 1), :]
    pick_col = column(pick_row, PICKS)

    def choose():
        ids = lax.broadcasted_iota(jnp.int32, (PICKS, SP), 1)
        mine[...] = nn(jnp.where(ids == pick_col, 1.0, 0.0).astype(BF16), y[...]).astype(BF16)

    pl.when(upper)(choose)
    pl.when(sec == 2)(greet_second)
    pl.when(last)(greet_third)

    def rows(p, zz, lane):
        return pl.ds(pl.multiple_of((2 * (2 * zz + lane) + p) * PICKS, PICKS), PICKS)

    def pick_to(k):
        zz = lax.rem(z + k, 4)
        return pltpu.make_async_remote_copy(
            src_ref=mine,
            dst_ref=picked.at[rows(par, z, c)],
            send_sem=pick_send,
            recv_sem=pick_recv.at[par, z],
            device_id=(3, 2 * zz + c),
            device_id_type=MESH,
        )

    def came(p, k):
        zz = lax.rem(z + k, 4)
        return pltpu.make_async_remote_copy(
            src_ref=mine,
            dst_ref=picked.at[rows(p, zz, c)],
            send_sem=pick_send,
            recv_sem=pick_recv.at[p, zz],
            device_id=other_core,
            device_id_type=MESH,
        )

    def forward(p, k):
        part = picked.at[rows(p, lax.rem(z + k, 4), c)]
        return pltpu.make_async_remote_copy(
            src_ref=part,
            dst_ref=part,
            send_sem=core_send,
            recv_sem=core_recv,
            device_id=other_core,
            device_id_type=MESH,
        )

    def span(ref, count, send, recv):
        part = ref.at[pl.ds(0, count)]
        return pltpu.make_async_remote_copy(
            src_ref=part,
            dst_ref=part,
            send_sem=send,
            recv_sem=recv,
            device_id=other_core,
            device_id_type=MESH,
        )

    def pick_second():
        for k in (1, 2, 3, 0):
            pick_to(k).start()

    def pick_third():
        own = pltpu.make_async_copy(mine, picked.at[rows(1, z, c)], own_sem)
        own.start()
        for k in range(1, 4):
            pick_to(k).start()
        for e in range(8):
            for p in range(2):
                at = pl.ds((2 * e + p) * PICKS, PICKS)
                labels[at, :] = column(info[e, 2 + p : 3 + p, :][:, :PICKS], PICKS)
                counts[at, :] = column(info[e, 4 + p : 5 + p, :][:, :PICKS].astype(F32), PICKS)
        own.wait()
        forward(1, 0).start()
        for k in range(4):
            came(0, k).wait_recv()
            forward(0, k).start()
            if k:
                came(1, k).wait_recv()
                forward(1, k).start()
        span(picked, 8 * PICKS, core_send, core_recv).wait_recv()

    pl.when(sec == 2)(pick_second)
    pl.when(last)(pick_third)
    g_f = gain[...].astype(F32)[0:1]
    own = OWN
    tiles = [(t * HEAD_T, HEAD_T) for t in range(own // HEAD_T)] + [
        (own - own % HEAD_T, own % HEAD_T)
    ]

    def over_tiles(body):
        def step(t, carry):
            body(pl.multiple_of(t * HEAD_T, HEAD_T), HEAD_T)
            return carry

        lax.fori_loop(0, own // HEAD_T, step, 0)
        body(own - own % HEAD_T, own % HEAD_T)

    def forward_part():
        af[...] = rms_scale(picked[...].astype(F32), g_f).astype(BF16)
        fold = lambda op, block: functools.reduce(
            op, [block[:, k * 128 : (k + 1) * 128] for k in range(block.shape[1] // 128)]
        )
        top = daf.at[:, pl.ds(0, 128)]
        top[...] = jnp.full((16 * PICKS, 128), NEG, F32)

        def product(start, size):
            ids = lax.broadcasted_iota(jnp.int32, (16 * PICKS, size), 1) + (dp * own + start)
            block = nt(af[...], table[pl.ds(start, size), :])
            block = jnp.where(ids < VOCAB, block, NEG)
            scores[:, pl.ds(start, size)] = block
            top[...] = jnp.maximum(top[...], fold(jnp.maximum, block))

        over_tiles(product)
        top_col = jnp.max(top[...], axis=1, keepdims=True)
        total = daf.at[:, pl.ds(128, 128)]
        target = daf.at[:, pl.ds(256, 128)]
        total[...] = jnp.zeros((16 * PICKS, 128), F32)
        target[...] = jnp.zeros((16 * PICKS, 128), F32)

        def exponents(start, size):
            ids = lax.broadcasted_iota(jnp.int32, (16 * PICKS, size), 1) + (dp * own + start)
            block = scores[:, pl.ds(start, size)]
            grown = jnp.exp(block - top_col)
            scores[:, pl.ds(start, size)] = grown
            total[...] += fold(jnp.add, grown)
            target[...] += fold(jnp.add, jnp.where(ids == labels[...], block, 0.0))

        over_tiles(exponents)
        stat[...] = jnp.zeros_like(stat)
        columns = (
            top_col,
            jnp.sum(total[...], axis=1, keepdims=True),
            jnp.sum(target[...], axis=1, keepdims=True),
        )
        for k, values in enumerate(columns):
            for i, row in enumerate(as_rows(values)):
                stat[4 * k + i : 4 * k + i + 1, :] = row
        stats[dp] = stat[...]
        for k in range(1, 8):
            pltpu.make_async_remote_copy(
                src_ref=stat,
                dst_ref=stats.at[dp],
                send_sem=stat_send,
                recv_sem=stat_recv,
                device_id=(3, lax.rem(dp + k, 8)),
                device_id_type=MESH,
            ).start()
        every = span(stats, 7, stat_send, stat_recv)
        every.wait_recv()
        tops = [stats[e, 0:4, :] for e in range(8)]
        best = functools.reduce(jnp.maximum, tops)
        sums = sum(stats[e, 4:8, :] * jnp.exp(tops[e] - best) for e in range(8))
        hits = sum(stats[e, 8:12, :] for e in range(8))
        log_total = best + jnp.log(sums)
        log_col = jnp.concatenate([column(log_total[k : k + 1], 128) for k in range(4)], axis=0)
        hit_col = jnp.concatenate([column(hits[k : k + 1], 128) for k in range(4)], axis=0)
        loss = jnp.sum(
            jnp.where(counts[...] > 0, log_col - hit_col, 0.0), axis=0, keepdims=True
        )
        lane = lax.broadcasted_iota(jnp.int32, (1, 128), 1)
        small[6:7, :] = jnp.where(jnp.logical_and(lane == 0, dp == 0), loss, 0.0)
        shrink = jnp.exp(top_col - log_col)

        def slopes(start, size):
            ids = lax.broadcasted_iota(jnp.int32, (16 * PICKS, size), 1) + (dp * own + start)
            hit = jnp.where(ids == labels[...], 1.0, 0.0)
            block = (scores[:, pl.ds(start, size)] * shrink - hit) * counts[...]
            dlow[:, pl.ds(start, size)] = block.astype(BF16)

        over_tiles(slopes)
        for b in range(3):
            cols = pl.ds(b * 256, 256)
            daf[:, cols] = nn(dlow[...], table[:, cols])
        every.wait_send()
        span(picked, 3 * PICKS, pick_send, core_recv).wait_send()
        span(picked, 8 * PICKS, core_send, core_recv).wait_send()

    def swap(p, zz):
        return pltpu.make_async_remote_copy(
            src_ref=daf.at[rows(p, zz, 1 - c)],
            dst_ref=rx_core.at[pl.ds((2 * zz + p) * PICKS, PICKS)],
            send_sem=swap_send,
            recv_sem=swap_recv,
            device_id=other_core,
            device_id_type=MESH,
        )

    def back_to(p, k):
        zz = lax.rem(z + k, 4)
        return pltpu.make_async_remote_copy(
            src_ref=low.at[pl.ds(pl.multiple_of((2 * zz + p) * PICKS, PICKS), PICKS)],
            dst_ref=rx.at[z],
            send_sem=daf_send,
            recv_sem=daf_recv,
            device_id=(2 + p, 2 * zz + c),
            device_id_type=MESH,
        )

    def table_part(start, size):
        there = pl.ds(start, size)
        value = tn(dlow[:, there], af[...])
        fresh[there, :] = value
        pltpu.make_async_copy(fresh.at[there], d_table.at[there], zero_sem).start()
        folded = jnp.sum(value * value, axis=0, keepdims=True)
        small[7:8, :] += functools.reduce(
            jnp.add, [folded[:, k * 128 : (k + 1) * 128] for k in range(6)]
        )

    def third():
        forward_part()
        for zz in range(4):
            for p in range(2):
                swap(p, zz).start()
        table_part(own - own % HEAD_T, own % HEAD_T)
        span(rx_core, 8 * PICKS, swap_send, swap_recv).wait_recv()
        for zz in range(4):
            for p in range(2):
                there = pl.ds((2 * zz + p) * PICKS, PICKS)
                low[there, :] = (daf[rows(p, zz, c), :] + rx_core[there, :]).astype(BF16)
        for k in (1, 2, 3, 0):
            back_to(0, k).start()
            if k:
                back_to(1, k).start()

        def step(t, carry):
            table_part(pl.multiple_of(t * HEAD_T, HEAD_T), HEAD_T)
            return carry

        lax.fori_loop(0, own // HEAD_T, step, 0)
        rx[z] = low[pl.ds(pl.multiple_of((2 * z + 1) * PICKS, PICKS), PICKS), :]
        span(rx_core, 8 * PICKS, swap_send, swap_recv).wait_send()
        span(low, 7 * PICKS, daf_send, daf_recv).wait_send()
        span(rx, 3, daf_send, daf_recv).wait_recv()

    def second():
        span(picked, 4 * PICKS, pick_send, core_recv).wait_send()
        span(rx, 4, daf_send, daf_recv).wait_recv()

    pl.when(last)(third)
    pl.when(sec == 2)(second)

    def finish():
        summed = rx[0].astype(F32)
        for k in range(1, 4):
            summed = summed + rx[k].astype(F32)
        grad, dg_f = rms_back(mine[...].astype(F32), g_f, summed)
        for k in range(6):
            small[k : k + 1, :] = dg_f[:, k * 128 : (k + 1) * 128]
        ids = lax.broadcasted_iota(jnp.int32, (SP, PICKS), 0)
        spread = jnp.where(ids == pick_row, 1.0, 0.0).astype(BF16)
        rest = grad
        out = jnp.zeros((SP, D), F32)
        for _ in range(3):
            part = rest.astype(BF16)
            out = out + nn(spread, part)
            rest = rest - part.astype(F32)
        d_top[...] = out.astype(BF16)

    def none():
        d_top[...] = jnp.zeros_like(d_top)

    pl.when(upper)(finish)
    pl.when(jnp.logical_not(upper))(none)
    all_zero.wait()


def head_call(y, picks, info, gain, table):
    low = lambda *shape: pltpu.VMEM(shape, BF16)
    wide = lambda *shape: pltpu.VMEM(shape, F32)
    n = 16 * PICKS
    return pl.pallas_call(
        head_kernel,
        out_shape=(
            jax.ShapeDtypeStruct((SP, D), BF16),
            jax.ShapeDtypeStruct((OWN, D), F32),
            jax.ShapeDtypeStruct((8, 128), F32),
        ),
        in_specs=[VMEM] * 5,
        out_specs=(VMEM, ANY, VMEM),
        scratch_shapes=[
            low(PICKS, D),
            low(n, D),
            low(n, D),
            wide(n, OWN),
            low(n, OWN),
            pltpu.VMEM((n, 1), jnp.int32),
            wide(n, 1),
            wide(16, 128),
            wide(8, 16, 128),
            wide(n, D),
            wide(8 * PICKS, D),
            low(8 * PICKS, D),
            low(4, PICKS, D),
            wide(OWN, D),
            pltpu.SemaphoreType.DMA,
            pltpu.SemaphoreType.DMA,
            pltpu.SemaphoreType.DMA,
            pltpu.SemaphoreType.DMA((2, 4)),
        ]
        + [pltpu.SemaphoreType.DMA] * 8,
        compiler_params=pltpu.CompilerParams(
            collective_id=3, has_side_effects=True, vmem_limit_bytes=56 * 2**20
        ),
        name="head",
    )(y, picks, info, gain, table)


def open_anywhere(codes, labels, picks, classes, null_mask, starts, table, frequency):
    sec = lax.axis_index("section")
    d = lax.axis_index("dp")
    par = lax.rem(sec, 2)
    own = table.shape[0]
    row_index, counted, _, position = jax.vmap(row_layout)(starts, classes, null_mask, codes)
    picked_labels = jnp.take_along_axis(labels, picks, axis=1)
    picked_counts = jnp.take_along_axis(counted, picks, axis=1).astype(jnp.int32)
    row_index = jnp.pad(row_index, ((0, 0), (0, SP - SLOTS)), constant_values=-1)
    info = jnp.concatenate([row_index, picked_labels, picked_counts], axis=1)
    info = lax.all_gather(info, "dp", axis=0, tiled=True)
    all_labels = info[:, SP : SP + PICKS].reshape(-1)
    all_counts = info[:, SP + PICKS :].reshape(-1).astype(F32)
    gain_row = lax.slice_in_dim(table, VOCAB % own, VOCAB % own + 1)[0].astype(F32)
    holds = (sec == 3) & (d == VOCAB // own)
    g_f = lax.psum(jnp.where(holds, gain_row, 0.0), ("section", "dp"))
    position = jnp.pad(position[par], (0, SP - SLOTS))
    angles = position.astype(F32)[:, None] * frequency[None, :]
    cosine = jnp.tile(jnp.cos(angles), (1, 4))
    sine = jnp.tile(jnp.concatenate([-jnp.sin(angles), jnp.sin(angles)], axis=1), (1, 2))
    gathered = lax.all_gather(table, "dp", axis=0, tiled=True)[:WROWS]
    other = lax.ppermute(gathered, "section", [(0, 1), (1, 0), (2, 3), (3, 2)])
    weights = jnp.where((sec == 1) | (sec == 2), gathered, other)
    local = jnp.where(sec == 0, info[:, :SP].reshape(-1), -1) - d * own
    onehot = (local[:, None] == jnp.arange(own)[None, :]).astype(BF16)
    looked = (nn(onehot, table) * math.sqrt(D)).astype(BF16)
    looked = lax.psum_scatter(looked, "dp", scatter_dimension=0, tiled=True).reshape(2, SP, D)
    from_first = lax.ppermute(looked[1], "section", [(0, 1)])
    x0 = jnp.where(sec == 0, looked[0], from_first)
    return weights, x0, local, all_labels, all_counts, g_f, cosine, sine


def head_anywhere(y, my_picks, all_labels, all_counts, g_f, table):
    sec = lax.axis_index("section")
    d = lax.axis_index("dp")
    n_sec = lax.axis_size("section")
    n_dp = lax.axis_size("dp")
    own = table.shape[0]
    picked = jnp.take(y, my_picks, axis=0)
    all_picked = lax.all_gather(picked, ("section", "dp"), axis=0, tiled=False)
    all_picked = all_picked.reshape(n_sec, n_dp, PICKS, D)[2:].transpose(1, 0, 2, 3)
    all_picked = all_picked.reshape(-1, D).astype(F32)
    af = jnp.where(sec == 3, rms_scale(all_picked, g_f), 0.0).astype(BF16)
    vocab_ids = d * own + jnp.arange(own)
    logits = jnp.where(vocab_ids[None, :] < VOCAB, nt(af, table), NEG)
    local_max = jnp.max(logits, axis=1)
    hit = vocab_ids[None, :] == all_labels[:, None]
    sums = jnp.stack(
        [
            local_max,
            jnp.sum(jnp.exp(logits - local_max[:, None]), axis=1),
            jnp.sum(jnp.where(hit, logits, 0.0), axis=1),
        ]
    )
    every = lax.all_gather(sums, "dp", axis=0, tiled=False)
    top = jnp.max(every[:, 0], axis=0)
    total = jnp.sum(every[:, 1] * jnp.exp(every[:, 0] - top), axis=0)
    target = jnp.sum(every[:, 2], axis=0)
    log_total = top + jnp.log(total)
    loss_part = jnp.where(
        (sec == 3) & (d == 0), jnp.sum(jnp.where(all_counts > 0, log_total - target, 0.0)), 0.0
    )
    dlogits = (jnp.exp(logits - log_total[:, None]) - hit.astype(F32)) * all_counts[:, None]
    dlogits = jnp.where(sec == 3, dlogits, 0.0).astype(BF16)
    d_table = tn(dlogits, af)
    daf = lax.psum(nn(dlogits, table), "dp")
    daf = lax.dynamic_slice_in_dim(daf, d * 2 * PICKS, 2 * PICKS).reshape(2, PICKS, D)
    daf = jnp.where(sec == 3, daf[1], lax.ppermute(daf[0], "section", [(3, 2)]))
    d_own, dg_f = rms_pull(picked.astype(F32), g_f, daf)
    dg_f = jnp.where(sec >= 2, dg_f, 0.0)
    spread = (jnp.arange(SP)[:, None] == my_picks[None, :]).astype(F32)
    d_top = jnp.dot(spread, d_own, precision=lax.Precision.HIGHEST).astype(BF16)
    return d_top, d_table, dg_f, loss_part


def shards(codes, labels, picks, classes, null_mask, starts, master, momentum, average):
    sec = lax.axis_index("section")
    d = lax.axis_index("dp")
    n_dp = lax.axis_size("dp")
    n_sec = lax.axis_size("section")
    par = lax.rem(sec, 2)
    own = master.shape[0]
    learn_rate = rate_factor * math.sqrt(own * n_sec * n_dp)
    beside = [(0, 1), (1, 0), (2, 3), (3, 2)]
    fast = n_sec == 4 and n_dp == 8 and own == OWN
    gain_at = VOCAB // own
    frequency = rope_base ** (-jnp.arange(HD // 2, dtype=F32) * 2.0 / HD)

    if fast:
        wide = jnp.tile(frequency[None, :], (1, 4))
        weights, x0, info, gain, cosine, sine, table = gather_and_embed(
            master, codes, labels, picks, starts, classes, null_mask, wide
        )
        all_index = info[:, :2, :SP].reshape(-1)
        local = jnp.where(sec == 0, all_index, -1) - d * own
    else:
        table = master.astype(BF16)
        opened = open_anywhere(codes, labels, picks, classes, null_mask, starts, table, frequency)
        weights, x0, local, all_labels, all_counts, g_f, cosine, sine = opened
    around = (cosine, sine, starts)

    y0 = forward_call(False, x0, weights, *around)[0]
    x = jnp.where(sec < 2, x0, lax.ppermute(y0, "section", [(0, 2), (1, 3)]))
    y, *kept = forward_call(True, x, weights, *around)

    if fast:
        d_top, d_table, small = head_call(y, picks, info, gain, table)
    else:
        d_top, d_table, dg_f, loss_part = head_anywhere(
            y, picks[par], all_labels, all_counts, g_f, table
        )

    once = backward_call(d_top, x, weights, *around, kept)
    dy = lax.ppermute(once[0], "section", [(2, 0), (3, 1)])
    dx0, left, right, tail = lax.cond(
        sec < 2, lambda: tuple(backward_call(dy, x, weights, *around, kept)), lambda: tuple(once)
    )

    if fast:
        grad, squares = reduce_and_scatter(left, right, tail, d_table, dx0, local[None, :])
        totals = share_norm(small, squares, n_sec, n_dp)
        dg_f, loss_sum, grad_norm = totals[:6].reshape(-1), totals[6, 0], totals[8, 0]
        count_sum = jnp.sum(info[:, 4:6, :PICKS].astype(F32))
    else:
        grads = matrix_gradients(left, right, tail)
        grads = grads.astype(F32) + lax.ppermute(grads, "section", beside).astype(F32)
        grads = jnp.pad(grads.astype(BF16), ((0, own * n_dp - WROWS), (0, 0)))
        grad = lax.psum_scatter(grads, "dp", scatter_dimension=0, tiled=True).astype(F32)
        grad = jnp.where(sec == 3, d_table, grad)
        pair = jnp.stack([dx0, lax.ppermute(dx0, "section", [(1, 0)])])
        all_dx = lax.all_gather(pair, "dp", axis=0, tiled=True).reshape(-1, D)
        onehot = (jnp.arange(own)[:, None] == local[None, :]).astype(BF16)
        grad = jnp.where(sec == 0, nn(onehot, all_dx) * math.sqrt(D), grad)
        totals = (dg_f, jnp.sum(grad * grad), loss_part)
        dg_f, squares, loss_sum = lax.psum(totals, ("section", "dp"))
        count_sum = jnp.sum(all_counts)
        grad_norm = jnp.sqrt(squares + jnp.sum(dg_f * dg_f))
    gain_here = (jnp.arange(own) == VOCAB % own)[:, None] & (sec == 3) & (d == gain_at)
    grad = grad + jnp.where(gain_here, dg_f[None, :], 0.0)
    clipped = grad * jnp.minimum(1.0, clip_limit / (grad_norm + norm_eps))
    new_momentum = momentum_decay * momentum + clipped
    new_master = master - learn_rate * (clipped + momentum_decay * new_momentum)
    new_average = average_decay * average + (1.0 - average_decay) * new_master
    return loss_sum, count_sum, grad_norm, new_master, new_momentum, new_average


def solution(mesh):
    split = P("dp", None)
    whole = P(("section", "dp"), None)
    return jax.shard_map(
        shards,
        mesh=mesh,
        in_specs=(split,) * 6 + (whole,) * 3,
        out_specs=(P(), P(), P(), whole, whole, whole),
        check_vma=False,
    )
```

```python
import functools
import math

import jax
import jax.numpy as jnp
from jax import lax
from jax.experimental import pallas as pl
from jax.experimental.pallas import tpu as pltpu
from jax.sharding import PartitionSpec as P

D = 768
HEADS = 12
HD = 64
FF = 2048
VOCAB = 16384
CLASSES = 1001
SLOTS = 264
SP = 272
PICKS = 32
SEGS = 3
MATS = 4 * D + 3 * FF
WROWS = 9232

F32 = jnp.float32
BF16 = jnp.bfloat16

rope_base = 10000.0
clip_limit = 1.0
rate_factor = 0.25
momentum_decay = 0.9
average_decay = 0.8
norm_eps = 1e-06


def nn(left, right):
    return jnp.dot(left, right, preferred_element_type=F32)


def tn(left, right):
    return lax.dot_general(left, right, (((0,), (0,)), ((), ())), preferred_element_type=F32)


def nt(left, right):
    return lax.dot_general(left, right, (((1,), (1,)), ((), ())), preferred_element_type=F32)


def rms_scale(value_in, gain):
    return (
        value_in * lax.rsqrt(jnp.mean(value_in * value_in, axis=-1, keepdims=True) + norm_eps) * gain
    )


def rms_pull(value_in, gain, grad):
    inv = lax.rsqrt(jnp.mean(value_in * value_in, axis=-1, keepdims=True) + norm_eps)
    unit = value_in * inv
    scaled = grad * gain
    grad_in = inv * (scaled - unit * jnp.mean(scaled * unit, axis=-1, keepdims=True))
    return grad_in, jnp.sum(grad * unit, axis=0)


def row_layout(starts_row, classes_row, null_row, codes_row):
    slot_ids = jnp.arange(SLOTS, dtype=jnp.int32)
    segment = jnp.sum((starts_row[None, 1:] <= slot_ids[:, None]).astype(jnp.int32), axis=1)
    seg_start = jnp.sum(
        jnp.where(segment[:, None] == jnp.arange(SEGS + 1)[None, :], starts_row[None, :], 0), axis=1
    )
    position = slot_ids - seg_start
    live_end = starts_row[SEGS]
    is_first = (position == 0) & (slot_ids < live_end)
    clamped = jnp.minimum(segment, SEGS - 1)
    hit = clamped[:, None] == jnp.arange(SEGS)[None, :]
    class_row = jnp.sum(
        jnp.where(hit, jnp.where(null_row > 0, CLASSES - 1, classes_row)[None, :], 0), axis=1
    )
    row_index = jnp.where(is_first, VOCAB + class_row, codes_row)
    following = jnp.concatenate([segment[1:], jnp.full((1,), SEGS + 1, jnp.int32)])
    counted = (following == segment) & (slot_ids + 1 < live_end)
    return row_index, counted, segment, position


MESH = pl.DeviceIdType.MESH
ANY = pl.BlockSpec(memory_space=pl.ANY)
VMEM = pl.BlockSpec(memory_space=pltpu.VMEM)
SMEM = pl.BlockSpec(memory_space=pltpu.SMEM)

OWN = 2176
SPLIT = 1152
COUNT = (18, 16, 18, 16, 11)
ROWS = (64, 64, 64, 64, 48)
HELD = (0, SPLIT, OWN, OWN + SPLIT, 2 * OWN)
LARGE = (16, 14, 16, 14, 11)
SMALL = 4
SMALL_ROWS = 32
LANE = 2 * OWN + 11 * 48
LAG = 2
WINDOW = 2
HOP = 2
PIECES = ((0, 64), (64, 64), (128, 64), (192, 64), (256, 16))
TURN = 6
CHOP = 4
CLAG = 3
AHEAD = 4
CWAIT = 6


def class_base(k, lane):
    if k == 4:
        return 4 * OWN
    return OWN * (2 * (k // 2) + lane) + SPLIT * (k % 2)


def place():
    sec = lax.axis_index("section")
    dp = lax.axis_index("dp")
    z = dp // 2
    c = lax.rem(dp, 2)
    par = lax.rem(sec, 2)
    home = jnp.logical_or(sec == 1, sec == 2)
    return sec, dp, z, c, par, home


def greet_neighbours(sec, dp, z, c, par, turns):
    barrier = pltpu.get_barrier_semaphore()

    def greet(s, e):
        pl.semaphore_signal(barrier, 1, device_id=(s, e), device_id_type=MESH)

    greet(sec, dp + 1 - 2 * c)
    greet(sec + 1 - 2 * par, dp)
    pl.when(z > 0)(lambda: greet(sec, dp - 2))
    pl.when(z < 3)(lambda: greet(sec, dp + 2))
    count = 2 + (z > 0).astype(jnp.int32) + (z < 3).astype(jnp.int32)
    for sender, receiver in turns:
        pl.when(sec == receiver)(lambda sender=sender: greet(sender, dp))
        count = count + (sec == sender).astype(jnp.int32)
    pl.semaphore_wait(barrier, count)


def hop_targets(sec, dp, c, par):
    return {
        "up": (sec, dp + 2),
        "down": (sec, dp - 2),
        "x": (sec + 1 - 2 * par, dp),
        "core": (sec, dp + 1 - 2 * c),
    }


HOPS = ("up", "down", "x", "core")


def tree(z, c, home):
    both = jnp.logical_and
    either = jnp.logical_or
    no = jnp.logical_not
    far = z >= 2
    mid = both(z >= 1, z <= 2)
    never = z < 0
    away = no(home)
    as_int = lambda flag: flag.astype(jnp.int32)
    out = []
    for block in (0, 1):
        for half in (0, 1):
            mine = home if half == 0 else away
            other = no(mine)
            source = both(z == block, home)
            if half == 0:
                early = (lambda j: j < TURN) if block == 0 else (lambda j: j < 0)
                near_x = lambda j, block=block, early=early: both(z == 1 - block, early(j))
                hop_x = lambda j, near_x=near_x: both(home, near_x(j))
                got_x = lambda j, near_x=near_x: both(away, near_x(j))
                along = lambda j, early=early: either(home, no(early(j)))
            else:
                hop_x = lambda j, block=block: both(away, z == 1 - block)
                got_x = lambda j, block=block: both(home, z == 1 - block)
                along = lambda j: away
            at_owner = both(z == block, away)
            if block == 0:
                up = lambda j, along=along, mine=mine: either(both(z == 0, along(j)), both(mid, mine))
                down = lambda j: never
                from_up = lambda j: never
            else:
                up = lambda j, mine=mine: both(mid, mine)
                down = lambda j, along=along: both(z == 1, along(j))
                from_up = lambda j, got_x=got_x: both(z == 0, no(got_x(j)))
            send_x = lambda j, source=source, mine=mine, hop_x=hop_x: either(
                either(source, both(far, mine)), hop_x(j)
            )
            from_x = lambda j, at_owner=at_owner, other=other, got_x=got_x: either(
                either(at_owner, both(far, other)), got_x(j)
            )
            from_down = lambda j, source=source, from_x=from_x, from_up=from_up: no(
                either(source, either(from_x(j), from_up(j)))
            )
            depth = jnp.abs(z - block) + as_int(far) * (half + as_int(other))
            if half == 0:
                depth = depth + (1 - as_int(far)) * as_int(away)
            else:
                depth = depth + (1 - as_int(far)) * jnp.where(
                    away, 1, 2 * as_int(z == 1 - block)
                )
            out.append(
                (source, dict(up=up, down=down, x=send_x), dict(up=from_up, down=from_down, x=from_x), depth)
            )
    lane0 = c == 0
    source = both(both(z == 2, home), lane0)
    sends = dict(
        up=lambda j: both(z == 2, lane0),
        down=lambda j: both(mid, lane0),
        x=lambda j: source,
    )
    parents = dict(
        up=lambda j: both(z <= 1, lane0),
        down=lambda j: both(z == 3, lane0),
        x=lambda j: both(both(z == 2, away), lane0),
    )
    out.append((source, sends, parents, jnp.abs(z - 2) + as_int(away)))
    return out


def segment_of(starts, r, slot):
    bounds = [starts[r, j] for j in range(SEGS + 1)]
    count = lambda at: functools.reduce(
        jnp.add, [(at >= bounds[j]).astype(jnp.int32) for j in range(1, SEGS + 1)]
    )
    segment = count(slot)
    begin = jnp.where(
        segment == 0, bounds[0], jnp.where(segment == 1, bounds[1], jnp.where(segment == 2, bounds[2], bounds[3]))
    )
    counted = jnp.logical_and(count(slot + 1) == segment, slot + 1 < bounds[SEGS])
    return segment, slot - begin, counted, slot < bounds[SEGS]


def open_kernel(
    master, codes, labels, picks, starts, classes, nulls, frequency, out, x0, info, gain, cosine,
    sine, table, exact, master_sem, recv_sem, recv_c, core_sem, send_sem, sent, mine, rx_core, rx_up, rx_down,
    swap_send, swap_recv, x_send, x_recv, line_send, up_recv, down_recv, last_send, last_recv,
    note, note_send, note_recv, gain_send, gain_recv,
):
    sec, dp, z, c, par, home = place()
    targets = hop_targets(sec, dp, c, par)
    classes_of = tree(z, c, home)
    gain_dp = VOCAB // (OWN)
    holds_gain = jnp.logical_and(sec == 3, dp == gain_dp)

    parts = [pl.ds(k * (OWN // 4), OWN // 4) for k in range(4)]
    def place_own(part, value):
        start = pl.multiple_of(dp * OWN + part.start, 16)
        out[pl.ds(start, part.size), :] = value

    fetch = [
        pltpu.make_async_copy(master.at[part], exact.at[part], master_sem.at[k])
        for k, part in enumerate(parts)
    ]
    for one in fetch:
        one.start()

    barrier = pltpu.get_barrier_semaphore()

    def greet(s, e):
        pl.semaphore_signal(barrier, 1, device_id=(s, e), device_id_type=MESH)

    for k in range(1, 8):
        greet(sec, lax.rem(dp + k, 8))
    greet(sec + 1 - 2 * par, dp)
    pl.when(sec == 2)(lambda: greet(0, dp))
    pl.when(sec == 1)(lambda: greet(2, dp))
    pl.when(jnp.logical_and(sec == 2, dp != gain_dp))(lambda: greet(3, gain_dp))

    slot_row = lax.broadcasted_iota(jnp.int32, (1, SLOTS), 1)
    note[...] = jnp.full(note.shape, -1, jnp.int32)
    for r in range(2):
        segment, position, _, live = segment_of(starts, r, slot_row)
        names = [classes[r, j] + (CLASSES - 1 - classes[r, j]) * nulls[r, j] for j in range(SEGS)]
        name = jnp.where(segment == 0, names[0], jnp.where(segment == 1, names[1], names[2]))
        opens = jnp.logical_and(position == 0, live)
        note[r : r + 1, :SLOTS] = jnp.where(opens, VOCAB + name, codes[r : r + 1, :])
        chosen = picks[r : r + 1, :]
        ids = lax.broadcasted_iota(jnp.int32, (SLOTS, PICKS), 0)
        label_col = column(labels[r : r + 1, :], SLOTS)
        note[2 + r : 3 + r, :PICKS] = jnp.sum(
            jnp.where(ids == chosen, label_col, 0), axis=0, keepdims=True
        )
        note[4 + r : 5 + r, :PICKS] = segment_of(starts, r, chosen)[2].astype(jnp.int32)
    info[dp] = note[...]
    for one, part in zip(fetch, parts):
        one.wait()
        value = exact[part, :].astype(BF16)
        table[part, :] = value
        pl.when(jnp.logical_and(home, z < 2))(lambda part=part, value=value: place_own(part, value))
    pl.when(classes_of[4][0])(
        lambda: place_own(pl.ds(0, 11 * 48), exact[pl.ds(0, 11 * 48), :].astype(BF16))
    )
    count = 8 + jnp.logical_or(sec == 0, sec == 2).astype(jnp.int32)
    pl.semaphore_wait(barrier, count + 7 * holds_gain.astype(jnp.int32))
    for k in range(1, 8):
        pltpu.make_async_remote_copy(
            src_ref=note,
            dst_ref=info.at[dp],
            send_sem=note_send,
            recv_sem=note_recv,
            device_id=(sec, lax.rem(dp + k, 8)),
            device_id_type=MESH,
        ).start()
    noted = pltpu.make_async_remote_copy(
        src_ref=info.at[pl.ds(0, 7)],
        dst_ref=info.at[pl.ds(0, 7)],
        send_sem=note_send,
        recv_sem=note_recv,
        device_id=targets["core"],
        device_id_type=MESH,
    )

    gain_rows = table.at[pl.ds(VOCAB % (OWN), 16)]

    def gain_to(s, e):
        return pltpu.make_async_remote_copy(
            src_ref=gain_rows,
            dst_ref=gain,
            send_sem=gain_send,
            recv_sem=gain_recv,
            device_id=(s, e),
            device_id_type=MESH,
        )

    def send_gain():
        for e in range(8):
            gain_to(2, e).start()
            if e != gain_dp:
                gain_to(3, e).start()
        gain[...] = gain_rows[...]

    pl.when(holds_gain)(send_gain)

    def copy(k, hop, offset, rows, recv, slot):
        part = out.at[pl.ds(pl.multiple_of(class_base(k, c) + offset, 16), rows)]
        return pltpu.make_async_remote_copy(
            src_ref=part,
            dst_ref=part,
            send_sem=send_sem.at[k, HOPS.index(hop), slot],
            recv_sem=recv,
            device_id=targets[hop],
            device_id_type=MESH,
        )

    def piece(k, j, small):
        source, sends, _, _ = classes_of[k]
        recv = recv_c.at[j] if k == 4 else recv_sem.at[k, j]
        slot = lax.rem(j, WINDOW)
        rows = SMALL_ROWS if small else ROWS[k]
        offset = ROWS[k] * LARGE[k] + rows * (j - LARGE[k]) if small else rows * j

        def send(hop):
            to = core_sem.at[k] if hop == "core" else recv
            before = j >= WINDOW if hop == "core" else jnp.logical_and(j >= WINDOW, sends[hop](j - WINDOW))
            if small:
                was_large = j < LARGE[k] + WINDOW
                wide_one = copy(k, hop, 0, ROWS[k], to, slot)
                pl.when(jnp.logical_and(before, was_large))(wide_one.wait_send)
                before = jnp.logical_and(before, jnp.logical_not(was_large))
            one = copy(k, hop, offset, rows, to, slot)
            pl.when(before)(one.wait_send)
            one.start()

        pl.when(jnp.logical_not(source))(copy(k, "x", offset, rows, recv, slot).wait_recv)
        for hop in HOPS[:3]:
            pl.when(sends[hop](j))(lambda hop=hop: send(hop))
        send("core")

    first = sec == 0
    second = sec == 2

    def slot(k):
        return pl.ds(pl.multiple_of(k * SP, 16), SP)

    def order(i):
        low = (z <= 1).astype(jnp.int32)
        return low * (3 - i) + (1 - low) * i

    def swap(k):
        return pltpu.make_async_remote_copy(
            src_ref=sent.at[slot(k)],
            dst_ref=rx_core.at[slot(k)],
            send_sem=swap_send,
            recv_sem=swap_recv.at[k],
            device_id=targets["core"],
            device_id_type=MESH,
        )

    def cross(zz):
        return pltpu.make_async_remote_copy(
            src_ref=mine.at[slot(4 + zz)],
            dst_ref=mine.at[slot(zz)],
            send_sem=x_send,
            recv_sem=x_recv.at[zz],
            device_id=(2, dp),
            device_id_type=MESH,
        )

    def piece_of(k, q):
        start, size = PIECES[q]
        return pl.ds(pl.multiple_of(k * SP + start, 16), size)

    def go(zz, q, ref, recv, hop):
        return pltpu.make_async_remote_copy(
            src_ref=mine.at[piece_of(zz, q)],
            dst_ref=ref.at[piece_of(zz, q)],
            send_sem=line_send,
            recv_sem=recv.at[zz, q],
            device_id=targets[hop],
            device_id_type=MESH,
        )

    def go_up(zz, q):
        return go(zz, q, rx_down, down_recv, "up")

    def go_down(zz, q):
        return go(zz, q, rx_up, up_recv, "down")

    def add(there, ref):
        mine[there, :] = (mine[there, :].astype(F32) + ref[there, :].astype(F32)).astype(BF16)

    def look(row):
        local = column(info[row // 2, pl.ds(lax.rem(row, 2), 1), :][:, :SP], SP) - dp * OWN
        ids = lax.broadcasted_iota(jnp.int32, (SP, OWN), 1)
        onehot = jnp.where(ids == local, 1.0, 0.0).astype(BF16)
        return (nn(onehot, table[...]) * math.sqrt(D)).astype(BF16)

    def lookup(b):
        zz = order(b // 2)
        p = 1 - lax.rem(b, 2)
        k = 4 * p + zz
        sent[slot(k), :] = look(2 * (2 * zz + 1 - c) + p)
        swap(k).start()
        mine[slot(k), :] = look(2 * (2 * zz + c) + p)
        swap(k).wait_recv()
        add(slot(k), rx_core)
        pl.when(p == 1)(lambda: cross(zz).start())

    def chain(zz, q):
        def from_below():
            go_up(zz, q).wait_recv()
            add(piece_of(zz, q), rx_down)

        def from_above():
            go_down(zz, q).wait_recv()
            add(piece_of(zz, q), rx_up)

        if q == 0:
            pl.when(second)(cross(zz).wait_recv)
        pl.when(jnp.logical_and(zz >= z, z > 0))(from_below)
        pl.when(jnp.logical_and(zz <= z, z < 3))(from_above)
        pl.when(zz > z)(lambda: go_up(zz, q).start())
        pl.when(zz < z)(lambda: go_down(zz, q).start())

    def chains(i):
        for o in range(4):
            zz = order(o)
            hops = jnp.maximum(
                z * (zz >= z).astype(jnp.int32), (3 - z) * (zz <= z).astype(jnp.int32)
            )
            for q in range(5):
                now = i == 2 * o + 2 + sec + HOP * hops + q
                pl.when(now)(lambda zz=zz, q=q: chain(zz, q))

    segment, position, _, _ = segment_of(starts, par, lax.broadcasted_iota(jnp.int32, (SP, 128), 0))
    angles = position.astype(F32) * frequency[...]
    lanes = lax.broadcasted_iota(jnp.int32, (SP, 128), 1)
    cosine[...] = jnp.cos(angles)
    sine[...] = jnp.where(lax.rem(lanes, 64) < 32, -1.0, 1.0) * jnp.sin(angles)
    noted.wait_recv()

    def step(i, carry):
        for k in range(5):
            j = i - LAG * classes_of[k][3]
            now = jnp.logical_and(j >= 0, j < LARGE[k])
            if k == 4:
                now = jnp.logical_and(now, c == 0)
            pl.when(now)(lambda k=k, j=j: piece(k, j, False))
            if k < 4:
                now = jnp.logical_and(j >= LARGE[k], j < LARGE[k] + SMALL)
                pl.when(now)(lambda k=k, j=j: piece(k, j, True))
        pl.when(jnp.logical_and(first, i < 8))(lambda: lookup(i))
        pl.when(jnp.logical_or(first, second))(lambda: chains(i))
        pl.when(jnp.logical_and(second, i == last_step))(lambda: last().start())
        return carry

    last_step = 6 + 2 + 2 + 3 * HOP + 4 + 1

    def last():
        return pltpu.make_async_remote_copy(
            src_ref=mine.at[slot(z)],
            dst_ref=x0,
            send_sem=last_send,
            recv_sem=last_recv,
            device_id=(1, dp),
            device_id_type=MESH,
        )

    lax.fori_loop(0, max(LARGE[0] + SMALL + 5 * LAG, last_step + 1), step, 0)

    def blocks(count, sem):
        return pltpu.make_async_remote_copy(
            src_ref=mine.at[pl.ds(0, count * SP)],
            dst_ref=mine.at[pl.ds(0, count * SP)],
            send_sem=sem,
            recv_sem=sem,
            device_id=targets["core"],
            device_id_type=MESH,
        )

    def end_first():
        blocks(8, swap_send).wait_send()
        blocks(4, x_send).wait_send()
        blocks(3, line_send).wait_send()
        x0[...] = mine[slot(z), :]

    def end_second():
        blocks(3, line_send).wait_send()
        last().wait_send()

    def none():
        x0[...] = jnp.zeros_like(x0)

    pl.when(first)(end_first)
    pl.when(second)(end_second)
    pl.when(sec == 1)(last().wait_recv)
    pl.when(sec >= 2)(none)

    noted.wait_send()

    def gain_sent():
        for e in range(15):
            gain_to(2, 0).wait_send()

    pl.when(holds_gain)(gain_sent)
    pl.when(jnp.logical_and(sec >= 2, jnp.logical_not(holds_gain)))(gain_to(2, dp).wait_recv)

    def drain(k):
        count, rows = (LARGE[4], ROWS[4]) if k == 4 else (LARGE[k] + SMALL, SMALL_ROWS)
        _, sends, _, _ = classes_of[k]
        for j in range(count - WINDOW, count):
            for hop in HOPS[:3]:
                one = copy(k, hop, 0, rows, core_sem.at[k], j % WINDOW)
                pl.when(sends[hop](j))(one.wait_send)
            copy(k, "core", 0, rows, core_sem.at[k], j % WINDOW).wait_send()
        if k == 0:
            for j in range(TURN - WINDOW, TURN):
                one = copy(k, "x", 0, ROWS[0], core_sem.at[k], j % WINDOW)
                last_one = jnp.logical_not(sends["x"](j + WINDOW))
                pl.when(jnp.logical_and(sends["x"](j), last_one))(one.wait_send)

    def came(k):
        count, rows = COUNT[k], ROWS[k]
        part = out.at[pl.ds(pl.multiple_of(class_base(k, 1 - c), 16), count * rows)]
        pltpu.make_async_remote_copy(
            src_ref=part,
            dst_ref=part,
            send_sem=send_sem.at[k, 3, 0],
            recv_sem=core_sem.at[k],
            device_id=targets["core"],
            device_id_type=MESH,
        ).wait_recv()

    for k in range(4):
        drain(k)
        came(k)
    pl.when(c == 0)(lambda: drain(4))
    pl.when(c == 1)(lambda: came(4))


def gather_and_embed(master, codes, labels, picks, starts, classes, nulls, frequency):
    rows = lambda n: pltpu.VMEM((n * SP, D), BF16)
    return pl.pallas_call(
        open_kernel,
        out_shape=(
            jax.ShapeDtypeStruct((WROWS, D), BF16),
            jax.ShapeDtypeStruct((SP, D), BF16),
            jax.ShapeDtypeStruct((8, 8, 384), jnp.int32),
            jax.ShapeDtypeStruct((16, D), BF16),
            jax.ShapeDtypeStruct((SP, 128), F32),
            jax.ShapeDtypeStruct((SP, 128), F32),
            jax.ShapeDtypeStruct((OWN, D), BF16),
        ),
        in_specs=[ANY] + [VMEM] * 3 + [SMEM] * 3 + [VMEM],
        out_specs=(VMEM,) * 7,
        scratch_shapes=[
            pltpu.VMEM((OWN, D), F32),
            pltpu.SemaphoreType.DMA((4,)),
            pltpu.SemaphoreType.DMA((4, 20)),
            pltpu.SemaphoreType.DMA((11,)),
            pltpu.SemaphoreType.DMA((5,)),
            pltpu.SemaphoreType.DMA((5, 4, WINDOW)),
            rows(8),
            rows(8),
            rows(8),
            rows(4),
            rows(4),
            pltpu.SemaphoreType.DMA,
            pltpu.SemaphoreType.DMA((8,)),
            pltpu.SemaphoreType.DMA,
            pltpu.SemaphoreType.DMA((4,)),
            pltpu.SemaphoreType.DMA,
            pltpu.SemaphoreType.DMA((4, 5)),
            pltpu.SemaphoreType.DMA((4, 5)),
            pltpu.SemaphoreType.DMA,
            pltpu.SemaphoreType.DMA,
            pltpu.VMEM((8, 384), jnp.int32),
        ]
        + [pltpu.SemaphoreType.DMA] * 4,
        compiler_params=pltpu.CompilerParams(
            collective_id=0, has_side_effects=True, vmem_limit_bytes=56 * 2**20
        ),
        name="gather_and_embed",
    )(master, codes, labels, picks, starts, classes, nulls, frequency)


def close_kernel(
    left_any, right_any, tail, start, block, index, out, squares, left, right, loc, sent, rx_core,
    rx_up, rx_down, rx_x, summed, ring, all_dx, load_sem, core_sem, recv_sem, recv_c, core_send,
    send_sem, ring_sem, dx_own, dx_send, line_recv, cross_recv, turn_recv, dx_core_send,
    dx_core_recv, ready,
):
    sec, dp, z, c, par, home = place()
    targets = hop_targets(sec, dp, c, par)
    classes = tree(z, c, home)
    loads = [
        pltpu.make_async_copy(left_any, left, load_sem.at[0]),
        pltpu.make_async_copy(right_any, right, load_sem.at[1]),
    ]
    for one in loads:
        one.start()
    del start
    greet_neighbours(sec, dp, z, c, par, ((1, 2), (0, 2)))
    pl.when(sec == 0)(
        lambda: pl.semaphore_signal(ready, 1, device_id=(2, dp), device_id_type=MESH)
    )
    for one in loads:
        one.wait()

    def place_of(hop, k, j):
        offset = j * ROWS[k]
        if hop == "down":
            base = (0, 0, 0, SPLIT, OWN)[k]
        elif hop == "up":
            base = (0, SPLIT, OWN, OWN, OWN + SPLIT)[k]
        else:
            base = HELD[k]
        return pl.ds(pl.multiple_of(base + offset, 16), ROWS[k])

    def gradient(first_row, size):
        first_row = jnp.int32(first_row)
        bounds = (D, 2 * D, 3 * D, 4 * D, 4 * D + 2 * FF)
        matrix = functools.reduce(
            jnp.add, [(first_row >= bound).astype(jnp.int32) for bound in bounds]
        )
        cols = pl.ds(pl.multiple_of(first_row, 128), size)
        return tn(left[:, cols], right[matrix]).astype(BF16)

    def core_copy(k, offset, rows, sem):
        part = pl.ds(pl.multiple_of(HELD[k] + offset, 16), rows)
        return pltpu.make_async_remote_copy(
            src_ref=sent.at[part],
            dst_ref=rx_core.at[part],
            send_sem=core_send,
            recv_sem=sem,
            device_id=targets["core"],
            device_id_type=MESH,
        )

    def form(k, t):
        there = pl.ds(pl.multiple_of(HELD[k] + 128 * t, 128), 128)
        sent[there, :] = gradient(class_base(k, 1 - c) + 128 * t, 128)
        core_copy(k, 128 * t, 128, core_sem.at[k, t]).start()
        loc[there, :] = gradient(class_base(k, c) + 128 * t, 128)

    last_rows = 11 * 48

    def form_last(into):
        for t in range(4):
            into[pl.ds(HELD[4] + 128 * t, 128), :] = gradient(4 * OWN + 128 * t, 128)
        into[pl.ds(HELD[4] + 512, 16), :] = tail[...]

    def form_for_other():
        form_last(sent)
        core_copy(4, 0, last_rows, core_sem.at[4, 0]).start()

    squares[...] = jnp.zeros_like(squares)

    def count_squares(value):
        folded = value * value
        size = folded.shape[0]
        while size > 8 and size % 16 == 0:
            size //= 2
            folded = folded[:size] + folded[size:]
        for part in range(size // 8):
            for n in range(D // 128):
                squares[...] += folded[part * 8 : (part + 1) * 8, n * 128 : (n + 1) * 128]

    rx = dict(up=rx_up, down=rx_down, x=rx_x)

    def onward(k, hop, j):
        back = dict(up="down", down="up", x="x")[hop]
        return landing(k, back, hop, j)

    def landing(k, back, hop, j):
        index = ("up", "down", "x").index(back)
        part = pl.ds(pl.multiple_of(HELD[k] + j * ROWS[k], 16), ROWS[k])
        return pltpu.make_async_remote_copy(
            src_ref=loc.at[part],
            dst_ref=rx[back].at[place_of(back, k, j)],
            send_sem=send_sem.at[k],
            recv_sem=recv_c.at[index, j] if k == 4 else recv_sem.at[index, k, j],
            device_id=targets[hop],
            device_id_type=MESH,
        )

    def gathered(k, j):
        part = pl.ds(pl.multiple_of(HELD[k] + j * ROWS[k], 16), ROWS[k])
        if k == 4:
            pl.when(j == 0)(lambda: core_copy(4, 0, last_rows, core_sem.at[4, 0]).wait_recv())
        else:
            pl.when(lax.rem(j, 2) == 0)(
                lambda: core_copy(k, 64 * j, 128, core_sem.at[k, j // 2]).wait_recv()
            )
        acc = summed.at[pl.ds(0, ROWS[k])]
        acc[...] = loc[part, :].astype(F32) + rx_core[part, :].astype(F32)
        for hop in HOPS[:3]:
            if (hop, k) in (("down", 0), ("down", 1)):
                continue

            def add(hop=hop):
                landing(k, hop, hop, j).wait_recv()
                acc[...] += rx[hop][place_of(hop, k, j), :].astype(F32)

            pl.when(classes[k][1][hop](j))(add)
        return part, acc

    def relay(k, j):
        part, acc = gathered(k, j)
        loc[part, :] = acc[...].astype(BF16)
        for hop in HOPS[:3]:
            pl.when(classes[k][2][hop](j))(lambda hop=hop: onward(k, hop, j).start())

    def write(slot, rows, offset):
        return pltpu.make_async_copy(
            ring.at[pl.ds(pl.multiple_of(slot * 64, 64), rows)],
            out.at[pl.ds(pl.multiple_of(offset, 16), rows)],
            ring_sem.at[slot],
        )

    def finish(k, j):
        _, acc = gathered(k, j)
        slot = 4 * (k % 2) + lax.rem(j, 4)
        copy = write(slot, ROWS[k], SPLIT * (k % 2) + j * ROWS[k])
        pl.when(j >= 4)(copy.wait)
        value = acc[...]
        ring[pl.ds(pl.multiple_of(slot * 64, 64), ROWS[k]), :] = value
        copy.start()
        count_squares(value)

    first = sec == 0
    second = sec == 2
    in_line = jnp.logical_or(first, second)
    p_line = second.astype(jnp.int32)
    both = jnp.logical_and

    def dx_part(p, zz):
        return all_dx.at[pl.ds(pl.multiple_of((2 * (2 * zz + c) + p) * SP, 16), SP)]

    def move(p, zz, send, recv, target):
        return pltpu.make_async_remote_copy(
            src_ref=dx_part(p, zz),
            dst_ref=dx_part(p, zz),
            send_sem=send,
            recv_sem=recv,
            device_id=target,
            device_id_type=MESH,
        )

    def line(zz, hop):
        return move(p_line, zz, dx_send, line_recv.at[zz], targets[hop])

    def cross(zz):
        return move(1, zz, dx_send, cross_recv.at[zz], (0, dp))

    def dx_to_core(p, zz):
        return move(p, zz, dx_core_send, dx_core_recv, targets["core"])

    def aside(zz):
        pl.when(first)(lambda: dx_to_core(0, zz).start())
        pl.when(second)(lambda: cross(zz).start())

    def crossed(zz):
        cross(zz).wait_recv()
        dx_to_core(1, zz).start()

    def blocks(count, send, recv):
        return pltpu.make_async_remote_copy(
            src_ref=all_dx.at[pl.ds(0, count * SP)],
            dst_ref=all_dx.at[pl.ds(0, count * SP)],
            send_sem=send,
            recv_sem=recv,
            device_id=targets["core"],
            device_id_type=MESH,
        )

    turned = pltpu.make_async_remote_copy(
        src_ref=block,
        dst_ref=dx_part(1, z),
        send_sem=dx_send,
        recv_sem=turn_recv,
        device_id=(2, dp),
        device_id_type=MESH,
    )
    pl.when(sec == 1)(turned.start)

    def pass_own():
        pl.when(z < 3)(lambda: line(z, "up").start())
        pl.when(z > 0)(lambda: line(z, "down").start())
        aside(z)

    def own_first():
        own = pltpu.make_async_copy(block, dx_part(0, z), dx_own)
        own.start()
        own.wait()
        pass_own()

    def own_second():
        turned.wait_recv()
        pl.semaphore_wait(ready, 1)
        pass_own()

    pl.when(first)(own_first)

    def from_below(k):
        line(z - k, "up").wait_recv()
        pl.when(z < 3)(lambda: line(z - k, "up").start())
        aside(z - k)

    def from_above(k):
        line(z + k, "down").wait_recv()
        pl.when(z > 0)(lambda: line(z + k, "down").start())
        aside(z + k)

    def tile(t):
        ids = lax.broadcasted_iota(jnp.int32, (SP, 16 * SP), 0) + t * SP
        onehot = jnp.where(ids == index[...], 1.0, 0.0).astype(BF16)
        value = nn(onehot, all_dx[...]) * math.sqrt(D)
        slot = lax.rem(t, 2)
        copy = write_tile(slot, t)
        pl.when(t >= 2)(copy.wait)
        ring[pl.ds(pl.multiple_of(slot * SP, 16), SP), :] = value
        copy.start()
        count_squares(value)

    def write_tile(slot, t):
        return pltpu.make_async_copy(
            ring.at[pl.ds(pl.multiple_of(slot * SP, 16), SP)],
            out.at[pl.ds(pl.multiple_of(t * SP, 16), SP)],
            ring_sem.at[slot],
        )

    def collect(i):
        pl.when(both(second, i == CHOP + AHEAD))(own_second)
        for k in range(1, 4):
            now = i == CHOP * (k + p_line) + AHEAD * p_line
            pl.when(both(now, z >= k))(lambda k=k: from_below(k))
            pl.when(both(now, z + k <= 3))(lambda k=k: from_above(k))

    begin = 5 * CHOP + 1

    def embed(i):
        pl.when(i == 2 * CHOP)(lambda: crossed(z))
        for k in range(1, 4):
            pl.when(both(i == CHOP * (k + 2), z >= k))(lambda k=k: crossed(z - k))
            pl.when(both(i == CHOP * (k + 2), z + k <= 3))(lambda k=k: crossed(z + k))
        pl.when(i == begin)(lambda: blocks(8, dx_core_send, dx_core_recv).wait_recv())
        t = i - begin
        pl.when(both(t >= 0, t < OWN // SP))(lambda: tile(t))

    def step(i, carry):
        for k in range(4):
            turn_now = both(lax.rem(i, 2) == k // 2, i < COUNT[k] + k // 2)
            pl.when(turn_now)(lambda k=k: form(k, i // 2))
        pl.when(both(i == CWAIT - 1, c == 0))(lambda: form_last(loc))
        pl.when(both(i == CWAIT - 1, c == 1))(form_for_other)
        for k in range(5):
            source, _, _, depth = classes[k]
            j = i - CLAG * ((5, 5, 4, 4, 3)[k] - depth) - (0, 0, 1, 1, CWAIT)[k]
            now = both(j >= 0, j < COUNT[k])
            if k == 4:
                now = both(now, c == 0)
            pl.when(both(now, jnp.logical_not(source)))(lambda k=k, j=j: relay(k, j))
            pl.when(both(now, source))(lambda k=k, j=j: finish(k, j))
        pl.when(in_line)(lambda: collect(i))
        pl.when(first)(lambda: embed(i))
        return carry

    lax.fori_loop(0, max(18 + 5 * CLAG, begin + OWN // SP), step, 0)
    pl.when(first)(lambda: blocks(8, dx_core_send, dx_core_recv).wait_send())

    def dx_sent(count):
        blocks(count, dx_send, dx_core_recv).wait_send()

    middle = both(z >= 1, z <= 2)
    ends = jnp.logical_not(middle)
    pl.when(jnp.logical_or(sec == 1, both(first, ends)))(lambda: dx_sent(1))
    pl.when(both(first, middle))(lambda: dx_sent(5))
    pl.when(both(second, ends))(lambda: dx_sent(5))
    pl.when(both(second, middle))(lambda: dx_sent(9))
    def sent_core(rows):
        part = pl.ds(0, rows)
        pltpu.make_async_remote_copy(
            src_ref=sent.at[part],
            dst_ref=rx_core.at[part],
            send_sem=core_send,
            recv_sem=core_sem.at[4, 0],
            device_id=targets["core"],
            device_id_type=MESH,
        ).wait_send()

    pl.when(c == 0)(lambda: sent_core(2 * OWN))
    pl.when(c == 1)(lambda: sent_core(LANE))
    for k in range(5):
        part = pl.ds(HELD[k], COUNT[k] * ROWS[k])
        gone = pltpu.make_async_remote_copy(
            src_ref=loc.at[part],
            dst_ref=rx_x.at[part],
            send_sem=send_sem.at[k],
            recv_sem=core_sem.at[4, 0],
            device_id=targets["x"],
            device_id_type=MESH,
        )
        away = jnp.logical_not(classes[k][0])
        pl.when(both(away, c == 0) if k == 4 else away)(gone.wait_send)

    def drain_half(k):
        for j in range(COUNT[k] - 4, COUNT[k]):
            write(4 * (k % 2) + j % 4, ROWS[k], 0).wait()

    def drain_tiles():
        for slot in range(2):
            write_tile(slot, 0).wait()

    for k in range(5):
        pl.when(classes[k][0])(lambda k=k: drain_half(k))
    pl.when(first)(drain_tiles)


def reduce_and_scatter(left, right, tail, start, block, index):
    low = lambda *shape: pltpu.VMEM(shape, BF16)
    dma = pltpu.SemaphoreType.DMA
    return pl.pallas_call(
        close_kernel,
        out_shape=(
            jax.ShapeDtypeStruct((OWN, D), F32),
            jax.ShapeDtypeStruct((8, 128), F32),
        ),
        in_specs=[ANY, ANY, VMEM, ANY, VMEM, VMEM],
        out_specs=(ANY, VMEM),
        input_output_aliases={3: 0},
        scratch_shapes=[
            low(SP, MATS),
            low(6, SP, D),
            low(LANE, D),
            low(LANE, D),
            low(LANE, D),
            low(OWN + SPLIT + 11 * 48, D),
            low(OWN + 11 * 48, D),
            low(LANE, D),
            pltpu.VMEM((64, D), F32),
            pltpu.VMEM((2 * SP, D), F32),
            low(16 * SP, D),
            dma((2,)),
            dma((5, 9)),
            dma((3, 4, 18)),
            dma((3, 11)),
            dma,
            dma((5,)),
            dma((8,)),
            dma,
            dma,
            dma((4,)),
            dma((4,)),
            dma,
            dma,
            dma,
            pltpu.SemaphoreType.REGULAR,
        ],
        compiler_params=pltpu.CompilerParams(
            collective_id=1, has_side_effects=True, vmem_limit_bytes=63 * 2**20
        ),
        name="reduce_and_scatter",
    )(left, right, tail, start, block, index)


def norm_kernel(n_sec, n_dp, small, squares, out, block, every, send_sem, recv_sem):
    sec = lax.axis_index("section")
    dp = lax.axis_index("dp")
    n = n_sec * n_dp
    me = sec * n_dp + dp
    barrier = pltpu.get_barrier_semaphore()

    def peer(k):
        other = lax.rem(me + k, n)
        return (other // n_dp, lax.rem(other, n_dp))

    def greet(k, carry):
        pl.semaphore_signal(barrier, 1, device_id=peer(k), device_id_type=MESH)
        return carry

    lax.fori_loop(1, n, greet, 0)
    block[...] = small[...]
    block[7:8, :] += jnp.sum(squares[...], axis=0, keepdims=True)
    every[me] = block[...]
    pl.semaphore_wait(barrier, n - 1)

    def send(k, carry):
        pltpu.make_async_remote_copy(
            src_ref=block,
            dst_ref=every.at[me],
            send_sem=send_sem,
            recv_sem=recv_sem,
            device_id=peer(k),
            device_id_type=MESH,
        ).start()
        return carry

    lax.fori_loop(1, n, send, 0)
    others = pltpu.make_async_remote_copy(
        src_ref=every.at[pl.ds(0, n - 1)],
        dst_ref=every.at[pl.ds(0, n - 1)],
        send_sem=send_sem,
        recv_sem=recv_sem,
        device_id=peer(1),
        device_id_type=MESH,
    )
    others.wait_recv()
    total = every[0]
    for k in range(1, n):
        total = total + every[k]
    gains = jnp.sum(total[0:6] * total[0:6], axis=0, keepdims=True)
    norm = jnp.sqrt(jnp.sum(gains + total[7:8], axis=1, keepdims=True))
    out[0:8, :] = total
    out[8:16, :] = jnp.broadcast_to(norm, (8, 128))
    others.wait_send()


def share_norm(small, squares, n_sec, n_dp):
    return pl.pallas_call(
        functools.partial(norm_kernel, n_sec, n_dp),
        out_shape=jax.ShapeDtypeStruct((16, 128), F32),
        in_specs=[VMEM, VMEM],
        out_specs=VMEM,
        scratch_shapes=[
            pltpu.VMEM((8, 128), F32),
            pltpu.VMEM((n_sec * n_dp, 8, 128), F32),
            pltpu.SemaphoreType.DMA,
            pltpu.SemaphoreType.DMA,
        ],
        compiler_params=pltpu.CompilerParams(collective_id=8, has_side_effects=True),
        name="share_norm",
    )(small, squares)


NEG = -1e30
FT = 256


def turn(block, cosine, sine, lanes):
    ahead = pltpu.roll(block, 96, 1)
    behind = pltpu.roll(block, 32, 1)
    return block * cosine + jnp.where(lax.rem(lanes, 64) < 32, ahead, behind) * sine


def see(starts):
    par = lax.rem(lax.axis_index("section"), 2)
    rows = lax.broadcasted_iota(jnp.int32, (SP, SP), 0)
    cols = lax.broadcasted_iota(jnp.int32, (SP, SP), 1)
    same = segment_of(starts, par, rows)[0] == segment_of(starts, par, cols)[0]
    allowed = jnp.logical_and(same, cols <= rows)
    return jnp.where(allowed, 0.0, NEG)


def hide(starts):
    par = lax.rem(lax.axis_index("section"), 2)
    rows = lax.broadcasted_iota(jnp.int32, (SP, SP), 0)
    cols = lax.broadcasted_iota(jnp.int32, (SP, SP), 1)
    same = segment_of(starts, par, rows)[0] == segment_of(starts, par, cols)[0]
    return jnp.where(jnp.logical_and(same, rows <= cols), 0.0, NEG)


def softmax_of(scores, unseen):
    masked = scores + unseen
    grown = jnp.exp(masked - jnp.max(masked, axis=-1, keepdims=True))
    return grown / jnp.sum(grown, axis=-1, keepdims=True)


def weight_copies(w_any, w, sems):
    bounds = (0, 3 * D, 4 * D, 4 * D + FF, 4 * D + 2 * FF, MATS, WROWS)
    return [
        pltpu.make_async_copy(
            w_any.at[pl.ds(lo, hi - lo)], w.at[pl.ds(lo, hi - lo)], sems.at[i]
        )
        for i, (lo, hi) in enumerate(zip(bounds[:-1], bounds[1:]))
    ]


def forward_kernel(keep, x, w_any, cosine, sine, starts, y, *refs):
    kept = refs[:7] if keep else ()
    q, k, v, o, h, gate, up, w, m, unseen, sems, keep_sems, *hop_sems = refs[len(kept) :]
    sec = lax.axis_index("section")
    dp = lax.axis_index("dp")
    lower = sec < 2
    if not keep:
        barrier = pltpu.get_barrier_semaphore()
        pl.when(jnp.logical_not(lower))(
            lambda: pl.semaphore_signal(barrier, 1, device_id=(sec - 2, dp), device_id_type=MESH)
        )

    def hop(b):
        part = y.at[:, pl.ds(b * 256, 256)]
        return pltpu.make_async_remote_copy(
            src_ref=part,
            dst_ref=part,
            send_sem=hop_sems[0].at[b],
            recv_sem=hop_sems[1].at[b],
            device_id=(sec + 2, dp),
            device_id_type=MESH,
        )

    def put(i):
        if keep:
            pltpu.make_async_copy((q, k, v, o, h, gate, up)[i], kept[i], keep_sems.at[i]).start()

    def run():
        copies = weight_copies(w_any, w, sems)
        for i in (5, 0, 1, 2, 3, 4):
            copies[i].start()
        unseen[...] = see(starts)
        lanes = lax.broadcasted_iota(jnp.int32, (SP, 128), 1)
        first = lanes < 64
        copies[5].wait()
        gains = w[pl.ds(MATS, 16), :].astype(F32)
        stream = x[...].astype(F32)
        a1 = rms_scale(stream, gains[0:1]).astype(BF16)
        copies[0].wait()

        def project(b, carry):
            cols = pl.ds(pl.multiple_of(b * 256, 256), 256)
            raw_q = nn(a1, w[pl.ds(0, D), cols])
            raw_k = nn(a1, w[pl.ds(D, D), cols])
            raw_v = nn(a1, w[pl.ds(2 * D, D), cols])
            v[:, cols] = raw_v.astype(BF16)
            for part in range(2):
                there = pl.ds(pl.multiple_of(b * 256 + part * 128, 128), 128)
                here = slice(part * 128, (part + 1) * 128)
                turned_q = turn(raw_q[:, here], cosine[...], sine[...], lanes)
                q[:, there] = (turned_q * HD ** (-0.5)).astype(BF16)
                k[:, there] = turn(raw_k[:, here], cosine[...], sine[...], lanes).astype(BF16)
            return carry

        lax.fori_loop(0, D // 256, project, 0, unroll=True)
        for i in range(3):
            put(i)

        def attend(b, carry):
            cols = pl.ds(pl.multiple_of(b * 128, 128), 128)
            qb, kb, vb = q[:, cols], k[:, cols], v[:, cols]
            zero = jnp.zeros_like(qb)
            p0 = softmax_of(nt(jnp.where(first, qb, zero), kb), unseen[...]).astype(BF16)
            p1 = softmax_of(nt(jnp.where(first, zero, qb), kb), unseen[...]).astype(BF16)
            o[:, cols] = jnp.where(first, nn(p0, vb), nn(p1, vb)).astype(BF16)
            return carry

        lax.fori_loop(0, HEADS // 2, attend, 0, unroll=True)
        put(3)
        copies[1].wait()
        for b in range(3):
            cols = pl.ds(b * 256, 256)
            h[:, cols] = x[:, cols].astype(F32) + nn(o[...], w[pl.ds(3 * D, D), cols])
        put(4)
        a2 = rms_scale(h[...], gains[1:2]).astype(BF16)
        copies[2].wait()
        copies[3].wait()

        def widen(b, carry):
            cols = pl.ds(pl.multiple_of(b * FT, FT), FT)
            g = nt(a2, w[pl.ds(pl.multiple_of(4 * D + b * FT, FT), FT), :])
            u = nt(a2, w[pl.ds(pl.multiple_of(4 * D + FF + b * FT, FT), FT), :])
            gate[:, cols] = g
            up[:, cols] = u
            m[:, cols] = (g / (1.0 + jnp.exp(-g)) * u).astype(BF16)
            return carry

        lax.fori_loop(0, FF // FT, widen, 0, unroll=True)
        put(5)
        put(6)
        copies[4].wait()

        if not keep:
            pl.semaphore_wait(barrier, 1)
        for b in range(3):
            cols = pl.ds(b * 256, 256)
            y[:, cols] = (h[:, cols] + nn(m[...], w[pl.ds(4 * D + 2 * FF, FF), cols])).astype(BF16)
            if not keep:
                hop(b).start()
        for i, part in enumerate(kept):
            pltpu.make_async_copy((q, k, v, o, h, gate, up)[i], part, keep_sems.at[i]).wait()
        if not keep:
            for b in range(3):
                hop(b).wait_send()
            y[...] = x[...]

    if keep:
        run()
        return
    pl.when(lower)(run)

    def arrive():
        for b in range(3):
            hop(b).wait_recv()

    pl.when(jnp.logical_not(lower))(arrive)


KEPT = ((D, BF16), (D, BF16), (D, BF16), (D, BF16), (D, F32), (FF, F32), (FF, F32))


def forward_call(keep, x, weights, cosine, sine, starts):
    low = jax.ShapeDtypeStruct((SP, D), BF16)
    kept = tuple(jax.ShapeDtypeStruct((SP, n), t) for n, t in KEPT) if keep else ()
    return pl.pallas_call(
        functools.partial(forward_kernel, keep),
        out_shape=(low,) + kept,
        in_specs=[VMEM, ANY, VMEM, VMEM, SMEM],
        out_specs=(VMEM,) + (ANY,) * len(kept),
        scratch_shapes=[pltpu.VMEM((SP, n), t) for n, t in KEPT]
        + [
            pltpu.VMEM((WROWS, D), BF16),
            pltpu.VMEM((SP, FF), BF16),
            pltpu.VMEM((SP, SP), F32),
            pltpu.SemaphoreType.DMA((6,)),
            pltpu.SemaphoreType.DMA((7,)),
        ]
        + ([] if keep else [pltpu.SemaphoreType.DMA((3,))] * 2),
        compiler_params=pltpu.CompilerParams(vmem_limit_bytes=56 * 2**20)
        if keep
        else pltpu.CompilerParams(
            collective_id=6, has_side_effects=True, vmem_limit_bytes=56 * 2**20
        ),
        name="layer_forward_kept" if keep else "layer_forward",
    )(x, weights, cosine, sine, starts)


def rms_back(value_in, gain, grad):
    inv = lax.rsqrt(jnp.mean(value_in * value_in, axis=-1, keepdims=True) + norm_eps)
    unit = value_in * inv
    scaled = grad * gain
    grad_in = inv * (scaled - unit * jnp.mean(scaled * unit, axis=-1, keepdims=True))
    return grad_in, jnp.sum(grad * unit, axis=0, keepdims=True)


def backward_kernel(send, dy, x, w_any, cosine, sine, starts, *refs):
    kept, refs = refs[:7], refs[7:]
    dx, left, right, tail, refs = *refs[:4], refs[4:]
    q, k, v, o, h, gate, up, w, dgate, dup, m, da, do, dq, dk, dv, a1, a2, db, *refs = refs
    unseen, sems, keep_sems, out_sems, *hop_sems = refs
    sec = lax.axis_index("section")
    dp = lax.axis_index("dp")
    upper = sec >= 2
    if send:
        barrier = pltpu.get_barrier_semaphore()
        pl.when(jnp.logical_not(upper))(
            lambda: pl.semaphore_signal(barrier, 1, device_id=(sec + 2, dp), device_id_type=MESH)
        )

    def hop():
        return pltpu.make_async_remote_copy(
            src_ref=dx,
            dst_ref=dx,
            send_sem=hop_sems[0],
            recv_sem=hop_sems[1],
            device_id=(sec - 2, dp),
            device_id_type=MESH,
        )

    outs = []

    def put(source, target):
        copy = pltpu.make_async_copy(source, target, out_sems.at[len(outs)])
        copy.start()
        outs.append(copy)
    def run():
        copies = weight_copies(w_any, w, sems)
        taken = [
            pltpu.make_async_copy(part, (q, k, v, o, h, gate, up)[i], keep_sems.at[i])
            for i, part in enumerate(kept)
        ]
        for one in (
            copies[4], taken[5], taken[6], copies[5], copies[2], copies[3], taken[4], copies[1],
            taken[0], taken[1], taken[2], copies[0], taken[3],
        ):
            one.start()
        unseen[...] = hide(starts)
        lanes = lax.broadcasted_iota(jnp.int32, (SP, 128), 1)
        first = lanes < 64
        copies[4].wait()
        taken[5].wait()
        taken[6].wait()

        def open_mlp(b, carry):
            cols = pl.ds(pl.multiple_of(b * FT, FT), FT)
            dm = nt(dy[...], w[pl.ds(pl.multiple_of(4 * D + 2 * FF + b * FT, FT), FT), :])
            g = gate[:, cols]
            u = up[:, cols]
            sig = 1.0 / (1.0 + jnp.exp(-g))
            dgate[:, cols] = (dm * u * sig * (1.0 + g * (1.0 - sig))).astype(BF16)
            dup[:, cols] = (dm * g * sig).astype(BF16)
            m[:, cols] = (g * sig * u).astype(BF16)
            return carry

        lax.fori_loop(0, FF // FT, open_mlp, 0, unroll=True)
        for i, part in enumerate((dgate, dup, m)):
            put(part, left.at[:, pl.ds(4 * D + i * FF, FF)])
        put(dy, right.at[5])
        copies[5].wait()
        gains = w[pl.ds(MATS, 16), :].astype(F32)
        copies[2].wait()
        copies[3].wait()

        def close_mlp(b, carry):
            cols = pl.ds(pl.multiple_of(b * 256, 256), 256)
            da[:, cols] = nn(dgate[...], w[pl.ds(4 * D, FF), cols]) + nn(
                dup[...], w[pl.ds(4 * D + FF, FF), cols]
            )
            return carry

        lax.fori_loop(0, 3, close_mlp, 0, unroll=True)
        taken[4].wait()
        dh, dg_mlp = rms_back(h[...], gains[1:2], da[...])
        dh = dh + dy[...].astype(F32)
        db[...] = dh.astype(BF16)
        a2[...] = rms_scale(h[...], gains[1:2]).astype(BF16)
        put(db, right.at[3])
        put(a2, right.at[4])
        copies[1].wait()
        for b in range(3):
            do[:, pl.ds(b * 256, 256)] = nt(db[...], w[pl.ds(3 * D + b * 256, 256), :]).astype(BF16)

        for i in range(3):
            taken[i].wait()

        def attend(b, carry):
            cols = pl.ds(pl.multiple_of(b * 128, 128), 128)
            qb, kb, vb, dob = q[:, cols], k[:, cols], v[:, cols], do[:, cols]
            zero = jnp.zeros_like(qb)
            parts = []
            for head in range(2):
                keep = first if head == 0 else jnp.logical_not(first)
                masked = nt(jnp.where(keep, kb, zero), qb) + unseen[...]
                grown = jnp.exp(masked - jnp.max(masked, axis=0, keepdims=True))
                probs = grown / jnp.sum(grown, axis=0, keepdims=True)
                dprobs = nt(jnp.where(keep, vb, zero), dob)
                along = jnp.sum(probs * dprobs, axis=0, keepdims=True)
                dscores = (probs * (dprobs - along)).astype(BF16)
                parts.append((tn(dscores, kb), nn(dscores, qb), nn(probs.astype(BF16), dob)))
            dqb = jnp.where(first, parts[0][0], parts[1][0]) * HD ** (-0.5)
            dkb = jnp.where(first, parts[0][1], parts[1][1])
            dq[:, cols] = turn(dqb, cosine[...], -sine[...], lanes).astype(BF16)
            dk[:, cols] = turn(dkb, cosine[...], -sine[...], lanes).astype(BF16)
            dv[:, cols] = jnp.where(first, parts[0][2], parts[1][2]).astype(BF16)
            return carry

        lax.fori_loop(0, HEADS // 2, attend, 0, unroll=True)
        for i, part in enumerate((dq, dk, dv)):
            put(part, right.at[i])
        copies[0].wait()
        for b in range(3):
            rows = lambda i, b=b: w[pl.ds(i * D + b * 256, 256), :]
            da[:, pl.ds(b * 256, 256)] = (
                nt(dq[...], rows(0)) + nt(dk[...], rows(1)) + nt(dv[...], rows(2))
            )
        stream = x[...].astype(F32)
        a1[...] = rms_scale(stream, gains[0:1]).astype(BF16)
        for i in range(3):
            put(a1, left.at[:, pl.ds(i * D, D)])
        taken[3].wait()
        put(o, left.at[:, pl.ds(3 * D, D)])
        dstream, dg_attn = rms_back(stream, gains[0:1], da[...])
        dx[...] = (dstream + dh).astype(BF16)
        if send:
            pl.semaphore_wait(barrier, 1)
            hop().start()
        ids = lax.broadcasted_iota(jnp.int32, (16, D), 0)
        tail[...] = jnp.where(ids == 0, dg_attn, jnp.where(ids == 1, dg_mlp, 0.0)).astype(BF16)
        for copy in outs:
            copy.wait()
        if send:
            hop().wait_send()

    if not send:
        run()
        return
    pl.when(upper)(run)
    pl.when(jnp.logical_not(upper))(lambda: hop().wait_recv())


def backward_call(send, dy, x, weights, cosine, sine, starts, kept):
    wide = pltpu.VMEM((SP, FF), BF16)
    narrow = pltpu.VMEM((SP, D), BF16)
    return pl.pallas_call(
        functools.partial(backward_kernel, send),
        out_shape=(
            jax.ShapeDtypeStruct((SP, D), BF16),
            jax.ShapeDtypeStruct((SP, MATS), BF16),
            jax.ShapeDtypeStruct((6, SP, D), BF16),
            jax.ShapeDtypeStruct((16, D), BF16),
        ),
        in_specs=[VMEM, VMEM, ANY, VMEM, VMEM, SMEM] + [ANY] * 7,
        out_specs=(VMEM, ANY, ANY, VMEM),
        scratch_shapes=[pltpu.VMEM((SP, n), t) for n, t in KEPT]
        + [
            pltpu.VMEM((WROWS, D), BF16),
            wide,
            wide,
            wide,
            pltpu.VMEM((SP, D), F32),
        ]
        + [narrow] * 7
        + [
            pltpu.VMEM((SP, SP), F32),
            pltpu.SemaphoreType.DMA((6,)),
            pltpu.SemaphoreType.DMA((7,)),
            pltpu.SemaphoreType.DMA((13,)),
        ]
        + ([pltpu.SemaphoreType.DMA] * 2 if send else []),
        compiler_params=pltpu.CompilerParams(
            collective_id=7, has_side_effects=True, vmem_limit_bytes=60 * 2**20
        )
        if send
        else pltpu.CompilerParams(vmem_limit_bytes=60 * 2**20),
        name="layer_backward_send" if send else "layer_backward",
    )(dy, x, weights, cosine, sine, starts, *kept)


def matrix_gradients(left, right, tail):
    parts = [(0, 0), (D, 1), (2 * D, 2), (3 * D, 3), (4 * D, 4), (4 * D + FF, 4), (4 * D + 2 * FF, 5)]
    ends = [start for start, _ in parts[1:]] + [MATS]
    rows = [
        tn(left[:, start:end], right[i]).astype(BF16) for (start, i), end in zip(parts, ends)
    ]
    return jnp.concatenate(rows + [tail], axis=0)


HEAD_T = 256


def column(row, size):
    there = lax.broadcasted_iota(jnp.int32, (size, size), 0)
    here = lax.broadcasted_iota(jnp.int32, (size, size), 1)
    zero = jnp.zeros((), row.dtype)
    return jnp.sum(jnp.where(there == here, row, zero), axis=1, keepdims=True)


def as_rows(values):
    there = lax.broadcasted_iota(jnp.int32, (128, 128), 0)
    here = lax.broadcasted_iota(jnp.int32, (128, 128), 1)
    return [
        jnp.sum(
            jnp.where(there == here, values[k * 128 : (k + 1) * 128], 0.0), axis=0, keepdims=True
        )
        for k in range(4)
    ]


def head_kernel(
    y, picks, info, gain, table, d_top, d_table, small, mine, picked, af, scores, dlow, labels,
    counts, stat, stats, daf, rx_core, low, rx, fresh, zero_sem, own_sem, pick_send, pick_recv,
    core_send, core_recv, stat_send, stat_recv, swap_send, swap_recv, daf_send, daf_recv,
):
    sec, dp, z, c, par, home = place()
    last = sec == 3
    upper = sec >= 2
    barrier = pltpu.get_barrier_semaphore()
    other_core = (3, dp + 1 - 2 * c)

    def greet(s, e):
        pl.semaphore_signal(barrier, 1, device_id=(s, e), device_id_type=MESH)

    def greet_second():
        for k in range(4):
            greet(3, 2 * k + c)
        pl.semaphore_wait(barrier, 4)

    def greet_third():
        for k in range(4):
            greet(2, 2 * k + c)
        for k in range(1, 8):
            greet(3, lax.rem(dp + k, 8))
        pl.semaphore_wait(barrier, 11)

    all_zero = pltpu.make_async_copy(fresh, d_table, zero_sem)

    def zeros():
        fresh[...] = jnp.zeros_like(fresh)
        all_zero.start()

    pl.when(jnp.logical_not(last))(zeros)
    small[...] = jnp.zeros_like(small)
    pick_row = picks[pl.ds(par, 1), :]
    pick_col = column(pick_row, PICKS)

    def choose():
        ids = lax.broadcasted_iota(jnp.int32, (PICKS, SP), 1)
        mine[...] = nn(jnp.where(ids == pick_col, 1.0, 0.0).astype(BF16), y[...]).astype(BF16)

    pl.when(upper)(choose)
    pl.when(sec == 2)(greet_second)
    pl.when(last)(greet_third)

    def rows(p, zz, lane):
        return pl.ds(pl.multiple_of((2 * (2 * zz + lane) + p) * PICKS, PICKS), PICKS)

    def pick_to(k):
        zz = lax.rem(z + k, 4)
        return pltpu.make_async_remote_copy(
            src_ref=mine,
            dst_ref=picked.at[rows(par, z, c)],
            send_sem=pick_send,
            recv_sem=pick_recv.at[par, z],
            device_id=(3, 2 * zz + c),
            device_id_type=MESH,
        )

    def came(p, k):
        zz = lax.rem(z + k, 4)
        return pltpu.make_async_remote_copy(
            src_ref=mine,
            dst_ref=picked.at[rows(p, zz, c)],
            send_sem=pick_send,
            recv_sem=pick_recv.at[p, zz],
            device_id=other_core,
            device_id_type=MESH,
        )

    def forward(p, k):
        part = picked.at[rows(p, lax.rem(z + k, 4), c)]
        return pltpu.make_async_remote_copy(
            src_ref=part,
            dst_ref=part,
            send_sem=core_send,
            recv_sem=core_recv,
            device_id=other_core,
            device_id_type=MESH,
        )

    def span(ref, count, send, recv):
        part = ref.at[pl.ds(0, count)]
        return pltpu.make_async_remote_copy(
            src_ref=part,
            dst_ref=part,
            send_sem=send,
            recv_sem=recv,
            device_id=other_core,
            device_id_type=MESH,
        )

    def pick_second():
        for k in (1, 2, 3, 0):
            pick_to(k).start()

    def pick_third():
        own = pltpu.make_async_copy(mine, picked.at[rows(1, z, c)], own_sem)
        own.start()
        for k in range(1, 4):
            pick_to(k).start()
        for e in range(8):
            for p in range(2):
                at = pl.ds((2 * e + p) * PICKS, PICKS)
                labels[at, :] = column(info[e, 2 + p : 3 + p, :][:, :PICKS], PICKS)
                counts[at, :] = column(info[e, 4 + p : 5 + p, :][:, :PICKS].astype(F32), PICKS)
        own.wait()
        forward(1, 0).start()
        for k in range(4):
            came(0, k).wait_recv()
            forward(0, k).start()
            if k:
                came(1, k).wait_recv()
                forward(1, k).start()
        span(picked, 8 * PICKS, core_send, core_recv).wait_recv()

    pl.when(sec == 2)(pick_second)
    pl.when(last)(pick_third)
    g_f = gain[...].astype(F32)[0:1]
    own = OWN
    tiles = [(t * HEAD_T, HEAD_T) for t in range(own // HEAD_T)] + [
        (own - own % HEAD_T, own % HEAD_T)
    ]

    def over_tiles(body):
        def step(t, carry):
            body(pl.multiple_of(t * HEAD_T, HEAD_T), HEAD_T)
            return carry

        lax.fori_loop(0, own // HEAD_T, step, 0, unroll=True)
        body(own - own % HEAD_T, own % HEAD_T)

    def forward_part():
        af[...] = rms_scale(picked[...].astype(F32), g_f).astype(BF16)
        fold = lambda op, block: functools.reduce(
            op, [block[:, k * 128 : (k + 1) * 128] for k in range(block.shape[1] // 128)]
        )
        top = daf.at[:, pl.ds(0, 128)]
        top[...] = jnp.full((16 * PICKS, 128), NEG, F32)

        def product(start, size):
            ids = lax.broadcasted_iota(jnp.int32, (16 * PICKS, size), 1) + (dp * own + start)
            block = nt(af[...], table[pl.ds(start, size), :])
            block = jnp.where(ids < VOCAB, block, NEG)
            scores[:, pl.ds(start, size)] = block
            top[...] = jnp.maximum(top[...], fold(jnp.maximum, block))

        over_tiles(product)
        top_col = jnp.max(top[...], axis=1, keepdims=True)
        total = daf.at[:, pl.ds(128, 128)]
        target = daf.at[:, pl.ds(256, 128)]
        total[...] = jnp.zeros((16 * PICKS, 128), F32)
        target[...] = jnp.zeros((16 * PICKS, 128), F32)

        def exponents(start, size):
            ids = lax.broadcasted_iota(jnp.int32, (16 * PICKS, size), 1) + (dp * own + start)
            block = scores[:, pl.ds(start, size)]
            grown = jnp.exp(block - top_col)
            scores[:, pl.ds(start, size)] = grown
            total[...] += fold(jnp.add, grown)
            target[...] += fold(jnp.add, jnp.where(ids == labels[...], block, 0.0))

        over_tiles(exponents)
        stat[...] = jnp.zeros_like(stat)
        columns = (
            top_col,
            jnp.sum(total[...], axis=1, keepdims=True),
            jnp.sum(target[...], axis=1, keepdims=True),
        )
        for k, values in enumerate(columns):
            for i, row in enumerate(as_rows(values)):
                stat[4 * k + i : 4 * k + i + 1, :] = row
        stats[dp] = stat[...]
        for k in range(1, 8):
            pltpu.make_async_remote_copy(
                src_ref=stat,
                dst_ref=stats.at[dp],
                send_sem=stat_send,
                recv_sem=stat_recv,
                device_id=(3, lax.rem(dp + k, 8)),
                device_id_type=MESH,
            ).start()
        every = span(stats, 7, stat_send, stat_recv)
        every.wait_recv()
        tops = [stats[e, 0:4, :] for e in range(8)]
        best = functools.reduce(jnp.maximum, tops)
        sums = sum(stats[e, 4:8, :] * jnp.exp(tops[e] - best) for e in range(8))
        hits = sum(stats[e, 8:12, :] for e in range(8))
        log_total = best + jnp.log(sums)
        log_col = jnp.concatenate([column(log_total[k : k + 1], 128) for k in range(4)], axis=0)
        hit_col = jnp.concatenate([column(hits[k : k + 1], 128) for k in range(4)], axis=0)
        loss = jnp.sum(
            jnp.where(counts[...] > 0, log_col - hit_col, 0.0), axis=0, keepdims=True
        )
        lane = lax.broadcasted_iota(jnp.int32, (1, 128), 1)
        small[6:7, :] = jnp.where(jnp.logical_and(lane == 0, dp == 0), loss, 0.0)
        shrink = jnp.exp(top_col - log_col)

        def slopes(start, size):
            ids = lax.broadcasted_iota(jnp.int32, (16 * PICKS, size), 1) + (dp * own + start)
            hit = jnp.where(ids == labels[...], 1.0, 0.0)
            block = (scores[:, pl.ds(start, size)] * shrink - hit) * counts[...]
            dlow[:, pl.ds(start, size)] = block.astype(BF16)

        over_tiles(slopes)
        for b in range(3):
            cols = pl.ds(b * 256, 256)
            daf[:, cols] = nn(dlow[...], table[:, cols])
        every.wait_send()
        span(picked, 3 * PICKS, pick_send, core_recv).wait_send()
        span(picked, 8 * PICKS, core_send, core_recv).wait_send()

    def swap(p, zz):
        return pltpu.make_async_remote_copy(
            src_ref=daf.at[rows(p, zz, 1 - c)],
            dst_ref=rx_core.at[pl.ds((2 * zz + p) * PICKS, PICKS)],
            send_sem=swap_send,
            recv_sem=swap_recv,
            device_id=other_core,
            device_id_type=MESH,
        )

    def back_to(p, k):
        zz = lax.rem(z + k, 4)
        return pltpu.make_async_remote_copy(
            src_ref=low.at[pl.ds(pl.multiple_of((2 * zz + p) * PICKS, PICKS), PICKS)],
            dst_ref=rx.at[z],
            send_sem=daf_send,
            recv_sem=daf_recv,
            device_id=(2 + p, 2 * zz + c),
            device_id_type=MESH,
        )

    def table_part(start, size):
        there = pl.ds(start, size)
        value = tn(dlow[:, there], af[...])
        fresh[there, :] = value
        pltpu.make_async_copy(fresh.at[there], d_table.at[there], zero_sem).start()
        folded = jnp.sum(value * value, axis=0, keepdims=True)
        small[7:8, :] += functools.reduce(
            jnp.add, [folded[:, k * 128 : (k + 1) * 128] for k in range(6)]
        )

    def third():
        forward_part()
        for zz in range(4):
            for p in range(2):
                swap(p, zz).start()
        table_part(own - own % HEAD_T, own % HEAD_T)
        span(rx_core, 8 * PICKS, swap_send, swap_recv).wait_recv()
        for zz in range(4):
            for p in range(2):
                there = pl.ds((2 * zz + p) * PICKS, PICKS)
                low[there, :] = (daf[rows(p, zz, c), :] + rx_core[there, :]).astype(BF16)
        for k in (1, 2, 3, 0):
            back_to(0, k).start()
            if k:
                back_to(1, k).start()

        def step(t, carry):
            table_part(pl.multiple_of(t * HEAD_T, HEAD_T), HEAD_T)
            return carry

        lax.fori_loop(0, own // HEAD_T, step, 0, unroll=True)
        rx[z] = low[pl.ds(pl.multiple_of((2 * z + 1) * PICKS, PICKS), PICKS), :]
        span(rx_core, 8 * PICKS, swap_send, swap_recv).wait_send()
        span(low, 7 * PICKS, daf_send, daf_recv).wait_send()
        span(rx, 3, daf_send, daf_recv).wait_recv()

    def second():
        span(picked, 4 * PICKS, pick_send, core_recv).wait_send()
        span(rx, 4, daf_send, daf_recv).wait_recv()

    pl.when(last)(third)
    pl.when(sec == 2)(second)

    def finish():
        summed = rx[0].astype(F32)
        for k in range(1, 4):
            summed = summed + rx[k].astype(F32)
        grad, dg_f = rms_back(mine[...].astype(F32), g_f, summed)
        for k in range(6):
            small[k : k + 1, :] = dg_f[:, k * 128 : (k + 1) * 128]
        ids = lax.broadcasted_iota(jnp.int32, (SP, PICKS), 0)
        spread = jnp.where(ids == pick_row, 1.0, 0.0).astype(BF16)
        rest = grad
        out = jnp.zeros((SP, D), F32)
        for _ in range(3):
            part = rest.astype(BF16)
            out = out + nn(spread, part)
            rest = rest - part.astype(F32)
        d_top[...] = out.astype(BF16)

    def none():
        d_top[...] = jnp.zeros_like(d_top)

    pl.when(upper)(finish)
    pl.when(jnp.logical_not(upper))(none)
    all_zero.wait()


def head_call(y, picks, info, gain, table):
    low = lambda *shape: pltpu.VMEM(shape, BF16)
    wide = lambda *shape: pltpu.VMEM(shape, F32)
    n = 16 * PICKS
    return pl.pallas_call(
        head_kernel,
        out_shape=(
            jax.ShapeDtypeStruct((SP, D), BF16),
            jax.ShapeDtypeStruct((OWN, D), F32),
            jax.ShapeDtypeStruct((8, 128), F32),
        ),
        in_specs=[VMEM] * 5,
        out_specs=(VMEM, ANY, VMEM),
        scratch_shapes=[
            low(PICKS, D),
            low(n, D),
            low(n, D),
            wide(n, OWN),
            low(n, OWN),
            pltpu.VMEM((n, 1), jnp.int32),
            wide(n, 1),
            wide(16, 128),
            wide(8, 16, 128),
            wide(n, D),
            wide(8 * PICKS, D),
            low(8 * PICKS, D),
            low(4, PICKS, D),
            wide(OWN, D),
            pltpu.SemaphoreType.DMA,
            pltpu.SemaphoreType.DMA,
            pltpu.SemaphoreType.DMA,
            pltpu.SemaphoreType.DMA((2, 4)),
        ]
        + [pltpu.SemaphoreType.DMA] * 8,
        compiler_params=pltpu.CompilerParams(
            collective_id=3, has_side_effects=True, vmem_limit_bytes=56 * 2**20
        ),
        name="head",
    )(y, picks, info, gain, table)


def open_anywhere(codes, labels, picks, classes, null_mask, starts, table, frequency):
    sec = lax.axis_index("section")
    d = lax.axis_index("dp")
    par = lax.rem(sec, 2)
    own = table.shape[0]
    row_index, counted, _, position = jax.vmap(row_layout)(starts, classes, null_mask, codes)
    picked_labels = jnp.take_along_axis(labels, picks, axis=1)
    picked_counts = jnp.take_along_axis(counted, picks, axis=1).astype(jnp.int32)
    row_index = jnp.pad(row_index, ((0, 0), (0, SP - SLOTS)), constant_values=-1)
    info = jnp.concatenate([row_index, picked_labels, picked_counts], axis=1)
    info = lax.all_gather(info, "dp", axis=0, tiled=True)
    all_labels = info[:, SP : SP + PICKS].reshape(-1)
    all_counts = info[:, SP + PICKS :].reshape(-1).astype(F32)
    gain_row = lax.slice_in_dim(table, VOCAB % own, VOCAB % own + 1)[0].astype(F32)
    holds = (sec == 3) & (d == VOCAB // own)
    g_f = lax.psum(jnp.where(holds, gain_row, 0.0), ("section", "dp"))
    position = jnp.pad(position[par], (0, SP - SLOTS))
    angles = position.astype(F32)[:, None] * frequency[None, :]
    cosine = jnp.tile(jnp.cos(angles), (1, 4))
    sine = jnp.tile(jnp.concatenate([-jnp.sin(angles), jnp.sin(angles)], axis=1), (1, 2))
    gathered = lax.all_gather(table, "dp", axis=0, tiled=True)[:WROWS]
    other = lax.ppermute(gathered, "section", [(0, 1), (1, 0), (2, 3), (3, 2)])
    weights = jnp.where((sec == 1) | (sec == 2), gathered, other)
    local = jnp.where(sec == 0, info[:, :SP].reshape(-1), -1) - d * own
    onehot = (local[:, None] == jnp.arange(own)[None, :]).astype(BF16)
    looked = (nn(onehot, table) * math.sqrt(D)).astype(BF16)
    looked = lax.psum_scatter(looked, "dp", scatter_dimension=0, tiled=True).reshape(2, SP, D)
    from_first = lax.ppermute(looked[1], "section", [(0, 1)])
    x0 = jnp.where(sec == 0, looked[0], from_first)
    return weights, x0, local, all_labels, all_counts, g_f, cosine, sine


def head_anywhere(y, my_picks, all_labels, all_counts, g_f, table):
    sec = lax.axis_index("section")
    d = lax.axis_index("dp")
    n_sec = lax.axis_size("section")
    n_dp = lax.axis_size("dp")
    own = table.shape[0]
    picked = jnp.take(y, my_picks, axis=0)
    all_picked = lax.all_gather(picked, ("section", "dp"), axis=0, tiled=False)
    all_picked = all_picked.reshape(n_sec, n_dp, PICKS, D)[2:].transpose(1, 0, 2, 3)
    all_picked = all_picked.reshape(-1, D).astype(F32)
    af = jnp.where(sec == 3, rms_scale(all_picked, g_f), 0.0).astype(BF16)
    vocab_ids = d * own + jnp.arange(own)
    logits = jnp.where(vocab_ids[None, :] < VOCAB, nt(af, table), NEG)
    local_max = jnp.max(logits, axis=1)
    hit = vocab_ids[None, :] == all_labels[:, None]
    sums = jnp.stack(
        [
            local_max,
            jnp.sum(jnp.exp(logits - local_max[:, None]), axis=1),
            jnp.sum(jnp.where(hit, logits, 0.0), axis=1),
        ]
    )
    every = lax.all_gather(sums, "dp", axis=0, tiled=False)
    top = jnp.max(every[:, 0], axis=0)
    total = jnp.sum(every[:, 1] * jnp.exp(every[:, 0] - top), axis=0)
    target = jnp.sum(every[:, 2], axis=0)
    log_total = top + jnp.log(total)
    loss_part = jnp.where(
        (sec == 3) & (d == 0), jnp.sum(jnp.where(all_counts > 0, log_total - target, 0.0)), 0.0
    )
    dlogits = (jnp.exp(logits - log_total[:, None]) - hit.astype(F32)) * all_counts[:, None]
    dlogits = jnp.where(sec == 3, dlogits, 0.0).astype(BF16)
    d_table = tn(dlogits, af)
    daf = lax.psum(nn(dlogits, table), "dp")
    daf = lax.dynamic_slice_in_dim(daf, d * 2 * PICKS, 2 * PICKS).reshape(2, PICKS, D)
    daf = jnp.where(sec == 3, daf[1], lax.ppermute(daf[0], "section", [(3, 2)]))
    d_own, dg_f = rms_pull(picked.astype(F32), g_f, daf)
    dg_f = jnp.where(sec >= 2, dg_f, 0.0)
    spread = (jnp.arange(SP)[:, None] == my_picks[None, :]).astype(F32)
    d_top = jnp.dot(spread, d_own, precision=lax.Precision.HIGHEST).astype(BF16)
    return d_top, d_table, dg_f, loss_part


def shards(codes, labels, picks, classes, null_mask, starts, master, momentum, average):
    sec = lax.axis_index("section")
    d = lax.axis_index("dp")
    n_dp = lax.axis_size("dp")
    n_sec = lax.axis_size("section")
    par = lax.rem(sec, 2)
    own = master.shape[0]
    learn_rate = rate_factor * math.sqrt(own * n_sec * n_dp)
    beside = [(0, 1), (1, 0), (2, 3), (3, 2)]
    fast = n_sec == 4 and n_dp == 8 and own == OWN
    gain_at = VOCAB // own
    frequency = rope_base ** (-jnp.arange(HD // 2, dtype=F32) * 2.0 / HD)

    if fast:
        wide = jnp.tile(frequency[None, :], (1, 4))
        weights, x0, info, gain, cosine, sine, table = gather_and_embed(
            master, codes, labels, picks, starts, classes, null_mask, wide
        )
        all_index = info[:, :2, :SP].reshape(-1)
        local = jnp.where(sec == 0, all_index, -1) - d * own
    else:
        table = master.astype(BF16)
        opened = open_anywhere(codes, labels, picks, classes, null_mask, starts, table, frequency)
        weights, x0, local, all_labels, all_counts, g_f, cosine, sine = opened
    around = (cosine, sine, starts)

    x = forward_call(False, x0, weights, *around)[0]
    y, *kept = forward_call(True, x, weights, *around)

    if fast:
        d_top, d_table, small = head_call(y, picks, info, gain, table)
    else:
        d_top, d_table, dg_f, loss_part = head_anywhere(
            y, picks[par], all_labels, all_counts, g_f, table
        )

    once = backward_call(True, d_top, x, weights, *around, kept)
    dx0, left, right, tail = lax.cond(
        sec < 2,
        lambda: tuple(backward_call(False, once[0], x, weights, *around, kept)),
        lambda: tuple(once),
    )

    if fast:
        grad, squares = reduce_and_scatter(left, right, tail, d_table, dx0, local[None, :])
        totals = share_norm(small, squares, n_sec, n_dp)
        dg_f, loss_sum, grad_norm = totals[:6].reshape(-1), totals[6, 0], totals[8, 0]
        count_sum = jnp.sum(info[:, 4:6, :PICKS].astype(F32))
    else:
        grads = matrix_gradients(left, right, tail)
        grads = grads.astype(F32) + lax.ppermute(grads, "section", beside).astype(F32)
        grads = jnp.pad(grads.astype(BF16), ((0, own * n_dp - WROWS), (0, 0)))
        grad = lax.psum_scatter(grads, "dp", scatter_dimension=0, tiled=True).astype(F32)
        grad = jnp.where(sec == 3, d_table, grad)
        pair = jnp.stack([dx0, lax.ppermute(dx0, "section", [(1, 0)])])
        all_dx = lax.all_gather(pair, "dp", axis=0, tiled=True).reshape(-1, D)
        onehot = (jnp.arange(own)[:, None] == local[None, :]).astype(BF16)
        grad = jnp.where(sec == 0, nn(onehot, all_dx) * math.sqrt(D), grad)
        totals = (dg_f, jnp.sum(grad * grad), loss_part)
        dg_f, squares, loss_sum = lax.psum(totals, ("section", "dp"))
        count_sum = jnp.sum(all_counts)
        grad_norm = jnp.sqrt(squares + jnp.sum(dg_f * dg_f))
    gain_here = (jnp.arange(own) == VOCAB % own)[:, None] & (sec == 3) & (d == gain_at)
    grad = grad + jnp.where(gain_here, dg_f[None, :], 0.0)
    clipped = grad * jnp.minimum(1.0, clip_limit / (grad_norm + norm_eps))
    new_momentum = momentum_decay * momentum + clipped
    new_master = master - learn_rate * (clipped + momentum_decay * new_momentum)
    new_average = average_decay * average + (1.0 - average_decay) * new_master
    return loss_sum, count_sum, grad_norm, new_master, new_momentum, new_average


def solution(mesh):
    split = P("dp", None)
    whole = P(("section", "dp"), None)
    return jax.shard_map(
        shards,
        mesh=mesh,
        in_specs=(split,) * 6 + (whole,) * 3,
        out_specs=(P(), P(), P(), whole, whole, whole),
        check_vma=False,
    )
```

```python
import functools
import math

import jax
import jax.numpy as jnp
from jax import lax
from jax.experimental import pallas as pl
from jax.experimental.pallas import tpu as pltpu
from jax.sharding import PartitionSpec as P

D = 768
HEADS = 12
HD = 64
FF = 2048
VOCAB = 16384
CLASSES = 1001
SLOTS = 264
SP = 272
PICKS = 32
SEGS = 3
MATS = 4 * D + 3 * FF
WROWS = 9232

F32 = jnp.float32
BF16 = jnp.bfloat16

rope_base = 10000.0
clip_limit = 1.0
rate_factor = 0.25
momentum_decay = 0.9
average_decay = 0.8
norm_eps = 1e-06


def nn(left, right):
    return jnp.dot(left, right, preferred_element_type=F32)


def tn(left, right):
    return lax.dot_general(left, right, (((0,), (0,)), ((), ())), preferred_element_type=F32)


def nt(left, right):
    return lax.dot_general(left, right, (((1,), (1,)), ((), ())), preferred_element_type=F32)


def rms_scale(value_in, gain):
    return (
        value_in * lax.rsqrt(jnp.mean(value_in * value_in, axis=-1, keepdims=True) + norm_eps) * gain
    )


def rms_pull(value_in, gain, grad):
    inv = lax.rsqrt(jnp.mean(value_in * value_in, axis=-1, keepdims=True) + norm_eps)
    unit = value_in * inv
    scaled = grad * gain
    grad_in = inv * (scaled - unit * jnp.mean(scaled * unit, axis=-1, keepdims=True))
    return grad_in, jnp.sum(grad * unit, axis=0)


def row_layout(starts_row, classes_row, null_row, codes_row):
    slot_ids = jnp.arange(SLOTS, dtype=jnp.int32)
    segment = jnp.sum((starts_row[None, 1:] <= slot_ids[:, None]).astype(jnp.int32), axis=1)
    seg_start = jnp.sum(
        jnp.where(segment[:, None] == jnp.arange(SEGS + 1)[None, :], starts_row[None, :], 0), axis=1
    )
    position = slot_ids - seg_start
    live_end = starts_row[SEGS]
    is_first = (position == 0) & (slot_ids < live_end)
    clamped = jnp.minimum(segment, SEGS - 1)
    hit = clamped[:, None] == jnp.arange(SEGS)[None, :]
    class_row = jnp.sum(
        jnp.where(hit, jnp.where(null_row > 0, CLASSES - 1, classes_row)[None, :], 0), axis=1
    )
    row_index = jnp.where(is_first, VOCAB + class_row, codes_row)
    following = jnp.concatenate([segment[1:], jnp.full((1,), SEGS + 1, jnp.int32)])
    counted = (following == segment) & (slot_ids + 1 < live_end)
    return row_index, counted, segment, position


MESH = pl.DeviceIdType.MESH
ANY = pl.BlockSpec(memory_space=pl.ANY)
VMEM = pl.BlockSpec(memory_space=pltpu.VMEM)
SMEM = pl.BlockSpec(memory_space=pltpu.SMEM)

OWN = 2176
SPLIT = 1152
COUNT = (18, 16, 18, 16, 11)
ROWS = (64, 64, 64, 64, 48)
HELD = (0, SPLIT, OWN, OWN + SPLIT, 2 * OWN)
LARGE = (16, 14, 16, 14, 11)
SMALL = 4
SMALL_ROWS = 32
LANE = 2 * OWN + 11 * 48
LAG = 2
WINDOW = 2
HOP = 2
PIECES = ((0, 64), (64, 64), (128, 64), (192, 64), (256, 16))
TURN = 6
CHOP = 4
CLAG = 3
AHEAD = 4
CWAIT = 6


def class_base(k, lane):
    if k == 4:
        return 4 * OWN
    return OWN * (2 * (k // 2) + lane) + SPLIT * (k % 2)


def place():
    sec = lax.axis_index("section")
    dp = lax.axis_index("dp")
    z = dp // 2
    c = lax.rem(dp, 2)
    par = lax.rem(sec, 2)
    home = jnp.logical_or(sec == 1, sec == 2)
    return sec, dp, z, c, par, home


def greet_neighbours(sec, dp, z, c, par, turns):
    barrier = pltpu.get_barrier_semaphore()

    def greet(s, e):
        pl.semaphore_signal(barrier, 1, device_id=(s, e), device_id_type=MESH)

    greet(sec, dp + 1 - 2 * c)
    greet(sec + 1 - 2 * par, dp)
    pl.when(z > 0)(lambda: greet(sec, dp - 2))
    pl.when(z < 3)(lambda: greet(sec, dp + 2))
    count = 2 + (z > 0).astype(jnp.int32) + (z < 3).astype(jnp.int32)
    for sender, receiver in turns:
        pl.when(sec == receiver)(lambda sender=sender: greet(sender, dp))
        count = count + (sec == sender).astype(jnp.int32)
    pl.semaphore_wait(barrier, count)


def hop_targets(sec, dp, c, par):
    return {
        "up": (sec, dp + 2),
        "down": (sec, dp - 2),
        "x": (sec + 1 - 2 * par, dp),
        "core": (sec, dp + 1 - 2 * c),
    }


HOPS = ("up", "down", "x", "core")


def tree(z, c, home):
    both = jnp.logical_and
    either = jnp.logical_or
    no = jnp.logical_not
    far = z >= 2
    mid = both(z >= 1, z <= 2)
    never = z < 0
    away = no(home)
    as_int = lambda flag: flag.astype(jnp.int32)
    out = []
    for block in (0, 1):
        for half in (0, 1):
            mine = home if half == 0 else away
            other = no(mine)
            source = both(z == block, home)
            if half == 0:
                early = (lambda j: j < TURN) if block == 0 else (lambda j: j < 0)
                near_x = lambda j, block=block, early=early: both(z == 1 - block, early(j))
                hop_x = lambda j, near_x=near_x: both(home, near_x(j))
                got_x = lambda j, near_x=near_x: both(away, near_x(j))
                along = lambda j, early=early: either(home, no(early(j)))
            else:
                hop_x = lambda j, block=block: both(away, z == 1 - block)
                got_x = lambda j, block=block: both(home, z == 1 - block)
                along = lambda j: away
            at_owner = both(z == block, away)
            if block == 0:
                up = lambda j, along=along, mine=mine: either(both(z == 0, along(j)), both(mid, mine))
                down = lambda j: never
                from_up = lambda j: never
            else:
                up = lambda j, mine=mine: both(mid, mine)
                down = lambda j, along=along: both(z == 1, along(j))
                from_up = lambda j, got_x=got_x: both(z == 0, no(got_x(j)))
            send_x = lambda j, source=source, mine=mine, hop_x=hop_x: either(
                either(source, both(far, mine)), hop_x(j)
            )
            from_x = lambda j, at_owner=at_owner, other=other, got_x=got_x: either(
                either(at_owner, both(far, other)), got_x(j)
            )
            from_down = lambda j, source=source, from_x=from_x, from_up=from_up: no(
                either(source, either(from_x(j), from_up(j)))
            )
            depth = jnp.abs(z - block) + as_int(far) * (half + as_int(other))
            if half == 0:
                depth = depth + (1 - as_int(far)) * as_int(away)
            else:
                depth = depth + (1 - as_int(far)) * jnp.where(
                    away, 1, 2 * as_int(z == 1 - block)
                )
            out.append(
                (source, dict(up=up, down=down, x=send_x), dict(up=from_up, down=from_down, x=from_x), depth)
            )
    lane0 = c == 0
    source = both(both(z == 2, home), lane0)
    sends = dict(
        up=lambda j: both(z == 2, lane0),
        down=lambda j: both(mid, lane0),
        x=lambda j: source,
    )
    parents = dict(
        up=lambda j: both(z <= 1, lane0),
        down=lambda j: both(z == 3, lane0),
        x=lambda j: both(both(z == 2, away), lane0),
    )
    out.append((source, sends, parents, jnp.abs(z - 2) + as_int(away)))
    return out


def segment_of(starts, r, slot):
    bounds = [starts[r, j] for j in range(SEGS + 1)]
    count = lambda at: functools.reduce(
        jnp.add, [(at >= bounds[j]).astype(jnp.int32) for j in range(1, SEGS + 1)]
    )
    segment = count(slot)
    begin = jnp.where(
        segment == 0, bounds[0], jnp.where(segment == 1, bounds[1], jnp.where(segment == 2, bounds[2], bounds[3]))
    )
    counted = jnp.logical_and(count(slot + 1) == segment, slot + 1 < bounds[SEGS])
    return segment, slot - begin, counted, slot < bounds[SEGS]


def open_kernel(
    master, codes, labels, picks, starts, classes, nulls, frequency, out, x0, info, gain, cosine,
    sine, table, exact, master_sem, recv_sem, recv_c, core_sem, send_sem, sent, mine, rx_core, rx_up, rx_down,
    swap_send, swap_recv, x_send, x_recv, line_send, up_recv, down_recv, last_send, last_recv,
    note, note_send, note_recv, gain_send, gain_recv,
):
    sec, dp, z, c, par, home = place()
    targets = hop_targets(sec, dp, c, par)
    classes_of = tree(z, c, home)
    gain_dp = VOCAB // (OWN)
    holds_gain = jnp.logical_and(sec == 3, dp == gain_dp)

    parts = [pl.ds(k * (OWN // 4), OWN // 4) for k in range(4)]
    def place_own(part, value):
        start = pl.multiple_of(dp * OWN + part.start, 16)
        out[pl.ds(start, part.size), :] = value

    fetch = [
        pltpu.make_async_copy(master.at[part], exact.at[part], master_sem.at[k])
        for k, part in enumerate(parts)
    ]
    for one in fetch:
        one.start()

    barrier = pltpu.get_barrier_semaphore()

    def greet(s, e):
        pl.semaphore_signal(barrier, 1, device_id=(s, e), device_id_type=MESH)

    for k in range(1, 8):
        greet(sec, lax.rem(dp + k, 8))
    greet(sec + 1 - 2 * par, dp)
    pl.when(sec == 2)(lambda: greet(0, dp))
    pl.when(sec == 1)(lambda: greet(2, dp))
    pl.when(jnp.logical_and(sec == 2, dp != gain_dp))(lambda: greet(3, gain_dp))

    slot_row = lax.broadcasted_iota(jnp.int32, (1, SLOTS), 1)
    note[...] = jnp.full(note.shape, -1, jnp.int32)
    for r in range(2):
        segment, position, _, live = segment_of(starts, r, slot_row)
        names = [classes[r, j] + (CLASSES - 1 - classes[r, j]) * nulls[r, j] for j in range(SEGS)]
        name = jnp.where(segment == 0, names[0], jnp.where(segment == 1, names[1], names[2]))
        opens = jnp.logical_and(position == 0, live)
        note[r : r + 1, :SLOTS] = jnp.where(opens, VOCAB + name, codes[r : r + 1, :])
        chosen = picks[r : r + 1, :]
        ids = lax.broadcasted_iota(jnp.int32, (SLOTS, PICKS), 0)
        label_col = column(labels[r : r + 1, :], SLOTS)
        note[2 + r : 3 + r, :PICKS] = jnp.sum(
            jnp.where(ids == chosen, label_col, 0), axis=0, keepdims=True
        )
        note[4 + r : 5 + r, :PICKS] = segment_of(starts, r, chosen)[2].astype(jnp.int32)
    info[dp] = note[...]
    for one, part in zip(fetch, parts):
        one.wait()
        value = exact[part, :].astype(BF16)
        table[part, :] = value
        pl.when(jnp.logical_and(home, z < 2))(lambda part=part, value=value: place_own(part, value))
    pl.when(classes_of[4][0])(
        lambda: place_own(pl.ds(0, 11 * 48), exact[pl.ds(0, 11 * 48), :].astype(BF16))
    )
    count = 8 + jnp.logical_or(sec == 0, sec == 2).astype(jnp.int32)
    pl.semaphore_wait(barrier, count + 7 * holds_gain.astype(jnp.int32))
    for k in range(1, 8):
        pltpu.make_async_remote_copy(
            src_ref=note,
            dst_ref=info.at[dp],
            send_sem=note_send,
            recv_sem=note_recv,
            device_id=(sec, lax.rem(dp + k, 8)),
            device_id_type=MESH,
        ).start()
    noted = pltpu.make_async_remote_copy(
        src_ref=info.at[pl.ds(0, 7)],
        dst_ref=info.at[pl.ds(0, 7)],
        send_sem=note_send,
        recv_sem=note_recv,
        device_id=targets["core"],
        device_id_type=MESH,
    )

    gain_rows = table.at[pl.ds(VOCAB % (OWN), 16)]

    def gain_to(s, e):
        return pltpu.make_async_remote_copy(
            src_ref=gain_rows,
            dst_ref=gain,
            send_sem=gain_send,
            recv_sem=gain_recv,
            device_id=(s, e),
            device_id_type=MESH,
        )

    def send_gain():
        for e in range(8):
            gain_to(2, e).start()
            if e != gain_dp:
                gain_to(3, e).start()
        gain[...] = gain_rows[...]

    pl.when(holds_gain)(send_gain)

    def copy(k, hop, offset, rows, recv, slot):
        part = out.at[pl.ds(pl.multiple_of(class_base(k, c) + offset, 16), rows)]
        return pltpu.make_async_remote_copy(
            src_ref=part,
            dst_ref=part,
            send_sem=send_sem.at[k, HOPS.index(hop), slot],
            recv_sem=recv,
            device_id=targets[hop],
            device_id_type=MESH,
        )

    def piece(k, j, small):
        source, sends, _, _ = classes_of[k]
        recv = recv_c.at[j] if k == 4 else recv_sem.at[k, j]
        slot = lax.rem(j, WINDOW)
        rows = SMALL_ROWS if small else ROWS[k]
        offset = ROWS[k] * LARGE[k] + rows * (j - LARGE[k]) if small else rows * j

        def send(hop):
            to = core_sem.at[k] if hop == "core" else recv
            before = j >= WINDOW if hop == "core" else jnp.logical_and(j >= WINDOW, sends[hop](j - WINDOW))
            if small:
                was_large = j < LARGE[k] + WINDOW
                wide_one = copy(k, hop, 0, ROWS[k], to, slot)
                pl.when(jnp.logical_and(before, was_large))(wide_one.wait_send)
                before = jnp.logical_and(before, jnp.logical_not(was_large))
            one = copy(k, hop, offset, rows, to, slot)
            pl.when(before)(one.wait_send)
            one.start()

        pl.when(jnp.logical_not(source))(copy(k, "x", offset, rows, recv, slot).wait_recv)
        for hop in HOPS[:3]:
            pl.when(sends[hop](j))(lambda hop=hop: send(hop))
        send("core")

    first = sec == 0
    second = sec == 2

    def slot(k):
        return pl.ds(pl.multiple_of(k * SP, 16), SP)

    def order(i):
        low = (z <= 1).astype(jnp.int32)
        return low * (3 - i) + (1 - low) * i

    def swap(k):
        return pltpu.make_async_remote_copy(
            src_ref=sent.at[slot(k)],
            dst_ref=rx_core.at[slot(k)],
            send_sem=swap_send,
            recv_sem=swap_recv.at[k],
            device_id=targets["core"],
            device_id_type=MESH,
        )

    def cross(zz):
        return pltpu.make_async_remote_copy(
            src_ref=mine.at[slot(4 + zz)],
            dst_ref=mine.at[slot(zz)],
            send_sem=x_send,
            recv_sem=x_recv.at[zz],
            device_id=(2, dp),
            device_id_type=MESH,
        )

    def piece_of(k, q):
        start, size = PIECES[q]
        return pl.ds(pl.multiple_of(k * SP + start, 16), size)

    def go(zz, q, ref, recv, hop):
        return pltpu.make_async_remote_copy(
            src_ref=mine.at[piece_of(zz, q)],
            dst_ref=ref.at[piece_of(zz, q)],
            send_sem=line_send,
            recv_sem=recv.at[zz, q],
            device_id=targets[hop],
            device_id_type=MESH,
        )

    def go_up(zz, q):
        return go(zz, q, rx_down, down_recv, "up")

    def go_down(zz, q):
        return go(zz, q, rx_up, up_recv, "down")

    def add(there, ref):
        mine[there, :] = (mine[there, :].astype(F32) + ref[there, :].astype(F32)).astype(BF16)

    def look(row):
        local = column(info[row // 2, pl.ds(lax.rem(row, 2), 1), :][:, :SP], SP) - dp * OWN
        ids = lax.broadcasted_iota(jnp.int32, (SP, OWN), 1)
        onehot = jnp.where(ids == local, 1.0, 0.0).astype(BF16)
        return (nn(onehot, table[...]) * math.sqrt(D)).astype(BF16)

    def lookup(b):
        zz = order(b // 2)
        p = 1 - lax.rem(b, 2)
        k = 4 * p + zz
        sent[slot(k), :] = look(2 * (2 * zz + 1 - c) + p)
        swap(k).start()
        mine[slot(k), :] = look(2 * (2 * zz + c) + p)
        swap(k).wait_recv()
        add(slot(k), rx_core)
        pl.when(p == 1)(lambda: cross(zz).start())

    def chain(zz, q):
        def from_below():
            go_up(zz, q).wait_recv()
            add(piece_of(zz, q), rx_down)

        def from_above():
            go_down(zz, q).wait_recv()
            add(piece_of(zz, q), rx_up)

        if q == 0:
            pl.when(second)(cross(zz).wait_recv)
        pl.when(jnp.logical_and(zz >= z, z > 0))(from_below)
        pl.when(jnp.logical_and(zz <= z, z < 3))(from_above)
        pl.when(zz > z)(lambda: go_up(zz, q).start())
        pl.when(zz < z)(lambda: go_down(zz, q).start())

    def chains(i):
        for o in range(4):
            zz = order(o)
            hops = jnp.maximum(
                z * (zz >= z).astype(jnp.int32), (3 - z) * (zz <= z).astype(jnp.int32)
            )
            for q in range(5):
                now = i == 2 * o + 2 + sec + HOP * hops + q
                pl.when(now)(lambda zz=zz, q=q: chain(zz, q))

    segment, position, _, _ = segment_of(starts, par, lax.broadcasted_iota(jnp.int32, (SP, 128), 0))
    angles = position.astype(F32) * frequency[...]
    lanes = lax.broadcasted_iota(jnp.int32, (SP, 128), 1)
    cosine[...] = jnp.cos(angles)
    sine[...] = jnp.where(lax.rem(lanes, 64) < 32, -1.0, 1.0) * jnp.sin(angles)
    noted.wait_recv()

    def step(i, carry):
        for k in range(5):
            j = i - LAG * classes_of[k][3]
            now = jnp.logical_and(j >= 0, j < LARGE[k])
            if k == 4:
                now = jnp.logical_and(now, c == 0)
            pl.when(now)(lambda k=k, j=j: piece(k, j, False))
            if k < 4:
                now = jnp.logical_and(j >= LARGE[k], j < LARGE[k] + SMALL)
                pl.when(now)(lambda k=k, j=j: piece(k, j, True))
        pl.when(jnp.logical_and(first, i < 8))(lambda: lookup(i))
        pl.when(jnp.logical_or(first, second))(lambda: chains(i))
        pl.when(jnp.logical_and(second, i == last_step))(lambda: last().start())
        return carry

    last_step = 6 + 2 + 2 + 3 * HOP + 4 + 1

    def last():
        return pltpu.make_async_remote_copy(
            src_ref=mine.at[slot(z)],
            dst_ref=x0,
            send_sem=last_send,
            recv_sem=last_recv,
            device_id=(1, dp),
            device_id_type=MESH,
        )

    lax.fori_loop(0, max(LARGE[0] + SMALL + 5 * LAG, last_step + 1), step, 0)

    def blocks(count, sem):
        return pltpu.make_async_remote_copy(
            src_ref=mine.at[pl.ds(0, count * SP)],
            dst_ref=mine.at[pl.ds(0, count * SP)],
            send_sem=sem,
            recv_sem=sem,
            device_id=targets["core"],
            device_id_type=MESH,
        )

    def end_first():
        blocks(8, swap_send).wait_send()
        blocks(4, x_send).wait_send()
        blocks(3, line_send).wait_send()
        x0[...] = mine[slot(z), :]

    def end_second():
        blocks(3, line_send).wait_send()
        last().wait_send()

    def none():
        x0[...] = jnp.zeros_like(x0)

    pl.when(first)(end_first)
    pl.when(second)(end_second)
    pl.when(sec == 1)(last().wait_recv)
    pl.when(sec >= 2)(none)

    noted.wait_send()

    def gain_sent():
        for e in range(15):
            gain_to(2, 0).wait_send()

    pl.when(holds_gain)(gain_sent)
    pl.when(jnp.logical_and(sec >= 2, jnp.logical_not(holds_gain)))(gain_to(2, dp).wait_recv)

    def drain(k):
        count, rows = (LARGE[4], ROWS[4]) if k == 4 else (LARGE[k] + SMALL, SMALL_ROWS)
        _, sends, _, _ = classes_of[k]
        for j in range(count - WINDOW, count):
            for hop in HOPS[:3]:
                one = copy(k, hop, 0, rows, core_sem.at[k], j % WINDOW)
                pl.when(sends[hop](j))(one.wait_send)
            copy(k, "core", 0, rows, core_sem.at[k], j % WINDOW).wait_send()
        if k == 0:
            for j in range(TURN - WINDOW, TURN):
                one = copy(k, "x", 0, ROWS[0], core_sem.at[k], j % WINDOW)
                last_one = jnp.logical_not(sends["x"](j + WINDOW))
                pl.when(jnp.logical_and(sends["x"](j), last_one))(one.wait_send)

    def came(k):
        count, rows = COUNT[k], ROWS[k]
        part = out.at[pl.ds(pl.multiple_of(class_base(k, 1 - c), 16), count * rows)]
        pltpu.make_async_remote_copy(
            src_ref=part,
            dst_ref=part,
            send_sem=send_sem.at[k, 3, 0],
            recv_sem=core_sem.at[k],
            device_id=targets["core"],
            device_id_type=MESH,
        ).wait_recv()

    for k in range(4):
        drain(k)
        came(k)
    pl.when(c == 0)(lambda: drain(4))
    pl.when(c == 1)(lambda: came(4))


def gather_and_embed(master, codes, labels, picks, starts, classes, nulls, frequency):
    rows = lambda n: pltpu.VMEM((n * SP, D), BF16)
    return pl.pallas_call(
        open_kernel,
        out_shape=(
            jax.ShapeDtypeStruct((WROWS, D), BF16),
            jax.ShapeDtypeStruct((SP, D), BF16),
            jax.ShapeDtypeStruct((8, 8, 384), jnp.int32),
            jax.ShapeDtypeStruct((16, D), BF16),
            jax.ShapeDtypeStruct((SP, 128), F32),
            jax.ShapeDtypeStruct((SP, 128), F32),
            jax.ShapeDtypeStruct((OWN, D), BF16),
        ),
        in_specs=[ANY] + [VMEM] * 3 + [SMEM] * 3 + [VMEM],
        out_specs=(VMEM,) * 7,
        scratch_shapes=[
            pltpu.VMEM((OWN, D), F32),
            pltpu.SemaphoreType.DMA((4,)),
            pltpu.SemaphoreType.DMA((4, 20)),
            pltpu.SemaphoreType.DMA((11,)),
            pltpu.SemaphoreType.DMA((5,)),
            pltpu.SemaphoreType.DMA((5, 4, WINDOW)),
            rows(8),
            rows(8),
            rows(8),
            rows(4),
            rows(4),
            pltpu.SemaphoreType.DMA,
            pltpu.SemaphoreType.DMA((8,)),
            pltpu.SemaphoreType.DMA,
            pltpu.SemaphoreType.DMA((4,)),
            pltpu.SemaphoreType.DMA,
            pltpu.SemaphoreType.DMA((4, 5)),
            pltpu.SemaphoreType.DMA((4, 5)),
            pltpu.SemaphoreType.DMA,
            pltpu.SemaphoreType.DMA,
            pltpu.VMEM((8, 384), jnp.int32),
        ]
        + [pltpu.SemaphoreType.DMA] * 4,
        compiler_params=pltpu.CompilerParams(
            collective_id=0, has_side_effects=True, vmem_limit_bytes=56 * 2**20
        ),
        name="gather_and_embed",
    )(master, codes, labels, picks, starts, classes, nulls, frequency)


def close_kernel(
    left_any, right_any, tail, start, block, index, out, squares, left, right, loc, sent, rx_core,
    rx_up, rx_down, rx_x, summed, ring, all_dx, load_sem, core_sem, recv_sem, recv_c, core_send,
    send_sem, ring_sem, dx_own, dx_send, line_recv, cross_recv, turn_recv, dx_core_send,
    dx_core_recv, ready,
):
    sec, dp, z, c, par, home = place()
    targets = hop_targets(sec, dp, c, par)
    classes = tree(z, c, home)
    loads = [
        pltpu.make_async_copy(left_any, left, load_sem.at[0]),
        pltpu.make_async_copy(right_any, right, load_sem.at[1]),
    ]
    for one in loads:
        one.start()
    del start
    greet_neighbours(sec, dp, z, c, par, ((1, 2), (0, 2)))
    pl.when(sec == 0)(
        lambda: pl.semaphore_signal(ready, 1, device_id=(2, dp), device_id_type=MESH)
    )
    for one in loads:
        one.wait()

    def place_of(hop, k, j):
        offset = j * ROWS[k]
        if hop == "down":
            base = (0, 0, 0, SPLIT, OWN)[k]
        elif hop == "up":
            base = (0, SPLIT, OWN, OWN, OWN + SPLIT)[k]
        else:
            base = HELD[k]
        return pl.ds(pl.multiple_of(base + offset, 16), ROWS[k])

    def gradient(first_row, size):
        first_row = jnp.int32(first_row)
        bounds = (D, 2 * D, 3 * D, 4 * D, 4 * D + 2 * FF)
        matrix = functools.reduce(
            jnp.add, [(first_row >= bound).astype(jnp.int32) for bound in bounds]
        )
        cols = pl.ds(pl.multiple_of(first_row, 128), size)
        return tn(left[:, cols], right[matrix]).astype(BF16)

    def core_copy(k, offset, rows, sem):
        part = pl.ds(pl.multiple_of(HELD[k] + offset, 16), rows)
        return pltpu.make_async_remote_copy(
            src_ref=sent.at[part],
            dst_ref=rx_core.at[part],
            send_sem=core_send,
            recv_sem=sem,
            device_id=targets["core"],
            device_id_type=MESH,
        )

    def form(k, t):
        there = pl.ds(pl.multiple_of(HELD[k] + 128 * t, 128), 128)
        sent[there, :] = gradient(class_base(k, 1 - c) + 128 * t, 128)
        core_copy(k, 128 * t, 128, core_sem.at[k, t]).start()
        loc[there, :] = gradient(class_base(k, c) + 128 * t, 128)

    last_rows = 11 * 48

    def form_last(into):
        for t in range(4):
            into[pl.ds(HELD[4] + 128 * t, 128), :] = gradient(4 * OWN + 128 * t, 128)
        into[pl.ds(HELD[4] + 512, 16), :] = tail[...]

    def form_for_other():
        form_last(sent)
        core_copy(4, 0, last_rows, core_sem.at[4, 0]).start()

    squares[...] = jnp.zeros_like(squares)

    def count_squares(value):
        folded = value * value
        size = folded.shape[0]
        while size > 8 and size % 16 == 0:
            size //= 2
            folded = folded[:size] + folded[size:]
        for part in range(size // 8):
            for n in range(D // 128):
                squares[...] += folded[part * 8 : (part + 1) * 8, n * 128 : (n + 1) * 128]

    rx = dict(up=rx_up, down=rx_down, x=rx_x)

    def onward(k, hop, j):
        back = dict(up="down", down="up", x="x")[hop]
        return landing(k, back, hop, j)

    def landing(k, back, hop, j):
        index = ("up", "down", "x").index(back)
        part = pl.ds(pl.multiple_of(HELD[k] + j * ROWS[k], 16), ROWS[k])
        return pltpu.make_async_remote_copy(
            src_ref=loc.at[part],
            dst_ref=rx[back].at[place_of(back, k, j)],
            send_sem=send_sem.at[k],
            recv_sem=recv_c.at[index, j] if k == 4 else recv_sem.at[index, k, j],
            device_id=targets[hop],
            device_id_type=MESH,
        )

    def gathered(k, j):
        part = pl.ds(pl.multiple_of(HELD[k] + j * ROWS[k], 16), ROWS[k])
        if k == 4:
            pl.when(j == 0)(lambda: core_copy(4, 0, last_rows, core_sem.at[4, 0]).wait_recv())
        else:
            pl.when(lax.rem(j, 2) == 0)(
                lambda: core_copy(k, 64 * j, 128, core_sem.at[k, j // 2]).wait_recv()
            )
        acc = summed.at[pl.ds(0, ROWS[k])]
        acc[...] = loc[part, :].astype(F32) + rx_core[part, :].astype(F32)
        for hop in HOPS[:3]:
            if (hop, k) in (("down", 0), ("down", 1)):
                continue

            def add(hop=hop):
                landing(k, hop, hop, j).wait_recv()
                acc[...] += rx[hop][place_of(hop, k, j), :].astype(F32)

            pl.when(classes[k][1][hop](j))(add)
        return part, acc

    def relay(k, j):
        part, acc = gathered(k, j)
        loc[part, :] = acc[...].astype(BF16)
        for hop in HOPS[:3]:
            pl.when(classes[k][2][hop](j))(lambda hop=hop: onward(k, hop, j).start())

    def write(slot, rows, offset):
        return pltpu.make_async_copy(
            ring.at[pl.ds(pl.multiple_of(slot * 64, 64), rows)],
            out.at[pl.ds(pl.multiple_of(offset, 16), rows)],
            ring_sem.at[slot],
        )

    def finish(k, j):
        _, acc = gathered(k, j)
        slot = 4 * (k % 2) + lax.rem(j, 4)
        copy = write(slot, ROWS[k], SPLIT * (k % 2) + j * ROWS[k])
        pl.when(j >= 4)(copy.wait)
        value = acc[...]
        ring[pl.ds(pl.multiple_of(slot * 64, 64), ROWS[k]), :] = value
        copy.start()
        count_squares(value)

    first = sec == 0
    second = sec == 2
    in_line = jnp.logical_or(first, second)
    p_line = second.astype(jnp.int32)
    both = jnp.logical_and

    def dx_part(p, zz):
        return all_dx.at[pl.ds(pl.multiple_of((2 * (2 * zz + c) + p) * SP, 16), SP)]

    def move(p, zz, send, recv, target):
        return pltpu.make_async_remote_copy(
            src_ref=dx_part(p, zz),
            dst_ref=dx_part(p, zz),
            send_sem=send,
            recv_sem=recv,
            device_id=target,
            device_id_type=MESH,
        )

    def line(zz, hop):
        return move(p_line, zz, dx_send, line_recv.at[zz], targets[hop])

    def cross(zz):
        return move(1, zz, dx_send, cross_recv.at[zz], (0, dp))

    def dx_to_core(p, zz):
        return move(p, zz, dx_core_send, dx_core_recv, targets["core"])

    def aside(zz):
        pl.when(first)(lambda: dx_to_core(0, zz).start())
        pl.when(second)(lambda: cross(zz).start())

    def crossed(zz):
        cross(zz).wait_recv()
        dx_to_core(1, zz).start()

    def blocks(count, send, recv):
        return pltpu.make_async_remote_copy(
            src_ref=all_dx.at[pl.ds(0, count * SP)],
            dst_ref=all_dx.at[pl.ds(0, count * SP)],
            send_sem=send,
            recv_sem=recv,
            device_id=targets["core"],
            device_id_type=MESH,
        )

    turned = pltpu.make_async_remote_copy(
        src_ref=block,
        dst_ref=dx_part(1, z),
        send_sem=dx_send,
        recv_sem=turn_recv,
        device_id=(2, dp),
        device_id_type=MESH,
    )
    pl.when(sec == 1)(turned.start)

    def pass_own():
        pl.when(z < 3)(lambda: line(z, "up").start())
        pl.when(z > 0)(lambda: line(z, "down").start())
        aside(z)

    def own_first():
        own = pltpu.make_async_copy(block, dx_part(0, z), dx_own)
        own.start()
        own.wait()
        pass_own()

    def own_second():
        turned.wait_recv()
        pl.semaphore_wait(ready, 1)
        pass_own()

    pl.when(first)(own_first)

    def from_below(k):
        line(z - k, "up").wait_recv()
        pl.when(z < 3)(lambda: line(z - k, "up").start())
        aside(z - k)

    def from_above(k):
        line(z + k, "down").wait_recv()
        pl.when(z > 0)(lambda: line(z + k, "down").start())
        aside(z + k)

    def tile(t):
        ids = lax.broadcasted_iota(jnp.int32, (SP, 16 * SP), 0) + t * SP
        onehot = jnp.where(ids == index[...], 1.0, 0.0).astype(BF16)
        value = nn(onehot, all_dx[...]) * math.sqrt(D)
        slot = lax.rem(t, 2)
        copy = write_tile(slot, t)
        pl.when(t >= 2)(copy.wait)
        ring[pl.ds(pl.multiple_of(slot * SP, 16), SP), :] = value
        copy.start()
        count_squares(value)

    def write_tile(slot, t):
        return pltpu.make_async_copy(
            ring.at[pl.ds(pl.multiple_of(slot * SP, 16), SP)],
            out.at[pl.ds(pl.multiple_of(t * SP, 16), SP)],
            ring_sem.at[slot],
        )

    def collect(i):
        pl.when(both(second, i == CHOP + AHEAD))(own_second)
        for k in range(1, 4):
            now = i == CHOP * (k + p_line) + AHEAD * p_line
            pl.when(both(now, z >= k))(lambda k=k: from_below(k))
            pl.when(both(now, z + k <= 3))(lambda k=k: from_above(k))

    begin = 5 * CHOP + 1

    def embed(i):
        pl.when(i == 2 * CHOP)(lambda: crossed(z))
        for k in range(1, 4):
            pl.when(both(i == CHOP * (k + 2), z >= k))(lambda k=k: crossed(z - k))
            pl.when(both(i == CHOP * (k + 2), z + k <= 3))(lambda k=k: crossed(z + k))
        pl.when(i == begin)(lambda: blocks(8, dx_core_send, dx_core_recv).wait_recv())
        t = i - begin
        pl.when(both(t >= 0, t < OWN // SP))(lambda: tile(t))

    def step(i, carry):
        for k in range(4):
            turn_now = both(lax.rem(i, 2) == k // 2, i < COUNT[k] + k // 2)
            pl.when(turn_now)(lambda k=k: form(k, i // 2))
        pl.when(both(i == CWAIT - 1, c == 0))(lambda: form_last(loc))
        pl.when(both(i == CWAIT - 1, c == 1))(form_for_other)
        for k in range(5):
            source, _, _, depth = classes[k]
            j = i - CLAG * ((5, 5, 4, 4, 3)[k] - depth) - (0, 0, 1, 1, CWAIT)[k]
            now = both(j >= 0, j < COUNT[k])
            if k == 4:
                now = both(now, c == 0)
            pl.when(both(now, jnp.logical_not(source)))(lambda k=k, j=j: relay(k, j))
            pl.when(both(now, source))(lambda k=k, j=j: finish(k, j))
        pl.when(in_line)(lambda: collect(i))
        pl.when(first)(lambda: embed(i))
        return carry

    lax.fori_loop(0, max(18 + 5 * CLAG, begin + OWN // SP), step, 0)
    pl.when(first)(lambda: blocks(8, dx_core_send, dx_core_recv).wait_send())

    def dx_sent(count):
        blocks(count, dx_send, dx_core_recv).wait_send()

    middle = both(z >= 1, z <= 2)
    ends = jnp.logical_not(middle)
    pl.when(jnp.logical_or(sec == 1, both(first, ends)))(lambda: dx_sent(1))
    pl.when(both(first, middle))(lambda: dx_sent(5))
    pl.when(both(second, ends))(lambda: dx_sent(5))
    pl.when(both(second, middle))(lambda: dx_sent(9))
    def sent_core(rows):
        part = pl.ds(0, rows)
        pltpu.make_async_remote_copy(
            src_ref=sent.at[part],
            dst_ref=rx_core.at[part],
            send_sem=core_send,
            recv_sem=core_sem.at[4, 0],
            device_id=targets["core"],
            device_id_type=MESH,
        ).wait_send()

    pl.when(c == 0)(lambda: sent_core(2 * OWN))
    pl.when(c == 1)(lambda: sent_core(LANE))
    for k in range(5):
        part = pl.ds(HELD[k], COUNT[k] * ROWS[k])
        gone = pltpu.make_async_remote_copy(
            src_ref=loc.at[part],
            dst_ref=rx_x.at[part],
            send_sem=send_sem.at[k],
            recv_sem=core_sem.at[4, 0],
            device_id=targets["x"],
            device_id_type=MESH,
        )
        away = jnp.logical_not(classes[k][0])
        pl.when(both(away, c == 0) if k == 4 else away)(gone.wait_send)

    def drain_half(k):
        for j in range(COUNT[k] - 4, COUNT[k]):
            write(4 * (k % 2) + j % 4, ROWS[k], 0).wait()

    def drain_tiles():
        for slot in range(2):
            write_tile(slot, 0).wait()

    for k in range(5):
        pl.when(classes[k][0])(lambda k=k: drain_half(k))
    pl.when(first)(drain_tiles)


def reduce_and_scatter(left, right, tail, start, block, index):
    low = lambda *shape: pltpu.VMEM(shape, BF16)
    dma = pltpu.SemaphoreType.DMA
    return pl.pallas_call(
        close_kernel,
        out_shape=(
            jax.ShapeDtypeStruct((OWN, D), F32),
            jax.ShapeDtypeStruct((8, 128), F32),
        ),
        in_specs=[ANY, ANY, VMEM, ANY, VMEM, VMEM],
        out_specs=(ANY, VMEM),
        input_output_aliases={3: 0},
        scratch_shapes=[
            low(SP, MATS),
            low(6, SP, D),
            low(LANE, D),
            low(LANE, D),
            low(LANE, D),
            low(OWN + SPLIT + 11 * 48, D),
            low(OWN + 11 * 48, D),
            low(LANE, D),
            pltpu.VMEM((64, D), F32),
            pltpu.VMEM((2 * SP, D), F32),
            low(16 * SP, D),
            dma((2,)),
            dma((5, 9)),
            dma((3, 4, 18)),
            dma((3, 11)),
            dma,
            dma((5,)),
            dma((8,)),
            dma,
            dma,
            dma((4,)),
            dma((4,)),
            dma,
            dma,
            dma,
            pltpu.SemaphoreType.REGULAR,
        ],
        compiler_params=pltpu.CompilerParams(
            collective_id=1, has_side_effects=True, vmem_limit_bytes=63 * 2**20
        ),
        name="reduce_and_scatter",
    )(left, right, tail, start, block, index)


def norm_kernel(n_sec, n_dp, small, squares, out, block, every, send_sem, recv_sem):
    sec = lax.axis_index("section")
    dp = lax.axis_index("dp")
    n = n_sec * n_dp
    me = sec * n_dp + dp
    barrier = pltpu.get_barrier_semaphore()

    def peer(k):
        other = lax.rem(me + k, n)
        return (other // n_dp, lax.rem(other, n_dp))

    def greet(k, carry):
        pl.semaphore_signal(barrier, 1, device_id=peer(k), device_id_type=MESH)
        return carry

    lax.fori_loop(1, n, greet, 0)
    block[...] = small[...]
    block[7:8, :] += jnp.sum(squares[...], axis=0, keepdims=True)
    every[me] = block[...]
    pl.semaphore_wait(barrier, n - 1)

    def send(k, carry):
        pltpu.make_async_remote_copy(
            src_ref=block,
            dst_ref=every.at[me],
            send_sem=send_sem,
            recv_sem=recv_sem,
            device_id=peer(k),
            device_id_type=MESH,
        ).start()
        return carry

    lax.fori_loop(1, n, send, 0)
    others = pltpu.make_async_remote_copy(
        src_ref=every.at[pl.ds(0, n - 1)],
        dst_ref=every.at[pl.ds(0, n - 1)],
        send_sem=send_sem,
        recv_sem=recv_sem,
        device_id=peer(1),
        device_id_type=MESH,
    )
    others.wait_recv()
    total = every[0]
    for k in range(1, n):
        total = total + every[k]
    gains = jnp.sum(total[0:6] * total[0:6], axis=0, keepdims=True)
    norm = jnp.sqrt(jnp.sum(gains + total[7:8], axis=1, keepdims=True))
    out[0:8, :] = total
    out[8:16, :] = jnp.broadcast_to(norm, (8, 128))
    others.wait_send()


def share_norm(small, squares, n_sec, n_dp):
    return pl.pallas_call(
        functools.partial(norm_kernel, n_sec, n_dp),
        out_shape=jax.ShapeDtypeStruct((16, 128), F32),
        in_specs=[VMEM, VMEM],
        out_specs=VMEM,
        scratch_shapes=[
            pltpu.VMEM((8, 128), F32),
            pltpu.VMEM((n_sec * n_dp, 8, 128), F32),
            pltpu.SemaphoreType.DMA,
            pltpu.SemaphoreType.DMA,
        ],
        compiler_params=pltpu.CompilerParams(
            collective_id=8, has_side_effects=True, vmem_limit_bytes=2**20
        ),
        cost_estimate=pl.CostEstimate(
            flops=10**10, bytes_accessed=4 * 10**7, transcendentals=0
        ),
        name="share_norm",
    )(small, squares)


NEG = -1e30
FT = 256


def turn(block, cosine, sine, lanes):
    ahead = pltpu.roll(block, 96, 1)
    behind = pltpu.roll(block, 32, 1)
    return block * cosine + jnp.where(lax.rem(lanes, 64) < 32, ahead, behind) * sine


def see(starts):
    par = lax.rem(lax.axis_index("section"), 2)
    rows = lax.broadcasted_iota(jnp.int32, (SP, SP), 0)
    cols = lax.broadcasted_iota(jnp.int32, (SP, SP), 1)
    same = segment_of(starts, par, rows)[0] == segment_of(starts, par, cols)[0]
    allowed = jnp.logical_and(same, cols <= rows)
    return jnp.where(allowed, 0.0, NEG)


def hide(starts):
    par = lax.rem(lax.axis_index("section"), 2)
    rows = lax.broadcasted_iota(jnp.int32, (SP, SP), 0)
    cols = lax.broadcasted_iota(jnp.int32, (SP, SP), 1)
    same = segment_of(starts, par, rows)[0] == segment_of(starts, par, cols)[0]
    return jnp.where(jnp.logical_and(same, rows <= cols), 0.0, NEG)


def softmax_of(scores, unseen):
    masked = scores + unseen
    grown = jnp.exp(masked - jnp.max(masked, axis=-1, keepdims=True))
    return grown / jnp.sum(grown, axis=-1, keepdims=True)


def weight_copies(w_any, w, sems):
    bounds = (0, 3 * D, 4 * D, 4 * D + FF, 4 * D + 2 * FF, MATS, WROWS)
    return [
        pltpu.make_async_copy(
            w_any.at[pl.ds(lo, hi - lo)], w.at[pl.ds(lo, hi - lo)], sems.at[i]
        )
        for i, (lo, hi) in enumerate(zip(bounds[:-1], bounds[1:]))
    ]


def forward_kernel(keep, x, w_any, cosine, sine, starts, y, *refs):
    kept = refs[:7] if keep else ()
    q, k, v, o, h, gate, up, w, m, unseen, sems, keep_sems, *hop_sems = refs[len(kept) :]
    sec = lax.axis_index("section")
    dp = lax.axis_index("dp")
    lower = sec < 2
    if not keep:
        barrier = pltpu.get_barrier_semaphore()
        pl.when(jnp.logical_not(lower))(
            lambda: pl.semaphore_signal(barrier, 1, device_id=(sec - 2, dp), device_id_type=MESH)
        )

    def hop(b):
        part = y.at[:, pl.ds(b * 256, 256)]
        return pltpu.make_async_remote_copy(
            src_ref=part,
            dst_ref=part,
            send_sem=hop_sems[0].at[b],
            recv_sem=hop_sems[1].at[b],
            device_id=(sec + 2, dp),
            device_id_type=MESH,
        )

    def put(i):
        if keep:
            pltpu.make_async_copy((q, k, v, o, h, gate, up)[i], kept[i], keep_sems.at[i]).start()

    def run():
        copies = weight_copies(w_any, w, sems)
        for i in (5, 0, 1, 2, 3, 4):
            copies[i].start()
        unseen[...] = see(starts)
        lanes = lax.broadcasted_iota(jnp.int32, (SP, 128), 1)
        first = lanes < 64
        copies[5].wait()
        gains = w[pl.ds(MATS, 16), :].astype(F32)
        stream = x[...].astype(F32)
        a1 = rms_scale(stream, gains[0:1]).astype(BF16)
        copies[0].wait()

        def project(b, carry):
            cols = pl.ds(pl.multiple_of(b * 256, 256), 256)
            raw_q = nn(a1, w[pl.ds(0, D), cols])
            raw_k = nn(a1, w[pl.ds(D, D), cols])
            raw_v = nn(a1, w[pl.ds(2 * D, D), cols])
            v[:, cols] = raw_v.astype(BF16)
            for part in range(2):
                there = pl.ds(pl.multiple_of(b * 256 + part * 128, 128), 128)
                here = slice(part * 128, (part + 1) * 128)
                turned_q = turn(raw_q[:, here], cosine[...], sine[...], lanes)
                q[:, there] = (turned_q * HD ** (-0.5)).astype(BF16)
                k[:, there] = turn(raw_k[:, here], cosine[...], sine[...], lanes).astype(BF16)
            return carry

        lax.fori_loop(0, D // 256, project, 0, unroll=True)
        for i in range(3):
            put(i)

        def attend(b, carry):
            cols = pl.ds(pl.multiple_of(b * 128, 128), 128)
            qb, kb, vb = q[:, cols], k[:, cols], v[:, cols]
            zero = jnp.zeros_like(qb)
            p0 = softmax_of(nt(jnp.where(first, qb, zero), kb), unseen[...]).astype(BF16)
            p1 = softmax_of(nt(jnp.where(first, zero, qb), kb), unseen[...]).astype(BF16)
            o[:, cols] = jnp.where(first, nn(p0, vb), nn(p1, vb)).astype(BF16)
            return carry

        lax.fori_loop(0, HEADS // 2, attend, 0, unroll=True)
        put(3)
        copies[1].wait()
        for b in range(3):
            cols = pl.ds(b * 256, 256)
            h[:, cols] = x[:, cols].astype(F32) + nn(o[...], w[pl.ds(3 * D, D), cols])
        put(4)
        a2 = rms_scale(h[...], gains[1:2]).astype(BF16)
        copies[2].wait()
        copies[3].wait()

        def widen(b, carry):
            cols = pl.ds(pl.multiple_of(b * FT, FT), FT)
            g = nt(a2, w[pl.ds(pl.multiple_of(4 * D + b * FT, FT), FT), :])
            u = nt(a2, w[pl.ds(pl.multiple_of(4 * D + FF + b * FT, FT), FT), :])
            gate[:, cols] = g
            up[:, cols] = u
            m[:, cols] = (g / (1.0 + jnp.exp(-g)) * u).astype(BF16)
            return carry

        lax.fori_loop(0, FF // FT, widen, 0, unroll=True)
        put(5)
        put(6)
        copies[4].wait()

        if not keep:
            pl.semaphore_wait(barrier, 1)
        for b in range(3):
            cols = pl.ds(b * 256, 256)
            y[:, cols] = (h[:, cols] + nn(m[...], w[pl.ds(4 * D + 2 * FF, FF), cols])).astype(BF16)
            if not keep:
                hop(b).start()
        for i, part in enumerate(kept):
            pltpu.make_async_copy((q, k, v, o, h, gate, up)[i], part, keep_sems.at[i]).wait()
        if not keep:
            for b in range(3):
                hop(b).wait_send()
            y[...] = x[...]

    if keep:
        run()
        return
    pl.when(lower)(run)

    def arrive():
        for b in range(3):
            hop(b).wait_recv()

    pl.when(jnp.logical_not(lower))(arrive)


KEPT = ((D, BF16), (D, BF16), (D, BF16), (D, BF16), (D, F32), (FF, F32), (FF, F32))


def forward_call(keep, x, weights, cosine, sine, starts):
    low = jax.ShapeDtypeStruct((SP, D), BF16)
    kept = tuple(jax.ShapeDtypeStruct((SP, n), t) for n, t in KEPT) if keep else ()
    return pl.pallas_call(
        functools.partial(forward_kernel, keep),
        out_shape=(low,) + kept,
        in_specs=[VMEM, ANY, VMEM, VMEM, SMEM],
        out_specs=(VMEM,) + (ANY,) * len(kept),
        scratch_shapes=[pltpu.VMEM((SP, n), t) for n, t in KEPT]
        + [
            pltpu.VMEM((WROWS, D), BF16),
            pltpu.VMEM((SP, FF), BF16),
            pltpu.VMEM((SP, SP), F32),
            pltpu.SemaphoreType.DMA((6,)),
            pltpu.SemaphoreType.DMA((7,)),
        ]
        + ([] if keep else [pltpu.SemaphoreType.DMA((3,))] * 2),
        compiler_params=pltpu.CompilerParams(vmem_limit_bytes=56 * 2**20)
        if keep
        else pltpu.CompilerParams(
            collective_id=6, has_side_effects=True, vmem_limit_bytes=56 * 2**20
        ),
        name="layer_forward_kept" if keep else "layer_forward",
    )(x, weights, cosine, sine, starts)


def rms_back(value_in, gain, grad):
    inv = lax.rsqrt(jnp.mean(value_in * value_in, axis=-1, keepdims=True) + norm_eps)
    unit = value_in * inv
    scaled = grad * gain
    grad_in = inv * (scaled - unit * jnp.mean(scaled * unit, axis=-1, keepdims=True))
    return grad_in, jnp.sum(grad * unit, axis=0, keepdims=True)


def backward_kernel(send, dy, x, w_any, cosine, sine, starts, *refs):
    kept, refs = refs[:7], refs[7:]
    dx, left, right, tail, refs = *refs[:4], refs[4:]
    q, k, v, o, h, gate, up, w, dgate, dup, m, da, do, dq, dk, dv, a1, a2, db, *refs = refs
    unseen, sems, keep_sems, out_sems, *hop_sems = refs
    sec = lax.axis_index("section")
    dp = lax.axis_index("dp")
    upper = sec >= 2
    if send:
        barrier = pltpu.get_barrier_semaphore()
        pl.when(jnp.logical_not(upper))(
            lambda: pl.semaphore_signal(barrier, 1, device_id=(sec + 2, dp), device_id_type=MESH)
        )

    def hop():
        return pltpu.make_async_remote_copy(
            src_ref=dx,
            dst_ref=dx,
            send_sem=hop_sems[0],
            recv_sem=hop_sems[1],
            device_id=(sec - 2, dp),
            device_id_type=MESH,
        )

    outs = []

    def put(source, target):
        copy = pltpu.make_async_copy(source, target, out_sems.at[len(outs)])
        copy.start()
        outs.append(copy)
    def run():
        copies = weight_copies(w_any, w, sems)
        taken = [
            pltpu.make_async_copy(part, (q, k, v, o, h, gate, up)[i], keep_sems.at[i])
            for i, part in enumerate(kept)
        ]
        for one in (
            copies[4], taken[5], taken[6], copies[5], copies[2], copies[3], taken[4], copies[1],
            taken[0], taken[1], taken[2], copies[0], taken[3],
        ):
            one.start()
        unseen[...] = hide(starts)
        lanes = lax.broadcasted_iota(jnp.int32, (SP, 128), 1)
        first = lanes < 64
        copies[4].wait()
        taken[5].wait()
        taken[6].wait()

        def open_mlp(b, carry):
            cols = pl.ds(pl.multiple_of(b * FT, FT), FT)
            dm = nt(dy[...], w[pl.ds(pl.multiple_of(4 * D + 2 * FF + b * FT, FT), FT), :])
            g = gate[:, cols]
            u = up[:, cols]
            sig = 1.0 / (1.0 + jnp.exp(-g))
            dgate[:, cols] = (dm * u * sig * (1.0 + g * (1.0 - sig))).astype(BF16)
            dup[:, cols] = (dm * g * sig).astype(BF16)
            m[:, cols] = (g * sig * u).astype(BF16)
            return carry

        lax.fori_loop(0, FF // FT, open_mlp, 0, unroll=True)
        for i, part in enumerate((dgate, dup, m)):
            put(part, left.at[:, pl.ds(4 * D + i * FF, FF)])
        put(dy, right.at[5])
        copies[5].wait()
        gains = w[pl.ds(MATS, 16), :].astype(F32)
        copies[2].wait()
        copies[3].wait()

        def close_mlp(b, carry):
            cols = pl.ds(pl.multiple_of(b * 256, 256), 256)
            da[:, cols] = nn(dgate[...], w[pl.ds(4 * D, FF), cols]) + nn(
                dup[...], w[pl.ds(4 * D + FF, FF), cols]
            )
            return carry

        lax.fori_loop(0, 3, close_mlp, 0, unroll=True)
        taken[4].wait()
        dh, dg_mlp = rms_back(h[...], gains[1:2], da[...])
        dh = dh + dy[...].astype(F32)
        db[...] = dh.astype(BF16)
        a2[...] = rms_scale(h[...], gains[1:2]).astype(BF16)
        put(db, right.at[3])
        put(a2, right.at[4])
        copies[1].wait()
        for b in range(3):
            do[:, pl.ds(b * 256, 256)] = nt(db[...], w[pl.ds(3 * D + b * 256, 256), :]).astype(BF16)

        for i in range(3):
            taken[i].wait()

        def attend(b, carry):
            cols = pl.ds(pl.multiple_of(b * 128, 128), 128)
            qb, kb, vb, dob = q[:, cols], k[:, cols], v[:, cols], do[:, cols]
            zero = jnp.zeros_like(qb)
            parts = []
            for head in range(2):
                keep = first if head == 0 else jnp.logical_not(first)
                masked = nt(jnp.where(keep, kb, zero), qb) + unseen[...]
                grown = jnp.exp(masked - jnp.max(masked, axis=0, keepdims=True))
                probs = grown / jnp.sum(grown, axis=0, keepdims=True)
                dprobs = nt(jnp.where(keep, vb, zero), dob)
                along = jnp.sum(probs * dprobs, axis=0, keepdims=True)
                dscores = (probs * (dprobs - along)).astype(BF16)
                parts.append((tn(dscores, kb), nn(dscores, qb), nn(probs.astype(BF16), dob)))
            dqb = jnp.where(first, parts[0][0], parts[1][0]) * HD ** (-0.5)
            dkb = jnp.where(first, parts[0][1], parts[1][1])
            dq[:, cols] = turn(dqb, cosine[...], -sine[...], lanes).astype(BF16)
            dk[:, cols] = turn(dkb, cosine[...], -sine[...], lanes).astype(BF16)
            dv[:, cols] = jnp.where(first, parts[0][2], parts[1][2]).astype(BF16)
            return carry

        lax.fori_loop(0, HEADS // 2, attend, 0, unroll=True)
        for i, part in enumerate((dq, dk, dv)):
            put(part, right.at[i])
        copies[0].wait()
        for b in range(3):
            rows = lambda i, b=b: w[pl.ds(i * D + b * 256, 256), :]
            da[:, pl.ds(b * 256, 256)] = (
                nt(dq[...], rows(0)) + nt(dk[...], rows(1)) + nt(dv[...], rows(2))
            )
        stream = x[...].astype(F32)
        a1[...] = rms_scale(stream, gains[0:1]).astype(BF16)
        for i in range(3):
            put(a1, left.at[:, pl.ds(i * D, D)])
        taken[3].wait()
        put(o, left.at[:, pl.ds(3 * D, D)])
        dstream, dg_attn = rms_back(stream, gains[0:1], da[...])
        dx[...] = (dstream + dh).astype(BF16)
        if send:
            pl.semaphore_wait(barrier, 1)
            hop().start()
        ids = lax.broadcasted_iota(jnp.int32, (16, D), 0)
        tail[...] = jnp.where(ids == 0, dg_attn, jnp.where(ids == 1, dg_mlp, 0.0)).astype(BF16)
        for copy in outs:
            copy.wait()
        if send:
            hop().wait_send()

    if not send:
        run()
        return
    pl.when(upper)(run)
    pl.when(jnp.logical_not(upper))(lambda: hop().wait_recv())


def backward_call(send, dy, x, weights, cosine, sine, starts, kept):
    wide = pltpu.VMEM((SP, FF), BF16)
    narrow = pltpu.VMEM((SP, D), BF16)
    return pl.pallas_call(
        functools.partial(backward_kernel, send),
        out_shape=(
            jax.ShapeDtypeStruct((SP, D), BF16),
            jax.ShapeDtypeStruct((SP, MATS), BF16),
            jax.ShapeDtypeStruct((6, SP, D), BF16),
            jax.ShapeDtypeStruct((16, D), BF16),
        ),
        in_specs=[VMEM, VMEM, ANY, VMEM, VMEM, SMEM] + [ANY] * 7,
        out_specs=(VMEM, ANY, ANY, VMEM),
        scratch_shapes=[pltpu.VMEM((SP, n), t) for n, t in KEPT]
        + [
            pltpu.VMEM((WROWS, D), BF16),
            wide,
            wide,
            wide,
            pltpu.VMEM((SP, D), F32),
        ]
        + [narrow] * 7
        + [
            pltpu.VMEM((SP, SP), F32),
            pltpu.SemaphoreType.DMA((6,)),
            pltpu.SemaphoreType.DMA((7,)),
            pltpu.SemaphoreType.DMA((13,)),
        ]
        + ([pltpu.SemaphoreType.DMA] * 2 if send else []),
        compiler_params=pltpu.CompilerParams(
            collective_id=7, has_side_effects=True, vmem_limit_bytes=60 * 2**20
        )
        if send
        else pltpu.CompilerParams(vmem_limit_bytes=60 * 2**20),
        name="layer_backward_send" if send else "layer_backward",
    )(dy, x, weights, cosine, sine, starts, *kept)


def matrix_gradients(left, right, tail):
    parts = [(0, 0), (D, 1), (2 * D, 2), (3 * D, 3), (4 * D, 4), (4 * D + FF, 4), (4 * D + 2 * FF, 5)]
    ends = [start for start, _ in parts[1:]] + [MATS]
    rows = [
        tn(left[:, start:end], right[i]).astype(BF16) for (start, i), end in zip(parts, ends)
    ]
    return jnp.concatenate(rows + [tail], axis=0)


HEAD_T = 256


def column(row, size):
    there = lax.broadcasted_iota(jnp.int32, (size, size), 0)
    here = lax.broadcasted_iota(jnp.int32, (size, size), 1)
    zero = jnp.zeros((), row.dtype)
    return jnp.sum(jnp.where(there == here, row, zero), axis=1, keepdims=True)


def as_rows(values):
    there = lax.broadcasted_iota(jnp.int32, (128, 128), 0)
    here = lax.broadcasted_iota(jnp.int32, (128, 128), 1)
    return [
        jnp.sum(
            jnp.where(there == here, values[k * 128 : (k + 1) * 128], 0.0), axis=0, keepdims=True
        )
        for k in range(4)
    ]


def head_kernel(
    y, picks, info, gain, table, d_top, d_table, small, mine, picked, af, scores, dlow, labels,
    counts, stat, stats, daf, rx_core, low, rx, fresh, zero_sem, own_sem, pick_send, pick_recv,
    core_send, core_recv, stat_send, stat_recv, swap_send, swap_recv, daf_send, daf_recv,
):
    sec, dp, z, c, par, home = place()
    last = sec == 3
    upper = sec >= 2
    barrier = pltpu.get_barrier_semaphore()
    other_core = (3, dp + 1 - 2 * c)

    def greet(s, e):
        pl.semaphore_signal(barrier, 1, device_id=(s, e), device_id_type=MESH)

    def greet_second():
        for k in range(4):
            greet(3, 2 * k + c)
        pl.semaphore_wait(barrier, 4)

    def greet_third():
        for k in range(4):
            greet(2, 2 * k + c)
        for k in range(1, 8):
            greet(3, lax.rem(dp + k, 8))
        pl.semaphore_wait(barrier, 11)

    all_zero = pltpu.make_async_copy(fresh, d_table, zero_sem)

    def zeros():
        fresh[...] = jnp.zeros_like(fresh)
        all_zero.start()

    pl.when(jnp.logical_not(last))(zeros)
    small[...] = jnp.zeros_like(small)
    pick_row = picks[pl.ds(par, 1), :]
    pick_col = column(pick_row, PICKS)

    def choose():
        ids = lax.broadcasted_iota(jnp.int32, (PICKS, SP), 1)
        mine[...] = nn(jnp.where(ids == pick_col, 1.0, 0.0).astype(BF16), y[...]).astype(BF16)

    pl.when(upper)(choose)
    pl.when(sec == 2)(greet_second)
    pl.when(last)(greet_third)

    def rows(p, zz, lane):
        return pl.ds(pl.multiple_of((2 * (2 * zz + lane) + p) * PICKS, PICKS), PICKS)

    def pick_to(k):
        zz = lax.rem(z + k, 4)
        return pltpu.make_async_remote_copy(
            src_ref=mine,
            dst_ref=picked.at[rows(par, z, c)],
            send_sem=pick_send,
            recv_sem=pick_recv.at[par, z],
            device_id=(3, 2 * zz + c),
            device_id_type=MESH,
        )

    def came(p, k):
        zz = lax.rem(z + k, 4)
        return pltpu.make_async_remote_copy(
            src_ref=mine,
            dst_ref=picked.at[rows(p, zz, c)],
            send_sem=pick_send,
            recv_sem=pick_recv.at[p, zz],
            device_id=other_core,
            device_id_type=MESH,
        )

    def forward(p, k):
        part = picked.at[rows(p, lax.rem(z + k, 4), c)]
        return pltpu.make_async_remote_copy(
            src_ref=part,
            dst_ref=part,
            send_sem=core_send,
            recv_sem=core_recv,
            device_id=other_core,
            device_id_type=MESH,
        )

    def span(ref, count, send, recv):
        part = ref.at[pl.ds(0, count)]
        return pltpu.make_async_remote_copy(
            src_ref=part,
            dst_ref=part,
            send_sem=send,
            recv_sem=recv,
            device_id=other_core,
            device_id_type=MESH,
        )

    def pick_second():
        for k in (1, 2, 3, 0):
            pick_to(k).start()

    def pick_third():
        own = pltpu.make_async_copy(mine, picked.at[rows(1, z, c)], own_sem)
        own.start()
        for k in range(1, 4):
            pick_to(k).start()
        for e in range(8):
            for p in range(2):
                at = pl.ds((2 * e + p) * PICKS, PICKS)
                labels[at, :] = column(info[e, 2 + p : 3 + p, :][:, :PICKS], PICKS)
                counts[at, :] = column(info[e, 4 + p : 5 + p, :][:, :PICKS].astype(F32), PICKS)
        own.wait()
        forward(1, 0).start()
        for k in range(4):
            came(0, k).wait_recv()
            forward(0, k).start()
            if k:
                came(1, k).wait_recv()
                forward(1, k).start()
        span(picked, 8 * PICKS, core_send, core_recv).wait_recv()

    pl.when(sec == 2)(pick_second)
    pl.when(last)(pick_third)
    g_f = gain[...].astype(F32)[0:1]
    own = OWN
    tiles = [(t * HEAD_T, HEAD_T) for t in range(own // HEAD_T)] + [
        (own - own % HEAD_T, own % HEAD_T)
    ]

    def over_tiles(body):
        def step(t, carry):
            body(pl.multiple_of(t * HEAD_T, HEAD_T), HEAD_T)
            return carry

        lax.fori_loop(0, own // HEAD_T, step, 0, unroll=True)
        body(own - own % HEAD_T, own % HEAD_T)

    def forward_part():
        af[...] = rms_scale(picked[...].astype(F32), g_f).astype(BF16)
        fold = lambda op, block: functools.reduce(
            op, [block[:, k * 128 : (k + 1) * 128] for k in range(block.shape[1] // 128)]
        )
        top = daf.at[:, pl.ds(0, 128)]
        top[...] = jnp.full((16 * PICKS, 128), NEG, F32)

        def product(start, size):
            ids = lax.broadcasted_iota(jnp.int32, (16 * PICKS, size), 1) + (dp * own + start)
            block = nt(af[...], table[pl.ds(start, size), :])
            block = jnp.where(ids < VOCAB, block, NEG)
            scores[:, pl.ds(start, size)] = block
            top[...] = jnp.maximum(top[...], fold(jnp.maximum, block))

        over_tiles(product)
        top_col = jnp.max(top[...], axis=1, keepdims=True)
        total = daf.at[:, pl.ds(128, 128)]
        target = daf.at[:, pl.ds(256, 128)]
        total[...] = jnp.zeros((16 * PICKS, 128), F32)
        target[...] = jnp.zeros((16 * PICKS, 128), F32)

        def exponents(start, size):
            ids = lax.broadcasted_iota(jnp.int32, (16 * PICKS, size), 1) + (dp * own + start)
            block = scores[:, pl.ds(start, size)]
            grown = jnp.exp(block - top_col)
            scores[:, pl.ds(start, size)] = grown
            total[...] += fold(jnp.add, grown)
            target[...] += fold(jnp.add, jnp.where(ids == labels[...], block, 0.0))

        over_tiles(exponents)
        stat[...] = jnp.zeros_like(stat)
        columns = (
            top_col,
            jnp.sum(total[...], axis=1, keepdims=True),
            jnp.sum(target[...], axis=1, keepdims=True),
        )
        for k, values in enumerate(columns):
            for i, row in enumerate(as_rows(values)):
                stat[4 * k + i : 4 * k + i + 1, :] = row
        stats[dp] = stat[...]
        for k in range(1, 8):
            pltpu.make_async_remote_copy(
                src_ref=stat,
                dst_ref=stats.at[dp],
                send_sem=stat_send,
                recv_sem=stat_recv,
                device_id=(3, lax.rem(dp + k, 8)),
                device_id_type=MESH,
            ).start()
        every = span(stats, 7, stat_send, stat_recv)
        every.wait_recv()
        tops = [stats[e, 0:4, :] for e in range(8)]
        best = functools.reduce(jnp.maximum, tops)
        sums = sum(stats[e, 4:8, :] * jnp.exp(tops[e] - best) for e in range(8))
        hits = sum(stats[e, 8:12, :] for e in range(8))
        log_total = best + jnp.log(sums)
        log_col = jnp.concatenate([column(log_total[k : k + 1], 128) for k in range(4)], axis=0)
        hit_col = jnp.concatenate([column(hits[k : k + 1], 128) for k in range(4)], axis=0)
        loss = jnp.sum(
            jnp.where(counts[...] > 0, log_col - hit_col, 0.0), axis=0, keepdims=True
        )
        lane = lax.broadcasted_iota(jnp.int32, (1, 128), 1)
        small[6:7, :] = jnp.where(jnp.logical_and(lane == 0, dp == 0), loss, 0.0)
        shrink = jnp.exp(top_col - log_col)

        def slopes(start, size):
            ids = lax.broadcasted_iota(jnp.int32, (16 * PICKS, size), 1) + (dp * own + start)
            hit = jnp.where(ids == labels[...], 1.0, 0.0)
            block = (scores[:, pl.ds(start, size)] * shrink - hit) * counts[...]
            dlow[:, pl.ds(start, size)] = block.astype(BF16)

        over_tiles(slopes)
        for b in range(3):
            cols = pl.ds(b * 256, 256)
            daf[:, cols] = nn(dlow[...], table[:, cols])
        every.wait_send()
        span(picked, 3 * PICKS, pick_send, core_recv).wait_send()
        span(picked, 8 * PICKS, core_send, core_recv).wait_send()

    def swap(p, zz):
        return pltpu.make_async_remote_copy(
            src_ref=daf.at[rows(p, zz, 1 - c)],
            dst_ref=rx_core.at[pl.ds((2 * zz + p) * PICKS, PICKS)],
            send_sem=swap_send,
            recv_sem=swap_recv,
            device_id=other_core,
            device_id_type=MESH,
        )

    def back_to(p, k):
        zz = lax.rem(z + k, 4)
        return pltpu.make_async_remote_copy(
            src_ref=low.at[pl.ds(pl.multiple_of((2 * zz + p) * PICKS, PICKS), PICKS)],
            dst_ref=rx.at[z],
            send_sem=daf_send,
            recv_sem=daf_recv,
            device_id=(2 + p, 2 * zz + c),
            device_id_type=MESH,
        )

    def table_part(start, size):
        there = pl.ds(start, size)
        value = tn(dlow[:, there], af[...])
        fresh[there, :] = value
        pltpu.make_async_copy(fresh.at[there], d_table.at[there], zero_sem).start()
        folded = jnp.sum(value * value, axis=0, keepdims=True)
        small[7:8, :] += functools.reduce(
            jnp.add, [folded[:, k * 128 : (k + 1) * 128] for k in range(6)]
        )

    def third():
        forward_part()
        for zz in range(4):
            for p in range(2):
                swap(p, zz).start()
        table_part(own - own % HEAD_T, own % HEAD_T)
        span(rx_core, 8 * PICKS, swap_send, swap_recv).wait_recv()
        for zz in range(4):
            for p in range(2):
                there = pl.ds((2 * zz + p) * PICKS, PICKS)
                low[there, :] = (daf[rows(p, zz, c), :] + rx_core[there, :]).astype(BF16)
        for k in (1, 2, 3, 0):
            back_to(0, k).start()
            if k:
                back_to(1, k).start()

        def step(t, carry):
            table_part(pl.multiple_of(t * HEAD_T, HEAD_T), HEAD_T)
            return carry

        lax.fori_loop(0, own // HEAD_T, step, 0, unroll=True)
        rx[z] = low[pl.ds(pl.multiple_of((2 * z + 1) * PICKS, PICKS), PICKS), :]
        span(rx_core, 8 * PICKS, swap_send, swap_recv).wait_send()
        span(low, 7 * PICKS, daf_send, daf_recv).wait_send()
        span(rx, 3, daf_send, daf_recv).wait_recv()

    def second():
        span(picked, 4 * PICKS, pick_send, core_recv).wait_send()
        span(rx, 4, daf_send, daf_recv).wait_recv()

    pl.when(last)(third)
    pl.when(sec == 2)(second)

    def finish():
        summed = rx[0].astype(F32)
        for k in range(1, 4):
            summed = summed + rx[k].astype(F32)
        grad, dg_f = rms_back(mine[...].astype(F32), g_f, summed)
        for k in range(6):
            small[k : k + 1, :] = dg_f[:, k * 128 : (k + 1) * 128]
        ids = lax.broadcasted_iota(jnp.int32, (SP, PICKS), 0)
        spread = jnp.where(ids == pick_row, 1.0, 0.0).astype(BF16)
        rest = grad
        out = jnp.zeros((SP, D), F32)
        for _ in range(3):
            part = rest.astype(BF16)
            out = out + nn(spread, part)
            rest = rest - part.astype(F32)
        d_top[...] = out.astype(BF16)

    def none():
        d_top[...] = jnp.zeros_like(d_top)

    pl.when(upper)(finish)
    pl.when(jnp.logical_not(upper))(none)
    all_zero.wait()


def head_call(y, picks, info, gain, table):
    low = lambda *shape: pltpu.VMEM(shape, BF16)
    wide = lambda *shape: pltpu.VMEM(shape, F32)
    n = 16 * PICKS
    return pl.pallas_call(
        head_kernel,
        out_shape=(
            jax.ShapeDtypeStruct((SP, D), BF16),
            jax.ShapeDtypeStruct((OWN, D), F32),
            jax.ShapeDtypeStruct((8, 128), F32),
        ),
        in_specs=[VMEM] * 5,
        out_specs=(VMEM, ANY, VMEM),
        scratch_shapes=[
            low(PICKS, D),
            low(n, D),
            low(n, D),
            wide(n, OWN),
            low(n, OWN),
            pltpu.VMEM((n, 1), jnp.int32),
            wide(n, 1),
            wide(16, 128),
            wide(8, 16, 128),
            wide(n, D),
            wide(8 * PICKS, D),
            low(8 * PICKS, D),
            low(4, PICKS, D),
            wide(OWN, D),
            pltpu.SemaphoreType.DMA,
            pltpu.SemaphoreType.DMA,
            pltpu.SemaphoreType.DMA,
            pltpu.SemaphoreType.DMA((2, 4)),
        ]
        + [pltpu.SemaphoreType.DMA] * 8,
        compiler_params=pltpu.CompilerParams(
            collective_id=3, has_side_effects=True, vmem_limit_bytes=56 * 2**20
        ),
        name="head",
    )(y, picks, info, gain, table)


def open_anywhere(codes, labels, picks, classes, null_mask, starts, table, frequency):
    sec = lax.axis_index("section")
    d = lax.axis_index("dp")
    par = lax.rem(sec, 2)
    own = table.shape[0]
    row_index, counted, _, position = jax.vmap(row_layout)(starts, classes, null_mask, codes)
    picked_labels = jnp.take_along_axis(labels, picks, axis=1)
    picked_counts = jnp.take_along_axis(counted, picks, axis=1).astype(jnp.int32)
    row_index = jnp.pad(row_index, ((0, 0), (0, SP - SLOTS)), constant_values=-1)
    info = jnp.concatenate([row_index, picked_labels, picked_counts], axis=1)
    info = lax.all_gather(info, "dp", axis=0, tiled=True)
    all_labels = info[:, SP : SP + PICKS].reshape(-1)
    all_counts = info[:, SP + PICKS :].reshape(-1).astype(F32)
    gain_row = lax.slice_in_dim(table, VOCAB % own, VOCAB % own + 1)[0].astype(F32)
    holds = (sec == 3) & (d == VOCAB // own)
    g_f = lax.psum(jnp.where(holds, gain_row, 0.0), ("section", "dp"))
    position = jnp.pad(position[par], (0, SP - SLOTS))
    angles = position.astype(F32)[:, None] * frequency[None, :]
    cosine = jnp.tile(jnp.cos(angles), (1, 4))
    sine = jnp.tile(jnp.concatenate([-jnp.sin(angles), jnp.sin(angles)], axis=1), (1, 2))
    gathered = lax.all_gather(table, "dp", axis=0, tiled=True)[:WROWS]
    other = lax.ppermute(gathered, "section", [(0, 1), (1, 0), (2, 3), (3, 2)])
    weights = jnp.where((sec == 1) | (sec == 2), gathered, other)
    local = jnp.where(sec == 0, info[:, :SP].reshape(-1), -1) - d * own
    onehot = (local[:, None] == jnp.arange(own)[None, :]).astype(BF16)
    looked = (nn(onehot, table) * math.sqrt(D)).astype(BF16)
    looked = lax.psum_scatter(looked, "dp", scatter_dimension=0, tiled=True).reshape(2, SP, D)
    from_first = lax.ppermute(looked[1], "section", [(0, 1)])
    x0 = jnp.where(sec == 0, looked[0], from_first)
    return weights, x0, local, all_labels, all_counts, g_f, cosine, sine


def head_anywhere(y, my_picks, all_labels, all_counts, g_f, table):
    sec = lax.axis_index("section")
    d = lax.axis_index("dp")
    n_sec = lax.axis_size("section")
    n_dp = lax.axis_size("dp")
    own = table.shape[0]
    picked = jnp.take(y, my_picks, axis=0)
    all_picked = lax.all_gather(picked, ("section", "dp"), axis=0, tiled=False)
    all_picked = all_picked.reshape(n_sec, n_dp, PICKS, D)[2:].transpose(1, 0, 2, 3)
    all_picked = all_picked.reshape(-1, D).astype(F32)
    af = jnp.where(sec == 3, rms_scale(all_picked, g_f), 0.0).astype(BF16)
    vocab_ids = d * own + jnp.arange(own)
    logits = jnp.where(vocab_ids[None, :] < VOCAB, nt(af, table), NEG)
    local_max = jnp.max(logits, axis=1)
    hit = vocab_ids[None, :] == all_labels[:, None]
    sums = jnp.stack(
        [
            local_max,
            jnp.sum(jnp.exp(logits - local_max[:, None]), axis=1),
            jnp.sum(jnp.where(hit, logits, 0.0), axis=1),
        ]
    )
    every = lax.all_gather(sums, "dp", axis=0, tiled=False)
    top = jnp.max(every[:, 0], axis=0)
    total = jnp.sum(every[:, 1] * jnp.exp(every[:, 0] - top), axis=0)
    target = jnp.sum(every[:, 2], axis=0)
    log_total = top + jnp.log(total)
    loss_part = jnp.where(
        (sec == 3) & (d == 0), jnp.sum(jnp.where(all_counts > 0, log_total - target, 0.0)), 0.0
    )
    dlogits = (jnp.exp(logits - log_total[:, None]) - hit.astype(F32)) * all_counts[:, None]
    dlogits = jnp.where(sec == 3, dlogits, 0.0).astype(BF16)
    d_table = tn(dlogits, af)
    daf = lax.psum(nn(dlogits, table), "dp")
    daf = lax.dynamic_slice_in_dim(daf, d * 2 * PICKS, 2 * PICKS).reshape(2, PICKS, D)
    daf = jnp.where(sec == 3, daf[1], lax.ppermute(daf[0], "section", [(3, 2)]))
    d_own, dg_f = rms_pull(picked.astype(F32), g_f, daf)
    dg_f = jnp.where(sec >= 2, dg_f, 0.0)
    spread = (jnp.arange(SP)[:, None] == my_picks[None, :]).astype(F32)
    d_top = jnp.dot(spread, d_own, precision=lax.Precision.HIGHEST).astype(BF16)
    return d_top, d_table, dg_f, loss_part


UPDATE_ROWS = 272


def update_kernel(rate, gain_block, gain_row, totals, grad, master, momentum, average, out_m, out_v, out_a):
    block = pl.program_id(0)
    value = grad[...]
    sec = lax.axis_index("section")
    dp = lax.axis_index("dp")
    here = jnp.logical_and(jnp.logical_and(sec == 3, dp == VOCAB // OWN), block == gain_block)
    ids = lax.broadcasted_iota(jnp.int32, value.shape, 0)
    gain = jnp.concatenate([totals[k : k + 1, :] for k in range(6)], axis=1)
    value = value + jnp.where(jnp.logical_and(ids == gain_row, here), gain, 0.0)
    scale = jnp.minimum(1.0, clip_limit / (totals[8:9, 0:1] + norm_eps))
    clipped = value * scale
    new_momentum = momentum_decay * momentum[...] + clipped
    new_master = master[...] - rate * (clipped + momentum_decay * new_momentum)
    out_v[...] = new_momentum
    out_m[...] = new_master
    out_a[...] = average_decay * average[...] + (1.0 - average_decay) * new_master


def update(rate, totals, grad, master, momentum, average):
    rows = pl.BlockSpec((UPDATE_ROWS, D), lambda i: (i, 0))
    like = jax.ShapeDtypeStruct((OWN, D), F32)
    at = VOCAB % OWN
    return pl.pallas_call(
        functools.partial(update_kernel, rate, at // UPDATE_ROWS, at % UPDATE_ROWS),
        grid=(OWN // UPDATE_ROWS,),
        out_shape=(like, like, like),
        in_specs=[pl.BlockSpec((16, 128), lambda i: (0, 0))] + [rows] * 4,
        out_specs=(rows, rows, rows),
        compiler_params=pltpu.CompilerParams(vmem_limit_bytes=47 * 2**20),
        name="update",
    )(totals, grad, master, momentum, average)


def shards(codes, labels, picks, classes, null_mask, starts, master, momentum, average):
    sec = lax.axis_index("section")
    d = lax.axis_index("dp")
    n_dp = lax.axis_size("dp")
    n_sec = lax.axis_size("section")
    par = lax.rem(sec, 2)
    own = master.shape[0]
    learn_rate = rate_factor * math.sqrt(own * n_sec * n_dp)
    beside = [(0, 1), (1, 0), (2, 3), (3, 2)]
    fast = n_sec == 4 and n_dp == 8 and own == OWN
    gain_at = VOCAB // own
    frequency = rope_base ** (-jnp.arange(HD // 2, dtype=F32) * 2.0 / HD)

    if fast:
        wide = jnp.tile(frequency[None, :], (1, 4))
        weights, x0, info, gain, cosine, sine, table = gather_and_embed(
            master, codes, labels, picks, starts, classes, null_mask, wide
        )
        all_index = info[:, :2, :SP].reshape(-1)
        local = jnp.where(sec == 0, all_index, -1) - d * own
    else:
        table = master.astype(BF16)
        opened = open_anywhere(codes, labels, picks, classes, null_mask, starts, table, frequency)
        weights, x0, local, all_labels, all_counts, g_f, cosine, sine = opened
    around = (cosine, sine, starts)

    x = forward_call(False, x0, weights, *around)[0]
    y, *kept = forward_call(True, x, weights, *around)

    if fast:
        d_top, d_table, small = head_call(y, picks, info, gain, table)
    else:
        d_top, d_table, dg_f, loss_part = head_anywhere(
            y, picks[par], all_labels, all_counts, g_f, table
        )

    once = backward_call(True, d_top, x, weights, *around, kept)
    dx0, left, right, tail = lax.cond(
        sec < 2,
        lambda: tuple(backward_call(False, once[0], x, weights, *around, kept)),
        lambda: tuple(once),
    )

    if fast:
        grad, squares = reduce_and_scatter(left, right, tail, d_table, dx0, local[None, :])
        totals = share_norm(small, squares, n_sec, n_dp)
        count_sum = jnp.sum(info[:, 4:6, :PICKS].astype(F32))
        updated = update(learn_rate, totals, grad, master, momentum, average)
        return totals[6, 0], count_sum, totals[8, 0], *updated
    else:
        grads = matrix_gradients(left, right, tail)
        grads = grads.astype(F32) + lax.ppermute(grads, "section", beside).astype(F32)
        grads = jnp.pad(grads.astype(BF16), ((0, own * n_dp - WROWS), (0, 0)))
        grad = lax.psum_scatter(grads, "dp", scatter_dimension=0, tiled=True).astype(F32)
        grad = jnp.where(sec == 3, d_table, grad)
        pair = jnp.stack([dx0, lax.ppermute(dx0, "section", [(1, 0)])])
        all_dx = lax.all_gather(pair, "dp", axis=0, tiled=True).reshape(-1, D)
        onehot = (jnp.arange(own)[:, None] == local[None, :]).astype(BF16)
        grad = jnp.where(sec == 0, nn(onehot, all_dx) * math.sqrt(D), grad)
        totals = (dg_f, jnp.sum(grad * grad), loss_part)
        dg_f, squares, loss_sum = lax.psum(totals, ("section", "dp"))
        count_sum = jnp.sum(all_counts)
        grad_norm = jnp.sqrt(squares + jnp.sum(dg_f * dg_f))
    gain_here = (jnp.arange(own) == VOCAB % own)[:, None] & (sec == 3) & (d == gain_at)
    grad = grad + jnp.where(gain_here, dg_f[None, :], 0.0)
    clipped = grad * jnp.minimum(1.0, clip_limit / (grad_norm + norm_eps))
    new_momentum = momentum_decay * momentum + clipped
    new_master = master - learn_rate * (clipped + momentum_decay * new_momentum)
    new_average = average_decay * average + (1.0 - average_decay) * new_master
    return loss_sum, count_sum, grad_norm, new_master, new_momentum, new_average


def solution(mesh):
    split = P("dp", None)
    whole = P(("section", "dp"), None)
    return jax.shard_map(
        shards,
        mesh=mesh,
        in_specs=(split,) * 6 + (whole,) * 3,
        out_specs=(P(), P(), P(), whole, whole, whole),
        check_vma=False,
    )
```

```python
import functools
import math

import jax
import jax.numpy as jnp
from jax import lax
from jax.experimental import pallas as pl
from jax.experimental.pallas import tpu as pltpu
from jax.sharding import PartitionSpec as P

D = 768
HEADS = 12
HD = 64
FF = 2048
VOCAB = 16384
CLASSES = 1001
SLOTS = 264
SP = 272
PICKS = 32
SEGS = 3
MATS = 4 * D + 3 * FF
WROWS = 9232

F32 = jnp.float32
BF16 = jnp.bfloat16

rope_base = 10000.0
clip_limit = 1.0
rate_factor = 0.25
momentum_decay = 0.9
average_decay = 0.8
norm_eps = 1e-06


def nn(left, right):
    return jnp.dot(left, right, preferred_element_type=F32)


def tn(left, right):
    return lax.dot_general(left, right, (((0,), (0,)), ((), ())), preferred_element_type=F32)


def nt(left, right):
    return lax.dot_general(left, right, (((1,), (1,)), ((), ())), preferred_element_type=F32)


def rms_scale(value_in, gain):
    return (
        value_in * lax.rsqrt(jnp.mean(value_in * value_in, axis=-1, keepdims=True) + norm_eps) * gain
    )


def rms_pull(value_in, gain, grad):
    inv = lax.rsqrt(jnp.mean(value_in * value_in, axis=-1, keepdims=True) + norm_eps)
    unit = value_in * inv
    scaled = grad * gain
    grad_in = inv * (scaled - unit * jnp.mean(scaled * unit, axis=-1, keepdims=True))
    return grad_in, jnp.sum(grad * unit, axis=0)


def row_layout(starts_row, classes_row, null_row, codes_row):
    slot_ids = jnp.arange(SLOTS, dtype=jnp.int32)
    segment = jnp.sum((starts_row[None, 1:] <= slot_ids[:, None]).astype(jnp.int32), axis=1)
    seg_start = jnp.sum(
        jnp.where(segment[:, None] == jnp.arange(SEGS + 1)[None, :], starts_row[None, :], 0), axis=1
    )
    position = slot_ids - seg_start
    live_end = starts_row[SEGS]
    is_first = (position == 0) & (slot_ids < live_end)
    clamped = jnp.minimum(segment, SEGS - 1)
    hit = clamped[:, None] == jnp.arange(SEGS)[None, :]
    class_row = jnp.sum(
        jnp.where(hit, jnp.where(null_row > 0, CLASSES - 1, classes_row)[None, :], 0), axis=1
    )
    row_index = jnp.where(is_first, VOCAB + class_row, codes_row)
    following = jnp.concatenate([segment[1:], jnp.full((1,), SEGS + 1, jnp.int32)])
    counted = (following == segment) & (slot_ids + 1 < live_end)
    return row_index, counted, segment, position


MESH = pl.DeviceIdType.MESH
ANY = pl.BlockSpec(memory_space=pl.ANY)
VMEM = pl.BlockSpec(memory_space=pltpu.VMEM)
SMEM = pl.BlockSpec(memory_space=pltpu.SMEM)

OWN = 2176
SPLIT = 1152
COUNT = (18, 16, 18, 16, 11)
ROWS = (64, 64, 64, 64, 48)
HELD = (0, SPLIT, OWN, OWN + SPLIT, 2 * OWN)
LARGE = (16, 14, 16, 14, 11)
SMALL = 4
SMALL_ROWS = 32
LANE = 2 * OWN + 11 * 48
LAG = 2
WINDOW = 2
HOP = 2
PIECES = ((0, 64), (64, 64), (128, 64), (192, 64), (256, 16))
TURN = 6
CHOP = 4
CLAG = 3
AHEAD = 4
CWAIT = 6


def class_base(k, lane):
    if k == 4:
        return 4 * OWN
    return OWN * (2 * (k // 2) + lane) + SPLIT * (k % 2)


def place():
    sec = lax.axis_index("section")
    dp = lax.axis_index("dp")
    z = dp // 2
    c = lax.rem(dp, 2)
    par = lax.rem(sec, 2)
    home = jnp.logical_or(sec == 1, sec == 2)
    return sec, dp, z, c, par, home


def greet_neighbours(sec, dp, z, c, par, turns):
    barrier = pltpu.get_barrier_semaphore()

    def greet(s, e):
        pl.semaphore_signal(barrier, 1, device_id=(s, e), device_id_type=MESH)

    greet(sec, dp + 1 - 2 * c)
    greet(sec + 1 - 2 * par, dp)
    pl.when(z > 0)(lambda: greet(sec, dp - 2))
    pl.when(z < 3)(lambda: greet(sec, dp + 2))
    count = 2 + (z > 0).astype(jnp.int32) + (z < 3).astype(jnp.int32)
    for sender, receiver in turns:
        pl.when(sec == receiver)(lambda sender=sender: greet(sender, dp))
        count = count + (sec == sender).astype(jnp.int32)
    pl.semaphore_wait(barrier, count)


def hop_targets(sec, dp, c, par):
    return {
        "up": (sec, dp + 2),
        "down": (sec, dp - 2),
        "x": (sec + 1 - 2 * par, dp),
        "core": (sec, dp + 1 - 2 * c),
    }


HOPS = ("up", "down", "x", "core")


def tree(z, c, home):
    both = jnp.logical_and
    either = jnp.logical_or
    no = jnp.logical_not
    far = z >= 2
    mid = both(z >= 1, z <= 2)
    never = z < 0
    away = no(home)
    as_int = lambda flag: flag.astype(jnp.int32)
    out = []
    for block in (0, 1):
        for half in (0, 1):
            mine = home if half == 0 else away
            other = no(mine)
            source = both(z == block, home)
            if half == 0:
                early = (lambda j: j < TURN) if block == 0 else (lambda j: j < 0)
                near_x = lambda j, block=block, early=early: both(z == 1 - block, early(j))
                hop_x = lambda j, near_x=near_x: both(home, near_x(j))
                got_x = lambda j, near_x=near_x: both(away, near_x(j))
                along = lambda j, early=early: either(home, no(early(j)))
            else:
                hop_x = lambda j, block=block: both(away, z == 1 - block)
                got_x = lambda j, block=block: both(home, z == 1 - block)
                along = lambda j: away
            at_owner = both(z == block, away)
            if block == 0:
                up = lambda j, along=along, mine=mine: either(both(z == 0, along(j)), both(mid, mine))
                down = lambda j: never
                from_up = lambda j: never
            else:
                up = lambda j, mine=mine: both(mid, mine)
                down = lambda j, along=along: both(z == 1, along(j))
                from_up = lambda j, got_x=got_x: both(z == 0, no(got_x(j)))
            send_x = lambda j, source=source, mine=mine, hop_x=hop_x: either(
                either(source, both(far, mine)), hop_x(j)
            )
            from_x = lambda j, at_owner=at_owner, other=other, got_x=got_x: either(
                either(at_owner, both(far, other)), got_x(j)
            )
            from_down = lambda j, source=source, from_x=from_x, from_up=from_up: no(
                either(source, either(from_x(j), from_up(j)))
            )
            depth = jnp.abs(z - block) + as_int(far) * (half + as_int(other))
            if half == 0:
                depth = depth + (1 - as_int(far)) * as_int(away)
            else:
                depth = depth + (1 - as_int(far)) * jnp.where(
                    away, 1, 2 * as_int(z == 1 - block)
                )
            out.append(
                (source, dict(up=up, down=down, x=send_x), dict(up=from_up, down=from_down, x=from_x), depth)
            )
    lane0 = c == 0
    source = both(both(z == 2, home), lane0)
    sends = dict(
        up=lambda j: both(z == 2, lane0),
        down=lambda j: both(mid, lane0),
        x=lambda j: source,
    )
    parents = dict(
        up=lambda j: both(z <= 1, lane0),
        down=lambda j: both(z == 3, lane0),
        x=lambda j: both(both(z == 2, away), lane0),
    )
    out.append((source, sends, parents, jnp.abs(z - 2) + as_int(away)))
    return out


def segment_of(starts, r, slot):
    bounds = [starts[r, j] for j in range(SEGS + 1)]
    count = lambda at: functools.reduce(
        jnp.add, [(at >= bounds[j]).astype(jnp.int32) for j in range(1, SEGS + 1)]
    )
    segment = count(slot)
    begin = jnp.where(
        segment == 0, bounds[0], jnp.where(segment == 1, bounds[1], jnp.where(segment == 2, bounds[2], bounds[3]))
    )
    counted = jnp.logical_and(count(slot + 1) == segment, slot + 1 < bounds[SEGS])
    return segment, slot - begin, counted, slot < bounds[SEGS]


def open_kernel(
    master, codes, labels, picks, starts, classes, nulls, frequency, out, x0, info, gain, cosine,
    sine, table, exact, master_sem, recv_sem, recv_c, core_sem, send_sem, sent, mine, rx_core, rx_up, rx_down,
    swap_send, swap_recv, x_send, x_recv, line_send, up_recv, down_recv, last_send, last_recv,
    note, note_send, note_recv, gain_send, gain_recv,
):
    sec, dp, z, c, par, home = place()
    targets = hop_targets(sec, dp, c, par)
    classes_of = tree(z, c, home)
    gain_dp = VOCAB // (OWN)
    holds_gain = jnp.logical_and(sec == 3, dp == gain_dp)

    parts = [pl.ds(k * (OWN // 4), OWN // 4) for k in range(4)]
    def place_own(part, value):
        start = pl.multiple_of(dp * OWN + part.start, 16)
        out[pl.ds(start, part.size), :] = value

    fetch = [
        pltpu.make_async_copy(master.at[part], exact.at[part], master_sem.at[k])
        for k, part in enumerate(parts)
    ]
    for one in fetch:
        one.start()

    barrier = pltpu.get_barrier_semaphore()

    def greet(s, e):
        pl.semaphore_signal(barrier, 1, device_id=(s, e), device_id_type=MESH)

    for k in range(1, 8):
        greet(sec, lax.rem(dp + k, 8))
    greet(sec + 1 - 2 * par, dp)
    pl.when(sec == 2)(lambda: greet(0, dp))
    pl.when(sec == 1)(lambda: greet(2, dp))
    pl.when(jnp.logical_and(sec == 2, dp != gain_dp))(lambda: greet(3, gain_dp))

    slot_row = lax.broadcasted_iota(jnp.int32, (1, SLOTS), 1)
    note[...] = jnp.full(note.shape, -1, jnp.int32)
    for r in range(2):
        segment, position, _, live = segment_of(starts, r, slot_row)
        names = [classes[r, j] + (CLASSES - 1 - classes[r, j]) * nulls[r, j] for j in range(SEGS)]
        name = jnp.where(segment == 0, names[0], jnp.where(segment == 1, names[1], names[2]))
        opens = jnp.logical_and(position == 0, live)
        note[r : r + 1, :SLOTS] = jnp.where(opens, VOCAB + name, codes[r : r + 1, :])
        chosen = picks[r : r + 1, :]
        ids = lax.broadcasted_iota(jnp.int32, (SLOTS, PICKS), 0)
        label_col = column(labels[r : r + 1, :], SLOTS)
        note[2 + r : 3 + r, :PICKS] = jnp.sum(
            jnp.where(ids == chosen, label_col, 0), axis=0, keepdims=True
        )
        note[4 + r : 5 + r, :PICKS] = segment_of(starts, r, chosen)[2].astype(jnp.int32)
    info[dp] = note[...]
    for one, part in zip(fetch, parts):
        one.wait()
        value = exact[part, :].astype(BF16)
        table[part, :] = value
        pl.when(jnp.logical_and(home, z < 2))(lambda part=part, value=value: place_own(part, value))
    pl.when(classes_of[4][0])(
        lambda: place_own(pl.ds(0, 11 * 48), exact[pl.ds(0, 11 * 48), :].astype(BF16))
    )
    count = 8 + jnp.logical_or(sec == 0, sec == 2).astype(jnp.int32)
    pl.semaphore_wait(barrier, count + 7 * holds_gain.astype(jnp.int32))
    for k in range(1, 8):
        pltpu.make_async_remote_copy(
            src_ref=note,
            dst_ref=info.at[dp],
            send_sem=note_send,
            recv_sem=note_recv,
            device_id=(sec, lax.rem(dp + k, 8)),
            device_id_type=MESH,
        ).start()
    noted = pltpu.make_async_remote_copy(
        src_ref=info.at[pl.ds(0, 7)],
        dst_ref=info.at[pl.ds(0, 7)],
        send_sem=note_send,
        recv_sem=note_recv,
        device_id=targets["core"],
        device_id_type=MESH,
    )

    gain_rows = table.at[pl.ds(VOCAB % (OWN), 16)]

    def gain_to(s, e):
        return pltpu.make_async_remote_copy(
            src_ref=gain_rows,
            dst_ref=gain,
            send_sem=gain_send,
            recv_sem=gain_recv,
            device_id=(s, e),
            device_id_type=MESH,
        )

    def send_gain():
        for e in range(8):
            gain_to(2, e).start()
            if e != gain_dp:
                gain_to(3, e).start()
        gain[...] = gain_rows[...]

    pl.when(holds_gain)(send_gain)

    def copy(k, hop, offset, rows, recv, slot):
        part = out.at[pl.ds(pl.multiple_of(class_base(k, c) + offset, 16), rows)]
        return pltpu.make_async_remote_copy(
            src_ref=part,
            dst_ref=part,
            send_sem=send_sem.at[k, HOPS.index(hop), slot],
            recv_sem=recv,
            device_id=targets[hop],
            device_id_type=MESH,
        )

    def piece(k, j, small):
        source, sends, _, _ = classes_of[k]
        recv = recv_c.at[j] if k == 4 else recv_sem.at[k, j]
        slot = lax.rem(j, WINDOW)
        rows = SMALL_ROWS if small else ROWS[k]
        offset = ROWS[k] * LARGE[k] + rows * (j - LARGE[k]) if small else rows * j

        def send(hop):
            to = core_sem.at[k] if hop == "core" else recv
            before = j >= WINDOW if hop == "core" else jnp.logical_and(j >= WINDOW, sends[hop](j - WINDOW))
            if small:
                was_large = j < LARGE[k] + WINDOW
                wide_one = copy(k, hop, 0, ROWS[k], to, slot)
                pl.when(jnp.logical_and(before, was_large))(wide_one.wait_send)
                before = jnp.logical_and(before, jnp.logical_not(was_large))
            one = copy(k, hop, offset, rows, to, slot)
            pl.when(before)(one.wait_send)
            one.start()

        pl.when(jnp.logical_not(source))(copy(k, "x", offset, rows, recv, slot).wait_recv)
        for hop in HOPS[:3]:
            pl.when(sends[hop](j))(lambda hop=hop: send(hop))
        send("core")

    first = sec == 0
    second = sec == 2

    def slot(k):
        return pl.ds(pl.multiple_of(k * SP, 16), SP)

    def order(i):
        low = (z <= 1).astype(jnp.int32)
        return low * (3 - i) + (1 - low) * i

    def swap(k):
        return pltpu.make_async_remote_copy(
            src_ref=sent.at[slot(k)],
            dst_ref=rx_core.at[slot(k)],
            send_sem=swap_send,
            recv_sem=swap_recv.at[k],
            device_id=targets["core"],
            device_id_type=MESH,
        )

    def cross(zz):
        return pltpu.make_async_remote_copy(
            src_ref=mine.at[slot(4 + zz)],
            dst_ref=mine.at[slot(zz)],
            send_sem=x_send,
            recv_sem=x_recv.at[zz],
            device_id=(2, dp),
            device_id_type=MESH,
        )

    def piece_of(k, q):
        start, size = PIECES[q]
        return pl.ds(pl.multiple_of(k * SP + start, 16), size)

    def go(zz, q, ref, recv, hop):
        return pltpu.make_async_remote_copy(
            src_ref=mine.at[piece_of(zz, q)],
            dst_ref=ref.at[piece_of(zz, q)],
            send_sem=line_send,
            recv_sem=recv.at[zz, q],
            device_id=targets[hop],
            device_id_type=MESH,
        )

    def go_up(zz, q):
        return go(zz, q, rx_down, down_recv, "up")

    def go_down(zz, q):
        return go(zz, q, rx_up, up_recv, "down")

    def add(there, ref):
        mine[there, :] = (mine[there, :].astype(F32) + ref[there, :].astype(F32)).astype(BF16)

    def look(row):
        local = column(info[row // 2, pl.ds(lax.rem(row, 2), 1), :][:, :SP], SP) - dp * OWN
        ids = lax.broadcasted_iota(jnp.int32, (SP, OWN), 1)
        onehot = jnp.where(ids == local, 1.0, 0.0).astype(BF16)
        return (nn(onehot, table[...]) * math.sqrt(D)).astype(BF16)

    def lookup(b):
        zz = order(b // 2)
        p = 1 - lax.rem(b, 2)
        k = 4 * p + zz
        sent[slot(k), :] = look(2 * (2 * zz + 1 - c) + p)
        swap(k).start()
        mine[slot(k), :] = look(2 * (2 * zz + c) + p)
        swap(k).wait_recv()
        add(slot(k), rx_core)
        pl.when(p == 1)(lambda: cross(zz).start())

    def chain(zz, q):
        def from_below():
            go_up(zz, q).wait_recv()
            add(piece_of(zz, q), rx_down)

        def from_above():
            go_down(zz, q).wait_recv()
            add(piece_of(zz, q), rx_up)

        if q == 0:
            pl.when(second)(cross(zz).wait_recv)
        pl.when(jnp.logical_and(zz >= z, z > 0))(from_below)
        pl.when(jnp.logical_and(zz <= z, z < 3))(from_above)
        pl.when(zz > z)(lambda: go_up(zz, q).start())
        pl.when(zz < z)(lambda: go_down(zz, q).start())

    def chains(i):
        for o in range(4):
            zz = order(o)
            hops = jnp.maximum(
                z * (zz >= z).astype(jnp.int32), (3 - z) * (zz <= z).astype(jnp.int32)
            )
            for q in range(5):
                now = i == 2 * o + 2 + sec + HOP * hops + q
                pl.when(now)(lambda zz=zz, q=q: chain(zz, q))

    segment, position, _, _ = segment_of(starts, par, lax.broadcasted_iota(jnp.int32, (SP, 128), 0))
    angles = position.astype(F32) * frequency[...]
    lanes = lax.broadcasted_iota(jnp.int32, (SP, 128), 1)
    cosine[...] = jnp.cos(angles)
    sine[...] = jnp.where(lax.rem(lanes, 64) < 32, -1.0, 1.0) * jnp.sin(angles)
    noted.wait_recv()

    def step(i, carry):
        for k in range(5):
            j = i - LAG * classes_of[k][3]
            now = jnp.logical_and(j >= 0, j < LARGE[k])
            if k == 4:
                now = jnp.logical_and(now, c == 0)
            pl.when(now)(lambda k=k, j=j: piece(k, j, False))
            if k < 4:
                now = jnp.logical_and(j >= LARGE[k], j < LARGE[k] + SMALL)
                pl.when(now)(lambda k=k, j=j: piece(k, j, True))
        pl.when(jnp.logical_and(first, i < 8))(lambda: lookup(i))
        pl.when(jnp.logical_or(first, second))(lambda: chains(i))
        pl.when(jnp.logical_and(second, i == last_step))(lambda: last().start())
        return carry

    last_step = 6 + 2 + 2 + 3 * HOP + 4 + 1

    def last():
        return pltpu.make_async_remote_copy(
            src_ref=mine.at[slot(z)],
            dst_ref=x0,
            send_sem=last_send,
            recv_sem=last_recv,
            device_id=(1, dp),
            device_id_type=MESH,
        )

    lax.fori_loop(0, max(LARGE[0] + SMALL + 5 * LAG, last_step + 1), step, 0)

    def blocks(count, sem):
        return pltpu.make_async_remote_copy(
            src_ref=mine.at[pl.ds(0, count * SP)],
            dst_ref=mine.at[pl.ds(0, count * SP)],
            send_sem=sem,
            recv_sem=sem,
            device_id=targets["core"],
            device_id_type=MESH,
        )

    def end_first():
        blocks(8, swap_send).wait_send()
        blocks(4, x_send).wait_send()
        blocks(3, line_send).wait_send()
        x0[...] = mine[slot(z), :]

    def end_second():
        blocks(3, line_send).wait_send()
        last().wait_send()

    def none():
        x0[...] = jnp.zeros_like(x0)

    pl.when(first)(end_first)
    pl.when(second)(end_second)
    pl.when(sec == 1)(last().wait_recv)
    pl.when(sec >= 2)(none)

    noted.wait_send()

    def gain_sent():
        for e in range(15):
            gain_to(2, 0).wait_send()

    pl.when(holds_gain)(gain_sent)
    pl.when(jnp.logical_and(sec >= 2, jnp.logical_not(holds_gain)))(gain_to(2, dp).wait_recv)

    def drain(k):
        count, rows = (LARGE[4], ROWS[4]) if k == 4 else (LARGE[k] + SMALL, SMALL_ROWS)
        _, sends, _, _ = classes_of[k]
        for j in range(count - WINDOW, count):
            for hop in HOPS[:3]:
                one = copy(k, hop, 0, rows, core_sem.at[k], j % WINDOW)
                pl.when(sends[hop](j))(one.wait_send)
            copy(k, "core", 0, rows, core_sem.at[k], j % WINDOW).wait_send()
        if k == 0:
            for j in range(TURN - WINDOW, TURN):
                one = copy(k, "x", 0, ROWS[0], core_sem.at[k], j % WINDOW)
                last_one = jnp.logical_not(sends["x"](j + WINDOW))
                pl.when(jnp.logical_and(sends["x"](j), last_one))(one.wait_send)

    def came(k):
        count, rows = COUNT[k], ROWS[k]
        part = out.at[pl.ds(pl.multiple_of(class_base(k, 1 - c), 16), count * rows)]
        pltpu.make_async_remote_copy(
            src_ref=part,
            dst_ref=part,
            send_sem=send_sem.at[k, 3, 0],
            recv_sem=core_sem.at[k],
            device_id=targets["core"],
            device_id_type=MESH,
        ).wait_recv()

    for k in range(4):
        drain(k)
        came(k)
    pl.when(c == 0)(lambda: drain(4))
    pl.when(c == 1)(lambda: came(4))


def gather_and_embed(master, codes, labels, picks, starts, classes, nulls, frequency):
    rows = lambda n: pltpu.VMEM((n * SP, D), BF16)
    return pl.pallas_call(
        open_kernel,
        out_shape=(
            jax.ShapeDtypeStruct((WROWS, D), BF16),
            jax.ShapeDtypeStruct((SP, D), BF16),
            jax.ShapeDtypeStruct((8, 8, 384), jnp.int32),
            jax.ShapeDtypeStruct((16, D), BF16),
            jax.ShapeDtypeStruct((SP, 128), F32),
            jax.ShapeDtypeStruct((SP, 128), F32),
            jax.ShapeDtypeStruct((OWN, D), BF16),
        ),
        in_specs=[ANY] + [VMEM] * 3 + [SMEM] * 3 + [VMEM],
        out_specs=(VMEM,) * 7,
        scratch_shapes=[
            pltpu.VMEM((OWN, D), F32),
            pltpu.SemaphoreType.DMA((4,)),
            pltpu.SemaphoreType.DMA((4, 20)),
            pltpu.SemaphoreType.DMA((11,)),
            pltpu.SemaphoreType.DMA((5,)),
            pltpu.SemaphoreType.DMA((5, 4, WINDOW)),
            rows(8),
            rows(8),
            rows(8),
            rows(4),
            rows(4),
            pltpu.SemaphoreType.DMA,
            pltpu.SemaphoreType.DMA((8,)),
            pltpu.SemaphoreType.DMA,
            pltpu.SemaphoreType.DMA((4,)),
            pltpu.SemaphoreType.DMA,
            pltpu.SemaphoreType.DMA((4, 5)),
            pltpu.SemaphoreType.DMA((4, 5)),
            pltpu.SemaphoreType.DMA,
            pltpu.SemaphoreType.DMA,
            pltpu.VMEM((8, 384), jnp.int32),
        ]
        + [pltpu.SemaphoreType.DMA] * 4,
        compiler_params=pltpu.CompilerParams(
            collective_id=0, has_side_effects=True, vmem_limit_bytes=56 * 2**20
        ),
        name="gather_and_embed",
    )(master, codes, labels, picks, starts, classes, nulls, frequency)


def close_kernel(
    left_any, right_any, tail, start, block, info, out, squares, left, right, loc, sent, rx_core,
    rx_up, rx_down, rx_x, summed, ring, all_dx, load_sem, core_sem, recv_sem, recv_c, core_send,
    send_sem, ring_sem, dx_own, dx_send, line_recv, cross_recv, turn_recv, dx_core_send,
    dx_core_recv, index, ready,
):
    sec, dp, z, c, par, home = place()
    targets = hop_targets(sec, dp, c, par)
    classes = tree(z, c, home)
    loads = [
        pltpu.make_async_copy(left_any, left, load_sem.at[0]),
        pltpu.make_async_copy(right_any, right, load_sem.at[1]),
    ]
    for one in loads:
        one.start()
    del start
    greet_neighbours(sec, dp, z, c, par, ((1, 2), (0, 2)))
    pl.when(sec == 0)(
        lambda: pl.semaphore_signal(ready, 1, device_id=(2, dp), device_id_type=MESH)
    )
    for one in loads:
        one.wait()

    def place_of(hop, k, j):
        offset = j * ROWS[k]
        if hop == "down":
            base = (0, 0, 0, SPLIT, OWN)[k]
        elif hop == "up":
            base = (0, SPLIT, OWN, OWN, OWN + SPLIT)[k]
        else:
            base = HELD[k]
        return pl.ds(pl.multiple_of(base + offset, 16), ROWS[k])

    def gradient(first_row, size):
        first_row = jnp.int32(first_row)
        bounds = (D, 2 * D, 3 * D, 4 * D, 4 * D + 2 * FF)
        matrix = functools.reduce(
            jnp.add, [(first_row >= bound).astype(jnp.int32) for bound in bounds]
        )
        cols = pl.ds(pl.multiple_of(first_row, 128), size)
        return tn(left[:, cols], right[matrix]).astype(BF16)

    def core_copy(k, offset, rows, sem):
        part = pl.ds(pl.multiple_of(HELD[k] + offset, 16), rows)
        return pltpu.make_async_remote_copy(
            src_ref=sent.at[part],
            dst_ref=rx_core.at[part],
            send_sem=core_send,
            recv_sem=sem,
            device_id=targets["core"],
            device_id_type=MESH,
        )

    def form(k, t):
        there = pl.ds(pl.multiple_of(HELD[k] + 128 * t, 128), 128)
        sent[there, :] = gradient(class_base(k, 1 - c) + 128 * t, 128)
        core_copy(k, 128 * t, 128, core_sem.at[k, t]).start()
        loc[there, :] = gradient(class_base(k, c) + 128 * t, 128)

    last_rows = 11 * 48

    def form_last(into):
        for t in range(4):
            into[pl.ds(HELD[4] + 128 * t, 128), :] = gradient(4 * OWN + 128 * t, 128)
        into[pl.ds(HELD[4] + 512, 16), :] = tail[...]

    def form_for_other():
        form_last(sent)
        core_copy(4, 0, last_rows, core_sem.at[4, 0]).start()

    squares[...] = jnp.zeros_like(squares)

    def count_squares(value):
        folded = value * value
        size = folded.shape[0]
        while size > 8 and size % 16 == 0:
            size //= 2
            folded = folded[:size] + folded[size:]
        for part in range(size // 8):
            for n in range(D // 128):
                squares[...] += folded[part * 8 : (part + 1) * 8, n * 128 : (n + 1) * 128]

    rx = dict(up=rx_up, down=rx_down, x=rx_x)

    def onward(k, hop, j):
        back = dict(up="down", down="up", x="x")[hop]
        return landing(k, back, hop, j)

    def landing(k, back, hop, j):
        index = ("up", "down", "x").index(back)
        part = pl.ds(pl.multiple_of(HELD[k] + j * ROWS[k], 16), ROWS[k])
        return pltpu.make_async_remote_copy(
            src_ref=loc.at[part],
            dst_ref=rx[back].at[place_of(back, k, j)],
            send_sem=send_sem.at[k],
            recv_sem=recv_c.at[index, j] if k == 4 else recv_sem.at[index, k, j],
            device_id=targets[hop],
            device_id_type=MESH,
        )

    def gathered(k, j):
        part = pl.ds(pl.multiple_of(HELD[k] + j * ROWS[k], 16), ROWS[k])
        if k == 4:
            pl.when(j == 0)(lambda: core_copy(4, 0, last_rows, core_sem.at[4, 0]).wait_recv())
        else:
            pl.when(lax.rem(j, 2) == 0)(
                lambda: core_copy(k, 64 * j, 128, core_sem.at[k, j // 2]).wait_recv()
            )
        acc = summed.at[pl.ds(0, ROWS[k])]
        acc[...] = loc[part, :].astype(F32) + rx_core[part, :].astype(F32)
        for hop in HOPS[:3]:
            if (hop, k) in (("down", 0), ("down", 1)):
                continue

            def add(hop=hop):
                landing(k, hop, hop, j).wait_recv()
                acc[...] += rx[hop][place_of(hop, k, j), :].astype(F32)

            pl.when(classes[k][1][hop](j))(add)
        return part, acc

    def relay(k, j):
        part, acc = gathered(k, j)
        loc[part, :] = acc[...].astype(BF16)
        for hop in HOPS[:3]:
            pl.when(classes[k][2][hop](j))(lambda hop=hop: onward(k, hop, j).start())

    def write(slot, rows, offset):
        return pltpu.make_async_copy(
            ring.at[pl.ds(pl.multiple_of(slot * 64, 64), rows)],
            out.at[pl.ds(pl.multiple_of(offset, 16), rows)],
            ring_sem.at[slot],
        )

    def finish(k, j):
        _, acc = gathered(k, j)
        slot = 4 * (k % 2) + lax.rem(j, 4)
        copy = write(slot, ROWS[k], SPLIT * (k % 2) + j * ROWS[k])
        pl.when(j >= 4)(copy.wait)
        value = acc[...]
        ring[pl.ds(pl.multiple_of(slot * 64, 64), ROWS[k]), :] = value
        copy.start()
        count_squares(value)

    first = sec == 0
    second = sec == 2
    in_line = jnp.logical_or(first, second)
    p_line = second.astype(jnp.int32)
    both = jnp.logical_and

    def dx_part(p, zz):
        return all_dx.at[pl.ds(pl.multiple_of((2 * (2 * zz + c) + p) * SP, 16), SP)]

    def move(p, zz, send, recv, target):
        return pltpu.make_async_remote_copy(
            src_ref=dx_part(p, zz),
            dst_ref=dx_part(p, zz),
            send_sem=send,
            recv_sem=recv,
            device_id=target,
            device_id_type=MESH,
        )

    def line(zz, hop):
        return move(p_line, zz, dx_send, line_recv.at[zz], targets[hop])

    def cross(zz):
        return move(1, zz, dx_send, cross_recv.at[zz], (0, dp))

    def dx_to_core(p, zz):
        return move(p, zz, dx_core_send, dx_core_recv, targets["core"])

    def aside(zz):
        pl.when(first)(lambda: dx_to_core(0, zz).start())
        pl.when(second)(lambda: cross(zz).start())

    def crossed(zz):
        cross(zz).wait_recv()
        dx_to_core(1, zz).start()

    def blocks(count, send, recv):
        return pltpu.make_async_remote_copy(
            src_ref=all_dx.at[pl.ds(0, count * SP)],
            dst_ref=all_dx.at[pl.ds(0, count * SP)],
            send_sem=send,
            recv_sem=recv,
            device_id=targets["core"],
            device_id_type=MESH,
        )

    turned = pltpu.make_async_remote_copy(
        src_ref=block,
        dst_ref=dx_part(1, z),
        send_sem=dx_send,
        recv_sem=turn_recv,
        device_id=(2, dp),
        device_id_type=MESH,
    )
    pl.when(sec == 1)(turned.start)

    def pass_own():
        pl.when(z < 3)(lambda: line(z, "up").start())
        pl.when(z > 0)(lambda: line(z, "down").start())
        aside(z)

    def own_first():
        own = pltpu.make_async_copy(block, dx_part(0, z), dx_own)
        own.start()
        own.wait()
        pass_own()

    def own_second():
        turned.wait_recv()
        pl.semaphore_wait(ready, 1)
        pass_own()

    pl.when(first)(own_first)

    def list_rows():
        for e in range(8):
            for p in range(2):
                there = pl.ds((2 * e + p) * SP, SP)
                index[:, there] = info[e, p : p + 1, :][:, :SP] - dp * OWN

    pl.when(first)(list_rows)

    def from_below(k):
        line(z - k, "up").wait_recv()
        pl.when(z < 3)(lambda: line(z - k, "up").start())
        aside(z - k)

    def from_above(k):
        line(z + k, "down").wait_recv()
        pl.when(z > 0)(lambda: line(z + k, "down").start())
        aside(z + k)

    def tile(t):
        ids = lax.broadcasted_iota(jnp.int32, (SP, 16 * SP), 0) + t * SP
        onehot = jnp.where(ids == index[...], 1.0, 0.0).astype(BF16)
        value = nn(onehot, all_dx[...]) * math.sqrt(D)
        slot = lax.rem(t, 2)
        copy = write_tile(slot, t)
        pl.when(t >= 2)(copy.wait)
        ring[pl.ds(pl.multiple_of(slot * SP, 16), SP), :] = value
        copy.start()
        count_squares(value)

    def write_tile(slot, t):
        return pltpu.make_async_copy(
            ring.at[pl.ds(pl.multiple_of(slot * SP, 16), SP)],
            out.at[pl.ds(pl.multiple_of(t * SP, 16), SP)],
            ring_sem.at[slot],
        )

    def collect(i):
        pl.when(both(second, i == CHOP + AHEAD))(own_second)
        for k in range(1, 4):
            now = i == CHOP * (k + p_line) + AHEAD * p_line
            pl.when(both(now, z >= k))(lambda k=k: from_below(k))
            pl.when(both(now, z + k <= 3))(lambda k=k: from_above(k))

    begin = 5 * CHOP + 1

    def embed(i):
        pl.when(i == 2 * CHOP)(lambda: crossed(z))
        for k in range(1, 4):
            pl.when(both(i == CHOP * (k + 2), z >= k))(lambda k=k: crossed(z - k))
            pl.when(both(i == CHOP * (k + 2), z + k <= 3))(lambda k=k: crossed(z + k))
        pl.when(i == begin)(lambda: blocks(8, dx_core_send, dx_core_recv).wait_recv())
        t = i - begin
        pl.when(both(t >= 0, t < OWN // SP))(lambda: tile(t))

    def step(i, carry):
        for k in range(4):
            turn_now = both(lax.rem(i, 2) == k // 2, i < COUNT[k] + k // 2)
            pl.when(turn_now)(lambda k=k: form(k, i // 2))
        pl.when(both(i == CWAIT - 1, c == 0))(lambda: form_last(loc))
        pl.when(both(i == CWAIT - 1, c == 1))(form_for_other)
        for k in range(5):
            source, _, _, depth = classes[k]
            j = i - CLAG * ((5, 5, 4, 4, 3)[k] - depth) - (0, 0, 1, 1, CWAIT)[k]
            now = both(j >= 0, j < COUNT[k])
            if k == 4:
                now = both(now, c == 0)
            pl.when(both(now, jnp.logical_not(source)))(lambda k=k, j=j: relay(k, j))
            pl.when(both(now, source))(lambda k=k, j=j: finish(k, j))
        pl.when(in_line)(lambda: collect(i))
        pl.when(first)(lambda: embed(i))
        return carry

    lax.fori_loop(0, max(18 + 5 * CLAG, begin + OWN // SP), step, 0)
    pl.when(first)(lambda: blocks(8, dx_core_send, dx_core_recv).wait_send())

    def dx_sent(count):
        blocks(count, dx_send, dx_core_recv).wait_send()

    middle = both(z >= 1, z <= 2)
    ends = jnp.logical_not(middle)
    pl.when(jnp.logical_or(sec == 1, both(first, ends)))(lambda: dx_sent(1))
    pl.when(both(first, middle))(lambda: dx_sent(5))
    pl.when(both(second, ends))(lambda: dx_sent(5))
    pl.when(both(second, middle))(lambda: dx_sent(9))
    def sent_core(rows):
        part = pl.ds(0, rows)
        pltpu.make_async_remote_copy(
            src_ref=sent.at[part],
            dst_ref=rx_core.at[part],
            send_sem=core_send,
            recv_sem=core_sem.at[4, 0],
            device_id=targets["core"],
            device_id_type=MESH,
        ).wait_send()

    pl.when(c == 0)(lambda: sent_core(2 * OWN))
    pl.when(c == 1)(lambda: sent_core(LANE))
    for k in range(5):
        part = pl.ds(HELD[k], COUNT[k] * ROWS[k])
        gone = pltpu.make_async_remote_copy(
            src_ref=loc.at[part],
            dst_ref=rx_x.at[part],
            send_sem=send_sem.at[k],
            recv_sem=core_sem.at[4, 0],
            device_id=targets["x"],
            device_id_type=MESH,
        )
        away = jnp.logical_not(classes[k][0])
        pl.when(both(away, c == 0) if k == 4 else away)(gone.wait_send)

    def drain_half(k):
        for j in range(COUNT[k] - 4, COUNT[k]):
            write(4 * (k % 2) + j % 4, ROWS[k], 0).wait()

    def drain_tiles():
        for slot in range(2):
            write_tile(slot, 0).wait()

    for k in range(5):
        pl.when(classes[k][0])(lambda k=k: drain_half(k))
    pl.when(first)(drain_tiles)


def reduce_and_scatter(left, right, tail, start, block, info):
    low = lambda *shape: pltpu.VMEM(shape, BF16)
    dma = pltpu.SemaphoreType.DMA
    return pl.pallas_call(
        close_kernel,
        out_shape=(
            jax.ShapeDtypeStruct((OWN, D), F32),
            jax.ShapeDtypeStruct((8, 128), F32),
        ),
        in_specs=[ANY, ANY, VMEM, ANY, VMEM, VMEM],
        out_specs=(ANY, VMEM),
        input_output_aliases={3: 0},
        scratch_shapes=[
            low(SP, MATS),
            low(6, SP, D),
            low(LANE, D),
            low(LANE, D),
            low(LANE, D),
            low(OWN + SPLIT + 11 * 48, D),
            low(OWN + 11 * 48, D),
            low(LANE, D),
            pltpu.VMEM((64, D), F32),
            pltpu.VMEM((2 * SP, D), F32),
            low(16 * SP, D),
            dma((2,)),
            dma((5, 9)),
            dma((3, 4, 18)),
            dma((3, 11)),
            dma,
            dma((5,)),
            dma((8,)),
            dma,
            dma,
            dma((4,)),
            dma((4,)),
            dma,
            dma,
            dma,
            pltpu.VMEM((1, 16 * SP), jnp.int32),
            pltpu.SemaphoreType.REGULAR,
        ],
        compiler_params=pltpu.CompilerParams(
            collective_id=1, has_side_effects=True, vmem_limit_bytes=63 * 2**20
        ),
        name="reduce_and_scatter",
    )(left, right, tail, start, block, info)


def norm_kernel(n_sec, n_dp, small, squares, out, block, every, send_sem, recv_sem):
    sec = lax.axis_index("section")
    dp = lax.axis_index("dp")
    n = n_sec * n_dp
    me = sec * n_dp + dp
    barrier = pltpu.get_barrier_semaphore()

    def peer(k):
        other = lax.rem(me + k, n)
        return (other // n_dp, lax.rem(other, n_dp))

    def greet(k, carry):
        pl.semaphore_signal(barrier, 1, device_id=peer(k), device_id_type=MESH)
        return carry

    lax.fori_loop(1, n, greet, 0)
    block[...] = small[...]
    block[7:8, :] += jnp.sum(squares[...], axis=0, keepdims=True)
    every[me] = block[...]
    pl.semaphore_wait(barrier, n - 1)

    def send(k, carry):
        pltpu.make_async_remote_copy(
            src_ref=block,
            dst_ref=every.at[me],
            send_sem=send_sem,
            recv_sem=recv_sem,
            device_id=peer(k),
            device_id_type=MESH,
        ).start()
        return carry

    lax.fori_loop(1, n, send, 0)
    others = pltpu.make_async_remote_copy(
        src_ref=every.at[pl.ds(0, n - 1)],
        dst_ref=every.at[pl.ds(0, n - 1)],
        send_sem=send_sem,
        recv_sem=recv_sem,
        device_id=peer(1),
        device_id_type=MESH,
    )
    others.wait_recv()
    total = every[0]
    for k in range(1, n):
        total = total + every[k]
    gains = jnp.sum(total[0:6] * total[0:6], axis=0, keepdims=True)
    norm = jnp.sqrt(jnp.sum(gains + total[7:8], axis=1, keepdims=True))
    out[0:8, :] = total
    out[8:16, :] = jnp.broadcast_to(norm, (8, 128))
    others.wait_send()


def share_norm(small, squares, n_sec, n_dp):
    return pl.pallas_call(
        functools.partial(norm_kernel, n_sec, n_dp),
        out_shape=jax.ShapeDtypeStruct((16, 128), F32),
        in_specs=[VMEM, VMEM],
        out_specs=VMEM,
        scratch_shapes=[
            pltpu.VMEM((8, 128), F32),
            pltpu.VMEM((n_sec * n_dp, 8, 128), F32),
            pltpu.SemaphoreType.DMA,
            pltpu.SemaphoreType.DMA,
        ],
        compiler_params=pltpu.CompilerParams(
            collective_id=8, has_side_effects=True, vmem_limit_bytes=2**20
        ),
        cost_estimate=pl.CostEstimate(
            flops=10**10, bytes_accessed=4 * 10**7, transcendentals=0
        ),
        name="share_norm",
    )(small, squares)


NEG = -1e30
FT = 256


def turn(block, cosine, sine, lanes):
    ahead = pltpu.roll(block, 96, 1)
    behind = pltpu.roll(block, 32, 1)
    return block * cosine + jnp.where(lax.rem(lanes, 64) < 32, ahead, behind) * sine


def see(starts):
    par = lax.rem(lax.axis_index("section"), 2)
    rows = lax.broadcasted_iota(jnp.int32, (SP, SP), 0)
    cols = lax.broadcasted_iota(jnp.int32, (SP, SP), 1)
    same = segment_of(starts, par, rows)[0] == segment_of(starts, par, cols)[0]
    allowed = jnp.logical_and(same, cols <= rows)
    return jnp.where(allowed, 0.0, NEG)


def hide(starts):
    par = lax.rem(lax.axis_index("section"), 2)
    rows = lax.broadcasted_iota(jnp.int32, (SP, SP), 0)
    cols = lax.broadcasted_iota(jnp.int32, (SP, SP), 1)
    same = segment_of(starts, par, rows)[0] == segment_of(starts, par, cols)[0]
    return jnp.where(jnp.logical_and(same, rows <= cols), 0.0, NEG)


def softmax_of(scores, unseen):
    masked = scores + unseen
    grown = jnp.exp(masked - jnp.max(masked, axis=-1, keepdims=True))
    return grown / jnp.sum(grown, axis=-1, keepdims=True)


def weight_copies(w_any, w, sems):
    bounds = (0, 3 * D, 4 * D, 4 * D + FF, 4 * D + 2 * FF, MATS, WROWS)
    return [
        pltpu.make_async_copy(
            w_any.at[pl.ds(lo, hi - lo)], w.at[pl.ds(lo, hi - lo)], sems.at[i]
        )
        for i, (lo, hi) in enumerate(zip(bounds[:-1], bounds[1:]))
    ]


def forward_kernel(keep, x, w_any, cosine, sine, starts, y, *refs):
    kept = refs[:7] if keep else ()
    q, k, v, o, h, gate, up, w, m, unseen, sems, keep_sems, *hop_sems = refs[len(kept) :]
    sec = lax.axis_index("section")
    dp = lax.axis_index("dp")
    lower = sec < 2
    if not keep:
        barrier = pltpu.get_barrier_semaphore()
        pl.when(jnp.logical_not(lower))(
            lambda: pl.semaphore_signal(barrier, 1, device_id=(sec - 2, dp), device_id_type=MESH)
        )

    def hop(b):
        part = y.at[:, pl.ds(b * 256, 256)]
        return pltpu.make_async_remote_copy(
            src_ref=part,
            dst_ref=part,
            send_sem=hop_sems[0].at[b],
            recv_sem=hop_sems[1].at[b],
            device_id=(sec + 2, dp),
            device_id_type=MESH,
        )

    def put(i):
        if keep:
            pltpu.make_async_copy((q, k, v, o, h, gate, up)[i], kept[i], keep_sems.at[i]).start()

    def run():
        copies = weight_copies(w_any, w, sems)
        for i in (5, 0, 1, 2, 3, 4):
            copies[i].start()
        unseen[...] = see(starts)
        lanes = lax.broadcasted_iota(jnp.int32, (SP, 128), 1)
        first = lanes < 64
        copies[5].wait()
        gains = w[pl.ds(MATS, 16), :].astype(F32)
        stream = x[...].astype(F32)
        a1 = rms_scale(stream, gains[0:1]).astype(BF16)
        copies[0].wait()

        def project(b, carry):
            cols = pl.ds(pl.multiple_of(b * 256, 256), 256)
            raw_q = nn(a1, w[pl.ds(0, D), cols])
            raw_k = nn(a1, w[pl.ds(D, D), cols])
            raw_v = nn(a1, w[pl.ds(2 * D, D), cols])
            v[:, cols] = raw_v.astype(BF16)
            for part in range(2):
                there = pl.ds(pl.multiple_of(b * 256 + part * 128, 128), 128)
                here = slice(part * 128, (part + 1) * 128)
                turned_q = turn(raw_q[:, here], cosine[...], sine[...], lanes)
                q[:, there] = (turned_q * HD ** (-0.5)).astype(BF16)
                k[:, there] = turn(raw_k[:, here], cosine[...], sine[...], lanes).astype(BF16)
            return carry

        lax.fori_loop(0, D // 256, project, 0, unroll=True)
        for i in range(3):
            put(i)

        def attend(b, carry):
            cols = pl.ds(pl.multiple_of(b * 128, 128), 128)
            qb, kb, vb = q[:, cols], k[:, cols], v[:, cols]
            zero = jnp.zeros_like(qb)
            p0 = softmax_of(nt(jnp.where(first, qb, zero), kb), unseen[...]).astype(BF16)
            p1 = softmax_of(nt(jnp.where(first, zero, qb), kb), unseen[...]).astype(BF16)
            o[:, cols] = jnp.where(first, nn(p0, vb), nn(p1, vb)).astype(BF16)
            return carry

        lax.fori_loop(0, HEADS // 2, attend, 0, unroll=True)
        put(3)
        copies[1].wait()
        for b in range(3):
            cols = pl.ds(b * 256, 256)
            h[:, cols] = x[:, cols].astype(F32) + nn(o[...], w[pl.ds(3 * D, D), cols])
        put(4)
        a2 = rms_scale(h[...], gains[1:2]).astype(BF16)
        copies[2].wait()
        copies[3].wait()

        def widen(b, carry):
            cols = pl.ds(pl.multiple_of(b * FT, FT), FT)
            g = nt(a2, w[pl.ds(pl.multiple_of(4 * D + b * FT, FT), FT), :])
            u = nt(a2, w[pl.ds(pl.multiple_of(4 * D + FF + b * FT, FT), FT), :])
            gate[:, cols] = g
            up[:, cols] = u
            m[:, cols] = (g / (1.0 + jnp.exp(-g)) * u).astype(BF16)
            return carry

        lax.fori_loop(0, FF // FT, widen, 0, unroll=True)
        put(5)
        put(6)
        copies[4].wait()

        if not keep:
            pl.semaphore_wait(barrier, 1)
        for b in range(3):
            cols = pl.ds(b * 256, 256)
            y[:, cols] = (h[:, cols] + nn(m[...], w[pl.ds(4 * D + 2 * FF, FF), cols])).astype(BF16)
            if not keep:
                hop(b).start()
        for i, part in enumerate(kept):
            pltpu.make_async_copy((q, k, v, o, h, gate, up)[i], part, keep_sems.at[i]).wait()
        if not keep:
            for b in range(3):
                hop(b).wait_send()
            y[...] = x[...]

    if keep:
        run()
        return
    pl.when(lower)(run)

    def arrive():
        for b in range(3):
            hop(b).wait_recv()

    pl.when(jnp.logical_not(lower))(arrive)


KEPT = ((D, BF16), (D, BF16), (D, BF16), (D, BF16), (D, F32), (FF, F32), (FF, F32))


def forward_call(keep, x, weights, cosine, sine, starts):
    low = jax.ShapeDtypeStruct((SP, D), BF16)
    kept = tuple(jax.ShapeDtypeStruct((SP, n), t) for n, t in KEPT) if keep else ()
    return pl.pallas_call(
        functools.partial(forward_kernel, keep),
        out_shape=(low,) + kept,
        in_specs=[VMEM, ANY, VMEM, VMEM, SMEM],
        out_specs=(VMEM,) + (ANY,) * len(kept),
        scratch_shapes=[pltpu.VMEM((SP, n), t) for n, t in KEPT]
        + [
            pltpu.VMEM((WROWS, D), BF16),
            pltpu.VMEM((SP, FF), BF16),
            pltpu.VMEM((SP, SP), F32),
            pltpu.SemaphoreType.DMA((6,)),
            pltpu.SemaphoreType.DMA((7,)),
        ]
        + ([] if keep else [pltpu.SemaphoreType.DMA((3,))] * 2),
        compiler_params=pltpu.CompilerParams(vmem_limit_bytes=56 * 2**20)
        if keep
        else pltpu.CompilerParams(
            collective_id=6, has_side_effects=True, vmem_limit_bytes=56 * 2**20
        ),
        name="layer_forward_kept" if keep else "layer_forward",
    )(x, weights, cosine, sine, starts)


def rms_back(value_in, gain, grad):
    inv = lax.rsqrt(jnp.mean(value_in * value_in, axis=-1, keepdims=True) + norm_eps)
    unit = value_in * inv
    scaled = grad * gain
    grad_in = inv * (scaled - unit * jnp.mean(scaled * unit, axis=-1, keepdims=True))
    return grad_in, jnp.sum(grad * unit, axis=0, keepdims=True)


def backward_kernel(send, dy, x, w_any, cosine, sine, starts, *refs):
    kept, refs = refs[:7], refs[7:]
    dx, left, right, tail, refs = *refs[:4], refs[4:]
    q, k, v, o, h, gate, up, w, dgate, dup, m, da, do, dq, dk, dv, a1, a2, db, *refs = refs
    unseen, sems, keep_sems, out_sems, *hop_sems = refs
    sec = lax.axis_index("section")
    dp = lax.axis_index("dp")
    upper = sec >= 2
    if send:
        barrier = pltpu.get_barrier_semaphore()
        pl.when(jnp.logical_not(upper))(
            lambda: pl.semaphore_signal(barrier, 1, device_id=(sec + 2, dp), device_id_type=MESH)
        )

    def hop():
        return pltpu.make_async_remote_copy(
            src_ref=dx,
            dst_ref=dx,
            send_sem=hop_sems[0],
            recv_sem=hop_sems[1],
            device_id=(sec - 2, dp),
            device_id_type=MESH,
        )

    outs = []

    def put(source, target):
        copy = pltpu.make_async_copy(source, target, out_sems.at[len(outs)])
        copy.start()
        outs.append(copy)
    def run():
        copies = weight_copies(w_any, w, sems)
        taken = [
            pltpu.make_async_copy(part, (q, k, v, o, h, gate, up)[i], keep_sems.at[i])
            for i, part in enumerate(kept)
        ]
        for one in (
            copies[4], taken[5], taken[6], copies[5], copies[2], copies[3], taken[4], copies[1],
            taken[0], taken[1], taken[2], copies[0], taken[3],
        ):
            one.start()
        unseen[...] = hide(starts)
        lanes = lax.broadcasted_iota(jnp.int32, (SP, 128), 1)
        first = lanes < 64
        copies[4].wait()
        taken[5].wait()
        taken[6].wait()

        def open_mlp(b, carry):
            cols = pl.ds(pl.multiple_of(b * FT, FT), FT)
            dm = nt(dy[...], w[pl.ds(pl.multiple_of(4 * D + 2 * FF + b * FT, FT), FT), :])
            g = gate[:, cols]
            u = up[:, cols]
            sig = 1.0 / (1.0 + jnp.exp(-g))
            dgate[:, cols] = (dm * u * sig * (1.0 + g * (1.0 - sig))).astype(BF16)
            dup[:, cols] = (dm * g * sig).astype(BF16)
            m[:, cols] = (g * sig * u).astype(BF16)
            return carry

        lax.fori_loop(0, FF // FT, open_mlp, 0, unroll=True)
        for i, part in enumerate((dgate, dup, m)):
            put(part, left.at[:, pl.ds(4 * D + i * FF, FF)])
        put(dy, right.at[5])
        copies[5].wait()
        gains = w[pl.ds(MATS, 16), :].astype(F32)
        copies[2].wait()
        copies[3].wait()

        def close_mlp(b, carry):
            cols = pl.ds(pl.multiple_of(b * 256, 256), 256)
            da[:, cols] = nn(dgate[...], w[pl.ds(4 * D, FF), cols]) + nn(
                dup[...], w[pl.ds(4 * D + FF, FF), cols]
            )
            return carry

        lax.fori_loop(0, 3, close_mlp, 0, unroll=True)
        taken[4].wait()
        dh, dg_mlp = rms_back(h[...], gains[1:2], da[...])
        dh = dh + dy[...].astype(F32)
        db[...] = dh.astype(BF16)
        a2[...] = rms_scale(h[...], gains[1:2]).astype(BF16)
        put(db, right.at[3])
        put(a2, right.at[4])
        copies[1].wait()
        for b in range(3):
            do[:, pl.ds(b * 256, 256)] = nt(db[...], w[pl.ds(3 * D + b * 256, 256), :]).astype(BF16)

        for i in range(3):
            taken[i].wait()

        def attend(b, carry):
            cols = pl.ds(pl.multiple_of(b * 128, 128), 128)
            qb, kb, vb, dob = q[:, cols], k[:, cols], v[:, cols], do[:, cols]
            zero = jnp.zeros_like(qb)
            parts = []
            for head in range(2):
                keep = first if head == 0 else jnp.logical_not(first)
                masked = nt(jnp.where(keep, kb, zero), qb) + unseen[...]
                grown = jnp.exp(masked - jnp.max(masked, axis=0, keepdims=True))
                probs = grown / jnp.sum(grown, axis=0, keepdims=True)
                dprobs = nt(jnp.where(keep, vb, zero), dob)
                along = jnp.sum(probs * dprobs, axis=0, keepdims=True)
                dscores = (probs * (dprobs - along)).astype(BF16)
                parts.append((tn(dscores, kb), nn(dscores, qb), nn(probs.astype(BF16), dob)))
            dqb = jnp.where(first, parts[0][0], parts[1][0]) * HD ** (-0.5)
            dkb = jnp.where(first, parts[0][1], parts[1][1])
            dq[:, cols] = turn(dqb, cosine[...], -sine[...], lanes).astype(BF16)
            dk[:, cols] = turn(dkb, cosine[...], -sine[...], lanes).astype(BF16)
            dv[:, cols] = jnp.where(first, parts[0][2], parts[1][2]).astype(BF16)
            return carry

        lax.fori_loop(0, HEADS // 2, attend, 0, unroll=True)
        for i, part in enumerate((dq, dk, dv)):
            put(part, right.at[i])
        copies[0].wait()
        for b in range(3):
            rows = lambda i, b=b: w[pl.ds(i * D + b * 256, 256), :]
            da[:, pl.ds(b * 256, 256)] = (
                nt(dq[...], rows(0)) + nt(dk[...], rows(1)) + nt(dv[...], rows(2))
            )
        stream = x[...].astype(F32)
        a1[...] = rms_scale(stream, gains[0:1]).astype(BF16)
        for i in range(3):
            put(a1, left.at[:, pl.ds(i * D, D)])
        taken[3].wait()
        put(o, left.at[:, pl.ds(3 * D, D)])
        dstream, dg_attn = rms_back(stream, gains[0:1], da[...])
        dx[...] = (dstream + dh).astype(BF16)
        if send:
            pl.semaphore_wait(barrier, 1)
            hop().start()
        ids = lax.broadcasted_iota(jnp.int32, (16, D), 0)
        tail[...] = jnp.where(ids == 0, dg_attn, jnp.where(ids == 1, dg_mlp, 0.0)).astype(BF16)
        for copy in outs:
            copy.wait()
        if send:
            hop().wait_send()

    if not send:
        run()
        return
    pl.when(upper)(run)
    pl.when(jnp.logical_not(upper))(lambda: hop().wait_recv())


def backward_call(send, dy, x, weights, cosine, sine, starts, kept):
    wide = pltpu.VMEM((SP, FF), BF16)
    narrow = pltpu.VMEM((SP, D), BF16)
    return pl.pallas_call(
        functools.partial(backward_kernel, send),
        out_shape=(
            jax.ShapeDtypeStruct((SP, D), BF16),
            jax.ShapeDtypeStruct((SP, MATS), BF16),
            jax.ShapeDtypeStruct((6, SP, D), BF16),
            jax.ShapeDtypeStruct((16, D), BF16),
        ),
        in_specs=[VMEM, VMEM, ANY, VMEM, VMEM, SMEM] + [ANY] * 7,
        out_specs=(VMEM, ANY, ANY, VMEM),
        scratch_shapes=[pltpu.VMEM((SP, n), t) for n, t in KEPT]
        + [
            pltpu.VMEM((WROWS, D), BF16),
            wide,
            wide,
            wide,
            pltpu.VMEM((SP, D), F32),
        ]
        + [narrow] * 7
        + [
            pltpu.VMEM((SP, SP), F32),
            pltpu.SemaphoreType.DMA((6,)),
            pltpu.SemaphoreType.DMA((7,)),
            pltpu.SemaphoreType.DMA((13,)),
        ]
        + ([pltpu.SemaphoreType.DMA] * 2 if send else []),
        compiler_params=pltpu.CompilerParams(
            collective_id=7, has_side_effects=True, vmem_limit_bytes=60 * 2**20
        )
        if send
        else pltpu.CompilerParams(vmem_limit_bytes=60 * 2**20),
        name="layer_backward_send" if send else "layer_backward",
    )(dy, x, weights, cosine, sine, starts, *kept)


def matrix_gradients(left, right, tail):
    parts = [(0, 0), (D, 1), (2 * D, 2), (3 * D, 3), (4 * D, 4), (4 * D + FF, 4), (4 * D + 2 * FF, 5)]
    ends = [start for start, _ in parts[1:]] + [MATS]
    rows = [
        tn(left[:, start:end], right[i]).astype(BF16) for (start, i), end in zip(parts, ends)
    ]
    return jnp.concatenate(rows + [tail], axis=0)


HEAD_T = 256


def column(row, size):
    there = lax.broadcasted_iota(jnp.int32, (size, size), 0)
    here = lax.broadcasted_iota(jnp.int32, (size, size), 1)
    zero = jnp.zeros((), row.dtype)
    return jnp.sum(jnp.where(there == here, row, zero), axis=1, keepdims=True)


def as_rows(values):
    there = lax.broadcasted_iota(jnp.int32, (128, 128), 0)
    here = lax.broadcasted_iota(jnp.int32, (128, 128), 1)
    return [
        jnp.sum(
            jnp.where(there == here, values[k * 128 : (k + 1) * 128], 0.0), axis=0, keepdims=True
        )
        for k in range(4)
    ]


def head_kernel(
    y, picks, info, gain, table, d_top, d_table, small, mine, picked, af, scores, dlow, labels,
    counts, stat, stats, daf, rx_core, low, rx, fresh, zero_sem, own_sem, pick_send, pick_recv,
    core_send, core_recv, stat_send, stat_recv, swap_send, swap_recv, daf_send, daf_recv,
):
    sec, dp, z, c, par, home = place()
    last = sec == 3
    upper = sec >= 2
    barrier = pltpu.get_barrier_semaphore()
    other_core = (3, dp + 1 - 2 * c)

    def greet(s, e):
        pl.semaphore_signal(barrier, 1, device_id=(s, e), device_id_type=MESH)

    def greet_second():
        for k in range(4):
            greet(3, 2 * k + c)
        pl.semaphore_wait(barrier, 4)

    def greet_third():
        for k in range(4):
            greet(2, 2 * k + c)
        for k in range(1, 8):
            greet(3, lax.rem(dp + k, 8))
        pl.semaphore_wait(barrier, 11)

    all_zero = pltpu.make_async_copy(fresh, d_table, zero_sem)

    def zeros():
        fresh[...] = jnp.zeros_like(fresh)
        all_zero.start()

    pl.when(jnp.logical_not(last))(zeros)
    small[...] = jnp.zeros_like(small)
    pick_row = picks[pl.ds(par, 1), :]
    pick_col = column(pick_row, PICKS)

    def choose():
        ids = lax.broadcasted_iota(jnp.int32, (PICKS, SP), 1)
        mine[...] = nn(jnp.where(ids == pick_col, 1.0, 0.0).astype(BF16), y[...]).astype(BF16)

    pl.when(upper)(choose)
    pl.when(sec == 2)(greet_second)
    pl.when(last)(greet_third)

    def rows(p, zz, lane):
        return pl.ds(pl.multiple_of((2 * (2 * zz + lane) + p) * PICKS, PICKS), PICKS)

    def pick_to(k):
        zz = lax.rem(z + k, 4)
        return pltpu.make_async_remote_copy(
            src_ref=mine,
            dst_ref=picked.at[rows(par, z, c)],
            send_sem=pick_send,
            recv_sem=pick_recv.at[par, z],
            device_id=(3, 2 * zz + c),
            device_id_type=MESH,
        )

    def came(p, k):
        zz = lax.rem(z + k, 4)
        return pltpu.make_async_remote_copy(
            src_ref=mine,
            dst_ref=picked.at[rows(p, zz, c)],
            send_sem=pick_send,
            recv_sem=pick_recv.at[p, zz],
            device_id=other_core,
            device_id_type=MESH,
        )

    def forward(p, k):
        part = picked.at[rows(p, lax.rem(z + k, 4), c)]
        return pltpu.make_async_remote_copy(
            src_ref=part,
            dst_ref=part,
            send_sem=core_send,
            recv_sem=core_recv,
            device_id=other_core,
            device_id_type=MESH,
        )

    def span(ref, count, send, recv):
        part = ref.at[pl.ds(0, count)]
        return pltpu.make_async_remote_copy(
            src_ref=part,
            dst_ref=part,
            send_sem=send,
            recv_sem=recv,
            device_id=other_core,
            device_id_type=MESH,
        )

    def pick_second():
        for k in (1, 2, 3, 0):
            pick_to(k).start()

    def pick_third():
        own = pltpu.make_async_copy(mine, picked.at[rows(1, z, c)], own_sem)
        own.start()
        for k in range(1, 4):
            pick_to(k).start()
        for e in range(8):
            for p in range(2):
                at = pl.ds((2 * e + p) * PICKS, PICKS)
                labels[at, :] = column(info[e, 2 + p : 3 + p, :][:, :PICKS], PICKS)
                counts[at, :] = column(info[e, 4 + p : 5 + p, :][:, :PICKS].astype(F32), PICKS)
        own.wait()
        forward(1, 0).start()
        for k in range(4):
            came(0, k).wait_recv()
            forward(0, k).start()
            if k:
                came(1, k).wait_recv()
                forward(1, k).start()
        span(picked, 8 * PICKS, core_send, core_recv).wait_recv()

    pl.when(sec == 2)(pick_second)
    pl.when(last)(pick_third)
    g_f = gain[...].astype(F32)[0:1]
    own = OWN
    tiles = [(t * HEAD_T, HEAD_T) for t in range(own // HEAD_T)] + [
        (own - own % HEAD_T, own % HEAD_T)
    ]

    def over_tiles(body):
        def step(t, carry):
            body(pl.multiple_of(t * HEAD_T, HEAD_T), HEAD_T)
            return carry

        lax.fori_loop(0, own // HEAD_T, step, 0, unroll=True)
        body(own - own % HEAD_T, own % HEAD_T)

    def forward_part():
        af[...] = rms_scale(picked[...].astype(F32), g_f).astype(BF16)
        fold = lambda op, block: functools.reduce(
            op, [block[:, k * 128 : (k + 1) * 128] for k in range(block.shape[1] // 128)]
        )
        top = daf.at[:, pl.ds(0, 128)]
        top[...] = jnp.full((16 * PICKS, 128), NEG, F32)

        def product(start, size):
            ids = lax.broadcasted_iota(jnp.int32, (16 * PICKS, size), 1) + (dp * own + start)
            block = nt(af[...], table[pl.ds(start, size), :])
            block = jnp.where(ids < VOCAB, block, NEG)
            scores[:, pl.ds(start, size)] = block
            top[...] = jnp.maximum(top[...], fold(jnp.maximum, block))

        over_tiles(product)
        top_col = jnp.max(top[...], axis=1, keepdims=True)
        total = daf.at[:, pl.ds(128, 128)]
        target = daf.at[:, pl.ds(256, 128)]
        total[...] = jnp.zeros((16 * PICKS, 128), F32)
        target[...] = jnp.zeros((16 * PICKS, 128), F32)

        def exponents(start, size):
            ids = lax.broadcasted_iota(jnp.int32, (16 * PICKS, size), 1) + (dp * own + start)
            block = scores[:, pl.ds(start, size)]
            grown = jnp.exp(block - top_col)
            scores[:, pl.ds(start, size)] = grown
            total[...] += fold(jnp.add, grown)
            target[...] += fold(jnp.add, jnp.where(ids == labels[...], block, 0.0))

        over_tiles(exponents)
        stat[...] = jnp.zeros_like(stat)
        columns = (
            top_col,
            jnp.sum(total[...], axis=1, keepdims=True),
            jnp.sum(target[...], axis=1, keepdims=True),
        )
        for k, values in enumerate(columns):
            for i, row in enumerate(as_rows(values)):
                stat[4 * k + i : 4 * k + i + 1, :] = row
        stats[dp] = stat[...]
        for k in range(1, 8):
            pltpu.make_async_remote_copy(
                src_ref=stat,
                dst_ref=stats.at[dp],
                send_sem=stat_send,
                recv_sem=stat_recv,
                device_id=(3, lax.rem(dp + k, 8)),
                device_id_type=MESH,
            ).start()
        every = span(stats, 7, stat_send, stat_recv)
        every.wait_recv()
        tops = [stats[e, 0:4, :] for e in range(8)]
        best = functools.reduce(jnp.maximum, tops)
        sums = sum(stats[e, 4:8, :] * jnp.exp(tops[e] - best) for e in range(8))
        hits = sum(stats[e, 8:12, :] for e in range(8))
        log_total = best + jnp.log(sums)
        log_col = jnp.concatenate([column(log_total[k : k + 1], 128) for k in range(4)], axis=0)
        hit_col = jnp.concatenate([column(hits[k : k + 1], 128) for k in range(4)], axis=0)
        loss = jnp.sum(
            jnp.where(counts[...] > 0, log_col - hit_col, 0.0), axis=0, keepdims=True
        )
        lane = lax.broadcasted_iota(jnp.int32, (1, 128), 1)
        number = jnp.sum(counts[...], axis=0, keepdims=True)
        pair = jnp.where(lane == 0, loss, jnp.where(lane == 1, number, 0.0))
        small[6:7, :] = jnp.where(dp == 0, pair, 0.0)
        shrink = jnp.exp(top_col - log_col)

        def slopes(start, size):
            ids = lax.broadcasted_iota(jnp.int32, (16 * PICKS, size), 1) + (dp * own + start)
            hit = jnp.where(ids == labels[...], 1.0, 0.0)
            block = (scores[:, pl.ds(start, size)] * shrink - hit) * counts[...]
            dlow[:, pl.ds(start, size)] = block.astype(BF16)

        over_tiles(slopes)
        for b in range(3):
            cols = pl.ds(b * 256, 256)
            daf[:, cols] = nn(dlow[...], table[:, cols])
        every.wait_send()
        span(picked, 3 * PICKS, pick_send, core_recv).wait_send()
        span(picked, 8 * PICKS, core_send, core_recv).wait_send()

    def swap(p, zz):
        return pltpu.make_async_remote_copy(
            src_ref=daf.at[rows(p, zz, 1 - c)],
            dst_ref=rx_core.at[pl.ds((2 * zz + p) * PICKS, PICKS)],
            send_sem=swap_send,
            recv_sem=swap_recv,
            device_id=other_core,
            device_id_type=MESH,
        )

    def back_to(p, k):
        zz = lax.rem(z + k, 4)
        return pltpu.make_async_remote_copy(
            src_ref=low.at[pl.ds(pl.multiple_of((2 * zz + p) * PICKS, PICKS), PICKS)],
            dst_ref=rx.at[z],
            send_sem=daf_send,
            recv_sem=daf_recv,
            device_id=(2 + p, 2 * zz + c),
            device_id_type=MESH,
        )

    def table_part(start, size):
        there = pl.ds(start, size)
        value = tn(dlow[:, there], af[...])
        fresh[there, :] = value
        pltpu.make_async_copy(fresh.at[there], d_table.at[there], zero_sem).start()
        folded = jnp.sum(value * value, axis=0, keepdims=True)
        small[7:8, :] += functools.reduce(
            jnp.add, [folded[:, k * 128 : (k + 1) * 128] for k in range(6)]
        )

    def third():
        forward_part()
        for zz in range(4):
            for p in range(2):
                swap(p, zz).start()
        table_part(own - own % HEAD_T, own % HEAD_T)
        span(rx_core, 8 * PICKS, swap_send, swap_recv).wait_recv()
        for zz in range(4):
            for p in range(2):
                there = pl.ds((2 * zz + p) * PICKS, PICKS)
                low[there, :] = (daf[rows(p, zz, c), :] + rx_core[there, :]).astype(BF16)
        for k in (1, 2, 3, 0):
            back_to(0, k).start()
            if k:
                back_to(1, k).start()

        def step(t, carry):
            table_part(pl.multiple_of(t * HEAD_T, HEAD_T), HEAD_T)
            return carry

        lax.fori_loop(0, own // HEAD_T, step, 0, unroll=True)
        rx[z] = low[pl.ds(pl.multiple_of((2 * z + 1) * PICKS, PICKS), PICKS), :]
        span(rx_core, 8 * PICKS, swap_send, swap_recv).wait_send()
        span(low, 7 * PICKS, daf_send, daf_recv).wait_send()
        span(rx, 3, daf_send, daf_recv).wait_recv()

    def second():
        span(picked, 4 * PICKS, pick_send, core_recv).wait_send()
        span(rx, 4, daf_send, daf_recv).wait_recv()

    pl.when(last)(third)
    pl.when(sec == 2)(second)

    def finish():
        summed = rx[0].astype(F32)
        for k in range(1, 4):
            summed = summed + rx[k].astype(F32)
        grad, dg_f = rms_back(mine[...].astype(F32), g_f, summed)
        for k in range(6):
            small[k : k + 1, :] = dg_f[:, k * 128 : (k + 1) * 128]
        ids = lax.broadcasted_iota(jnp.int32, (SP, PICKS), 0)
        spread = jnp.where(ids == pick_row, 1.0, 0.0).astype(BF16)
        rest = grad
        out = jnp.zeros((SP, D), F32)
        for _ in range(3):
            part = rest.astype(BF16)
            out = out + nn(spread, part)
            rest = rest - part.astype(F32)
        d_top[...] = out.astype(BF16)

    def none():
        d_top[...] = jnp.zeros_like(d_top)

    pl.when(upper)(finish)
    pl.when(jnp.logical_not(upper))(none)
    all_zero.wait()


def head_call(y, picks, info, gain, table):
    low = lambda *shape: pltpu.VMEM(shape, BF16)
    wide = lambda *shape: pltpu.VMEM(shape, F32)
    n = 16 * PICKS
    return pl.pallas_call(
        head_kernel,
        out_shape=(
            jax.ShapeDtypeStruct((SP, D), BF16),
            jax.ShapeDtypeStruct((OWN, D), F32),
            jax.ShapeDtypeStruct((8, 128), F32),
        ),
        in_specs=[VMEM] * 5,
        out_specs=(VMEM, ANY, VMEM),
        scratch_shapes=[
            low(PICKS, D),
            low(n, D),
            low(n, D),
            wide(n, OWN),
            low(n, OWN),
            pltpu.VMEM((n, 1), jnp.int32),
            wide(n, 1),
            wide(16, 128),
            wide(8, 16, 128),
            wide(n, D),
            wide(8 * PICKS, D),
            low(8 * PICKS, D),
            low(4, PICKS, D),
            wide(OWN, D),
            pltpu.SemaphoreType.DMA,
            pltpu.SemaphoreType.DMA,
            pltpu.SemaphoreType.DMA,
            pltpu.SemaphoreType.DMA((2, 4)),
        ]
        + [pltpu.SemaphoreType.DMA] * 8,
        compiler_params=pltpu.CompilerParams(
            collective_id=3, has_side_effects=True, vmem_limit_bytes=56 * 2**20
        ),
        name="head",
    )(y, picks, info, gain, table)


def open_anywhere(codes, labels, picks, classes, null_mask, starts, table, frequency):
    sec = lax.axis_index("section")
    d = lax.axis_index("dp")
    par = lax.rem(sec, 2)
    own = table.shape[0]
    row_index, counted, _, position = jax.vmap(row_layout)(starts, classes, null_mask, codes)
    picked_labels = jnp.take_along_axis(labels, picks, axis=1)
    picked_counts = jnp.take_along_axis(counted, picks, axis=1).astype(jnp.int32)
    row_index = jnp.pad(row_index, ((0, 0), (0, SP - SLOTS)), constant_values=-1)
    info = jnp.concatenate([row_index, picked_labels, picked_counts], axis=1)
    info = lax.all_gather(info, "dp", axis=0, tiled=True)
    all_labels = info[:, SP : SP + PICKS].reshape(-1)
    all_counts = info[:, SP + PICKS :].reshape(-1).astype(F32)
    gain_row = lax.slice_in_dim(table, VOCAB % own, VOCAB % own + 1)[0].astype(F32)
    holds = (sec == 3) & (d == VOCAB // own)
    g_f = lax.psum(jnp.where(holds, gain_row, 0.0), ("section", "dp"))
    position = jnp.pad(position[par], (0, SP - SLOTS))
    angles = position.astype(F32)[:, None] * frequency[None, :]
    cosine = jnp.tile(jnp.cos(angles), (1, 4))
    sine = jnp.tile(jnp.concatenate([-jnp.sin(angles), jnp.sin(angles)], axis=1), (1, 2))
    gathered = lax.all_gather(table, "dp", axis=0, tiled=True)[:WROWS]
    other = lax.ppermute(gathered, "section", [(0, 1), (1, 0), (2, 3), (3, 2)])
    weights = jnp.where((sec == 1) | (sec == 2), gathered, other)
    local = jnp.where(sec == 0, info[:, :SP].reshape(-1), -1) - d * own
    onehot = (local[:, None] == jnp.arange(own)[None, :]).astype(BF16)
    looked = (nn(onehot, table) * math.sqrt(D)).astype(BF16)
    looked = lax.psum_scatter(looked, "dp", scatter_dimension=0, tiled=True).reshape(2, SP, D)
    from_first = lax.ppermute(looked[1], "section", [(0, 1)])
    x0 = jnp.where(sec == 0, looked[0], from_first)
    return weights, x0, local, all_labels, all_counts, g_f, cosine, sine


def head_anywhere(y, my_picks, all_labels, all_counts, g_f, table):
    sec = lax.axis_index("section")
    d = lax.axis_index("dp")
    n_sec = lax.axis_size("section")
    n_dp = lax.axis_size("dp")
    own = table.shape[0]
    picked = jnp.take(y, my_picks, axis=0)
    all_picked = lax.all_gather(picked, ("section", "dp"), axis=0, tiled=False)
    all_picked = all_picked.reshape(n_sec, n_dp, PICKS, D)[2:].transpose(1, 0, 2, 3)
    all_picked = all_picked.reshape(-1, D).astype(F32)
    af = jnp.where(sec == 3, rms_scale(all_picked, g_f), 0.0).astype(BF16)
    vocab_ids = d * own + jnp.arange(own)
    logits = jnp.where(vocab_ids[None, :] < VOCAB, nt(af, table), NEG)
    local_max = jnp.max(logits, axis=1)
    hit = vocab_ids[None, :] == all_labels[:, None]
    sums = jnp.stack(
        [
            local_max,
            jnp.sum(jnp.exp(logits - local_max[:, None]), axis=1),
            jnp.sum(jnp.where(hit, logits, 0.0), axis=1),
        ]
    )
    every = lax.all_gather(sums, "dp", axis=0, tiled=False)
    top = jnp.max(every[:, 0], axis=0)
    total = jnp.sum(every[:, 1] * jnp.exp(every[:, 0] - top), axis=0)
    target = jnp.sum(every[:, 2], axis=0)
    log_total = top + jnp.log(total)
    loss_part = jnp.where(
        (sec == 3) & (d == 0), jnp.sum(jnp.where(all_counts > 0, log_total - target, 0.0)), 0.0
    )
    dlogits = (jnp.exp(logits - log_total[:, None]) - hit.astype(F32)) * all_counts[:, None]
    dlogits = jnp.where(sec == 3, dlogits, 0.0).astype(BF16)
    d_table = tn(dlogits, af)
    daf = lax.psum(nn(dlogits, table), "dp")
    daf = lax.dynamic_slice_in_dim(daf, d * 2 * PICKS, 2 * PICKS).reshape(2, PICKS, D)
    daf = jnp.where(sec == 3, daf[1], lax.ppermute(daf[0], "section", [(3, 2)]))
    d_own, dg_f = rms_pull(picked.astype(F32), g_f, daf)
    dg_f = jnp.where(sec >= 2, dg_f, 0.0)
    spread = (jnp.arange(SP)[:, None] == my_picks[None, :]).astype(F32)
    d_top = jnp.dot(spread, d_own, precision=lax.Precision.HIGHEST).astype(BF16)
    return d_top, d_table, dg_f, loss_part


UPDATE_ROWS = 272


def update_kernel(rate, gain_block, gain_row, totals, grad, master, momentum, average, out_m, out_v, out_a):
    block = pl.program_id(0)
    value = grad[...]
    sec = lax.axis_index("section")
    dp = lax.axis_index("dp")
    here = jnp.logical_and(jnp.logical_and(sec == 3, dp == VOCAB // OWN), block == gain_block)
    ids = lax.broadcasted_iota(jnp.int32, value.shape, 0)
    gain = jnp.concatenate([totals[k : k + 1, :] for k in range(6)], axis=1)
    value = value + jnp.where(jnp.logical_and(ids == gain_row, here), gain, 0.0)
    scale = jnp.minimum(1.0, clip_limit / (totals[8:9, 0:1] + norm_eps))
    clipped = value * scale
    new_momentum = momentum_decay * momentum[...] + clipped
    new_master = master[...] - rate * (clipped + momentum_decay * new_momentum)
    out_v[...] = new_momentum
    out_m[...] = new_master
    out_a[...] = average_decay * average[...] + (1.0 - average_decay) * new_master


def update(rate, totals, grad, master, momentum, average):
    rows = pl.BlockSpec((UPDATE_ROWS, D), lambda i: (i, 0))
    like = jax.ShapeDtypeStruct((OWN, D), F32)
    at = VOCAB % OWN
    return pl.pallas_call(
        functools.partial(update_kernel, rate, at // UPDATE_ROWS, at % UPDATE_ROWS),
        grid=(OWN // UPDATE_ROWS,),
        out_shape=(like, like, like),
        in_specs=[pl.BlockSpec((16, 128), lambda i: (0, 0))] + [rows] * 4,
        out_specs=(rows, rows, rows),
        compiler_params=pltpu.CompilerParams(vmem_limit_bytes=47 * 2**20),
        name="update",
    )(totals, grad, master, momentum, average)


def shards(codes, labels, picks, classes, null_mask, starts, master, momentum, average):
    sec = lax.axis_index("section")
    d = lax.axis_index("dp")
    n_dp = lax.axis_size("dp")
    n_sec = lax.axis_size("section")
    par = lax.rem(sec, 2)
    own = master.shape[0]
    learn_rate = rate_factor * math.sqrt(own * n_sec * n_dp)
    beside = [(0, 1), (1, 0), (2, 3), (3, 2)]
    fast = n_sec == 4 and n_dp == 8 and own == OWN
    gain_at = VOCAB // own
    frequency = rope_base ** (-jnp.arange(HD // 2, dtype=F32) * 2.0 / HD)

    if fast:
        wide = jnp.tile(frequency[None, :], (1, 4))
        weights, x0, info, gain, cosine, sine, table = gather_and_embed(
            master, codes, labels, picks, starts, classes, null_mask, wide
        )
    else:
        table = master.astype(BF16)
        opened = open_anywhere(codes, labels, picks, classes, null_mask, starts, table, frequency)
        weights, x0, local, all_labels, all_counts, g_f, cosine, sine = opened
    around = (cosine, sine, starts)

    x = forward_call(False, x0, weights, *around)[0]
    y, *kept = forward_call(True, x, weights, *around)

    if fast:
        d_top, d_table, small = head_call(y, picks, info, gain, table)
    else:
        d_top, d_table, dg_f, loss_part = head_anywhere(
            y, picks[par], all_labels, all_counts, g_f, table
        )

    once = backward_call(True, d_top, x, weights, *around, kept)
    dx0, left, right, tail = lax.cond(
        sec < 2,
        lambda: tuple(backward_call(False, once[0], x, weights, *around, kept)),
        lambda: tuple(once),
    )

    if fast:
        grad, squares = reduce_and_scatter(left, right, tail, d_table, dx0, info)
        totals = share_norm(small, squares, n_sec, n_dp)
        updated = update(learn_rate, totals, grad, master, momentum, average)
        return totals[6, 0], totals[6, 1], totals[8, 0], *updated
    else:
        grads = matrix_gradients(left, right, tail)
        grads = grads.astype(F32) + lax.ppermute(grads, "section", beside).astype(F32)
        grads = jnp.pad(grads.astype(BF16), ((0, own * n_dp - WROWS), (0, 0)))
        grad = lax.psum_scatter(grads, "dp", scatter_dimension=0, tiled=True).astype(F32)
        grad = jnp.where(sec == 3, d_table, grad)
        pair = jnp.stack([dx0, lax.ppermute(dx0, "section", [(1, 0)])])
        all_dx = lax.all_gather(pair, "dp", axis=0, tiled=True).reshape(-1, D)
        onehot = (jnp.arange(own)[:, None] == local[None, :]).astype(BF16)
        grad = jnp.where(sec == 0, nn(onehot, all_dx) * math.sqrt(D), grad)
        totals = (dg_f, jnp.sum(grad * grad), loss_part)
        dg_f, squares, loss_sum = lax.psum(totals, ("section", "dp"))
        count_sum = jnp.sum(all_counts)
        grad_norm = jnp.sqrt(squares + jnp.sum(dg_f * dg_f))
    gain_here = (jnp.arange(own) == VOCAB % own)[:, None] & (sec == 3) & (d == gain_at)
    grad = grad + jnp.where(gain_here, dg_f[None, :], 0.0)
    clipped = grad * jnp.minimum(1.0, clip_limit / (grad_norm + norm_eps))
    new_momentum = momentum_decay * momentum + clipped
    new_master = master - learn_rate * (clipped + momentum_decay * new_momentum)
    new_average = average_decay * average + (1.0 - average_decay) * new_master
    return loss_sum, count_sum, grad_norm, new_master, new_momentum, new_average


def solution(mesh):
    split = P("dp", None)
    whole = P(("section", "dp"), None)
    return jax.shard_map(
        shards,
        mesh=mesh,
        in_specs=(split,) * 6 + (whole,) * 3,
        out_specs=(P(), P(), P(), whole, whole, whole),
        check_vma=False,
    )
```

```python
import functools
import math

import jax
import jax.numpy as jnp
from jax import lax
from jax.experimental import pallas as pl
from jax.experimental.pallas import tpu as pltpu
from jax.sharding import PartitionSpec as P

D = 768
HEADS = 12
HD = 64
FF = 2048
VOCAB = 16384
CLASSES = 1001
SLOTS = 264
SP = 272
PICKS = 32
SEGS = 3
MATS = 4 * D + 3 * FF
WROWS = 9232

F32 = jnp.float32
BF16 = jnp.bfloat16

rope_base = 10000.0
clip_limit = 1.0
rate_factor = 0.25
momentum_decay = 0.9
average_decay = 0.8
norm_eps = 1e-06


def nn(left, right):
    return jnp.dot(left, right, preferred_element_type=F32)


def tn(left, right):
    return lax.dot_general(left, right, (((0,), (0,)), ((), ())), preferred_element_type=F32)


def nt(left, right):
    return lax.dot_general(left, right, (((1,), (1,)), ((), ())), preferred_element_type=F32)


def rms_scale(value_in, gain):
    return (
        value_in * lax.rsqrt(jnp.mean(value_in * value_in, axis=-1, keepdims=True) + norm_eps) * gain
    )


def rms_pull(value_in, gain, grad):
    inv = lax.rsqrt(jnp.mean(value_in * value_in, axis=-1, keepdims=True) + norm_eps)
    unit = value_in * inv
    scaled = grad * gain
    grad_in = inv * (scaled - unit * jnp.mean(scaled * unit, axis=-1, keepdims=True))
    return grad_in, jnp.sum(grad * unit, axis=0)


def row_layout(starts_row, classes_row, null_row, codes_row):
    slot_ids = jnp.arange(SLOTS, dtype=jnp.int32)
    segment = jnp.sum((starts_row[None, 1:] <= slot_ids[:, None]).astype(jnp.int32), axis=1)
    seg_start = jnp.sum(
        jnp.where(segment[:, None] == jnp.arange(SEGS + 1)[None, :], starts_row[None, :], 0), axis=1
    )
    position = slot_ids - seg_start
    live_end = starts_row[SEGS]
    is_first = (position == 0) & (slot_ids < live_end)
    clamped = jnp.minimum(segment, SEGS - 1)
    hit = clamped[:, None] == jnp.arange(SEGS)[None, :]
    class_row = jnp.sum(
        jnp.where(hit, jnp.where(null_row > 0, CLASSES - 1, classes_row)[None, :], 0), axis=1
    )
    row_index = jnp.where(is_first, VOCAB + class_row, codes_row)
    following = jnp.concatenate([segment[1:], jnp.full((1,), SEGS + 1, jnp.int32)])
    counted = (following == segment) & (slot_ids + 1 < live_end)
    return row_index, counted, segment, position


MESH = pl.DeviceIdType.MESH
ANY = pl.BlockSpec(memory_space=pl.ANY)
VMEM = pl.BlockSpec(memory_space=pltpu.VMEM)
SMEM = pl.BlockSpec(memory_space=pltpu.SMEM)

OWN = 2176
SPLIT = 1152
COUNT = (18, 16, 18, 16, 11)
ROWS = (64, 64, 64, 64, 48)
HELD = (0, SPLIT, OWN, OWN + SPLIT, 2 * OWN)
LARGE = (16, 14, 16, 14, 11)
SMALL = 4
SMALL_ROWS = 32
LANE = 2 * OWN + 11 * 48
LAG = 2
WINDOW = 2
HOP = 2
PIECES = ((0, 64), (64, 64), (128, 64), (192, 64), (256, 16))
TURN = 6
CHOP = 4
CLAG = 3
AHEAD = 4
CWAIT = 6


def class_base(k, lane):
    if k == 4:
        return 4 * OWN
    return OWN * (2 * (k // 2) + lane) + SPLIT * (k % 2)


def place():
    sec = lax.axis_index("section")
    dp = lax.axis_index("dp")
    z = dp // 2
    c = lax.rem(dp, 2)
    par = lax.rem(sec, 2)
    home = jnp.logical_or(sec == 1, sec == 2)
    return sec, dp, z, c, par, home


def greet_neighbours(sec, dp, z, c, par, turns):
    barrier = pltpu.get_barrier_semaphore()

    def greet(s, e):
        pl.semaphore_signal(barrier, 1, device_id=(s, e), device_id_type=MESH)

    greet(sec, dp + 1 - 2 * c)
    greet(sec + 1 - 2 * par, dp)
    pl.when(z > 0)(lambda: greet(sec, dp - 2))
    pl.when(z < 3)(lambda: greet(sec, dp + 2))
    count = 2 + (z > 0).astype(jnp.int32) + (z < 3).astype(jnp.int32)
    for sender, receiver in turns:
        pl.when(sec == receiver)(lambda sender=sender: greet(sender, dp))
        count = count + (sec == sender).astype(jnp.int32)
    pl.semaphore_wait(barrier, count)


def hop_targets(sec, dp, c, par):
    return {
        "up": (sec, dp + 2),
        "down": (sec, dp - 2),
        "x": (sec + 1 - 2 * par, dp),
        "core": (sec, dp + 1 - 2 * c),
    }


HOPS = ("up", "down", "x", "core")


def tree(z, c, home):
    both = jnp.logical_and
    either = jnp.logical_or
    no = jnp.logical_not
    far = z >= 2
    mid = both(z >= 1, z <= 2)
    never = z < 0
    away = no(home)
    as_int = lambda flag: flag.astype(jnp.int32)
    out = []
    for block in (0, 1):
        for half in (0, 1):
            mine = home if half == 0 else away
            other = no(mine)
            source = both(z == block, home)
            if half == 0:
                early = (lambda j: j < TURN) if block == 0 else (lambda j: j < 0)
                near_x = lambda j, block=block, early=early: both(z == 1 - block, early(j))
                hop_x = lambda j, near_x=near_x: both(home, near_x(j))
                got_x = lambda j, near_x=near_x: both(away, near_x(j))
                along = lambda j, early=early: either(home, no(early(j)))
            else:
                hop_x = lambda j, block=block: both(away, z == 1 - block)
                got_x = lambda j, block=block: both(home, z == 1 - block)
                along = lambda j: away
            at_owner = both(z == block, away)
            if block == 0:
                up = lambda j, along=along, mine=mine: either(both(z == 0, along(j)), both(mid, mine))
                down = lambda j: never
                from_up = lambda j: never
            else:
                up = lambda j, mine=mine: both(mid, mine)
                down = lambda j, along=along: both(z == 1, along(j))
                from_up = lambda j, got_x=got_x: both(z == 0, no(got_x(j)))
            send_x = lambda j, source=source, mine=mine, hop_x=hop_x: either(
                either(source, both(far, mine)), hop_x(j)
            )
            from_x = lambda j, at_owner=at_owner, other=other, got_x=got_x: either(
                either(at_owner, both(far, other)), got_x(j)
            )
            from_down = lambda j, source=source, from_x=from_x, from_up=from_up: no(
                either(source, either(from_x(j), from_up(j)))
            )
            depth = jnp.abs(z - block) + as_int(far) * (half + as_int(other))
            if half == 0:
                depth = depth + (1 - as_int(far)) * as_int(away)
            else:
                depth = depth + (1 - as_int(far)) * jnp.where(
                    away, 1, 2 * as_int(z == 1 - block)
                )
            out.append(
                (source, dict(up=up, down=down, x=send_x), dict(up=from_up, down=from_down, x=from_x), depth)
            )
    lane0 = c == 0
    source = both(both(z == 2, home), lane0)
    sends = dict(
        up=lambda j: both(z == 2, lane0),
        down=lambda j: both(mid, lane0),
        x=lambda j: source,
    )
    parents = dict(
        up=lambda j: both(z <= 1, lane0),
        down=lambda j: both(z == 3, lane0),
        x=lambda j: both(both(z == 2, away), lane0),
    )
    out.append((source, sends, parents, jnp.abs(z - 2) + as_int(away)))
    return out


def segment_of(starts, r, slot):
    bounds = [starts[r, j] for j in range(SEGS + 1)]
    count = lambda at: functools.reduce(
        jnp.add, [(at >= bounds[j]).astype(jnp.int32) for j in range(1, SEGS + 1)]
    )
    segment = count(slot)
    begin = jnp.where(
        segment == 0, bounds[0], jnp.where(segment == 1, bounds[1], jnp.where(segment == 2, bounds[2], bounds[3]))
    )
    counted = jnp.logical_and(count(slot + 1) == segment, slot + 1 < bounds[SEGS])
    return segment, slot - begin, counted, slot < bounds[SEGS]


def open_kernel(
    master, codes, labels, picks, starts, classes, nulls, frequency, out, x0, info, gain, cosine,
    sine, table, exact, master_sem, recv_sem, recv_c, core_sem, send_sem, sent, mine, rx_core, rx_up, rx_down,
    swap_send, swap_recv, x_send, x_recv, line_send, up_recv, down_recv, last_send, last_recv,
    note, note_send, note_recv, gain_send, gain_recv,
):
    sec, dp, z, c, par, home = place()
    targets = hop_targets(sec, dp, c, par)
    classes_of = tree(z, c, home)
    gain_dp = VOCAB // (OWN)
    holds_gain = jnp.logical_and(sec == 3, dp == gain_dp)

    parts = [pl.ds(k * (OWN // 4), OWN // 4) for k in range(4)]
    def place_own(part, value):
        start = pl.multiple_of(dp * OWN + part.start, 16)
        out[pl.ds(start, part.size), :] = value

    fetch = [
        pltpu.make_async_copy(master.at[part], exact.at[part], master_sem.at[k])
        for k, part in enumerate(parts)
    ]
    for one in fetch:
        one.start()

    barrier = pltpu.get_barrier_semaphore()

    def greet(s, e):
        pl.semaphore_signal(barrier, 1, device_id=(s, e), device_id_type=MESH)

    for k in range(1, 8):
        greet(sec, lax.rem(dp + k, 8))
    greet(sec + 1 - 2 * par, dp)
    pl.when(sec == 2)(lambda: greet(0, dp))
    pl.when(sec == 1)(lambda: greet(2, dp))
    pl.when(jnp.logical_and(sec == 2, dp != gain_dp))(lambda: greet(3, gain_dp))

    slot_row = lax.broadcasted_iota(jnp.int32, (1, SLOTS), 1)
    note[...] = jnp.full(note.shape, -1, jnp.int32)
    for r in range(2):
        segment, position, _, live = segment_of(starts, r, slot_row)
        names = [classes[r, j] + (CLASSES - 1 - classes[r, j]) * nulls[r, j] for j in range(SEGS)]
        name = jnp.where(segment == 0, names[0], jnp.where(segment == 1, names[1], names[2]))
        opens = jnp.logical_and(position == 0, live)
        note[r : r + 1, :SLOTS] = jnp.where(opens, VOCAB + name, codes[r : r + 1, :])
        chosen = picks[r : r + 1, :]
        ids = lax.broadcasted_iota(jnp.int32, (SLOTS, PICKS), 0)
        label_col = column(labels[r : r + 1, :], SLOTS)
        note[2 + r : 3 + r, :PICKS] = jnp.sum(
            jnp.where(ids == chosen, label_col, 0), axis=0, keepdims=True
        )
        note[4 + r : 5 + r, :PICKS] = segment_of(starts, r, chosen)[2].astype(jnp.int32)
    info[dp] = note[...]
    for one, part in zip(fetch, parts):
        one.wait()
        value = exact[part, :].astype(BF16)
        table[part, :] = value
        pl.when(jnp.logical_and(home, z < 2))(lambda part=part, value=value: place_own(part, value))
    pl.when(classes_of[4][0])(
        lambda: place_own(pl.ds(0, 11 * 48), exact[pl.ds(0, 11 * 48), :].astype(BF16))
    )
    count = 8 + jnp.logical_or(sec == 0, sec == 2).astype(jnp.int32)
    pl.semaphore_wait(barrier, count + 7 * holds_gain.astype(jnp.int32))
    for k in range(1, 8):
        pltpu.make_async_remote_copy(
            src_ref=note,
            dst_ref=info.at[dp],
            send_sem=note_send,
            recv_sem=note_recv,
            device_id=(sec, lax.rem(dp + k, 8)),
            device_id_type=MESH,
        ).start()
    noted = pltpu.make_async_remote_copy(
        src_ref=info.at[pl.ds(0, 7)],
        dst_ref=info.at[pl.ds(0, 7)],
        send_sem=note_send,
        recv_sem=note_recv,
        device_id=targets["core"],
        device_id_type=MESH,
    )

    gain_rows = table.at[pl.ds(VOCAB % (OWN), 16)]

    def gain_to(s, e):
        return pltpu.make_async_remote_copy(
            src_ref=gain_rows,
            dst_ref=gain,
            send_sem=gain_send,
            recv_sem=gain_recv,
            device_id=(s, e),
            device_id_type=MESH,
        )

    def send_gain():
        for e in range(8):
            gain_to(2, e).start()
            if e != gain_dp:
                gain_to(3, e).start()
        gain[...] = gain_rows[...]

    pl.when(holds_gain)(send_gain)

    def copy(k, hop, offset, rows, recv, slot):
        part = out.at[pl.ds(pl.multiple_of(class_base(k, c) + offset, 16), rows)]
        return pltpu.make_async_remote_copy(
            src_ref=part,
            dst_ref=part,
            send_sem=send_sem.at[k, HOPS.index(hop), slot],
            recv_sem=recv,
            device_id=targets[hop],
            device_id_type=MESH,
        )

    def piece(k, j, small):
        source, sends, _, _ = classes_of[k]
        recv = recv_c.at[j] if k == 4 else recv_sem.at[k, j]
        slot = lax.rem(j, WINDOW)
        rows = SMALL_ROWS if small else ROWS[k]
        offset = ROWS[k] * LARGE[k] + rows * (j - LARGE[k]) if small else rows * j

        def send(hop):
            to = core_sem.at[k] if hop == "core" else recv
            before = j >= WINDOW if hop == "core" else jnp.logical_and(j >= WINDOW, sends[hop](j - WINDOW))
            if small:
                was_large = j < LARGE[k] + WINDOW
                wide_one = copy(k, hop, 0, ROWS[k], to, slot)
                pl.when(jnp.logical_and(before, was_large))(wide_one.wait_send)
                before = jnp.logical_and(before, jnp.logical_not(was_large))
            one = copy(k, hop, offset, rows, to, slot)
            pl.when(before)(one.wait_send)
            one.start()

        pl.when(jnp.logical_not(source))(copy(k, "x", offset, rows, recv, slot).wait_recv)
        for hop in HOPS[:3]:
            pl.when(sends[hop](j))(lambda hop=hop: send(hop))
        send("core")

    first = sec == 0
    second = sec == 2

    def slot(k):
        return pl.ds(pl.multiple_of(k * SP, 16), SP)

    def order(i):
        low = (z <= 1).astype(jnp.int32)
        return low * (3 - i) + (1 - low) * i

    def swap(k):
        return pltpu.make_async_remote_copy(
            src_ref=sent.at[slot(k)],
            dst_ref=rx_core.at[slot(k)],
            send_sem=swap_send,
            recv_sem=swap_recv.at[k],
            device_id=targets["core"],
            device_id_type=MESH,
        )

    def cross(zz):
        return pltpu.make_async_remote_copy(
            src_ref=mine.at[slot(4 + zz)],
            dst_ref=mine.at[slot(zz)],
            send_sem=x_send,
            recv_sem=x_recv.at[zz],
            device_id=(2, dp),
            device_id_type=MESH,
        )

    def piece_of(k, q):
        start, size = PIECES[q]
        return pl.ds(pl.multiple_of(k * SP + start, 16), size)

    def go(zz, q, ref, recv, hop):
        return pltpu.make_async_remote_copy(
            src_ref=mine.at[piece_of(zz, q)],
            dst_ref=ref.at[piece_of(zz, q)],
            send_sem=line_send,
            recv_sem=recv.at[zz, q],
            device_id=targets[hop],
            device_id_type=MESH,
        )

    def go_up(zz, q):
        return go(zz, q, rx_down, down_recv, "up")

    def go_down(zz, q):
        return go(zz, q, rx_up, up_recv, "down")

    def add(there, ref):
        mine[there, :] = (mine[there, :].astype(F32) + ref[there, :].astype(F32)).astype(BF16)

    def look(row):
        local = column(info[row // 2, pl.ds(lax.rem(row, 2), 1), :][:, :SP], SP) - dp * OWN
        ids = lax.broadcasted_iota(jnp.int32, (SP, OWN), 1)
        onehot = jnp.where(ids == local, 1.0, 0.0).astype(BF16)
        return (nn(onehot, table[...]) * math.sqrt(D)).astype(BF16)

    def lookup(b):
        zz = order(b // 2)
        p = 1 - lax.rem(b, 2)
        k = 4 * p + zz
        sent[slot(k), :] = look(2 * (2 * zz + 1 - c) + p)
        swap(k).start()
        mine[slot(k), :] = look(2 * (2 * zz + c) + p)
        swap(k).wait_recv()
        add(slot(k), rx_core)
        pl.when(p == 1)(lambda: cross(zz).start())

    def chain(zz, q):
        def from_below():
            go_up(zz, q).wait_recv()
            add(piece_of(zz, q), rx_down)

        def from_above():
            go_down(zz, q).wait_recv()
            add(piece_of(zz, q), rx_up)

        if q == 0:
            pl.when(second)(cross(zz).wait_recv)
        pl.when(jnp.logical_and(zz >= z, z > 0))(from_below)
        pl.when(jnp.logical_and(zz <= z, z < 3))(from_above)
        pl.when(zz > z)(lambda: go_up(zz, q).start())
        pl.when(zz < z)(lambda: go_down(zz, q).start())

    def chains(i):
        for o in range(4):
            zz = order(o)
            hops = jnp.maximum(
                z * (zz >= z).astype(jnp.int32), (3 - z) * (zz <= z).astype(jnp.int32)
            )
            for q in range(5):
                now = i == 2 * o + 2 + sec + HOP * hops + q
                pl.when(now)(lambda zz=zz, q=q: chain(zz, q))

    segment, position, _, _ = segment_of(starts, par, lax.broadcasted_iota(jnp.int32, (SP, 128), 0))
    angles = position.astype(F32) * frequency[...]
    lanes = lax.broadcasted_iota(jnp.int32, (SP, 128), 1)
    cosine[...] = jnp.cos(angles)
    sine[...] = jnp.where(lax.rem(lanes, 64) < 32, -1.0, 1.0) * jnp.sin(angles)
    noted.wait_recv()

    def step(i, carry):
        for k in range(5):
            j = i - LAG * classes_of[k][3]
            now = jnp.logical_and(j >= 0, j < LARGE[k])
            if k == 4:
                now = jnp.logical_and(now, c == 0)
            pl.when(now)(lambda k=k, j=j: piece(k, j, False))
            if k < 4:
                now = jnp.logical_and(j >= LARGE[k], j < LARGE[k] + SMALL)
                pl.when(now)(lambda k=k, j=j: piece(k, j, True))
        pl.when(jnp.logical_and(first, i < 8))(lambda: lookup(i))
        pl.when(jnp.logical_or(first, second))(lambda: chains(i))
        pl.when(jnp.logical_and(second, i == last_step))(lambda: last().start())
        return carry

    last_step = 6 + 2 + 2 + 3 * HOP + 4 + 1

    def last():
        return pltpu.make_async_remote_copy(
            src_ref=mine.at[slot(z)],
            dst_ref=x0,
            send_sem=last_send,
            recv_sem=last_recv,
            device_id=(1, dp),
            device_id_type=MESH,
        )

    lax.fori_loop(0, max(LARGE[0] + SMALL + 5 * LAG, last_step + 1), step, 0)

    def blocks(count, sem):
        return pltpu.make_async_remote_copy(
            src_ref=mine.at[pl.ds(0, count * SP)],
            dst_ref=mine.at[pl.ds(0, count * SP)],
            send_sem=sem,
            recv_sem=sem,
            device_id=targets["core"],
            device_id_type=MESH,
        )

    def end_first():
        blocks(8, swap_send).wait_send()
        blocks(4, x_send).wait_send()
        blocks(3, line_send).wait_send()
        x0[...] = mine[slot(z), :]

    def end_second():
        blocks(3, line_send).wait_send()
        last().wait_send()

    def none():
        x0[...] = jnp.zeros_like(x0)

    pl.when(first)(end_first)
    pl.when(second)(end_second)
    pl.when(sec == 1)(last().wait_recv)
    pl.when(sec >= 2)(none)

    noted.wait_send()

    def gain_sent():
        for e in range(15):
            gain_to(2, 0).wait_send()

    pl.when(holds_gain)(gain_sent)
    pl.when(jnp.logical_and(sec >= 2, jnp.logical_not(holds_gain)))(gain_to(2, dp).wait_recv)

    def drain(k):
        count, rows = (LARGE[4], ROWS[4]) if k == 4 else (LARGE[k] + SMALL, SMALL_ROWS)
        _, sends, _, _ = classes_of[k]
        for j in range(count - WINDOW, count):
            for hop in HOPS[:3]:
                one = copy(k, hop, 0, rows, core_sem.at[k], j % WINDOW)
                pl.when(sends[hop](j))(one.wait_send)
            copy(k, "core", 0, rows, core_sem.at[k], j % WINDOW).wait_send()
        if k == 0:
            for j in range(TURN - WINDOW, TURN):
                one = copy(k, "x", 0, ROWS[0], core_sem.at[k], j % WINDOW)
                last_one = jnp.logical_not(sends["x"](j + WINDOW))
                pl.when(jnp.logical_and(sends["x"](j), last_one))(one.wait_send)

    def came(k):
        count, rows = COUNT[k], ROWS[k]
        part = out.at[pl.ds(pl.multiple_of(class_base(k, 1 - c), 16), count * rows)]
        pltpu.make_async_remote_copy(
            src_ref=part,
            dst_ref=part,
            send_sem=send_sem.at[k, 3, 0],
            recv_sem=core_sem.at[k],
            device_id=targets["core"],
            device_id_type=MESH,
        ).wait_recv()

    for k in range(4):
        drain(k)
        came(k)
    pl.when(c == 0)(lambda: drain(4))
    pl.when(c == 1)(lambda: came(4))


def gather_and_embed(master, codes, labels, picks, starts, classes, nulls, frequency):
    rows = lambda n: pltpu.VMEM((n * SP, D), BF16)
    return pl.pallas_call(
        open_kernel,
        out_shape=(
            jax.ShapeDtypeStruct((WROWS, D), BF16),
            jax.ShapeDtypeStruct((SP, D), BF16),
            jax.ShapeDtypeStruct((8, 8, 384), jnp.int32),
            jax.ShapeDtypeStruct((16, D), BF16),
            jax.ShapeDtypeStruct((SP, 128), F32),
            jax.ShapeDtypeStruct((SP, 128), F32),
            jax.ShapeDtypeStruct((OWN, D), BF16),
        ),
        in_specs=[ANY] + [VMEM] * 3 + [SMEM] * 3 + [VMEM],
        out_specs=(VMEM,) * 7,
        scratch_shapes=[
            pltpu.VMEM((OWN, D), F32),
            pltpu.SemaphoreType.DMA((4,)),
            pltpu.SemaphoreType.DMA((4, 20)),
            pltpu.SemaphoreType.DMA((11,)),
            pltpu.SemaphoreType.DMA((5,)),
            pltpu.SemaphoreType.DMA((5, 4, WINDOW)),
            rows(8),
            rows(8),
            rows(8),
            rows(4),
            rows(4),
            pltpu.SemaphoreType.DMA,
            pltpu.SemaphoreType.DMA((8,)),
            pltpu.SemaphoreType.DMA,
            pltpu.SemaphoreType.DMA((4,)),
            pltpu.SemaphoreType.DMA,
            pltpu.SemaphoreType.DMA((4, 5)),
            pltpu.SemaphoreType.DMA((4, 5)),
            pltpu.SemaphoreType.DMA,
            pltpu.SemaphoreType.DMA,
            pltpu.VMEM((8, 384), jnp.int32),
        ]
        + [pltpu.SemaphoreType.DMA] * 4,
        compiler_params=pltpu.CompilerParams(
            collective_id=0, has_side_effects=True, vmem_limit_bytes=56 * 2**20
        ),
        name="gather_and_embed",
    )(master, codes, labels, picks, starts, classes, nulls, frequency)


def close_kernel(
    left_any, right_any, tail, start, block, info, out, squares, left, right, loc, sent, rx_core,
    rx_up, rx_down, rx_x, summed, ring, all_dx, load_sem, core_sem, recv_sem, recv_c, core_send,
    send_sem, ring_sem, dx_own, dx_send, line_recv, cross_recv, turn_recv, dx_core_send,
    dx_core_recv, index, ready,
):
    sec, dp, z, c, par, home = place()
    targets = hop_targets(sec, dp, c, par)
    classes = tree(z, c, home)
    loads = [
        pltpu.make_async_copy(left_any, left, load_sem.at[0]),
        pltpu.make_async_copy(right_any, right, load_sem.at[1]),
    ]
    for one in loads:
        one.start()
    del start
    greet_neighbours(sec, dp, z, c, par, ((1, 2), (0, 2)))
    pl.when(sec == 0)(
        lambda: pl.semaphore_signal(ready, 1, device_id=(2, dp), device_id_type=MESH)
    )
    for one in loads:
        one.wait()

    def place_of(hop, k, j):
        offset = j * ROWS[k]
        if hop == "down":
            base = (0, 0, 0, SPLIT, OWN)[k]
        elif hop == "up":
            base = (0, SPLIT, OWN, OWN, OWN + SPLIT)[k]
        else:
            base = HELD[k]
        return pl.ds(pl.multiple_of(base + offset, 16), ROWS[k])

    def gradient(first_row, size):
        first_row = jnp.int32(first_row)
        bounds = (D, 2 * D, 3 * D, 4 * D, 4 * D + 2 * FF)
        matrix = functools.reduce(
            jnp.add, [(first_row >= bound).astype(jnp.int32) for bound in bounds]
        )
        cols = pl.ds(pl.multiple_of(first_row, 128), size)
        return tn(left[:, cols], right[matrix]).astype(BF16)

    def core_copy(k, offset, rows, sem):
        part = pl.ds(pl.multiple_of(HELD[k] + offset, 16), rows)
        return pltpu.make_async_remote_copy(
            src_ref=sent.at[part],
            dst_ref=rx_core.at[part],
            send_sem=core_send,
            recv_sem=sem,
            device_id=targets["core"],
            device_id_type=MESH,
        )

    def form(k, t):
        there = pl.ds(pl.multiple_of(HELD[k] + 128 * t, 128), 128)
        sent[there, :] = gradient(class_base(k, 1 - c) + 128 * t, 128)
        core_copy(k, 128 * t, 128, core_sem.at[k, t]).start()
        loc[there, :] = gradient(class_base(k, c) + 128 * t, 128)

    last_rows = 11 * 48

    def form_last(into):
        for t in range(4):
            into[pl.ds(HELD[4] + 128 * t, 128), :] = gradient(4 * OWN + 128 * t, 128)
        into[pl.ds(HELD[4] + 512, 16), :] = tail[...]

    def form_for_other():
        form_last(sent)
        core_copy(4, 0, last_rows, core_sem.at[4, 0]).start()

    squares[...] = jnp.zeros_like(squares)

    def count_squares(value):
        folded = value * value
        size = folded.shape[0]
        while size > 8 and size % 16 == 0:
            size //= 2
            folded = folded[:size] + folded[size:]
        for part in range(size // 8):
            for n in range(D // 128):
                squares[...] += folded[part * 8 : (part + 1) * 8, n * 128 : (n + 1) * 128]

    rx = dict(up=rx_up, down=rx_down, x=rx_x)

    def onward(k, hop, j):
        back = dict(up="down", down="up", x="x")[hop]
        return landing(k, back, hop, j)

    def landing(k, back, hop, j):
        index = ("up", "down", "x").index(back)
        part = pl.ds(pl.multiple_of(HELD[k] + j * ROWS[k], 16), ROWS[k])
        return pltpu.make_async_remote_copy(
            src_ref=loc.at[part],
            dst_ref=rx[back].at[place_of(back, k, j)],
            send_sem=send_sem.at[k],
            recv_sem=recv_c.at[index, j] if k == 4 else recv_sem.at[index, k, j],
            device_id=targets[hop],
            device_id_type=MESH,
        )

    def gathered(k, j):
        part = pl.ds(pl.multiple_of(HELD[k] + j * ROWS[k], 16), ROWS[k])
        if k == 4:
            pl.when(j == 0)(lambda: core_copy(4, 0, last_rows, core_sem.at[4, 0]).wait_recv())
        else:
            pl.when(lax.rem(j, 2) == 0)(
                lambda: core_copy(k, 64 * j, 128, core_sem.at[k, j // 2]).wait_recv()
            )
        acc = summed.at[pl.ds(0, ROWS[k])]
        acc[...] = loc[part, :].astype(F32) + rx_core[part, :].astype(F32)
        for hop in HOPS[:3]:
            if (hop, k) in (("down", 0), ("down", 1)):
                continue

            def add(hop=hop):
                landing(k, hop, hop, j).wait_recv()
                acc[...] += rx[hop][place_of(hop, k, j), :].astype(F32)

            pl.when(classes[k][1][hop](j))(add)
        return part, acc

    def relay(k, j):
        part, acc = gathered(k, j)
        loc[part, :] = acc[...].astype(BF16)
        for hop in HOPS[:3]:
            pl.when(classes[k][2][hop](j))(lambda hop=hop: onward(k, hop, j).start())

    def write(slot, rows, offset):
        return pltpu.make_async_copy(
            ring.at[pl.ds(pl.multiple_of(slot * 64, 64), rows)],
            out.at[pl.ds(pl.multiple_of(offset, 16), rows)],
            ring_sem.at[slot],
        )

    def finish(k, j):
        _, acc = gathered(k, j)
        slot = 4 * (k % 2) + lax.rem(j, 4)
        copy = write(slot, ROWS[k], SPLIT * (k % 2) + j * ROWS[k])
        pl.when(j >= 4)(copy.wait)
        value = acc[...]
        ring[pl.ds(pl.multiple_of(slot * 64, 64), ROWS[k]), :] = value
        copy.start()
        count_squares(value)

    first = sec == 0
    second = sec == 2
    in_line = jnp.logical_or(first, second)
    p_line = second.astype(jnp.int32)
    both = jnp.logical_and

    def dx_part(p, zz):
        return all_dx.at[pl.ds(pl.multiple_of((2 * (2 * zz + c) + p) * SP, 16), SP)]

    def move(p, zz, send, recv, target):
        return pltpu.make_async_remote_copy(
            src_ref=dx_part(p, zz),
            dst_ref=dx_part(p, zz),
            send_sem=send,
            recv_sem=recv,
            device_id=target,
            device_id_type=MESH,
        )

    def line(zz, hop):
        return move(p_line, zz, dx_send, line_recv.at[zz], targets[hop])

    def cross(zz):
        return move(1, zz, dx_send, cross_recv.at[zz], (0, dp))

    def dx_to_core(p, zz):
        return move(p, zz, dx_core_send, dx_core_recv, targets["core"])

    def aside(zz):
        pl.when(first)(lambda: dx_to_core(0, zz).start())
        pl.when(second)(lambda: cross(zz).start())

    def crossed(zz):
        cross(zz).wait_recv()
        dx_to_core(1, zz).start()

    def blocks(count, send, recv):
        return pltpu.make_async_remote_copy(
            src_ref=all_dx.at[pl.ds(0, count * SP)],
            dst_ref=all_dx.at[pl.ds(0, count * SP)],
            send_sem=send,
            recv_sem=recv,
            device_id=targets["core"],
            device_id_type=MESH,
        )

    turned = pltpu.make_async_remote_copy(
        src_ref=block,
        dst_ref=dx_part(1, z),
        send_sem=dx_send,
        recv_sem=turn_recv,
        device_id=(2, dp),
        device_id_type=MESH,
    )
    pl.when(sec == 1)(turned.start)

    def pass_own():
        pl.when(z < 3)(lambda: line(z, "up").start())
        pl.when(z > 0)(lambda: line(z, "down").start())
        aside(z)

    def own_first():
        own = pltpu.make_async_copy(block, dx_part(0, z), dx_own)
        own.start()
        own.wait()
        pass_own()

    def own_second():
        turned.wait_recv()
        pl.semaphore_wait(ready, 1)
        pass_own()

    pl.when(first)(own_first)

    def list_rows():
        for e in range(8):
            for p in range(2):
                there = pl.ds((2 * e + p) * SP, SP)
                index[:, there] = info[e, p : p + 1, :][:, :SP] - dp * OWN

    pl.when(first)(list_rows)

    def from_below(k):
        line(z - k, "up").wait_recv()
        pl.when(z < 3)(lambda: line(z - k, "up").start())
        aside(z - k)

    def from_above(k):
        line(z + k, "down").wait_recv()
        pl.when(z > 0)(lambda: line(z + k, "down").start())
        aside(z + k)

    def tile(t):
        ids = lax.broadcasted_iota(jnp.int32, (SP, 16 * SP), 0) + t * SP
        onehot = jnp.where(ids == index[...], 1.0, 0.0).astype(BF16)
        value = nn(onehot, all_dx[...]) * math.sqrt(D)
        slot = lax.rem(t, 2)
        copy = write_tile(slot, t)
        pl.when(t >= 2)(copy.wait)
        ring[pl.ds(pl.multiple_of(slot * SP, 16), SP), :] = value
        copy.start()
        count_squares(value)

    def write_tile(slot, t):
        return pltpu.make_async_copy(
            ring.at[pl.ds(pl.multiple_of(slot * SP, 16), SP)],
            out.at[pl.ds(pl.multiple_of(t * SP, 16), SP)],
            ring_sem.at[slot],
        )

    def collect(i):
        pl.when(both(second, i == CHOP + AHEAD))(own_second)
        for k in range(1, 4):
            now = i == CHOP * (k + p_line) + AHEAD * p_line
            pl.when(both(now, z >= k))(lambda k=k: from_below(k))
            pl.when(both(now, z + k <= 3))(lambda k=k: from_above(k))

    begin = 5 * CHOP + 1

    def embed(i):
        pl.when(i == 2 * CHOP)(lambda: crossed(z))
        for k in range(1, 4):
            pl.when(both(i == CHOP * (k + 2), z >= k))(lambda k=k: crossed(z - k))
            pl.when(both(i == CHOP * (k + 2), z + k <= 3))(lambda k=k: crossed(z + k))
        pl.when(i == begin)(lambda: blocks(8, dx_core_send, dx_core_recv).wait_recv())
        t = i - begin
        pl.when(both(t >= 0, t < OWN // SP))(lambda: tile(t))

    def step(i, carry):
        for k in range(4):
            turn_now = both(lax.rem(i, 2) == k // 2, i < COUNT[k] + k // 2)
            pl.when(turn_now)(lambda k=k: form(k, i // 2))
        pl.when(both(i == CWAIT - 1, c == 0))(lambda: form_last(loc))
        pl.when(both(i == CWAIT - 1, c == 1))(form_for_other)
        for k in range(5):
            source, _, _, depth = classes[k]
            j = i - CLAG * ((5, 5, 4, 4, 3)[k] - depth) - (0, 0, 1, 1, CWAIT)[k]
            now = both(j >= 0, j < COUNT[k])
            if k == 4:
                now = both(now, c == 0)
            pl.when(both(now, jnp.logical_not(source)))(lambda k=k, j=j: relay(k, j))
            pl.when(both(now, source))(lambda k=k, j=j: finish(k, j))
        pl.when(in_line)(lambda: collect(i))
        pl.when(first)(lambda: embed(i))
        return carry

    lax.fori_loop(0, max(18 + 5 * CLAG, begin + OWN // SP), step, 0)
    pl.when(first)(lambda: blocks(8, dx_core_send, dx_core_recv).wait_send())

    def dx_sent(count):
        blocks(count, dx_send, dx_core_recv).wait_send()

    middle = both(z >= 1, z <= 2)
    ends = jnp.logical_not(middle)
    pl.when(jnp.logical_or(sec == 1, both(first, ends)))(lambda: dx_sent(1))
    pl.when(both(first, middle))(lambda: dx_sent(5))
    pl.when(both(second, ends))(lambda: dx_sent(5))
    pl.when(both(second, middle))(lambda: dx_sent(9))
    def sent_core(rows):
        part = pl.ds(0, rows)
        pltpu.make_async_remote_copy(
            src_ref=sent.at[part],
            dst_ref=rx_core.at[part],
            send_sem=core_send,
            recv_sem=core_sem.at[4, 0],
            device_id=targets["core"],
            device_id_type=MESH,
        ).wait_send()

    pl.when(c == 0)(lambda: sent_core(2 * OWN))
    pl.when(c == 1)(lambda: sent_core(LANE))
    for k in range(5):
        part = pl.ds(HELD[k], COUNT[k] * ROWS[k])
        gone = pltpu.make_async_remote_copy(
            src_ref=loc.at[part],
            dst_ref=rx_x.at[part],
            send_sem=send_sem.at[k],
            recv_sem=core_sem.at[4, 0],
            device_id=targets["x"],
            device_id_type=MESH,
        )
        away = jnp.logical_not(classes[k][0])
        pl.when(both(away, c == 0) if k == 4 else away)(gone.wait_send)

    def drain_half(k):
        for j in range(COUNT[k] - 4, COUNT[k]):
            write(4 * (k % 2) + j % 4, ROWS[k], 0).wait()

    def drain_tiles():
        for slot in range(2):
            write_tile(slot, 0).wait()

    for k in range(5):
        pl.when(classes[k][0])(lambda k=k: drain_half(k))
    pl.when(first)(drain_tiles)


def reduce_and_scatter(left, right, tail, start, block, info):
    low = lambda *shape: pltpu.VMEM(shape, BF16)
    dma = pltpu.SemaphoreType.DMA
    return pl.pallas_call(
        close_kernel,
        out_shape=(
            jax.ShapeDtypeStruct((OWN, D), F32),
            jax.ShapeDtypeStruct((8, 128), F32),
        ),
        in_specs=[ANY, ANY, VMEM, ANY, VMEM, VMEM],
        out_specs=(ANY, VMEM),
        input_output_aliases={3: 0},
        scratch_shapes=[
            low(SP, MATS),
            low(6, SP, D),
            low(LANE, D),
            low(LANE, D),
            low(LANE, D),
            low(OWN + SPLIT + 11 * 48, D),
            low(OWN + 11 * 48, D),
            low(LANE, D),
            pltpu.VMEM((64, D), F32),
            pltpu.VMEM((2 * SP, D), F32),
            low(16 * SP, D),
            dma((2,)),
            dma((5, 9)),
            dma((3, 4, 18)),
            dma((3, 11)),
            dma,
            dma((5,)),
            dma((8,)),
            dma,
            dma,
            dma((4,)),
            dma((4,)),
            dma,
            dma,
            dma,
            pltpu.VMEM((1, 16 * SP), jnp.int32),
            pltpu.SemaphoreType.REGULAR,
        ],
        compiler_params=pltpu.CompilerParams(
            collective_id=1, has_side_effects=True, vmem_limit_bytes=63 * 2**20
        ),
        name="reduce_and_scatter",
    )(left, right, tail, start, block, info)


def norm_kernel(n_sec, n_dp, small, squares, out, block, every, send_sem, recv_sem):
    sec = lax.axis_index("section")
    dp = lax.axis_index("dp")
    n = n_sec * n_dp
    me = sec * n_dp + dp
    barrier = pltpu.get_barrier_semaphore()

    def peer(k):
        other = lax.rem(me + k, n)
        return (other // n_dp, lax.rem(other, n_dp))

    def greet(k, carry):
        pl.semaphore_signal(barrier, 1, device_id=peer(k), device_id_type=MESH)
        return carry

    lax.fori_loop(1, n, greet, 0)
    block[...] = small[...]
    block[7:8, :] += jnp.sum(squares[...], axis=0, keepdims=True)
    every[me] = block[...]
    pl.semaphore_wait(barrier, n - 1)

    def send(k, carry):
        pltpu.make_async_remote_copy(
            src_ref=block,
            dst_ref=every.at[me],
            send_sem=send_sem,
            recv_sem=recv_sem,
            device_id=peer(k),
            device_id_type=MESH,
        ).start()
        return carry

    lax.fori_loop(1, n, send, 0)
    others = pltpu.make_async_remote_copy(
        src_ref=every.at[pl.ds(0, n - 1)],
        dst_ref=every.at[pl.ds(0, n - 1)],
        send_sem=send_sem,
        recv_sem=recv_sem,
        device_id=peer(1),
        device_id_type=MESH,
    )
    others.wait_recv()
    total = every[0]
    for k in range(1, n):
        total = total + every[k]
    gains = jnp.sum(total[0:6] * total[0:6], axis=0, keepdims=True)
    norm = jnp.sqrt(jnp.sum(gains + total[7:8], axis=1, keepdims=True))
    out[0:8, :] = total
    out[8:16, :] = jnp.broadcast_to(norm, (8, 128))
    others.wait_send()


def share_norm(small, squares, n_sec, n_dp):
    return pl.pallas_call(
        functools.partial(norm_kernel, n_sec, n_dp),
        out_shape=jax.ShapeDtypeStruct((16, 128), F32),
        in_specs=[VMEM, VMEM],
        out_specs=VMEM,
        scratch_shapes=[
            pltpu.VMEM((8, 128), F32),
            pltpu.VMEM((n_sec * n_dp, 8, 128), F32),
            pltpu.SemaphoreType.DMA,
            pltpu.SemaphoreType.DMA,
        ],
        compiler_params=pltpu.CompilerParams(
            collective_id=8, has_side_effects=True, vmem_limit_bytes=2**20
        ),
        cost_estimate=pl.CostEstimate(
            flops=10**10, bytes_accessed=4 * 10**7, transcendentals=0
        ),
        name="share_norm",
    )(small, squares)


NEG = -1e30
FT = 256


def turn(block, cosine, sine, lanes):
    ahead = pltpu.roll(block, 96, 1)
    behind = pltpu.roll(block, 32, 1)
    return block * cosine + jnp.where(lax.rem(lanes, 64) < 32, ahead, behind) * sine


def see(starts):
    par = lax.rem(lax.axis_index("section"), 2)
    rows = lax.broadcasted_iota(jnp.int32, (SP, SP), 0)
    cols = lax.broadcasted_iota(jnp.int32, (SP, SP), 1)
    same = segment_of(starts, par, rows)[0] == segment_of(starts, par, cols)[0]
    allowed = jnp.logical_and(same, cols <= rows)
    return jnp.where(allowed, 0.0, NEG)


def hide(starts):
    par = lax.rem(lax.axis_index("section"), 2)
    rows = lax.broadcasted_iota(jnp.int32, (SP, SP), 0)
    cols = lax.broadcasted_iota(jnp.int32, (SP, SP), 1)
    same = segment_of(starts, par, rows)[0] == segment_of(starts, par, cols)[0]
    return jnp.where(jnp.logical_and(same, rows <= cols), 0.0, NEG)


def softmax_of(scores, unseen):
    masked = scores + unseen
    grown = jnp.exp(masked - jnp.max(masked, axis=-1, keepdims=True))
    return grown / jnp.sum(grown, axis=-1, keepdims=True)


def weight_copies(w_any, w, sems):
    bounds = (0, 3 * D, 4 * D, 4 * D + FF, 4 * D + 2 * FF, MATS, WROWS)
    return [
        pltpu.make_async_copy(
            w_any.at[pl.ds(lo, hi - lo)], w.at[pl.ds(lo, hi - lo)], sems.at[i]
        )
        for i, (lo, hi) in enumerate(zip(bounds[:-1], bounds[1:]))
    ]


def forward_kernel(keep, x, w_any, cosine, sine, starts, y, *refs):
    kept = refs[:7] if keep else ()
    q, k, v, o, h, gate, up, w, m, unseen, sems, keep_sems, *hop_sems = refs[len(kept) :]
    sec = lax.axis_index("section")
    dp = lax.axis_index("dp")
    lower = sec < 2
    if not keep:
        barrier = pltpu.get_barrier_semaphore()
        pl.when(jnp.logical_not(lower))(
            lambda: pl.semaphore_signal(barrier, 1, device_id=(sec - 2, dp), device_id_type=MESH)
        )

    def hop(b):
        part = y.at[:, pl.ds(b * 256, 256)]
        return pltpu.make_async_remote_copy(
            src_ref=part,
            dst_ref=part,
            send_sem=hop_sems[0].at[b],
            recv_sem=hop_sems[1].at[b],
            device_id=(sec + 2, dp),
            device_id_type=MESH,
        )

    def put(i):
        if keep:
            pltpu.make_async_copy((q, k, v, o, h, gate, up)[i], kept[i], keep_sems.at[i]).start()

    def run():
        copies = weight_copies(w_any, w, sems)
        for i in (5, 0, 1, 2, 3, 4):
            copies[i].start()
        unseen[...] = see(starts)
        lanes = lax.broadcasted_iota(jnp.int32, (SP, 128), 1)
        first = lanes < 64
        copies[5].wait()
        gains = w[pl.ds(MATS, 16), :].astype(F32)
        stream = x[...].astype(F32)
        a1 = rms_scale(stream, gains[0:1]).astype(BF16)
        copies[0].wait()

        def project(b, carry):
            cols = pl.ds(pl.multiple_of(b * 256, 256), 256)
            raw_q = nn(a1, w[pl.ds(0, D), cols])
            raw_k = nn(a1, w[pl.ds(D, D), cols])
            raw_v = nn(a1, w[pl.ds(2 * D, D), cols])
            v[:, cols] = raw_v.astype(BF16)
            for part in range(2):
                there = pl.ds(pl.multiple_of(b * 256 + part * 128, 128), 128)
                here = slice(part * 128, (part + 1) * 128)
                turned_q = turn(raw_q[:, here], cosine[...], sine[...], lanes)
                q[:, there] = (turned_q * HD ** (-0.5)).astype(BF16)
                k[:, there] = turn(raw_k[:, here], cosine[...], sine[...], lanes).astype(BF16)
            return carry

        lax.fori_loop(0, D // 256, project, 0, unroll=True)
        for i in range(3):
            put(i)

        def attend(b, carry):
            cols = pl.ds(pl.multiple_of(b * 128, 128), 128)
            qb, kb, vb = q[:, cols], k[:, cols], v[:, cols]
            zero = jnp.zeros_like(qb)
            p0 = softmax_of(nt(jnp.where(first, qb, zero), kb), unseen[...]).astype(BF16)
            p1 = softmax_of(nt(jnp.where(first, zero, qb), kb), unseen[...]).astype(BF16)
            o[:, cols] = jnp.where(first, nn(p0, vb), nn(p1, vb)).astype(BF16)
            return carry

        lax.fori_loop(0, HEADS // 2, attend, 0, unroll=True)
        put(3)
        copies[1].wait()
        for b in range(3):
            cols = pl.ds(b * 256, 256)
            h[:, cols] = x[:, cols].astype(F32) + nn(o[...], w[pl.ds(3 * D, D), cols])
        put(4)
        a2 = rms_scale(h[...], gains[1:2]).astype(BF16)
        copies[2].wait()
        copies[3].wait()

        def widen(b, carry):
            cols = pl.ds(pl.multiple_of(b * FT, FT), FT)
            g = nt(a2, w[pl.ds(pl.multiple_of(4 * D + b * FT, FT), FT), :])
            u = nt(a2, w[pl.ds(pl.multiple_of(4 * D + FF + b * FT, FT), FT), :])
            gate[:, cols] = g
            up[:, cols] = u
            m[:, cols] = (g / (1.0 + jnp.exp(-g)) * u).astype(BF16)
            return carry

        lax.fori_loop(0, FF // FT, widen, 0, unroll=True)
        put(5)
        put(6)
        copies[4].wait()

        if not keep:
            pl.semaphore_wait(barrier, 1)
        for b in range(3):
            cols = pl.ds(b * 256, 256)
            y[:, cols] = (h[:, cols] + nn(m[...], w[pl.ds(4 * D + 2 * FF, FF), cols])).astype(BF16)
            if not keep:
                hop(b).start()
        for i, part in enumerate(kept):
            pltpu.make_async_copy((q, k, v, o, h, gate, up)[i], part, keep_sems.at[i]).wait()
        if not keep:
            for b in range(3):
                hop(b).wait_send()
            y[...] = x[...]

    if keep:
        run()
        return
    pl.when(lower)(run)

    def arrive():
        for b in range(3):
            hop(b).wait_recv()

    pl.when(jnp.logical_not(lower))(arrive)


KEPT = ((D, BF16), (D, BF16), (D, BF16), (D, BF16), (D, F32), (FF, F32), (FF, F32))


def forward_call(keep, x, weights, cosine, sine, starts):
    low = jax.ShapeDtypeStruct((SP, D), BF16)
    kept = tuple(jax.ShapeDtypeStruct((SP, n), t) for n, t in KEPT) if keep else ()
    return pl.pallas_call(
        functools.partial(forward_kernel, keep),
        out_shape=(low,) + kept,
        in_specs=[VMEM, ANY, VMEM, VMEM, SMEM],
        out_specs=(VMEM,) + (ANY,) * len(kept),
        scratch_shapes=[pltpu.VMEM((SP, n), t) for n, t in KEPT]
        + [
            pltpu.VMEM((WROWS, D), BF16),
            pltpu.VMEM((SP, FF), BF16),
            pltpu.VMEM((SP, SP), F32),
            pltpu.SemaphoreType.DMA((6,)),
            pltpu.SemaphoreType.DMA((7,)),
        ]
        + ([] if keep else [pltpu.SemaphoreType.DMA((3,))] * 2),
        compiler_params=pltpu.CompilerParams(vmem_limit_bytes=56 * 2**20)
        if keep
        else pltpu.CompilerParams(
            collective_id=6, has_side_effects=True, vmem_limit_bytes=56 * 2**20
        ),
        name="layer_forward_kept" if keep else "layer_forward",
    )(x, weights, cosine, sine, starts)


def rms_back(value_in, gain, grad):
    inv = lax.rsqrt(jnp.mean(value_in * value_in, axis=-1, keepdims=True) + norm_eps)
    unit = value_in * inv
    scaled = grad * gain
    grad_in = inv * (scaled - unit * jnp.mean(scaled * unit, axis=-1, keepdims=True))
    return grad_in, jnp.sum(grad * unit, axis=0, keepdims=True)


def backward_kernel(send, dy_any, x, w_any, cosine, sine, starts, *refs):
    kept, refs = refs[:7], refs[7:]
    dx, left, right, tail, refs = *refs[:4], refs[4:]
    q, k, v, o, h, gate, up, w, dgate, dup, m, da, do, dq, dk, dv, a1, a2, db, *refs = refs
    unseen, sems, keep_sems, out_sems, dy, dy_sem, *hop_sems = refs
    sec = lax.axis_index("section")
    dp = lax.axis_index("dp")
    upper = sec >= 2
    if send:
        barrier = pltpu.get_barrier_semaphore()
        pl.when(jnp.logical_not(upper))(
            lambda: pl.semaphore_signal(barrier, 1, device_id=(sec + 2, dp), device_id_type=MESH)
        )

    def hop():
        return pltpu.make_async_remote_copy(
            src_ref=dx,
            dst_ref=dx,
            send_sem=hop_sems[0],
            recv_sem=hop_sems[1],
            device_id=(sec - 2, dp),
            device_id_type=MESH,
        )

    outs = []

    def put(source, target):
        copy = pltpu.make_async_copy(source, target, out_sems.at[len(outs)])
        copy.start()
        outs.append(copy)
    def run():
        fetch = pltpu.make_async_copy(dy_any, dy, dy_sem)
        fetch.start()
        copies = weight_copies(w_any, w, sems)
        taken = [
            pltpu.make_async_copy(part, (q, k, v, o, h, gate, up)[i], keep_sems.at[i])
            for i, part in enumerate(kept)
        ]
        for one in (
            copies[4], taken[5], taken[6], copies[5], copies[2], copies[3], taken[4], copies[1],
            taken[0], taken[1], taken[2], copies[0], taken[3],
        ):
            one.start()
        unseen[...] = hide(starts)
        lanes = lax.broadcasted_iota(jnp.int32, (SP, 128), 1)
        first = lanes < 64
        fetch.wait()
        copies[4].wait()
        taken[5].wait()
        taken[6].wait()

        def open_mlp(b, carry):
            cols = pl.ds(pl.multiple_of(b * FT, FT), FT)
            dm = nt(dy[...], w[pl.ds(pl.multiple_of(4 * D + 2 * FF + b * FT, FT), FT), :])
            g = gate[:, cols]
            u = up[:, cols]
            sig = 1.0 / (1.0 + jnp.exp(-g))
            dgate[:, cols] = (dm * u * sig * (1.0 + g * (1.0 - sig))).astype(BF16)
            dup[:, cols] = (dm * g * sig).astype(BF16)
            m[:, cols] = (g * sig * u).astype(BF16)
            return carry

        lax.fori_loop(0, FF // FT, open_mlp, 0, unroll=True)
        for i, part in enumerate((dgate, dup, m)):
            put(part, left.at[:, pl.ds(4 * D + i * FF, FF)])
        put(dy, right.at[5])
        copies[5].wait()
        gains = w[pl.ds(MATS, 16), :].astype(F32)
        copies[2].wait()
        copies[3].wait()

        def close_mlp(b, carry):
            cols = pl.ds(pl.multiple_of(b * 256, 256), 256)
            da[:, cols] = nn(dgate[...], w[pl.ds(4 * D, FF), cols]) + nn(
                dup[...], w[pl.ds(4 * D + FF, FF), cols]
            )
            return carry

        lax.fori_loop(0, 3, close_mlp, 0, unroll=True)
        taken[4].wait()
        dh, dg_mlp = rms_back(h[...], gains[1:2], da[...])
        dh = dh + dy[...].astype(F32)
        db[...] = dh.astype(BF16)
        a2[...] = rms_scale(h[...], gains[1:2]).astype(BF16)
        put(db, right.at[3])
        put(a2, right.at[4])
        copies[1].wait()
        for b in range(3):
            do[:, pl.ds(b * 256, 256)] = nt(db[...], w[pl.ds(3 * D + b * 256, 256), :]).astype(BF16)

        for i in range(3):
            taken[i].wait()

        def attend(b, carry):
            cols = pl.ds(pl.multiple_of(b * 128, 128), 128)
            qb, kb, vb, dob = q[:, cols], k[:, cols], v[:, cols], do[:, cols]
            zero = jnp.zeros_like(qb)
            parts = []
            for head in range(2):
                keep = first if head == 0 else jnp.logical_not(first)
                masked = nt(jnp.where(keep, kb, zero), qb) + unseen[...]
                grown = jnp.exp(masked - jnp.max(masked, axis=0, keepdims=True))
                probs = grown / jnp.sum(grown, axis=0, keepdims=True)
                dprobs = nt(jnp.where(keep, vb, zero), dob)
                along = jnp.sum(probs * dprobs, axis=0, keepdims=True)
                dscores = (probs * (dprobs - along)).astype(BF16)
                parts.append((tn(dscores, kb), nn(dscores, qb), nn(probs.astype(BF16), dob)))
            dqb = jnp.where(first, parts[0][0], parts[1][0]) * HD ** (-0.5)
            dkb = jnp.where(first, parts[0][1], parts[1][1])
            dq[:, cols] = turn(dqb, cosine[...], -sine[...], lanes).astype(BF16)
            dk[:, cols] = turn(dkb, cosine[...], -sine[...], lanes).astype(BF16)
            dv[:, cols] = jnp.where(first, parts[0][2], parts[1][2]).astype(BF16)
            return carry

        lax.fori_loop(0, HEADS // 2, attend, 0, unroll=True)
        for i, part in enumerate((dq, dk, dv)):
            put(part, right.at[i])
        copies[0].wait()
        for b in range(3):
            rows = lambda i, b=b: w[pl.ds(i * D + b * 256, 256), :]
            da[:, pl.ds(b * 256, 256)] = (
                nt(dq[...], rows(0)) + nt(dk[...], rows(1)) + nt(dv[...], rows(2))
            )
        stream = x[...].astype(F32)
        a1[...] = rms_scale(stream, gains[0:1]).astype(BF16)
        for i in range(3):
            put(a1, left.at[:, pl.ds(i * D, D)])
        taken[3].wait()
        put(o, left.at[:, pl.ds(3 * D, D)])
        dstream, dg_attn = rms_back(stream, gains[0:1], da[...])
        dx[...] = (dstream + dh).astype(BF16)
        if send:
            pl.semaphore_wait(barrier, 1)
            hop().start()
        ids = lax.broadcasted_iota(jnp.int32, (16, D), 0)
        tail[...] = jnp.where(ids == 0, dg_attn, jnp.where(ids == 1, dg_mlp, 0.0)).astype(BF16)
        for copy in outs:
            copy.wait()
        if send:
            hop().wait_send()

    if not send:
        run()
        return
    pl.when(upper)(run)
    pl.when(jnp.logical_not(upper))(lambda: hop().wait_recv())


def backward_call(send, dy, x, weights, cosine, sine, starts, kept):
    wide = pltpu.VMEM((SP, FF), BF16)
    narrow = pltpu.VMEM((SP, D), BF16)
    return pl.pallas_call(
        functools.partial(backward_kernel, send),
        out_shape=(
            jax.ShapeDtypeStruct((SP, D), BF16),
            jax.ShapeDtypeStruct((SP, MATS), BF16),
            jax.ShapeDtypeStruct((6, SP, D), BF16),
            jax.ShapeDtypeStruct((16, D), BF16),
        ),
        in_specs=[ANY, VMEM, ANY, VMEM, VMEM, SMEM] + [ANY] * 7,
        out_specs=(VMEM, ANY, ANY, VMEM),
        scratch_shapes=[pltpu.VMEM((SP, n), t) for n, t in KEPT]
        + [
            pltpu.VMEM((WROWS, D), BF16),
            wide,
            wide,
            wide,
            pltpu.VMEM((SP, D), F32),
        ]
        + [narrow] * 7
        + [
            pltpu.VMEM((SP, SP), F32),
            pltpu.SemaphoreType.DMA((6,)),
            pltpu.SemaphoreType.DMA((7,)),
            pltpu.SemaphoreType.DMA((13,)),
            narrow,
            pltpu.SemaphoreType.DMA,
        ]
        + ([pltpu.SemaphoreType.DMA] * 2 if send else []),
        compiler_params=pltpu.CompilerParams(
            collective_id=7, has_side_effects=True, vmem_limit_bytes=60 * 2**20
        )
        if send
        else pltpu.CompilerParams(vmem_limit_bytes=60 * 2**20),
        name="layer_backward_send" if send else "layer_backward",
    )(dy, x, weights, cosine, sine, starts, *kept)


def matrix_gradients(left, right, tail):
    parts = [(0, 0), (D, 1), (2 * D, 2), (3 * D, 3), (4 * D, 4), (4 * D + FF, 4), (4 * D + 2 * FF, 5)]
    ends = [start for start, _ in parts[1:]] + [MATS]
    rows = [
        tn(left[:, start:end], right[i]).astype(BF16) for (start, i), end in zip(parts, ends)
    ]
    return jnp.concatenate(rows + [tail], axis=0)


HEAD_T = 256


def column(row, size):
    there = lax.broadcasted_iota(jnp.int32, (size, size), 0)
    here = lax.broadcasted_iota(jnp.int32, (size, size), 1)
    zero = jnp.zeros((), row.dtype)
    return jnp.sum(jnp.where(there == here, row, zero), axis=1, keepdims=True)


def as_rows(values):
    there = lax.broadcasted_iota(jnp.int32, (128, 128), 0)
    here = lax.broadcasted_iota(jnp.int32, (128, 128), 1)
    return [
        jnp.sum(
            jnp.where(there == here, values[k * 128 : (k + 1) * 128], 0.0), axis=0, keepdims=True
        )
        for k in range(4)
    ]


def head_kernel(
    y, picks, info, gain, table, d_top, d_table, small, mine, picked, af, scores, dlow, labels,
    counts, stat, stats, daf, rx_core, low, rx, fresh, zero_sem, own_sem, pick_send, pick_recv,
    core_send, core_recv, stat_send, stat_recv, swap_send, swap_recv, daf_send, daf_recv,
):
    sec, dp, z, c, par, home = place()
    last = sec == 3
    upper = sec >= 2
    barrier = pltpu.get_barrier_semaphore()
    other_core = (3, dp + 1 - 2 * c)

    def greet(s, e):
        pl.semaphore_signal(barrier, 1, device_id=(s, e), device_id_type=MESH)

    def greet_second():
        for k in range(4):
            greet(3, 2 * k + c)
        pl.semaphore_wait(barrier, 4)

    def greet_third():
        for k in range(4):
            greet(2, 2 * k + c)
        for k in range(1, 8):
            greet(3, lax.rem(dp + k, 8))
        pl.semaphore_wait(barrier, 11)

    all_zero = pltpu.make_async_copy(fresh, d_table, zero_sem)

    def zeros():
        fresh[...] = jnp.zeros_like(fresh)
        all_zero.start()

    pl.when(jnp.logical_not(last))(zeros)
    small[...] = jnp.zeros_like(small)
    pick_row = picks[pl.ds(par, 1), :]
    pick_col = column(pick_row, PICKS)

    def choose():
        ids = lax.broadcasted_iota(jnp.int32, (PICKS, SP), 1)
        mine[...] = nn(jnp.where(ids == pick_col, 1.0, 0.0).astype(BF16), y[...]).astype(BF16)

    pl.when(upper)(choose)
    pl.when(sec == 2)(greet_second)
    pl.when(last)(greet_third)

    def rows(p, zz, lane):
        return pl.ds(pl.multiple_of((2 * (2 * zz + lane) + p) * PICKS, PICKS), PICKS)

    def pick_to(k):
        zz = lax.rem(z + k, 4)
        return pltpu.make_async_remote_copy(
            src_ref=mine,
            dst_ref=picked.at[rows(par, z, c)],
            send_sem=pick_send,
            recv_sem=pick_recv.at[par, z],
            device_id=(3, 2 * zz + c),
            device_id_type=MESH,
        )

    def came(p, k):
        zz = lax.rem(z + k, 4)
        return pltpu.make_async_remote_copy(
            src_ref=mine,
            dst_ref=picked.at[rows(p, zz, c)],
            send_sem=pick_send,
            recv_sem=pick_recv.at[p, zz],
            device_id=other_core,
            device_id_type=MESH,
        )

    def forward(p, k):
        part = picked.at[rows(p, lax.rem(z + k, 4), c)]
        return pltpu.make_async_remote_copy(
            src_ref=part,
            dst_ref=part,
            send_sem=core_send,
            recv_sem=core_recv,
            device_id=other_core,
            device_id_type=MESH,
        )

    def span(ref, count, send, recv):
        part = ref.at[pl.ds(0, count)]
        return pltpu.make_async_remote_copy(
            src_ref=part,
            dst_ref=part,
            send_sem=send,
            recv_sem=recv,
            device_id=other_core,
            device_id_type=MESH,
        )

    def pick_second():
        for k in (1, 2, 3, 0):
            pick_to(k).start()

    def pick_third():
        own = pltpu.make_async_copy(mine, picked.at[rows(1, z, c)], own_sem)
        own.start()
        for k in range(1, 4):
            pick_to(k).start()
        for e in range(8):
            for p in range(2):
                at = pl.ds((2 * e + p) * PICKS, PICKS)
                labels[at, :] = column(info[e, 2 + p : 3 + p, :][:, :PICKS], PICKS)
                counts[at, :] = column(info[e, 4 + p : 5 + p, :][:, :PICKS].astype(F32), PICKS)
        own.wait()
        forward(1, 0).start()
        for k in range(4):
            came(0, k).wait_recv()
            forward(0, k).start()
            if k:
                came(1, k).wait_recv()
                forward(1, k).start()
        span(picked, 8 * PICKS, core_send, core_recv).wait_recv()

    pl.when(sec == 2)(pick_second)
    pl.when(last)(pick_third)
    g_f = gain[...].astype(F32)[0:1]
    own = OWN
    tiles = [(t * HEAD_T, HEAD_T) for t in range(own // HEAD_T)] + [
        (own - own % HEAD_T, own % HEAD_T)
    ]

    def over_tiles(body):
        def step(t, carry):
            body(pl.multiple_of(t * HEAD_T, HEAD_T), HEAD_T)
            return carry

        lax.fori_loop(0, own // HEAD_T, step, 0, unroll=True)
        body(own - own % HEAD_T, own % HEAD_T)

    def forward_part():
        af[...] = rms_scale(picked[...].astype(F32), g_f).astype(BF16)
        fold = lambda op, block: functools.reduce(
            op, [block[:, k * 128 : (k + 1) * 128] for k in range(block.shape[1] // 128)]
        )
        top = daf.at[:, pl.ds(0, 128)]
        top[...] = jnp.full((16 * PICKS, 128), NEG, F32)

        def product(start, size):
            ids = lax.broadcasted_iota(jnp.int32, (16 * PICKS, size), 1) + (dp * own + start)
            block = nt(af[...], table[pl.ds(start, size), :])
            block = jnp.where(ids < VOCAB, block, NEG)
            scores[:, pl.ds(start, size)] = block
            top[...] = jnp.maximum(top[...], fold(jnp.maximum, block))

        over_tiles(product)
        top_col = jnp.max(top[...], axis=1, keepdims=True)
        total = daf.at[:, pl.ds(128, 128)]
        target = daf.at[:, pl.ds(256, 128)]
        total[...] = jnp.zeros((16 * PICKS, 128), F32)
        target[...] = jnp.zeros((16 * PICKS, 128), F32)

        def exponents(start, size):
            ids = lax.broadcasted_iota(jnp.int32, (16 * PICKS, size), 1) + (dp * own + start)
            block = scores[:, pl.ds(start, size)]
            grown = jnp.exp(block - top_col)
            scores[:, pl.ds(start, size)] = grown
            total[...] += fold(jnp.add, grown)
            target[...] += fold(jnp.add, jnp.where(ids == labels[...], block, 0.0))

        over_tiles(exponents)
        stat[...] = jnp.zeros_like(stat)
        columns = (
            top_col,
            jnp.sum(total[...], axis=1, keepdims=True),
            jnp.sum(target[...], axis=1, keepdims=True),
        )
        for k, values in enumerate(columns):
            for i, row in enumerate(as_rows(values)):
                stat[4 * k + i : 4 * k + i + 1, :] = row
        stats[dp] = stat[...]
        for k in range(1, 8):
            pltpu.make_async_remote_copy(
                src_ref=stat,
                dst_ref=stats.at[dp],
                send_sem=stat_send,
                recv_sem=stat_recv,
                device_id=(3, lax.rem(dp + k, 8)),
                device_id_type=MESH,
            ).start()
        every = span(stats, 7, stat_send, stat_recv)
        every.wait_recv()
        tops = [stats[e, 0:4, :] for e in range(8)]
        best = functools.reduce(jnp.maximum, tops)
        sums = sum(stats[e, 4:8, :] * jnp.exp(tops[e] - best) for e in range(8))
        hits = sum(stats[e, 8:12, :] for e in range(8))
        log_total = best + jnp.log(sums)
        log_col = jnp.concatenate([column(log_total[k : k + 1], 128) for k in range(4)], axis=0)
        hit_col = jnp.concatenate([column(hits[k : k + 1], 128) for k in range(4)], axis=0)
        loss = jnp.sum(
            jnp.where(counts[...] > 0, log_col - hit_col, 0.0), axis=0, keepdims=True
        )
        lane = lax.broadcasted_iota(jnp.int32, (1, 128), 1)
        number = jnp.sum(counts[...], axis=0, keepdims=True)
        pair = jnp.where(lane == 0, loss, jnp.where(lane == 1, number, 0.0))
        small[6:7, :] = jnp.where(dp == 0, pair, 0.0)
        shrink = jnp.exp(top_col - log_col)

        def slopes(start, size):
            ids = lax.broadcasted_iota(jnp.int32, (16 * PICKS, size), 1) + (dp * own + start)
            hit = jnp.where(ids == labels[...], 1.0, 0.0)
            block = (scores[:, pl.ds(start, size)] * shrink - hit) * counts[...]
            dlow[:, pl.ds(start, size)] = block.astype(BF16)

        over_tiles(slopes)
        for b in range(3):
            cols = pl.ds(b * 256, 256)
            daf[:, cols] = nn(dlow[...], table[:, cols])
        every.wait_send()
        span(picked, 3 * PICKS, pick_send, core_recv).wait_send()
        span(picked, 8 * PICKS, core_send, core_recv).wait_send()

    def swap(p, zz):
        return pltpu.make_async_remote_copy(
            src_ref=daf.at[rows(p, zz, 1 - c)],
            dst_ref=rx_core.at[pl.ds((2 * zz + p) * PICKS, PICKS)],
            send_sem=swap_send,
            recv_sem=swap_recv,
            device_id=other_core,
            device_id_type=MESH,
        )

    def back_to(p, k):
        zz = lax.rem(z + k, 4)
        return pltpu.make_async_remote_copy(
            src_ref=low.at[pl.ds(pl.multiple_of((2 * zz + p) * PICKS, PICKS), PICKS)],
            dst_ref=rx.at[z],
            send_sem=daf_send,
            recv_sem=daf_recv,
            device_id=(2 + p, 2 * zz + c),
            device_id_type=MESH,
        )

    def table_part(start, size):
        there = pl.ds(start, size)
        value = tn(dlow[:, there], af[...])
        fresh[there, :] = value
        pltpu.make_async_copy(fresh.at[there], d_table.at[there], zero_sem).start()
        folded = jnp.sum(value * value, axis=0, keepdims=True)
        small[7:8, :] += functools.reduce(
            jnp.add, [folded[:, k * 128 : (k + 1) * 128] for k in range(6)]
        )

    def third():
        forward_part()
        for zz in range(4):
            for p in range(2):
                swap(p, zz).start()
        table_part(own - own % HEAD_T, own % HEAD_T)
        span(rx_core, 8 * PICKS, swap_send, swap_recv).wait_recv()
        for zz in range(4):
            for p in range(2):
                there = pl.ds((2 * zz + p) * PICKS, PICKS)
                low[there, :] = (daf[rows(p, zz, c), :] + rx_core[there, :]).astype(BF16)
        for k in (1, 2, 3, 0):
            back_to(0, k).start()
            if k:
                back_to(1, k).start()

        def step(t, carry):
            table_part(pl.multiple_of(t * HEAD_T, HEAD_T), HEAD_T)
            return carry

        lax.fori_loop(0, own // HEAD_T, step, 0, unroll=True)
        rx[z] = low[pl.ds(pl.multiple_of((2 * z + 1) * PICKS, PICKS), PICKS), :]
        span(rx_core, 8 * PICKS, swap_send, swap_recv).wait_send()
        span(low, 7 * PICKS, daf_send, daf_recv).wait_send()
        span(rx, 3, daf_send, daf_recv).wait_recv()

    def second():
        span(picked, 4 * PICKS, pick_send, core_recv).wait_send()
        span(rx, 4, daf_send, daf_recv).wait_recv()

    pl.when(last)(third)
    pl.when(sec == 2)(second)

    def finish():
        summed = rx[0].astype(F32)
        for k in range(1, 4):
            summed = summed + rx[k].astype(F32)
        grad, dg_f = rms_back(mine[...].astype(F32), g_f, summed)
        for k in range(6):
            small[k : k + 1, :] = dg_f[:, k * 128 : (k + 1) * 128]
        ids = lax.broadcasted_iota(jnp.int32, (SP, PICKS), 0)
        spread = jnp.where(ids == pick_row, 1.0, 0.0).astype(BF16)
        rest = grad
        out = jnp.zeros((SP, D), F32)
        for _ in range(3):
            part = rest.astype(BF16)
            out = out + nn(spread, part)
            rest = rest - part.astype(F32)
        d_top[...] = out.astype(BF16)

    def none():
        d_top[...] = jnp.zeros_like(d_top)

    pl.when(upper)(finish)
    pl.when(jnp.logical_not(upper))(none)
    all_zero.wait()


def head_call(y, picks, info, gain, table):
    low = lambda *shape: pltpu.VMEM(shape, BF16)
    wide = lambda *shape: pltpu.VMEM(shape, F32)
    n = 16 * PICKS
    return pl.pallas_call(
        head_kernel,
        out_shape=(
            jax.ShapeDtypeStruct((SP, D), BF16),
            jax.ShapeDtypeStruct((OWN, D), F32),
            jax.ShapeDtypeStruct((8, 128), F32),
        ),
        in_specs=[VMEM] * 5,
        out_specs=(VMEM, ANY, VMEM),
        scratch_shapes=[
            low(PICKS, D),
            low(n, D),
            low(n, D),
            wide(n, OWN),
            low(n, OWN),
            pltpu.VMEM((n, 1), jnp.int32),
            wide(n, 1),
            wide(16, 128),
            wide(8, 16, 128),
            wide(n, D),
            wide(8 * PICKS, D),
            low(8 * PICKS, D),
            low(4, PICKS, D),
            wide(OWN, D),
            pltpu.SemaphoreType.DMA,
            pltpu.SemaphoreType.DMA,
            pltpu.SemaphoreType.DMA,
            pltpu.SemaphoreType.DMA((2, 4)),
        ]
        + [pltpu.SemaphoreType.DMA] * 8,
        compiler_params=pltpu.CompilerParams(
            collective_id=3, has_side_effects=True, vmem_limit_bytes=56 * 2**20
        ),
        name="head",
    )(y, picks, info, gain, table)


def open_anywhere(codes, labels, picks, classes, null_mask, starts, table, frequency):
    sec = lax.axis_index("section")
    d = lax.axis_index("dp")
    par = lax.rem(sec, 2)
    own = table.shape[0]
    row_index, counted, _, position = jax.vmap(row_layout)(starts, classes, null_mask, codes)
    picked_labels = jnp.take_along_axis(labels, picks, axis=1)
    picked_counts = jnp.take_along_axis(counted, picks, axis=1).astype(jnp.int32)
    row_index = jnp.pad(row_index, ((0, 0), (0, SP - SLOTS)), constant_values=-1)
    info = jnp.concatenate([row_index, picked_labels, picked_counts], axis=1)
    info = lax.all_gather(info, "dp", axis=0, tiled=True)
    all_labels = info[:, SP : SP + PICKS].reshape(-1)
    all_counts = info[:, SP + PICKS :].reshape(-1).astype(F32)
    gain_row = lax.slice_in_dim(table, VOCAB % own, VOCAB % own + 1)[0].astype(F32)
    holds = (sec == 3) & (d == VOCAB // own)
    g_f = lax.psum(jnp.where(holds, gain_row, 0.0), ("section", "dp"))
    position = jnp.pad(position[par], (0, SP - SLOTS))
    angles = position.astype(F32)[:, None] * frequency[None, :]
    cosine = jnp.tile(jnp.cos(angles), (1, 4))
    sine = jnp.tile(jnp.concatenate([-jnp.sin(angles), jnp.sin(angles)], axis=1), (1, 2))
    gathered = lax.all_gather(table, "dp", axis=0, tiled=True)[:WROWS]
    other = lax.ppermute(gathered, "section", [(0, 1), (1, 0), (2, 3), (3, 2)])
    weights = jnp.where((sec == 1) | (sec == 2), gathered, other)
    local = jnp.where(sec == 0, info[:, :SP].reshape(-1), -1) - d * own
    onehot = (local[:, None] == jnp.arange(own)[None, :]).astype(BF16)
    looked = (nn(onehot, table) * math.sqrt(D)).astype(BF16)
    looked = lax.psum_scatter(looked, "dp", scatter_dimension=0, tiled=True).reshape(2, SP, D)
    from_first = lax.ppermute(looked[1], "section", [(0, 1)])
    x0 = jnp.where(sec == 0, looked[0], from_first)
    return weights, x0, local, all_labels, all_counts, g_f, cosine, sine


def head_anywhere(y, my_picks, all_labels, all_counts, g_f, table):
    sec = lax.axis_index("section")
    d = lax.axis_index("dp")
    n_sec = lax.axis_size("section")
    n_dp = lax.axis_size("dp")
    own = table.shape[0]
    picked = jnp.take(y, my_picks, axis=0)
    all_picked = lax.all_gather(picked, ("section", "dp"), axis=0, tiled=False)
    all_picked = all_picked.reshape(n_sec, n_dp, PICKS, D)[2:].transpose(1, 0, 2, 3)
    all_picked = all_picked.reshape(-1, D).astype(F32)
    af = jnp.where(sec == 3, rms_scale(all_picked, g_f), 0.0).astype(BF16)
    vocab_ids = d * own + jnp.arange(own)
    logits = jnp.where(vocab_ids[None, :] < VOCAB, nt(af, table), NEG)
    local_max = jnp.max(logits, axis=1)
    hit = vocab_ids[None, :] == all_labels[:, None]
    sums = jnp.stack(
        [
            local_max,
            jnp.sum(jnp.exp(logits - local_max[:, None]), axis=1),
            jnp.sum(jnp.where(hit, logits, 0.0), axis=1),
        ]
    )
    every = lax.all_gather(sums, "dp", axis=0, tiled=False)
    top = jnp.max(every[:, 0], axis=0)
    total = jnp.sum(every[:, 1] * jnp.exp(every[:, 0] - top), axis=0)
    target = jnp.sum(every[:, 2], axis=0)
    log_total = top + jnp.log(total)
    loss_part = jnp.where(
        (sec == 3) & (d == 0), jnp.sum(jnp.where(all_counts > 0, log_total - target, 0.0)), 0.0
    )
    dlogits = (jnp.exp(logits - log_total[:, None]) - hit.astype(F32)) * all_counts[:, None]
    dlogits = jnp.where(sec == 3, dlogits, 0.0).astype(BF16)
    d_table = tn(dlogits, af)
    daf = lax.psum(nn(dlogits, table), "dp")
    daf = lax.dynamic_slice_in_dim(daf, d * 2 * PICKS, 2 * PICKS).reshape(2, PICKS, D)
    daf = jnp.where(sec == 3, daf[1], lax.ppermute(daf[0], "section", [(3, 2)]))
    d_own, dg_f = rms_pull(picked.astype(F32), g_f, daf)
    dg_f = jnp.where(sec >= 2, dg_f, 0.0)
    spread = (jnp.arange(SP)[:, None] == my_picks[None, :]).astype(F32)
    d_top = jnp.dot(spread, d_own, precision=lax.Precision.HIGHEST).astype(BF16)
    return d_top, d_table, dg_f, loss_part


UPDATE_ROWS = 272


def update_kernel(rate, gain_block, gain_row, totals, grad, master, momentum, average, out_m, out_v, out_a):
    block = pl.program_id(0)
    value = grad[...]
    sec = lax.axis_index("section")
    dp = lax.axis_index("dp")
    here = jnp.logical_and(jnp.logical_and(sec == 3, dp == VOCAB // OWN), block == gain_block)
    ids = lax.broadcasted_iota(jnp.int32, value.shape, 0)
    gain = jnp.concatenate([totals[k : k + 1, :] for k in range(6)], axis=1)
    value = value + jnp.where(jnp.logical_and(ids == gain_row, here), gain, 0.0)
    scale = jnp.minimum(1.0, clip_limit / (totals[8:9, 0:1] + norm_eps))
    clipped = value * scale
    new_momentum = momentum_decay * momentum[...] + clipped
    new_master = master[...] - rate * (clipped + momentum_decay * new_momentum)
    out_v[...] = new_momentum
    out_m[...] = new_master
    out_a[...] = average_decay * average[...] + (1.0 - average_decay) * new_master


def update(rate, totals, grad, master, momentum, average):
    rows = pl.BlockSpec((UPDATE_ROWS, D), lambda i: (i, 0))
    like = jax.ShapeDtypeStruct((OWN, D), F32)
    at = VOCAB % OWN
    return pl.pallas_call(
        functools.partial(update_kernel, rate, at // UPDATE_ROWS, at % UPDATE_ROWS),
        grid=(OWN // UPDATE_ROWS,),
        out_shape=(like, like, like),
        in_specs=[pl.BlockSpec((16, 128), lambda i: (0, 0))] + [rows] * 4,
        out_specs=(rows, rows, rows),
        compiler_params=pltpu.CompilerParams(vmem_limit_bytes=47 * 2**20),
        name="update",
    )(totals, grad, master, momentum, average)


def shards(codes, labels, picks, classes, null_mask, starts, master, momentum, average):
    sec = lax.axis_index("section")
    d = lax.axis_index("dp")
    n_dp = lax.axis_size("dp")
    n_sec = lax.axis_size("section")
    par = lax.rem(sec, 2)
    own = master.shape[0]
    learn_rate = rate_factor * math.sqrt(own * n_sec * n_dp)
    beside = [(0, 1), (1, 0), (2, 3), (3, 2)]
    fast = n_sec == 4 and n_dp == 8 and own == OWN
    gain_at = VOCAB // own
    frequency = rope_base ** (-jnp.arange(HD // 2, dtype=F32) * 2.0 / HD)

    if fast:
        wide = jnp.tile(frequency[None, :], (1, 4))
        weights, x0, info, gain, cosine, sine, table = gather_and_embed(
            master, codes, labels, picks, starts, classes, null_mask, wide
        )
    else:
        table = master.astype(BF16)
        opened = open_anywhere(codes, labels, picks, classes, null_mask, starts, table, frequency)
        weights, x0, local, all_labels, all_counts, g_f, cosine, sine = opened
    around = (cosine, sine, starts)

    x = forward_call(False, x0, weights, *around)[0]
    y, *kept = forward_call(True, x, weights, *around)

    if fast:
        d_top, d_table, small = head_call(y, picks, info, gain, table)
    else:
        d_top, d_table, dg_f, loss_part = head_anywhere(
            y, picks[par], all_labels, all_counts, g_f, table
        )

    once = backward_call(True, d_top, x, weights, *around, kept)
    dx0, left, right, tail = lax.cond(
        sec < 2,
        lambda: tuple(backward_call(False, once[0], x, weights, *around, kept)),
        lambda: tuple(once),
    )

    if fast:
        grad, squares = reduce_and_scatter(left, right, tail, d_table, dx0, info)
        totals = share_norm(small, squares, n_sec, n_dp)
        updated = update(learn_rate, totals, grad, master, momentum, average)
        return totals[6, 0], totals[6, 1], totals[8, 0], *updated
    else:
        grads = matrix_gradients(left, right, tail)
        grads = grads.astype(F32) + lax.ppermute(grads, "section", beside).astype(F32)
        grads = jnp.pad(grads.astype(BF16), ((0, own * n_dp - WROWS), (0, 0)))
        grad = lax.psum_scatter(grads, "dp", scatter_dimension=0, tiled=True).astype(F32)
        grad = jnp.where(sec == 3, d_table, grad)
        pair = jnp.stack([dx0, lax.ppermute(dx0, "section", [(1, 0)])])
        all_dx = lax.all_gather(pair, "dp", axis=0, tiled=True).reshape(-1, D)
        onehot = (jnp.arange(own)[:, None] == local[None, :]).astype(BF16)
        grad = jnp.where(sec == 0, nn(onehot, all_dx) * math.sqrt(D), grad)
        totals = (dg_f, jnp.sum(grad * grad), loss_part)
        dg_f, squares, loss_sum = lax.psum(totals, ("section", "dp"))
        count_sum = jnp.sum(all_counts)
        grad_norm = jnp.sqrt(squares + jnp.sum(dg_f * dg_f))
    gain_here = (jnp.arange(own) == VOCAB % own)[:, None] & (sec == 3) & (d == gain_at)
    grad = grad + jnp.where(gain_here, dg_f[None, :], 0.0)
    clipped = grad * jnp.minimum(1.0, clip_limit / (grad_norm + norm_eps))
    new_momentum = momentum_decay * momentum + clipped
    new_master = master - learn_rate * (clipped + momentum_decay * new_momentum)
    new_average = average_decay * average + (1.0 - average_decay) * new_master
    return loss_sum, count_sum, grad_norm, new_master, new_momentum, new_average


def solution(mesh):
    split = P("dp", None)
    whole = P(("section", "dp"), None)
    return jax.shard_map(
        shards,
        mesh=mesh,
        in_specs=(split,) * 6 + (whole,) * 3,
        out_specs=(P(), P(), P(), whole, whole, whole),
        check_vma=False,
    )
```
